32 devices in a mesh: dp: 8 (over z, x), fsdp: 4 (over y, core).
Axes of the slice: x: 2, y: 2, z: 4, core: 2. Of those that a mesh axis runs over, the one named last changes fastest.
Arguments:
- patches: bfloat16 [256, 100, 1024], P(('dp', 'fsdp')), may hold values from -6 to 6
- cotangent: bfloat16 [256, 100, 1024], P(('dp', 'fsdp')), may hold values from -6 to 6
- pad_mask: int32 [256, 100], P(('dp', 'fsdp')), may hold values from 0 to 1, as said below
- attend_weight: float32 [1024, 3072], P(('dp', 'fsdp'))
- attend_first: float32 [1024, 3072], P(('dp', 'fsdp'))
- attend_second: float32 [1024, 3072], P(('dp', 'fsdp')), may hold values from 1.9868215e-13 to 7.947286e-13
- output_weight: float32 [1024, 1024], P(('dp', 'fsdp'))
- output_first: float32 [1024, 1024], P(('dp', 'fsdp'))
- output_second: float32 [1024, 1024], P(('dp', 'fsdp')), may hold values from 1.9868215e-13 to 7.947286e-13
- expand_weight: float32 [1024, 4096], P(('dp', 'fsdp'))
- expand_first: float32 [1024, 4096], P(('dp', 'fsdp'))
- expand_second: float32 [1024, 4096], P(('dp', 'fsdp')), may hold values from 1.9868215e-13 to 7.947286e-13
- shrink_weight: float32 [4096, 1024], P(('dp', 'fsdp'))
- shrink_first: float32 [4096, 1024], P(('dp', 'fsdp'))
- shrink_second: float32 [4096, 1024], P(('dp', 'fsdp')), may hold values from 1.9868215e-13 to 7.947286e-13
- vector_params: float32 [12, 1024], replicated
- vector_first: float32 [12, 1024], replicated, may hold values from -9.536743e-06 to 9.536743e-06
- vector_second: float32 [12, 1024], replicated, may hold values from 1.9868215e-13 to 7.947286e-13
- position_table: float32 [361, 32], replicated, may hold values from -5 to 5
- table_first: float32 [361, 32], replicated, may hold values from -9.536743e-06 to 9.536743e-06
- table_second: float32 [361, 32], replicated, may hold values from 1.9868215e-13 to 7.947286e-13
Outputs:
- block_out: bfloat16 [256, 100, 1024], P(('dp', 'fsdp'))
- input_grad: float32 [256, 100, 1024], P(('dp', 'fsdp'))
- attend_grad: float32 [1024, 3072], P(('dp', 'fsdp'))
- attend_first_new: float32 [1024, 3072], P(('dp', 'fsdp'))
- attend_second_new: float32 [1024, 3072], P(('dp', 'fsdp'))
- attend_new: float32 [1024, 3072], P(('dp', 'fsdp'))
- attend_copy: bfloat16 [1024, 3072], P(('dp', 'fsdp'))
- output_grad: float32 [1024, 1024], P(('dp', 'fsdp'))
- output_first_new: float32 [1024, 1024], P(('dp', 'fsdp'))
- output_second_new: float32 [1024, 1024], P(('dp', 'fsdp'))
- output_new: float32 [1024, 1024], P(('dp', 'fsdp'))
- output_copy: bfloat16 [1024, 1024], P(('dp', 'fsdp'))
- expand_grad: float32 [1024, 4096], P(('dp', 'fsdp'))
- expand_first_new: float32 [1024, 4096], P(('dp', 'fsdp'))
- expand_second_new: float32 [1024, 4096], P(('dp', 'fsdp'))
- expand_new: float32 [1024, 4096], P(('dp', 'fsdp'))
- expand_copy: bfloat16 [1024, 4096], P(('dp', 'fsdp'))
- shrink_grad: float32 [4096, 1024], P(('dp', 'fsdp'))
- shrink_first_new: float32 [4096, 1024], P(('dp', 'fsdp'))
- shrink_second_new: float32 [4096, 1024], P(('dp', 'fsdp'))
- shrink_new: float32 [4096, 1024], P(('dp', 'fsdp'))
- shrink_copy: bfloat16 [4096, 1024], P(('dp', 'fsdp'))
- vector_grad: float32 [12, 1024], replicated
- vector_first_new: float32 [12, 1024], replicated
- vector_second_new: float32 [12, 1024], replicated
- vector_new: float32 [12, 1024], replicated
- table_grad: float32 [361, 32], replicated
- table_first_new: float32 [361, 32], replicated
- table_second_new: float32 [361, 32], replicated
- table_new: float32 [361, 32], replicated
- clip_norm: float32 [], replicated
- matrix_norms: float32 [2, 4], replicated
The draws below stay inside these ranges and needn't reach their ends.
Inputs may be any that keep to these rules, and one draw needn't show every extreme that they name: `pad_mask`: patch 0 of every window is 1.
All inputs are finite; a program needn't handle non-finite values.
Results may differ from the reference program's by a relative error of at most 0.013.
The reference program's roundings to bfloat16 on the way count: a program that leaves them out, or rounds other values in their place, can miss the bound.
Values may be sent and summed in bfloat16 or wider, within the bound.
A program may use at most 256 MiB of HBM per device.

```python
import math
import jax
import jax.numpy as jnp
from jax import lax

D = 1024
HEADS = 32
FF = 4096
WS = 10
WIN_DEV = 8
STEP = 10
WP = 100
NREL = 361
ROWS_SMALL = 12
WINDOWS = 256
P_ALL = 12582912
N_DP = 8
N_FSDP = 4


def rising_rows(noise, low_end, high_end, fan_in):
    count = noise.shape[0]
    place = jnp.arange(count, dtype=jnp.float32) / max(count - 1, 1)
    factor = low_end + (high_end - low_end) * place
    return noise * factor[:, None] * fan_in ** (-0.5)


def rising_moment(noise, low_end, high_end):
    count = noise.shape[0]
    place = jnp.arange(count, dtype=jnp.float32) / max(count - 1, 1)
    factor = low_end + (high_end - low_end) * place
    return noise * factor[:, None] * (0.0056 * P_ALL ** (-0.5))


def draw_pad_mask(key, part):
    key = jax.random.fold_in(key, 5)
    window = jnp.arange(WINDOWS, dtype=jnp.int32)
    device = window // WIN_DEV
    inner = device % N_FSDP
    outer = device // N_FSDP
    permille = 150 + 300 * inner // max(N_FSDP - 1, 1) + 300 * outer // max(N_DP - 1, 1)
    roll = jax.random.randint(key, (WINDOWS, WP), 0, 1000)
    filled = (roll < permille[:, None]).astype(jnp.int32)
    first = (jnp.arange(WP, dtype=jnp.int32) == 0)[None, :]
    return jnp.where(first, 1, filled).astype(jnp.int32)


def draw_attend_weight(key, part):
    key = jax.random.fold_in(key, 11)
    noise = jax.random.normal(key, (D, 3 * D), jnp.float32)
    return rising_rows(noise, 0.6, 1.8, D)


def draw_output_weight(key, part):
    key = jax.random.fold_in(key, 13)
    noise = jax.random.normal(key, (D, D), jnp.float32)
    return rising_rows(noise, 0.6, 1.8, D // 8)


def draw_expand_weight(key, part):
    key = jax.random.fold_in(key, 17)
    noise = jax.random.normal(key, (D, FF), jnp.float32)
    return rising_rows(noise, 0.6, 1.8, D)


def draw_shrink_weight(key, part):
    key = jax.random.fold_in(key, 19)
    noise = jax.random.normal(key, (FF, D), jnp.float32)
    return rising_rows(noise, 0.6, 1.8, FF // 4)


def draw_attend_first(key, part):
    key = jax.random.fold_in(key, 31)
    noise = jnp.clip(jax.random.normal(key, (D, 3 * D), jnp.float32), -4.0, 4.0)
    return rising_moment(noise, 0.4, 2.0)


def draw_output_first(key, part):
    key = jax.random.fold_in(key, 37)
    noise = jnp.clip(jax.random.normal(key, (D, D), jnp.float32), -4.0, 4.0)
    return rising_moment(noise, 0.4, 2.0)


def draw_expand_first(key, part):
    key = jax.random.fold_in(key, 41)
    noise = jnp.clip(jax.random.normal(key, (D, FF), jnp.float32), -4.0, 4.0)
    return rising_moment(noise, 0.4, 2.0)


def draw_shrink_first(key, part):
    key = jax.random.fold_in(key, 43)
    noise = jnp.clip(jax.random.normal(key, (FF, D), jnp.float32), -4.0, 4.0)
    return rising_moment(noise, 0.4, 2.0)


def pack_rows(gains, shifts):
    row = jnp.arange(ROWS_SMALL, dtype=jnp.int32)[:, None]
    packed = jnp.where(row == 0, gains[0][None, :], shifts)
    return jnp.where(row == 5, gains[1][None, :], packed)


def draw_vector_params(key, part):
    key = jax.random.fold_in(key, 23)
    gain_key, shift_key = jax.random.split(key)
    place = jnp.arange(D, dtype=jnp.float32) / max(D - 1, 1)
    wobble = jax.random.normal(gain_key, (2, D), jnp.float32)
    gains = (0.5 + place)[None, :] * (1.0 + 0.15 * jnp.clip(wobble, -2.5, 2.5))
    shifts = 0.3 * jax.random.normal(shift_key, (ROWS_SMALL, D), jnp.float32)
    return pack_rows(gains, shifts)


def levels(key, shape, cuts, low, top_value):
    level = 1.0
    for dim, blocks in cuts:
        draws = jax.random.uniform(jax.random.fold_in(jax.random.fold_in(key, 6), dim), (blocks,), jnp.float32, low / len(cuts), top_value / len(cuts))
        level = level * jnp.repeat(jnp.exp(draws), shape[dim] // blocks).reshape((-1,) + (1,) * (len(shape) - 1 - dim))
    return level


def centred(rng, dims, deviation, limit, shards=(), kind=jnp.bfloat16):
    values = deviation * jax.random.normal(rng, dims, jnp.float32)
    if shards:
        values = values * levels(rng, dims, shards, -0.22, 0.18)
    return jnp.clip(values, -limit, limit).astype(kind)


def setup_inputs(seed: int = 0) -> dict:
    key_of = jax.random.split(jax.random.key(seed), 22)
    return {
        "patches": centred(key_of[0], (WINDOWS, WP, D), 1.0, 6.0, ((0, 32),)),
        "cotangent": centred(key_of[1], (WINDOWS, WP, D), 1.0, 6.0, ((0, 32),)),
        "pad_mask": draw_pad_mask(jax.random.fold_in(key_of[21], 71), 0),
        "attend_weight": draw_attend_weight(jax.random.fold_in(key_of[21], 71), 0),
        "attend_first": draw_attend_first(jax.random.fold_in(key_of[21], 71), 0),
        "attend_second": jnp.clip(jnp.exp(math.log(7.947285949987115e-13) - 1.3862944 * jax.random.uniform(key_of[5], (D, 3 * D), jnp.float32) ** levels(key_of[5], (D, 3 * D), ((0, 32),), -0.2, 0.2)), 1.9868214874967788e-13, 7.947285949987115e-13),
        "output_weight": draw_output_weight(jax.random.fold_in(key_of[21], 71), 0),
        "output_first": draw_output_first(jax.random.fold_in(key_of[21], 71), 0),
        "output_second": jnp.clip(jnp.exp(math.log(7.947285949987115e-13) - 1.3862944 * jax.random.uniform(key_of[8], (D, D), jnp.float32) ** levels(key_of[8], (D, D), ((0, 32),), -0.2, 0.2)), 1.9868214874967788e-13, 7.947285949987115e-13),
        "expand_weight": draw_expand_weight(jax.random.fold_in(key_of[21], 71), 0),
        "expand_first": draw_expand_first(jax.random.fold_in(key_of[21], 71), 0),
        "expand_second": jnp.clip(jnp.exp(math.log(7.947285949987115e-13) - 1.3862944 * jax.random.uniform(key_of[11], (D, FF), jnp.float32) ** levels(key_of[11], (D, FF), ((0, 32),), -0.2, 0.2)), 1.9868214874967788e-13, 7.947285949987115e-13),
        "shrink_weight": draw_shrink_weight(jax.random.fold_in(key_of[21], 71), 0),
        "shrink_first": draw_shrink_first(jax.random.fold_in(key_of[21], 71), 0),
        "shrink_second": jnp.clip(jnp.exp(math.log(7.947285949987115e-13) - 1.3862944 * jax.random.uniform(key_of[14], (FF, D), jnp.float32) ** levels(key_of[14], (FF, D), ((0, 32),), -0.2, 0.2)), 1.9868214874967788e-13, 7.947285949987115e-13),
        "vector_params": draw_vector_params(jax.random.fold_in(key_of[21], 71), 0),
        "vector_first": centred(key_of[16], (ROWS_SMALL, D), (0.0056 * P_ALL ** -0.5), 9.5367431640625e-06, (), jnp.float32),
        "vector_second": jnp.clip(jnp.exp(jax.random.uniform(key_of[17], (ROWS_SMALL, D), jnp.float32, math.log(1.9868214874967788e-13), math.log(7.947285949987115e-13))), 1.9868214874967788e-13, 7.947285949987115e-13),
        "position_table": centred(key_of[18], (NREL, HEADS), 1.0, 5.0, (), jnp.float32),
        "table_first": centred(key_of[19], (NREL, HEADS), (0.0056 * P_ALL ** -0.5), 9.5367431640625e-06, (), jnp.float32),
        "table_second": jnp.clip(jnp.exp(jax.random.uniform(key_of[20], (NREL, HEADS), jnp.float32, math.log(1.9868214874967788e-13), math.log(7.947285949987115e-13))), 1.9868214874967788e-13, 7.947285949987115e-13),
    }


EPSILON = 1e-05
MOMENT_ONE = 0.9
MOMENT_TWO = 0.999
LEARN_RATE = 0.3
DECAY = 0.01
ADAM_EPS = 1e-06
CLIP_LIMIT = 0.05
MASK_FILL = 10000.0
HIGH = lax.Precision.HIGHEST

@jax.custom_vjp
def low(v):
    return lax.optimization_barrier(v.astype(jnp.bfloat16)).astype(jnp.float32)

@jax.custom_vjp
def low_back(v):
    return v

def low_keep(v):
    return (low(v), None)

def low_pass(kept, grad):
    return (grad,)

def back_keep(v):
    return (v, None)

def back_low(kept, grad):
    return (low(grad),)
low.defvjp(low_keep, low_pass)
low_back.defvjp(back_keep, back_low)

def position_index(size):
    cells = jnp.arange(size * size, dtype=jnp.int32)
    rows = cells // size
    cols = cells % size
    drow = rows[:, None] - rows[None, :] + size - 1
    dcol = cols[:, None] - cols[None, :] + size - 1
    return (drow * (2 * size - 1) + dcol).astype(jnp.int32)

def normalize(value):
    centre = value - lax.optimization_barrier(jnp.mean(value, axis=-1, keepdims=True))
    spread = lax.rsqrt(lax.optimization_barrier(jnp.mean(centre * centre, axis=-1, keepdims=True)) + EPSILON)
    return centre * spread

def forward(source, keep, attend, output, expand, shrink, vectors, table):
    group, cells, width = source.shape
    head_dim = width // HEADS
    hidden_one = low(normalize(source) * vectors[0] + vectors[1])
    joint = jnp.einsum('gpd,de->gpe', hidden_one, attend, precision=HIGH)
    query = low_back(low(joint[..., :width] + vectors[2])).reshape(group, cells, HEADS, head_dim)
    keys = low_back(low(joint[..., width:2 * width])).reshape(group, cells, HEADS, head_dim)
    values = low_back(low(joint[..., 2 * width:] + vectors[3])).reshape(group, cells, HEADS, head_dim)
    bias = table[position_index(WS)].transpose(2, 0, 1)
    scores = jnp.einsum('gihd,gjhd->ghij', query, keys, precision=HIGH) * head_dim ** (-0.5)
    scores = scores + bias[None] + (keep[:, None, None, :] - 1.0) * MASK_FILL
    scores = low_back(scores)
    probs = jax.nn.softmax(scores, axis=-1)
    attended = jnp.einsum('ghij,gjhd->gihd', low(probs), values, precision=HIGH).reshape(group, cells, width)
    attended = low_back(low(attended))
    branch = low_back(jnp.einsum('gpd,de->gpe', attended, output, precision=HIGH) + vectors[4])
    middle = source + branch
    hidden_two = low(normalize(middle) * vectors[5] + vectors[6])
    before = jnp.einsum('gpd,df->gpf', hidden_two, expand, precision=HIGH) + vectors[8:].reshape(-1)
    before = low_back(before)
    activated = low(jax.nn.gelu(before, approximate=False))
    return middle + jnp.einsum('gpf,fd->gpd', activated, shrink, precision=HIGH) + vectors[7]

def moments(grad, first, second, weight, factor):
    clipped = grad * factor
    first_new = MOMENT_ONE * first + (1.0 - MOMENT_ONE) * clipped
    second_new = MOMENT_TWO * second + (1.0 - MOMENT_TWO) * clipped * clipped
    update = first_new / (1.0 - MOMENT_ONE ** STEP) / (jnp.sqrt(second_new / (1.0 - MOMENT_TWO ** STEP)) + ADAM_EPS) + DECAY * weight
    return (first_new, second_new, update)

def reference(patches, cotangent, pad_mask, attend_weight, attend_first, attend_second, output_weight, output_first, output_second, expand_weight, expand_first, expand_second, shrink_weight, shrink_first, shrink_second, vector_params, vector_first, vector_second, position_table, table_first, table_second):
    keep = pad_mask.astype(jnp.float32)
    total = jnp.sum(keep)
    masters = (attend_weight, output_weight, expand_weight, shrink_weight)
    copies = tuple((low(m) for m in masters))
    group = 2 * WIN_DEV
    width = patches.shape[2]
    source_all = patches.astype(jnp.float32).reshape(-1, group, WP, width)
    keep_all = keep.reshape(-1, group, WP)
    back_all = cotangent.astype(jnp.float32).reshape(-1, group, WP, width)

    def step(carry, item):
        source, keep_part, back = item

        def apply(xv, a, b, c, d, vec, tab):
            return forward(xv, keep_part, a, b, c, d, vec, tab)
        result, pull = jax.vjp(apply, source, copies[0], copies[1], copies[2], copies[3], vector_params, position_table)
        grads = pull(back * keep_part[..., None])
        carry = tuple((c + g for c, g in zip(carry, grads[1:])))
        return (carry, (result.astype(jnp.bfloat16), grads[0]))
    start = tuple((jnp.zeros(a.shape, jnp.float32) for a in (attend_weight, output_weight, expand_weight, shrink_weight, vector_params, position_table)))
    sums, (outputs, input_grads) = lax.scan(step, start, (source_all, keep_all, back_all))
    block_out = outputs.reshape(patches.shape)
    input_grad = input_grads.reshape(patches.shape) / total
    grads = tuple((g / total for g in sums))
    squares = sum((jnp.sum(g * g) for g in grads))
    clip_norm = jnp.sqrt(squares)
    factor = jnp.minimum(1.0, CLIP_LIMIT / clip_norm)
    firsts = (attend_first, output_first, expand_first, shrink_first)
    seconds = (attend_second, output_second, expand_second, shrink_second)
    matrix_outs = []
    weight_norms = []
    update_norms = []
    for index in range(4):
        first_new, second_new, update = moments(grads[index], firsts[index], seconds[index], masters[index], factor)
        weight_norm = jnp.sqrt(jnp.sum(masters[index] * masters[index]))
        update_norm = jnp.sqrt(jnp.sum(update * update))
        fresh = masters[index] - LEARN_RATE * (weight_norm / update_norm) * update
        matrix_outs.append((grads[index], first_new, second_new, fresh, fresh.astype(jnp.bfloat16)))
        weight_norms.append(weight_norm)
        update_norms.append(update_norm)
    vec_first, vec_second, vec_update = moments(grads[4], vector_first, vector_second, vector_params, factor)
    vec_ratio = jnp.sqrt(lax.optimization_barrier(jnp.sum(vector_params * vector_params, axis=1, keepdims=True))) / jnp.sqrt(lax.optimization_barrier(jnp.sum(vec_update * vec_update, axis=1, keepdims=True)))
    vec_fresh = vector_params - LEARN_RATE * vec_ratio * vec_update
    tab_first, tab_second, tab_update = moments(grads[5], table_first, table_second, position_table, factor)
    tab_ratio = jnp.sqrt(jnp.sum(position_table * position_table)) / jnp.sqrt(jnp.sum(tab_update * tab_update))
    tab_fresh = position_table - LEARN_RATE * tab_ratio * tab_update
    matrix_norms = jnp.stack([jnp.stack(weight_norms), jnp.stack(update_norms)])
    attend_o, output_o, expand_o, shrink_o = matrix_outs
    return (block_out, input_grad, attend_o[0], attend_o[1], attend_o[2], attend_o[3], attend_o[4], output_o[0], output_o[1], output_o[2], output_o[3], output_o[4], expand_o[0], expand_o[1], expand_o[2], expand_o[3], expand_o[4], shrink_o[0], shrink_o[1], shrink_o[2], shrink_o[3], shrink_o[4], grads[4], vec_first, vec_second, vec_fresh, grads[5], tab_first, tab_second, tab_fresh, clip_norm, matrix_norms)
```

```python
import functools

import jax
import jax.numpy as jnp
from jax import lax
from jax.experimental import pallas as pl
from jax.experimental.pallas import tpu as pltpu
from jax.sharding import PartitionSpec as P

MESH = pl.DeviceIdType.MESH
AXES = ("dp", "fsdp")
VMEM_LIMIT = 60 * 1024 * 1024

HEADS = 32
WS = 10
STEP = 10


EPSILON = 1e-05
MOMENT_ONE = 0.9
MOMENT_TWO = 0.999
LEARN_RATE = 0.3
DECAY = 0.01
ADAM_EPS = 1e-06
CLIP_LIMIT = 0.05
MASK_FILL = 10000.0
HIGH = lax.Precision.HIGHEST


def position_index(size):
    cells = jnp.arange(size * size, dtype=jnp.int32)
    rows = cells // size
    cols = cells % size
    drow = rows[:, None] - rows[None, :] + size - 1
    dcol = cols[:, None] - cols[None, :] + size - 1
    return drow * (2 * size - 1) + dcol


def normalize(value):
    centre = value - jnp.mean(value, axis=-1, keepdims=True)
    spread = lax.rsqrt(jnp.mean(centre * centre, axis=-1, keepdims=True) + EPSILON)
    return (centre * spread, spread)


def norm_back(grad_out, normed, spread, gain):
    scaled = grad_out * gain
    mean_one = jnp.mean(scaled, axis=-1, keepdims=True)
    mean_two = jnp.mean(scaled * normed, axis=-1, keepdims=True)
    return spread * (scaled - mean_one - normed * mean_two)


def gelu_slope(value):
    return (
        0.5 * (1.0 + lax.erf(value * 0.7071067811865476))
        + value * jnp.exp(-0.5 * value * value) * 0.3989422804014327
    )


def inner_product(left, right):
    return lax.dot_general(
        left, right, (((0,), (0,)), ((), ())), preferred_element_type=jnp.float32
    )


def times_transpose(left, right):
    return lax.dot_general(
        left, right, (((1,), (1,)), ((), ())), preferred_element_type=jnp.float32
    )


def moments(grad, first, second, weight, factor):
    clipped = grad * factor
    first_new = MOMENT_ONE * first + (1.0 - MOMENT_ONE) * clipped
    second_new = MOMENT_TWO * second + (1.0 - MOMENT_TWO) * clipped * clipped
    update = (
        first_new
        / (1.0 - MOMENT_ONE**STEP)
        / (jnp.sqrt(second_new / (1.0 - MOMENT_TWO**STEP)) + ADAM_EPS)
        + DECAY * weight
    )
    return (first_new, second_new, update)


class Place:
    def __init__(self, nz, sems):
        dp = lax.axis_index("dp")
        fsdp = lax.axis_index("fsdp")
        self.nz = nz
        self.z, self.x = dp // 2, dp % 2
        self.y, self.c = fsdp // 2, fsdp % 2
        self.sems = sems
        self.used = 0

    def sem(self):
        self.used += 1
        return self.sems.at[self.used - 1]

    def zplus(self, k):
        return lax.rem(self.z + k, self.nz)

    def to(self, z=None, x=None, y=None, c=None):
        z = self.z if z is None else z
        x = self.x if x is None else x
        y = self.y if y is None else y
        c = self.c if c is None else c
        return (z * 2 + x, y * 2 + c)

    def peers(self):
        found = [self.to(z=self.zplus(k)) for k in range(1, self.nz)]
        found.append(self.to(x=1 - self.x))
        found.append(self.to(y=1 - self.y))
        found.append(self.to(c=1 - self.c))
        return found

    def greet(self):
        barrier = pltpu.get_barrier_semaphore()
        peers = self.peers()
        for peer in peers:
            pl.semaphore_signal(barrier, inc=1, device_id=peer, device_id_type=MESH)
        pl.semaphore_wait(barrier, len(peers))

    def send(self, source, target, device):
        return pltpu.make_async_remote_copy(
            src_ref=source,
            dst_ref=target,
            send_sem=self.sem(),
            recv_sem=self.sem(),
            device_id=device,
            device_id_type=MESH,
        )

    def move(self, source, target):
        return pltpu.make_async_copy(source, target, self.sem())


def gather_sems(nz):
    return 2 * (nz - 1) + 18 * nz + 1


def gather_events(place, own, out):
    nz, z, x, y, c = place.nz, place.z, place.x, place.y, place.c
    half = own.shape[0] // 2
    ox, oy, oc = 1 - x, 1 - y, 1 - c
    xp, yp, cp = place.to(x=ox), place.to(y=oy), place.to(c=oc)
    zs = [lax.rem(z - k + nz, nz) for k in range(nz)]
    low, high = pl.ds(0, half), pl.ds(half, half)

    def forward(slot, device, part=None, source=None):
        if part is not None:
            slot = slot.at[part]
        return place.send(slot if source is None else source, slot, device)

    mine = place.move(own, out.at[z, x, y, c])
    along = [None] + [
        place.send(own, out.at[z, x, y, c], place.to(z=place.zplus(k))) for k in range(1, nz)
    ]
    line = [out.at[zs[k], x, y, c] for k in range(nz)]
    beside = [out.at[zs[k], ox, y, c] for k in range(nz)]
    across = [out.at[zs[k], x, oy, c] for k in range(nz)]
    corner = [out.at[zs[k], ox, oy, c] for k in range(nz)]
    first = lambda k: own if k == 0 else None
    x_full = [forward(line[k], xp, source=first(k)) for k in range(nz)]
    y_full = [forward(line[k], yp, source=first(k)) for k in range(nz)]
    c_line = [forward(line[k], cp, source=first(k)) for k in range(nz)]
    x_half = [forward(beside[k], yp, low) for k in range(nz)]
    y_half = [forward(across[k], xp, high) for k in range(nz)]
    c_beside = [forward(beside[k], cp) for k in range(nz)]
    c_across = [forward(across[k], cp) for k in range(nz)]
    c_low = [forward(corner[k], cp, low) for k in range(nz)]
    c_high = [forward(corner[k], cp, high) for k in range(nz)]

    def begin():
        for k in range(1, nz):
            along[k].start()
        x_full[0].start()
        y_full[0].start()
        c_line[0].start()
        mine.start()

    def on_line(k):
        along[k].wait_recv()
        x_full[k].start()
        y_full[k].start()
        c_line[k].start()

    def on_beside(k):
        x_full[k].wait_recv()
        x_half[k].start()
        c_beside[k].start()

    def on_across(k):
        y_full[k].wait_recv()
        y_half[k].start()
        c_across[k].start()

    def on_corner(k):
        x_half[k].wait_recv()
        c_low[k].start()
        y_half[k].wait_recv()
        c_high[k].start()

    def finish():
        mine.wait()
        for copies in (c_line, c_beside, c_across, c_low, c_high):
            for copy in copies:
                copy.wait_recv()
        for copies in (along[1:], x_full, y_full, c_line, x_half, y_half, c_beside, c_across, c_low, c_high):
            for copy in copies:
                copy.wait_send()

    events = [begin]
    for k in range(nz + 2):
        if 1 <= k < nz:
            events.append(functools.partial(on_line, k))
        if 1 <= k <= nz:
            events.append(functools.partial(on_beside, k - 1))
            events.append(functools.partial(on_across, k - 1))
        if 2 <= k:
            events.append(functools.partial(on_corner, k - 2))
    events.append(finish)
    return events


def scatter_sems(nz):
    return 4 * nz + 8 * nz + 8 * nz + 2 * (nz - 1)


def scatter_scratch(nz, rows, columns):
    shape = lambda *lead: pltpu.VMEM(lead + (columns,), jnp.bfloat16)
    return [
        shape(nz, 2, 2, rows),
        shape(nz, 2, 2, rows),
        shape(nz, rows // 2),
        shape(nz, rows // 2),
        shape(nz, rows),
        shape(nz, rows),
        shape(max(nz - 1, 1), rows),
    ]


def scatter_events(place, grads, total, scratch):
    nz, z, x, y, c = place.nz, place.z, place.x, place.y, place.c
    held, twin, corner_low, corner_high, from_x, from_y, from_z = scratch
    rows = total.shape[0]
    half = rows // 2
    ox, oy, oc = 1 - x, 1 - y, 1 - c
    xp, yp, cp = place.to(x=ox), place.to(y=oy), place.to(c=oc)
    order = list(range(1, nz)) + [0]
    zs = [place.zplus(k) for k in range(nz)]
    cell = {(0, 0): (x, y), (1, 0): (ox, y), (0, 1): (x, oy), (1, 1): (ox, oy)}
    quads = [(1, 1), (1, 0), (0, 1), (0, 0)]
    loads, twins = {}, {}
    for k in order:
        for q in quads:
            cx, cy = cell[q]
            loads[q, k] = place.move(grads.at[zs[k], cx, cy, c], held.at[zs[k], q[0], q[1]])
            twins[q, k] = place.send(grads.at[zs[k], cx, cy, oc], twin.at[zs[k], q[0], q[1]], cp)
    low, high = pl.ds(0, half), pl.ds(half, half)
    out_low = [place.send(held.at[zs[k], 1, 1, low], corner_low.at[zs[k]], xp) for k in range(nz)]
    out_high = [place.send(held.at[zs[k], 1, 1, high], corner_high.at[zs[k]], yp) for k in range(nz)]
    out_x = [place.send(held.at[zs[k], 1, 0], from_x.at[zs[k]], xp) for k in range(nz)]
    out_y = [place.send(held.at[zs[k], 0, 1], from_y.at[zs[k]], yp) for k in range(nz)]
    out_z = [None] + [
        place.send(held.at[zs[k], 0, 0], from_z.at[k - 1], place.to(z=zs[k])) for k in range(1, nz)
    ]

    def summed(target, parts):
        lo, n = target[1], target[2]

        def step(i, carry):
            at = pl.multiple_of(i * 16, 16)
            value = parts[0](at)
            for part in parts[1:]:
                value = value + part(at)
            target[0](lo + at, value)
            return carry

        lax.fori_loop(0, n // 16, step, 0)

    def read(ref, *index, lo=0):
        return lambda at: ref[index + (pl.ds(lo + at, 16),)].astype(jnp.float32)

    def write(ref, *index):
        def store(at, value):
            ref[index + (pl.ds(at, 16),)] = value.astype(ref.dtype)

        return store

    def begin():
        for k in order:
            for q in quads:
                twins[q, k].start()
                loads[q, k].start()

    def arrived(q, k):
        loads[q, k].wait()
        twins[q, k].wait_recv()

    def on_corner(k):
        arrived((1, 1), k)
        at = (zs[k], 1, 1)
        summed((write(held, *at), 0, rows), [read(held, *at), read(twin, *at)])
        out_low[k].start()
        out_high[k].start()

    def on_beside(k):
        arrived((1, 0), k)
        at = (zs[k], 1, 0)
        summed((write(held, *at), 0, half), [read(held, *at), read(twin, *at)])
        out_high[k].wait_recv()
        summed(
            (write(held, *at), half, half),
            [read(held, *at, lo=half), read(twin, *at, lo=half), read(corner_high, zs[k])],
        )
        out_x[k].start()

    def on_across(k):
        arrived((0, 1), k)
        at = (zs[k], 0, 1)
        summed((write(held, *at), half, half), [read(held, *at, lo=half), read(twin, *at, lo=half)])
        out_low[k].wait_recv()
        summed(
            (write(held, *at), 0, half),
            [read(held, *at), read(twin, *at), read(corner_low, zs[k])],
        )
        out_y[k].start()

    def on_line(k):
        arrived((0, 0), k)
        out_x[k].wait_recv()
        out_y[k].wait_recv()
        at = (zs[k], 0, 0)
        parts = [read(held, *at), read(twin, *at), read(from_x, zs[k]), read(from_y, zs[k])]
        if k:
            summed((write(held, *at), 0, rows), parts)
            out_z[k].start()
        else:
            for j in range(1, nz):
                out_z[j].wait_recv()
            parts = parts + [read(from_z, j) for j in range(nz - 1)]
            summed((write(total), 0, rows), parts)

    def finish():
        for copies in (list(twins.values()), out_low, out_high, out_x, out_y, out_z[1:]):
            for copy in copies:
                copy.wait_send()

    events = [begin]
    for i in range(nz + 2):
        if i < nz:
            events.append(functools.partial(on_corner, order[i]))
        if 1 <= i <= nz:
            events.append(functools.partial(on_beside, order[i - 1]))
            events.append(functools.partial(on_across, order[i - 1]))
        if 2 <= i:
            events.append(functools.partial(on_line, order[i - 2]))
    events.append(finish)
    return events


def interleave(lists):
    merged = []
    for i in range(max(len(events) for events in lists)):
        for events in lists:
            if i < len(events):
                merged.append(events[i])
    return merged


def gather_kernel(nz, count, *refs):
    owns, outs, lows = refs[:count], refs[count : 2 * count], refs[2 * count : 3 * count]
    place = Place(nz, refs[-1])
    for own, low in zip(owns, lows):
        low[...] = own[...].astype(low.dtype)
    place.greet()
    for event in interleave([gather_events(place, low, out) for low, out in zip(lows, outs)]):
        event()


def gather_all(nz, shards, collective):
    count = len(shards)
    return pl.pallas_call(
        functools.partial(gather_kernel, nz, count),
        name="gather_weights",
        out_shape=[jax.ShapeDtypeStruct((nz, 2, 2, 2) + s.shape, jnp.bfloat16) for s in shards],
        in_specs=[pl.BlockSpec(memory_space=pltpu.VMEM)] * count,
        out_specs=[pl.BlockSpec(memory_space=pl.ANY)] * count,
        scratch_shapes=[pltpu.VMEM(s.shape, jnp.bfloat16) for s in shards]
        + [pltpu.SemaphoreType.DMA((gather_sems(nz) * count,))],
        compiler_params=pltpu.CompilerParams(
            collective_id=collective, has_side_effects=True, vmem_limit_bytes=VMEM_LIMIT
        ),
    )(*shards)


def scatter_kernel(nz, count, *refs):
    grads, totals = refs[:count], refs[count : 2 * count]
    place = Place(nz, refs[-1])
    place.greet()
    lists = []
    for i in range(count):
        scratch = refs[2 * count + 7 * i : 2 * count + 7 * (i + 1)]
        lists.append(scatter_events(place, grads[i], totals[i], scratch))
    for event in interleave(lists):
        event()


def scatter_all(nz, grads, collective, name):
    count = len(grads)
    scratch = []
    for g in grads:
        scratch += scatter_scratch(nz, g.shape[4], g.shape[5])
    return pl.pallas_call(
        functools.partial(scatter_kernel, nz, count),
        name=name,
        out_shape=[jax.ShapeDtypeStruct(g.shape[4:], jnp.float32) for g in grads],
        in_specs=[pl.BlockSpec(memory_space=pl.ANY)] * count,
        out_specs=[pl.BlockSpec(memory_space=pltpu.VMEM)] * count,
        scratch_shapes=scratch + [pltpu.SemaphoreType.DMA((scatter_sems(nz) * count,))],
        compiler_params=pltpu.CompilerParams(
            collective_id=collective, has_side_effects=True, vmem_limit_bytes=VMEM_LIMIT
        ),
    )(*grads)


def spread_kernel(ndp, nfs, own, out, send_sems, recv_sems, sem):
    n = ndp * nfs
    dp, fsdp = lax.axis_index("dp"), lax.axis_index("fsdp")
    me = dp * nfs + fsdp
    barrier = pltpu.get_barrier_semaphore()

    def peer(k):
        other = lax.rem(me + k, n)
        return (other // nfs, lax.rem(other, nfs))

    def hello(k, carry):
        pl.semaphore_signal(barrier, inc=1, device_id=peer(k), device_id_type=MESH)
        return carry

    lax.fori_loop(1, n, hello, 0)
    pl.semaphore_wait(barrier, n - 1)

    def copy(k):
        return pltpu.make_async_remote_copy(
            src_ref=own,
            dst_ref=out.at[me],
            send_sem=send_sems.at[k],
            recv_sem=recv_sems.at[k],
            device_id=peer(k),
            device_id_type=MESH,
        )

    def start(k, carry):
        copy(k).start()
        return carry

    def done(k, carry):
        copy(k).wait()
        return carry

    lax.fori_loop(1, n, start, 0)
    mine = pltpu.make_async_copy(own, out.at[me], sem)
    mine.start()
    mine.wait()
    lax.fori_loop(1, n, done, 0)


def spread(ndp, nfs, block, collective, name):
    n = ndp * nfs
    return pl.pallas_call(
        functools.partial(spread_kernel, ndp, nfs),
        name=name,
        out_shape=jax.ShapeDtypeStruct((n,) + block.shape, block.dtype),
        in_specs=[pl.BlockSpec(memory_space=pltpu.VMEM)],
        out_specs=pl.BlockSpec(memory_space=pltpu.VMEM),
        scratch_shapes=[
            pltpu.SemaphoreType.DMA((n,)),
            pltpu.SemaphoreType.DMA((n,)),
            pltpu.SemaphoreType.DMA(()),
        ],
        compiler_params=pltpu.CompilerParams(collective_id=collective, has_side_effects=True),
    )(block)


def as_rows(values, rows):
    return jnp.pad(values, (0, rows * 128 - values.shape[0])).reshape(rows, 128)


def local(
    ndp,
    nfs,
    patches,
    cotangent,
    pad_mask,
    attend_weight,
    attend_first,
    attend_second,
    output_weight,
    output_first,
    output_second,
    expand_weight,
    expand_first,
    expand_second,
    shrink_weight,
    shrink_first,
    shrink_second,
    vector_params,
    vector_first,
    vector_second,
    position_table,
    table_first,
    table_second,
):
    windows, cells, width = patches.shape
    rows = windows * cells
    head_dim = width // HEADS
    scale = head_dim ** (-0.5)
    keep = pad_mask.astype(jnp.float32)
    local_count = jnp.sum(keep)
    devices = ndp * nfs
    nz = ndp // 2
    shard_rows = min(attend_weight.shape[0], shrink_weight.shape[0])
    direct = ndp % 2 == 0 and nfs == 4 and shard_rows % 32 == 0
    counts = spread(ndp, nfs, as_rows(local_count[None], 8), 0, "spread_count")
    total = jnp.sum(counts[:, 0, 0])
    masters = (attend_weight, output_weight, expand_weight, shrink_weight)
    if direct:
        gathered = [
            w.reshape(-1, w.shape[-1]) for w in gather_all(nz, masters, 1)
        ]
    else:
        gathered = [
            lax.all_gather(m.astype(jnp.bfloat16), AXES, axis=0, tiled=True) for m in masters
        ]
    w_attend, w_output, w_expand, w_shrink = gathered
    gain_one, shift_one = (vector_params[0], vector_params[1])
    query_bias, value_bias, output_bias = (vector_params[2], vector_params[3], vector_params[4])
    gain_two, shift_two, shrink_bias = (vector_params[5], vector_params[6], vector_params[7])
    expand_bias = vector_params[8:].reshape(-1)
    source = patches.reshape(rows, width).astype(jnp.float32)
    normed_one, rstd_one = normalize(source)
    hidden_one = (normed_one * gain_one + shift_one).astype(jnp.bfloat16)
    joint = jnp.dot(hidden_one, w_attend, preferred_element_type=jnp.float32)
    query = (
        (joint[:, :width] + query_bias)
        .astype(jnp.bfloat16)
        .reshape(windows, cells, HEADS, head_dim)
    )
    keys = joint[:, width : 2 * width].astype(jnp.bfloat16).reshape(windows, cells, HEADS, head_dim)
    values = (
        (joint[:, 2 * width :] + value_bias)
        .astype(jnp.bfloat16)
        .reshape(windows, cells, HEADS, head_dim)
    )
    relative = position_table.shape[0]
    onehot = (
        position_index(WS).reshape(-1)[:, None] == jnp.arange(relative, dtype=jnp.int32)[None, :]
    ).astype(jnp.float32)
    bias = (
        jnp.dot(onehot, position_table, precision=HIGH)
        .reshape(cells, cells, HEADS)
        .transpose(2, 0, 1)
    )
    scores = jnp.einsum("wihd,wjhd->whij", query, keys, preferred_element_type=jnp.float32) * scale
    scores = scores + bias[None] + (keep[:, None, None, :] - 1.0) * MASK_FILL
    probs = jax.nn.softmax(scores, axis=-1)
    probs_low = probs.astype(jnp.bfloat16)
    attended = jnp.einsum("whij,wjhd->wihd", probs_low, values, preferred_element_type=jnp.float32)
    attended = attended.reshape(rows, width).astype(jnp.bfloat16)
    middle = source + jnp.dot(attended, w_output, preferred_element_type=jnp.float32) + output_bias
    normed_two, rstd_two = normalize(middle)
    hidden_two = (normed_two * gain_two + shift_two).astype(jnp.bfloat16)
    before = jnp.dot(hidden_two, w_expand, preferred_element_type=jnp.float32) + expand_bias
    activated = jax.nn.gelu(before, approximate=False).astype(jnp.bfloat16)
    result = middle + jnp.dot(activated, w_shrink, preferred_element_type=jnp.float32) + shrink_bias
    block_out = result.astype(jnp.bfloat16).reshape(windows, cells, width)
    upstream = cotangent.reshape(rows, width).astype(jnp.float32) * keep.reshape(rows, 1)
    upstream_low = upstream.astype(jnp.bfloat16)
    grad_shrink = inner_product(activated, upstream_low)
    grad_shrink_bias = jnp.sum(upstream, axis=0)
    grad_act = times_transpose(upstream_low, w_shrink)
    grad_before = (grad_act * gelu_slope(before)).astype(jnp.bfloat16)
    grad_expand = inner_product(hidden_two, grad_before)
    grad_expand_bias = jnp.sum(grad_before.astype(jnp.float32), axis=0)
    grad_hidden_two = times_transpose(grad_before, w_expand)
    grad_gain_two = jnp.sum(grad_hidden_two * normed_two, axis=0)
    grad_shift_two = jnp.sum(grad_hidden_two, axis=0)
    grad_middle = upstream + norm_back(grad_hidden_two, normed_two, rstd_two, gain_two)
    grad_branch = grad_middle.astype(jnp.bfloat16)
    grad_output = inner_product(attended, grad_branch)
    grad_output_bias = jnp.sum(grad_branch.astype(jnp.float32), axis=0)
    grad_attended = (
        times_transpose(grad_branch, w_output)
        .astype(jnp.bfloat16)
        .reshape(windows, cells, HEADS, head_dim)
    )
    grad_probs = jnp.einsum(
        "wihd,wjhd->whij", grad_attended, values, preferred_element_type=jnp.float32
    )
    grad_scores = (
        probs * (grad_probs - jnp.sum(probs * grad_probs, axis=-1, keepdims=True))
    ).astype(jnp.bfloat16)
    grad_query = (
        jnp.einsum("whij,wjhd->wihd", grad_scores, keys, preferred_element_type=jnp.float32) * scale
    ).astype(jnp.bfloat16)
    grad_keys = (
        jnp.einsum("whij,wihd->wjhd", grad_scores, query, preferred_element_type=jnp.float32)
        * scale
    ).astype(jnp.bfloat16)
    grad_values = jnp.einsum(
        "whij,wihd->wjhd", probs_low, grad_attended, preferred_element_type=jnp.float32
    ).astype(jnp.bfloat16)
    grad_bias = (
        jnp.sum(grad_scores.astype(jnp.float32), axis=0)
        .transpose(1, 2, 0)
        .reshape(cells * cells, HEADS)
    )
    grad_table = lax.dot_general(onehot, grad_bias, (((0,), (0,)), ((), ())), precision=HIGH)
    grad_joint = jnp.concatenate(
        [
            grad_query.reshape(rows, width),
            grad_keys.reshape(rows, width),
            grad_values.reshape(rows, width),
        ],
        axis=1,
    )
    grad_attend = inner_product(hidden_one, grad_joint)
    grad_query_bias = jnp.sum(grad_query.reshape(rows, width).astype(jnp.float32), axis=0)
    grad_value_bias = jnp.sum(grad_values.reshape(rows, width).astype(jnp.float32), axis=0)
    grad_hidden_one = times_transpose(grad_joint, w_attend)
    grad_gain_one = jnp.sum(grad_hidden_one * normed_one, axis=0)
    grad_shift_one = jnp.sum(grad_hidden_one, axis=0)
    grad_source = grad_middle + norm_back(grad_hidden_one, normed_one, rstd_one, gain_one)
    vector_local = jnp.concatenate(
        [
            jnp.stack(
                [
                    grad_gain_one,
                    grad_shift_one,
                    grad_query_bias,
                    grad_value_bias,
                    grad_output_bias,
                    grad_gain_two,
                    grad_shift_two,
                    grad_shrink_bias,
                ]
            ),
            grad_expand_bias.reshape(-1, width),
        ],
        axis=0,
    )
    table_rows, table_heads = grad_table.shape
    small = jnp.concatenate([vector_local.reshape(-1), grad_table.reshape(-1)])
    block_rows = -(-small.shape[0] // (devices * 128))
    if direct:
        block_rows = -(-block_rows // 32) * 32
        grads = [
            g.astype(jnp.bfloat16).reshape(nz, 2, 2, 2, -1, g.shape[-1])
            for g in (grad_attend, grad_output, grad_expand, grad_shrink)
        ]
        packed = as_rows(small, devices * block_rows).astype(jnp.bfloat16)
        grads.append(packed.reshape(nz, 2, 2, 2, block_rows, 128))
        *owned, small_owned = scatter_all(nz, grads, 2, "scatter_grads")
    else:
        owned = [
            lax.psum_scatter(g, AXES, scatter_dimension=0, tiled=True)
            for g in (grad_attend, grad_output, grad_expand, grad_shrink)
        ]
        packed = as_rows(small, devices * block_rows)
        small_owned = lax.psum_scatter(packed, AXES, scatter_dimension=0, tiled=True)
    input_grad = (grad_source / total).reshape(windows, cells, width)
    matrix_grads = tuple((g / total for g in owned))
    grad_squares = jnp.stack([jnp.sum(g * g) for g in matrix_grads])
    weight_squares = jnp.stack([jnp.sum(m * m) for m in masters])
    sums = as_rows(jnp.concatenate([grad_squares, weight_squares]), 8)
    spread_one = spread(ndp, nfs, jnp.concatenate([sums, small_owned]), 3, "spread_small")
    totals = jnp.sum(spread_one[:, 0, :8], axis=0)
    grad_total, weight_total = totals[:4], totals[4:]
    small_sum = spread_one[:, 8:].reshape(-1) / total
    vector_grad = small_sum[: vector_local.size].reshape(vector_local.shape)
    table_grad = small_sum[vector_local.size : small.shape[0]].reshape(table_rows, table_heads)
    clip_norm = jnp.sqrt(
        jnp.sum(grad_total) + jnp.sum(vector_grad * vector_grad) + jnp.sum(table_grad * table_grad)
    )
    factor = jnp.minimum(1.0, CLIP_LIMIT / clip_norm)
    firsts = (attend_first, output_first, expand_first, shrink_first)
    seconds = (attend_second, output_second, expand_second, shrink_second)
    sectioned = [
        moments(matrix_grads[k], firsts[k], seconds[k], masters[k], factor) for k in range(4)
    ]
    update_squares = jnp.stack([jnp.sum(s[2] * s[2]) for s in sectioned])
    spread_two = spread(ndp, nfs, as_rows(update_squares, 8), 4, "spread_updates")
    update_total = jnp.sum(spread_two[:, 0, :4], axis=0)
    weight_norms = jnp.sqrt(weight_total)
    update_norms = jnp.sqrt(update_total)
    matrix_outs = []
    for k in range(4):
        fresh = masters[k] - LEARN_RATE * (weight_norms[k] / update_norms[k]) * sectioned[k][2]
        matrix_outs.append(
            (matrix_grads[k], sectioned[k][0], sectioned[k][1], fresh, fresh.astype(jnp.bfloat16))
        )
    vec_first, vec_second, vec_update = moments(
        vector_grad, vector_first, vector_second, vector_params, factor
    )
    vec_ratio = jnp.sqrt(jnp.sum(vector_params * vector_params, axis=1, keepdims=True)) / jnp.sqrt(
        jnp.sum(vec_update * vec_update, axis=1, keepdims=True)
    )
    vec_fresh = vector_params - LEARN_RATE * vec_ratio * vec_update
    tab_first, tab_second, tab_update = moments(
        table_grad, table_first, table_second, position_table, factor
    )
    tab_ratio = jnp.sqrt(jnp.sum(position_table * position_table)) / jnp.sqrt(
        jnp.sum(tab_update * tab_update)
    )
    tab_fresh = position_table - LEARN_RATE * tab_ratio * tab_update
    matrix_norms = jnp.stack([weight_norms, update_norms])
    attend_o, output_o, expand_o, shrink_o = matrix_outs
    return (
        block_out,
        input_grad,
        attend_o[0],
        attend_o[1],
        attend_o[2],
        attend_o[3],
        attend_o[4],
        output_o[0],
        output_o[1],
        output_o[2],
        output_o[3],
        output_o[4],
        expand_o[0],
        expand_o[1],
        expand_o[2],
        expand_o[3],
        expand_o[4],
        shrink_o[0],
        shrink_o[1],
        shrink_o[2],
        shrink_o[3],
        shrink_o[4],
        vector_grad,
        vec_first,
        vec_second,
        vec_fresh,
        table_grad,
        tab_first,
        tab_second,
        tab_fresh,
        clip_norm,
        matrix_norms,
    )


def solution(mesh):
    in_specs = (
        P(("dp", "fsdp"), None, None),
        P(("dp", "fsdp"), None, None),
        P(("dp", "fsdp"), None),
        P(("dp", "fsdp"), None),
        P(("dp", "fsdp"), None),
        P(("dp", "fsdp"), None),
        P(("dp", "fsdp"), None),
        P(("dp", "fsdp"), None),
        P(("dp", "fsdp"), None),
        P(("dp", "fsdp"), None),
        P(("dp", "fsdp"), None),
        P(("dp", "fsdp"), None),
        P(("dp", "fsdp"), None),
        P(("dp", "fsdp"), None),
        P(("dp", "fsdp"), None),
        P(),
        P(),
        P(),
        P(),
        P(),
        P(),
    )
    out_specs = (
        P(("dp", "fsdp"), None, None),
        P(("dp", "fsdp"), None, None),
        P(("dp", "fsdp"), None),
        P(("dp", "fsdp"), None),
        P(("dp", "fsdp"), None),
        P(("dp", "fsdp"), None),
        P(("dp", "fsdp"), None),
        P(("dp", "fsdp"), None),
        P(("dp", "fsdp"), None),
        P(("dp", "fsdp"), None),
        P(("dp", "fsdp"), None),
        P(("dp", "fsdp"), None),
        P(("dp", "fsdp"), None),
        P(("dp", "fsdp"), None),
        P(("dp", "fsdp"), None),
        P(("dp", "fsdp"), None),
        P(("dp", "fsdp"), None),
        P(("dp", "fsdp"), None),
        P(("dp", "fsdp"), None),
        P(("dp", "fsdp"), None),
        P(("dp", "fsdp"), None),
        P(("dp", "fsdp"), None),
        P(),
        P(),
        P(),
        P(),
        P(),
        P(),
        P(),
        P(),
        P(),
        P(),
    )
    sizes = (mesh.shape["dp"], mesh.shape["fsdp"])
    return jax.shard_map(functools.partial(local, *sizes), mesh=mesh, in_specs=in_specs, out_specs=out_specs, check_vma=False)
```

```python
import functools

import jax
import jax.numpy as jnp
from jax import lax
from jax.experimental import pallas as pl
from jax.experimental.pallas import tpu as pltpu
from jax.sharding import PartitionSpec as P

MESH = pl.DeviceIdType.MESH
AXES = ("dp", "fsdp")
VMEM_LIMIT = 60 * 1024 * 1024

HEADS = 32
WS = 10
STEP = 10


EPSILON = 1e-05
MOMENT_ONE = 0.9
MOMENT_TWO = 0.999
LEARN_RATE = 0.3
DECAY = 0.01
ADAM_EPS = 1e-06
CLIP_LIMIT = 0.05
MASK_FILL = 10000.0
HIGH = lax.Precision.HIGHEST
BF, F32 = jnp.bfloat16, jnp.float32


def position_index(size):
    cells = jnp.arange(size * size, dtype=jnp.int32)
    rows = cells // size
    cols = cells % size
    drow = rows[:, None] - rows[None, :] + size - 1
    dcol = cols[:, None] - cols[None, :] + size - 1
    return drow * (2 * size - 1) + dcol


def moments(grad, first, second, weight, factor):
    clipped = grad * factor
    first_new = MOMENT_ONE * first + (1.0 - MOMENT_ONE) * clipped
    second_new = MOMENT_TWO * second + (1.0 - MOMENT_TWO) * clipped * clipped
    update = (
        first_new
        / (1.0 - MOMENT_ONE**STEP)
        / (jnp.sqrt(second_new / (1.0 - MOMENT_TWO**STEP)) + ADAM_EPS)
        + DECAY * weight
    )
    return (first_new, second_new, update)


def whole(shape):
    zeros = (0,) * len(shape)
    return pl.BlockSpec(shape, lambda *s: zeros, pipeline_mode=pl.Buffered(1))


def whole_out(shape):
    zeros = (0,) * len(shape)
    return pl.BlockSpec(shape, lambda *s: zeros)


def struct(shape, dtype):
    return jax.ShapeDtypeStruct(shape, dtype)


HOP = 2.0


def link_us(shape, dtype):
    return 2 * shape[0] * shape[1] * jnp.dtype(dtype).itemsize / 95e3


class Place:
    def __init__(self, nz, sems):
        dp = lax.axis_index("dp")
        fsdp = lax.axis_index("fsdp")
        self.nz = nz
        self.z, self.x = dp // 2, dp % 2
        self.y, self.c = fsdp // 2, fsdp % 2
        self.sems = sems
        self.used = 0

    def sem(self):
        self.used += 1
        return self.sems.at[self.used - 1]

    def zplus(self, k):
        return lax.rem(self.z + k, self.nz)

    def to(self, z=None, x=None, y=None, c=None):
        z = self.z if z is None else z
        x = self.x if x is None else x
        y = self.y if y is None else y
        c = self.c if c is None else c
        return (z * 2 + x, y * 2 + c)

    def peers(self):
        found = [self.to(z=self.zplus(k)) for k in range(1, self.nz)]
        found.append(self.to(x=1 - self.x))
        found.append(self.to(y=1 - self.y))
        found.append(self.to(c=1 - self.c))
        return found

    def greet(self):
        barrier = pltpu.get_barrier_semaphore()
        peers = self.peers()
        for peer in peers:
            pl.semaphore_signal(barrier, inc=1, device_id=peer, device_id_type=MESH)
        pl.semaphore_wait(barrier, len(peers))

    def send(self, source, target, device):
        return pltpu.make_async_remote_copy(
            src_ref=source,
            dst_ref=target,
            send_sem=self.sem(),
            recv_sem=self.sem(),
            device_id=device,
            device_id_type=MESH,
        )

    def move(self, source, target):
        return pltpu.make_async_copy(source, target, self.sem())


def gather_sems(nz):
    return 2 * (nz - 1) + 18 * nz + 1


def gather_events(place, own, out):
    nz, z, x, y, c = place.nz, place.z, place.x, place.y, place.c
    half = own.shape[0] // 2
    ox, oy, oc = 1 - x, 1 - y, 1 - c
    xp, yp, cp = place.to(x=ox), place.to(y=oy), place.to(c=oc)
    zs = [lax.rem(z - k + nz, nz) for k in range(nz)]
    low, high = pl.ds(0, half), pl.ds(half, half)

    def forward(slot, device, part=None, source=None):
        if part is not None:
            slot = slot.at[part]
        return place.send(slot if source is None else source, slot, device)

    mine = place.move(own, out.at[z, x, y, c])
    along = [None] + [
        place.send(own, out.at[z, x, y, c], place.to(z=place.zplus(k))) for k in range(1, nz)
    ]
    line = [out.at[zs[k], x, y, c] for k in range(nz)]
    beside = [out.at[zs[k], ox, y, c] for k in range(nz)]
    across = [out.at[zs[k], x, oy, c] for k in range(nz)]
    corner = [out.at[zs[k], ox, oy, c] for k in range(nz)]
    first = lambda k: own if k == 0 else None
    x_full = [forward(line[k], xp, source=first(k)) for k in range(nz)]
    y_full = [forward(line[k], yp, source=first(k)) for k in range(nz)]
    c_line = [forward(line[k], cp, source=first(k)) for k in range(nz)]
    x_half = [forward(beside[k], yp, low) for k in range(nz)]
    y_half = [forward(across[k], xp, high) for k in range(nz)]
    c_beside = [forward(beside[k], cp) for k in range(nz)]
    c_across = [forward(across[k], cp) for k in range(nz)]
    c_low = [forward(corner[k], cp, low) for k in range(nz)]
    c_high = [forward(corner[k], cp, high) for k in range(nz)]

    def begin():
        for k in range(1, nz):
            along[k].start()
        x_full[0].start()
        y_full[0].start()
        c_line[0].start()
        mine.start()

    def on_line(k):
        along[k].wait_recv()
        x_full[k].start()
        y_full[k].start()
        c_line[k].start()

    def on_beside(k):
        x_full[k].wait_recv()
        x_half[k].start()
        c_beside[k].start()

    def on_across(k):
        y_full[k].wait_recv()
        y_half[k].start()
        c_across[k].start()

    def on_corner(k):
        x_half[k].wait_recv()
        c_low[k].start()
        y_half[k].wait_recv()
        c_high[k].start()

    def finish():
        mine.wait()
        for copies in (c_line, c_beside, c_across, c_low, c_high):
            for copy in copies:
                copy.wait_recv()
        for copies in (along[1:], x_full, y_full, c_line, x_half, y_half, c_beside, c_across, c_low, c_high):
            for copy in copies:
                copy.wait_send()

    unit = link_us(own.shape, own.dtype)
    events = [(0.0, begin)]
    for k in range(nz):
        if k:
            events.append((HOP + (1 + k) * unit, functools.partial(on_line, k)))
        near = HOP + unit if k == 0 else 2 * HOP + (2.5 + k) * unit
        events.append((near, functools.partial(on_beside, k)))
        events.append((near, functools.partial(on_across, k)))
        events.append((near + HOP + (1 + k * 0.3) * unit, functools.partial(on_corner, k)))
    return events, (4 * HOP + 7.5 * unit, finish)


def scatter_sems(nz):
    return 4 * nz + 8 * nz + 8 * nz + 2 * (nz - 1)


def scatter_scratch(nz, rows, columns):
    shape = lambda *lead: pltpu.VMEM(lead + (columns,), jnp.bfloat16)
    return [
        shape(nz, 2, 2, rows),
        shape(nz, 2, 2, rows),
        shape(nz, rows // 2),
        shape(nz, rows // 2),
        shape(nz, rows),
        shape(nz, rows),
        shape(max(nz - 1, 1), rows),
    ]


def scatter_events(place, grads, part, total, scratch):
    nz, z, x, y, c = place.nz, place.z, place.x, place.y, place.c
    held, twin, corner_low, corner_high, from_x, from_y, from_z = scratch
    rows, columns = total.shape
    half = rows // 2
    part = pl.ds(*part)
    ox, oy, oc = 1 - x, 1 - y, 1 - c
    xp, yp, cp = place.to(x=ox), place.to(y=oy), place.to(c=oc)
    order = list(range(1, nz)) + [0]
    zs = [place.zplus(k) for k in range(nz)]
    cell = {(0, 0): (x, y), (1, 0): (ox, y), (0, 1): (x, oy), (1, 1): (ox, oy)}
    quads = [(1, 1), (1, 0), (0, 1), (0, 0)]
    loads, twins = {}, {}
    for k in order:
        for q in quads:
            cx, cy = cell[q]
            loads[q, k] = place.move(grads.at[zs[k], cx, cy, c, part], held.at[zs[k], q[0], q[1]])
            twins[q, k] = place.send(grads.at[zs[k], cx, cy, oc, part], twin.at[zs[k], q[0], q[1]], cp)
    low, high = pl.ds(0, half), pl.ds(half, half)
    out_low = [place.send(held.at[zs[k], 1, 1, low], corner_low.at[zs[k]], xp) for k in range(nz)]
    out_high = [place.send(held.at[zs[k], 1, 1, high], corner_high.at[zs[k]], yp) for k in range(nz)]
    out_x = [place.send(held.at[zs[k], 1, 0], from_x.at[zs[k]], xp) for k in range(nz)]
    out_y = [place.send(held.at[zs[k], 0, 1], from_y.at[zs[k]], yp) for k in range(nz)]
    out_z = [None] + [
        place.send(held.at[zs[k], 0, 0], from_z.at[k - 1], place.to(z=zs[k])) for k in range(1, nz)
    ]

    def summed(target, parts):
        lo, n = target[1], target[2]

        def step(i, carry):
            at = pl.multiple_of(i * 16, 16)
            value = parts[0](at)
            for part in parts[1:]:
                value = value + part(at)
            target[0](lo + at, value)
            return carry

        lax.fori_loop(0, n // 16, step, 0)

    def read(ref, *index, lo=0):
        return lambda at: ref[index + (pl.ds(lo + at, 16),)].astype(jnp.float32)

    def write(ref, *index):
        def store(at, value):
            ref[index + (pl.ds(at, 16),)] = value.astype(ref.dtype)

        return store

    def begin():
        for q in quads[:1]:
            for k in order:
                twins[q, k].start()
                loads[q, k].start()
        for k in order:
            for q in quads[1:]:
                twins[q, k].start()
                loads[q, k].start()

    def arrived(q, k):
        loads[q, k].wait()
        twins[q, k].wait_recv()

    def on_corner(k):
        arrived((1, 1), k)
        at = (zs[k], 1, 1)
        summed((write(held, *at), 0, rows), [read(held, *at), read(twin, *at)])
        out_low[k].start()
        out_high[k].start()

    def on_beside(k):
        arrived((1, 0), k)
        at = (zs[k], 1, 0)
        summed((write(held, *at), 0, half), [read(held, *at), read(twin, *at)])
        out_high[k].wait_recv()
        summed(
            (write(held, *at), half, half),
            [read(held, *at, lo=half), read(twin, *at, lo=half), read(corner_high, zs[k])],
        )
        out_x[k].start()

    def on_across(k):
        arrived((0, 1), k)
        at = (zs[k], 0, 1)
        summed((write(held, *at), half, half), [read(held, *at, lo=half), read(twin, *at, lo=half)])
        out_low[k].wait_recv()
        summed(
            (write(held, *at), 0, half),
            [read(held, *at), read(twin, *at), read(corner_low, zs[k])],
        )
        out_y[k].start()

    def on_line(k):
        arrived((0, 0), k)
        out_x[k].wait_recv()
        out_y[k].wait_recv()
        at = (zs[k], 0, 0)
        parts = [read(held, *at), read(twin, *at), read(from_x, zs[k]), read(from_y, zs[k])]
        if k:
            summed((write(held, *at), 0, rows), parts)
            out_z[k].start()
        else:
            for j in range(1, nz):
                out_z[j].wait_recv()
            parts = parts + [read(from_z, j) for j in range(nz - 1)]
            summed((write(total), 0, rows), parts)

    def finish():
        for copies in (list(twins.values()), out_low, out_high, out_x, out_y, out_z[1:]):
            for copy in copies:
                copy.wait_send()

    unit = link_us((rows, columns), grads.dtype)
    core = 0.2 * unit
    events = [(0.0, begin)]
    for i, k in enumerate(order):
        early = 2 + core * (1 + 0.5 * i)
        events.append((early, functools.partial(on_corner, k)))
        events.append((early + HOP + (1 + 0.5 * i) * unit, functools.partial(on_beside, k)))
        events.append((early + HOP + (1 + 0.5 * i) * unit, functools.partial(on_across, k)))
        events.append((2 * HOP + 2 + core + (3 + i) * unit, functools.partial(on_line, k)))
    return events, (0.0, finish)


def plan_of(lists, steps, step_us):
    timed, ends = [], []
    for (events, end), offset in lists:
        timed += [(offset + at, i, event) for i, (at, event) in enumerate(events)]
        ends.append(end[1])
    timed.sort(key=lambda e: e[:2])
    before, after = {}, []
    for at, _, event in timed:
        step = -int(-at // step_us)
        if step < steps:
            before.setdefault(step, []).append(event)
        else:
            after.append(event)
    return before, after + ends


def fused_kernel(body, nz, counts, kinds, steps, step_us, *refs):
    n_in, n_out, n_scratch = counts
    n = len(kinds)
    ins, given = refs[:n_in], refs[n_in : n_in + n]
    refs = refs[n_in + n :]
    outs, made = refs[:n_out], refs[n_out : n_out + n]
    refs = refs[n_out + n :]
    scratch, spare = refs[:n_scratch], list(refs[n_scratch:-1])
    step = pl.program_id(0)
    place = Place(nz, refs[-1])
    lists, lows = [], []
    for kind, source, target in zip(kinds, given, made):
        if kind[0] == "gather":
            low = spare.pop(0)
            lows.append((source, low))
            events = gather_events(place, low, target)
        else:
            events = scatter_events(place, source, kind[2], target, [spare.pop(0) for _ in range(7)])
        lists.append((events, kind[1]))
    before, after = plan_of(lists, steps, step_us)

    @pl.when(step == 0)
    def _():
        for source, low in lows:
            low[...] = source[...].astype(low.dtype)
        place.greet()

    for at in sorted(before):

        @pl.when(step == at)
        def _(events=before[at]):
            for event in events:
                event()

    body(*ins, *outs, *scratch)

    @pl.when(step == steps - 1)
    def _():
        for event in after:
            event()


def call(body, name, steps, ins, in_specs, outs, out_specs, scratch=(), moves=(), nz=0, collective=None, step_us=1.0):
    scratch = list(scratch)
    params = dict(vmem_limit_bytes=VMEM_LIMIT)
    kinds = [m[:3] for m in moves]
    counts = (len(ins), len(outs), len(scratch))
    kernel = body
    if moves:
        params.update(collective_id=collective, has_side_effects=True)
        kernel = functools.partial(fused_kernel, body, nz, counts, kinds, steps, step_us)
    ins, in_specs, outs, out_specs = list(ins), list(in_specs), list(outs), list(out_specs)
    sems = 0
    for move in moves:
        array = move[3]
        ins.append(array)
        if move[0] == "gather":
            in_specs.append(whole(array.shape))
            outs.append(struct((nz, 2, 2, 2) + array.shape, move[2]))
            out_specs.append(pl.BlockSpec(memory_space=pl.ANY))
            scratch.append(pltpu.VMEM(array.shape, move[2]))
            sems += gather_sems(nz)
        else:
            in_specs.append(pl.BlockSpec(memory_space=pl.ANY))
            shape = (move[2][1], array.shape[5])
            outs.append(struct(shape, F32))
            out_specs.append(whole_out(shape))
            scratch += scatter_scratch(nz, *shape)
            sems += scatter_sems(nz)
    if moves:
        scratch.append(pltpu.SemaphoreType.DMA((sems,)))
    made = pl.pallas_call(
        kernel,
        name=name,
        grid=(steps,),
        out_shape=outs,
        in_specs=in_specs,
        out_specs=out_specs,
        scratch_shapes=scratch,
        compiler_params=pltpu.CompilerParams(**params),
    )(*ins)
    return made[: counts[1]], made[counts[1] :]


def times(left, right):
    return jnp.dot(left, right, preferred_element_type=jnp.float32)


def times_transpose(left, right):
    return lax.dot_general(
        left, right, (((1,), (1,)), ((), ())), preferred_element_type=jnp.float32
    )


def transpose_times(left, right):
    return lax.dot_general(
        left, right, (((0,), (0,)), ((), ())), preferred_element_type=jnp.float32
    )


def normalize(value):
    centre = value - jnp.mean(value, axis=-1, keepdims=True)
    rstd = lax.rsqrt(jnp.mean(centre * centre, axis=-1, keepdims=True) + EPSILON)
    return centre * rstd, rstd


def norm_back(grad_out, normed, rstd, gain):
    scaled = grad_out * gain
    mean_one = jnp.mean(scaled, axis=-1, keepdims=True)
    mean_two = jnp.mean(scaled * normed, axis=-1, keepdims=True)
    return rstd * (scaled - mean_one - normed * mean_two)


def eight(value):
    rows, columns = value.shape
    return jnp.sum(value.reshape(rows // 8, 8, columns), axis=0)


def gelu_parts(value):
    bell = jnp.exp(-0.5 * value * value)
    size = jnp.abs(value)
    t = 1.0 / (1.0 + 0.23164189 * size)
    tail = t * (
        0.127414796
        + t * (-0.142248368 + t * (0.7107068705 + t * (-0.7265760135 + t * 0.5307027145)))
    )
    tail = tail * bell
    phi_big = jnp.where(value >= 0.0, 1.0 - tail, tail)
    return phi_big, bell * 0.3989422804014327


STRIP = 32


def strips(rows, body, carry, unroll=2):
    def step(i, value):
        return body(pl.ds(pl.multiple_of(i * STRIP, STRIP), STRIP), value)

    return lax.fori_loop(0, rows // STRIP, step, carry, unroll=unroll)


def enter_kernel(patches, cotangent, keep, vec, hidden, source, upstream, bias_sum, spare):
    pair = pl.program_id(0)
    cells, width = patches.shape[1:]
    high = hidden.shape[0] // 2
    gain, shift = vec[0:1], vec[1:2]
    spare[...] = jnp.zeros_like(spare)
    for w in range(2):
        value = patches[w].astype(F32)
        spare[pl.ds(w * high, cells)] = value
    source[...] = spare[...].astype(BF)
    for w in range(2):
        normed, _ = normalize(spare[pl.ds(w * high, cells)])
        spare[pl.ds(w * high, cells)] = normed * gain + shift
    hidden[...] = spare[...].astype(BF)

    @pl.when(pair == 0)
    def _():
        bias_sum[...] = jnp.zeros_like(bias_sum)

    spare[...] = jnp.zeros_like(spare)
    for w in range(2):
        mask = jnp.concatenate([keep[w]] * (width // 128), axis=1)
        spare[pl.ds(w * high, cells)] = cotangent[w].astype(F32) * mask[:cells]
    bias_sum[...] += eight(spare[...])
    upstream[...] = spare[...].astype(BF)


def enter(patches, cotangent, keep, vec, **comm):
    windows, cells, width = patches.shape
    high = -(-cells // 8) * 8
    rows = windows * high
    block = pl.BlockSpec((2, cells, width), lambda s: (s, 0, 0))
    flat = pl.BlockSpec((2 * high, width), lambda s: (s, 0))
    return call(
        enter_kernel,
        "enter",
        steps=windows // 2,
        outs=[struct((rows, width), BF)] * 3 + [struct((8, width), F32)],
        in_specs=[
            block,
            block,
            pl.BlockSpec((2, high, 128), lambda s: (s, 0, 0)),
            whole(vec.shape),
        ],
        out_specs=[flat, flat, flat, whole_out((8, width))],
        scratch=[pltpu.VMEM((2 * high, width), F32)],
        ins=[patches, cotangent, keep, vec],
        **comm,
    )


def lanes_of(head):
    lane = lax.broadcasted_iota(jnp.int32, (1, 128), 1)
    return (lane // 32) == head


def pick(value, head):
    return jnp.where(lanes_of(head), value, jnp.zeros_like(value))


def attend_kernel(hidden, wq, wk, wv, vec, bias, mask, query, keys, values, probs, out):
    windows, high, columns = query.shape
    pairs = windows // 2
    group, pair = pl.program_id(0) // pairs, lax.rem(pl.program_id(0), pairs)

    @pl.when(pair == 0)
    def _():
        at = pl.ds(pl.multiple_of(group * columns, columns), columns)
        for weight, target, bias_row in ((wq, query, 2), (wk, keys, None), (wv, values, 3)):
            product = times(hidden[...], weight[...])
            if bias_row is not None:
                product = product + vec[bias_row : bias_row + 1, at]
            for w in range(windows):
                target[w] = product[w * high : (w + 1) * high].astype(BF)

    scale = 32 ** (-0.5)
    done = []
    for w in range(2):
        window = pair * 2 + w
        parts = []
        for g in range(columns // 128):
            at = pl.ds(g * 128, 128)
            q, k, v = query[window, :, at], keys[window, :, at], values[window, :, at]
            vt = v.T
            heads = []
            for h in range(4):
                score = times_transpose(pick(k, h), q) * scale
                score = score + bias[g * 4 + h, :, :high] + mask[window, :, :high]
                score = jnp.exp(score - jnp.max(score, axis=0, keepdims=True))
                prob = (score * (1.0 / jnp.sum(score, axis=0, keepdims=True))).astype(BF)
                probs[w, g * 4 + h, :, :high] = prob
                heads.append(times(vt[32 * h : 32 * h + 32], prob))
            parts.append(jnp.concatenate(heads, axis=0).T)
        done.append(jnp.concatenate(parts, axis=1))
    out[...] = jnp.concatenate(done, axis=0).astype(BF)


def attend(hidden, weight, vec, bias, mask, **comm):
    rows, width = hidden.shape
    windows, high, _ = mask.shape
    heads = bias.shape[0]
    columns = 256
    groups = width // columns
    per = columns // 32
    pairs = windows // 2
    cols = [
        pl.BlockSpec((width, columns), functools.partial(lambda j, s: (0, j * groups + s // pairs), j))
        for j in range(3)
    ]
    seen = pl.BlockSpec((windows, high, columns), lambda s: (0, 0, s // pairs))
    return call(
        attend_kernel,
        "attend",
        steps=groups * pairs,
        outs=[struct((windows, high, width), BF)] * 3
        + [struct((windows, heads, high, 128), BF), struct((rows, width), BF)],
        in_specs=[whole((rows, width))]
        + cols
        + [
            whole(vec.shape),
            pl.BlockSpec((per, high, 128), lambda s: (s // pairs, 0, 0)),
            whole(mask.shape),
        ],
        out_specs=[seen] * 3
        + [
            pl.BlockSpec((2, per, high, 128), lambda s: (lax.rem(s, pairs), s // pairs, 0, 0)),
            pl.BlockSpec((2 * high, columns), lambda s: (lax.rem(s, pairs), s // pairs)),
        ],
        ins=[hidden, weight, weight, weight, vec, bias, mask],
        **comm,
    )


def expand_kernel(attended, source, upstream, wo, we, vec, be, middle, hidden_t, act, slope, grad, hidden, spare):
    step = pl.program_id(0)
    rows, width = hidden.shape

    @pl.when(step == 0)
    def _():
        for j in range(2):
            at = pl.ds(j * (width // 2), width // 2)
            middle[:, at] = times(attended[...], wo[:, at]) + vec[4:5, at]

        def strip(at, carry):
            value = middle[at] + source[at].astype(F32)
            middle[at] = value
            normed, _ = normalize(value)
            hidden[at] = (normed * vec[5:6] + vec[6:7]).astype(BF)
            return carry

        strips(rows, strip, 0)
        hidden_t[...] = hidden[...].T

    @pl.when(step > 0)
    def _():
        spare[...] = times(hidden[...], we[...])

        def strip(at, carry):
            value = spare[at] + be[...]
            big, small = gelu_parts(value)
            act[at] = (value * big).astype(BF)
            slope[at] = (big + value * small).astype(BF)
            return carry

        strips(rows, strip, 0)
        grad[...] = transpose_times(act[...], upstream[...]).astype(BF)


def expand(attended, source, upstream, w_output, w_expand, vec, be, **comm):
    rows, width = attended.shape
    ff = w_expand.shape[1]
    chunk = 512
    at = lambda s: jnp.maximum(s - 1, 0)
    wide = pl.BlockSpec((rows, chunk), lambda s: (0, at(s)))
    return call(
        expand_kernel,
        "expand",
        steps=1 + ff // chunk,
        outs=[
            struct((rows, width), F32),
            struct((width, rows), BF),
            struct((rows, ff), BF),
            struct((rows, ff), BF),
            struct((ff, width), BF),
        ],
        in_specs=[whole((rows, width))] * 3
        + [
            whole((width, width)),
            pl.BlockSpec((width, chunk), lambda s: (0, at(s))),
            whole(vec.shape),
            pl.BlockSpec((1, chunk), lambda s: (0, at(s))),
        ],
        out_specs=[
            whole_out((rows, width)),
            whole_out((width, rows)),
            wide,
            wide,
            pl.BlockSpec((chunk, width), lambda s: (at(s), 0)),
        ],
        scratch=[pltpu.VMEM((rows, width), BF), pltpu.VMEM((rows, chunk), F32)],
        ins=[attended, source, upstream, w_output, w_expand, vec, be],
        **comm,
    )


def shrink_kernel(act, slope, ws, upstream, hidden_t, middle, vec, result, back, back_sum, grad, total):
    step = pl.program_id(0)
    rows, width = total.shape
    windows, cells, _ = result.shape
    high = rows // windows

    @pl.when(step == 0)
    def _():
        total[...] = middle[...] + vec[7:8]

    total[...] += times(act[...], ws[...])
    product = times_transpose(upstream[...], ws[...])
    back[...] = (product * slope[...].astype(F32)).astype(BF)
    back_sum[...] = jnp.sum(back[...].astype(F32), axis=0, keepdims=True)
    grad[...] = times(hidden_t[...], back[...]).astype(BF)

    @pl.when(step == pl.num_programs(0) - 1)
    def _():
        for w in range(windows):
            result[w] = total[pl.ds(w * high, cells)].astype(BF)


def shrink(act, slope, w_shrink, upstream, hidden_t, middle, vec, windows, cells, **comm):
    rows, ff = act.shape
    width = middle.shape[1]
    chunk = 512
    wide = pl.BlockSpec((rows, chunk), lambda s: (0, s))
    return call(
        shrink_kernel,
        "shrink",
        steps=ff // chunk,
        outs=[
            struct((windows, cells, width), BF),
            struct((rows, ff), BF),
            struct((1, ff), F32),
            struct((width, ff), BF),
        ],
        in_specs=[
            wide,
            wide,
            pl.BlockSpec((chunk, width), lambda s: (s, 0)),
            whole((rows, width)),
            whole((width, rows)),
            whole((rows, width)),
            whole(vec.shape),
        ],
        out_specs=[
            whole_out((windows, cells, width)),
            wide,
            pl.BlockSpec((1, chunk), lambda s: (0, s)),
            pl.BlockSpec((width, chunk), lambda s: (0, s)),
        ],
        scratch=[pltpu.VMEM((rows, width), F32)],
        ins=[act, slope, w_shrink, upstream, hidden_t, middle, vec],
        **comm,
    )


def inner_kernel(back, we, middle, upstream, attended, wo, vec, mid, grad, dout, sums, total, branch):
    step = pl.program_id(0)
    rows, width = total.shape
    windows, high, _ = dout.shape

    @pl.when(step == 0)
    def _():
        total[...] = jnp.zeros_like(total)

    total[...] += times_transpose(back[...], we[...])

    @pl.when(step == pl.num_programs(0) - 1)
    def _():
        zero = jnp.zeros((8, width), F32)

        def strip(at, carry):
            gain_sum, shift_sum, out_sum = carry
            normed, rstd = normalize(middle[at])
            value = total[at]
            grad_mid = upstream[at].astype(F32) + norm_back(value, normed, rstd, vec[5:6])
            mid[at] = grad_mid
            low = grad_mid.astype(BF)
            branch[at] = low
            return (
                gain_sum + eight(value * normed),
                shift_sum + eight(value),
                out_sum + eight(low.astype(F32)),
            )

        found = strips(rows, strip, (zero, zero, zero), unroll=1)
        for i in range(3):
            sums[i] = found[i]
        for j in range(2):
            at = pl.ds(j * (width // 2), width // 2)
            grad[:, at] = transpose_times(attended[...], branch[:, at]).astype(BF)
            product = times_transpose(branch[...], wo[at])
            for w in range(windows):
                dout[w, :, at] = product[w * high : (w + 1) * high].astype(BF)


def inner(back, w_expand, middle, upstream, attended, w_output, vec, windows, **comm):
    rows, ff = back.shape
    width = middle.shape[1]
    high = rows // windows
    chunk = 512
    return call(
        inner_kernel,
        "inner",
        steps=ff // chunk,
        outs=[
            struct((rows, width), F32),
            struct((width, width), BF),
            struct((windows, high, width), BF),
            struct((3, 8, width), F32),
        ],
        in_specs=[
            pl.BlockSpec((rows, chunk), lambda s: (0, s)),
            pl.BlockSpec((width, chunk), lambda s: (0, s)),
            whole((rows, width)),
            whole((rows, width)),
            whole((rows, width)),
            whole((width, width)),
            whole(vec.shape),
        ],
        out_specs=[
            whole_out((rows, width)),
            whole_out((width, width)),
            whole_out((windows, high, width)),
            whole_out((3, 8, width)),
        ],
        scratch=[pltpu.VMEM((rows, width), F32), pltpu.VMEM((rows, width), BF)],
        ins=[back, w_expand, middle, upstream, attended, w_output, vec],
        **comm,
    )


def unattend_kernel(query, keys, values, dout, probs, hidden, joint, grad, bias_low, sums, hidden_t, bias):
    step = pl.program_id(0)
    windows, high, columns = query.shape
    rows, width = hidden.shape
    pairs = windows // 2
    groups = width // columns
    pair = lax.rem(step, pairs)
    group = step // pairs
    scale = 32 ** (-0.5)

    @pl.when(step == 0)
    def _():
        hidden_t[...] = hidden[...].T

    @pl.when(step < pairs * groups)
    def _():
        @pl.when(pair == 0)
        def _():
            bias[...] = jnp.zeros_like(bias)

        done = []
        for w in range(2):
            window = pair * 2 + w
            parts = []
            for g in range(columns // 128):
                at = pl.ds(g * 128, 128)
                q, k, v = query[window, :, at], keys[window, :, at], values[window, :, at]
                d = dout[window, :, at]
                kt = k.T
                dq, dk, dv = [], None, None
                for h in range(4):
                    prob = probs[w, g * 4 + h, :, :high]
                    dp = times_transpose(pick(v, h), d)
                    soft = prob.astype(F32)
                    both = soft * dp
                    ds = (both - soft * jnp.sum(both, axis=0, keepdims=True)).astype(BF)
                    bias[g * 4 + h, :, :high] += ds.astype(F32)
                    dq.append(times(kt[32 * h : 32 * h + 32], ds))
                    one, two = pick(times(ds, q), h), pick(times(prob, d), h)
                    dk = one if dk is None else dk + one
                    dv = two if dv is None else dv + two
                parts.append((jnp.concatenate(dq, axis=0).T * scale, dk * scale, dv))
            done.append([jnp.concatenate([p[j] for p in parts], axis=1) for j in range(3)])

        @pl.when(pair == pairs - 1)
        def _():
            bias_low[...] = jnp.zeros_like(bias_low)
            bias_low[:, :high] = bias[...].astype(BF)

        at_rows = pl.ds(pl.multiple_of(pair * 2 * high, 16), 2 * high)
        for j in range(3):
            at = pl.ds(pl.multiple_of(j * width + group * columns, columns), columns)
            joint[at_rows, at] = jnp.concatenate([done[0][j], done[1][j]], axis=0).astype(BF)

    @pl.when(step >= pairs * groups)
    def _():
        chunk = grad.shape[1]
        at = pl.ds(pl.multiple_of((step - pairs * groups) * chunk, chunk), chunk)
        grad[...] = times(hidden_t[...], joint[:, at]).astype(BF)
        sums[...] = jnp.sum(joint[:, at].astype(F32), axis=0, keepdims=True)


def unattend(query, keys, values, dout, probs, hidden, **comm):
    windows, high, width = query.shape
    rows = hidden.shape[0]
    heads = probs.shape[1]
    columns, chunk = 256, 512
    groups, pairs = width // columns, windows // 2
    per = columns // 32
    steps = groups * pairs
    group = lambda s: jnp.minimum(s // pairs, groups - 1)
    pair = lambda s: jnp.where(s < steps, lax.rem(s, pairs), pairs - 1)
    later = lambda s: jnp.maximum(s - steps, 0)
    seen = pl.BlockSpec((windows, high, columns), lambda s: (0, 0, group(s)))
    return call(
        unattend_kernel,
        "unattend",
        steps=steps + 3 * width // chunk,
        outs=[
            struct((rows, 3 * width), BF),
            struct((width, 3 * width), BF),
            struct((heads, 128, 128), BF),
            struct((1, 3 * width), F32),
        ],
        in_specs=[seen] * 4
        + [
            pl.BlockSpec((2, per, high, 128), lambda s: (pair(s), group(s), 0, 0)),
            whole((rows, width)),
        ],
        out_specs=[
            whole_out((rows, 3 * width)),
            pl.BlockSpec((width, chunk), lambda s: (0, later(s))),
            pl.BlockSpec((per, 128, 128), lambda s: (group(s), 0, 0)),
            pl.BlockSpec((1, chunk), lambda s: (0, later(s))),
        ],
        scratch=[pltpu.VMEM((width, rows), BF), pltpu.VMEM((per, high, 128), F32)],
        ins=[query, keys, values, dout, probs, hidden],
        **comm,
    )


def leave_kernel(joint, wa, source, mid, vec, inverse, out, sums, total):
    step = pl.program_id(0)
    rows, width = total.shape
    windows, cells, _ = out.shape
    high = rows // windows

    @pl.when(step == 0)
    def _():
        total[...] = jnp.zeros_like(total)

    total[...] += times_transpose(joint[...], wa[...])

    @pl.when(step == pl.num_programs(0) - 1)
    def _():
        zero = jnp.zeros((8, width), F32)

        def strip(at, carry):
            gain_sum, shift_sum = carry
            normed, rstd = normalize(source[at].astype(F32))
            value = total[at]
            full = mid[at] + norm_back(value, normed, rstd, vec[0:1])
            total[at] = full * inverse[0, 0]
            return gain_sum + eight(value * normed), shift_sum + eight(value)

        found = strips(rows, strip, (zero, zero), unroll=1)
        for i in range(2):
            sums[i] = found[i]
        for w in range(windows):
            out[w] = total[pl.ds(w * high, cells)]


def leave(joint, w_attend, source, mid, vec, inverse, windows, cells, **comm):
    rows, width = source.shape
    chunk = 512
    return call(
        leave_kernel,
        "leave",
        steps=3 * width // chunk,
        outs=[struct((windows, cells, width), F32), struct((2, 8, width), F32)],
        in_specs=[
            pl.BlockSpec((rows, chunk), lambda s: (0, s)),
            pl.BlockSpec((width, chunk), lambda s: (0, s)),
            whole((rows, width)),
            whole((rows, width)),
            whole(vec.shape),
            pl.BlockSpec(memory_space=pltpu.SMEM),
        ],
        out_specs=[whole_out((windows, cells, width)), whole_out((2, 8, width))],
        scratch=[pltpu.VMEM((rows, width), F32)],
        ins=[joint, w_attend, source, mid, vec, inverse],
        **comm,
    )


def update_kernel(nz, pieces, step_number, *refs):
    refs = list(refs)
    take = lambda n: [refs.pop(0) for _ in range(n)]
    inverse, leave_sums, bias_sum, small = take(4)
    sums = take(len(pieces))
    masters, firsts, seconds = take(4), take(4), take(4)
    vec, vec_first, vec_second, table, table_first, table_second = take(6)
    grads_out, firsts_out, seconds_out, news_out, copies_out = (take(4) for _ in range(5))
    vec_out, table_out = take(4), take(4)
    (norms_out,) = take(1)
    message, got, message_two, got_two, vec_grad, heads_grad, sems = refs
    place = Place(nz, sems)
    place.greet()
    devices = nz * 8
    scale = inverse[0, 0]
    lane = lax.broadcasted_iota(jnp.int32, (8, 128), 1)
    top = lax.broadcasted_iota(jnp.int32, (8, 128), 0) == 0

    def rows_of(ref):
        return 8 if ref.shape[0] % 16 else 16

    def over(piece, body, carry):
        k, low, count = piece

        def step(i, value):
            at = pl.multiple_of(i * 16, 16)
            return body(k, pl.ds(low + at, 16), pl.ds(at, 16), value)

        return lax.fori_loop(0, count // 16, step, carry)

    def fold(value):
        value = eight(value)
        return functools.reduce(
            jnp.add, [value[:, i : i + 128] for i in range(0, value.shape[1], 128)]
        )

    zero = jnp.zeros((8, 128), F32)
    squares = [zero] * 8
    for p, piece in enumerate(pieces):

        def body(k, at, source, carry):
            grad = sums[p][source] * scale
            grads_out[k][at] = grad
            weight = masters[k][at]
            return carry[0] + fold(grad * grad), carry[1] + fold(weight * weight)

        k = piece[0]
        squares[k], squares[4 + k] = over(piece, body, (squares[k], squares[4 + k]))

    def packed(values):
        row = zero
        for i, value in enumerate(values):
            row = jnp.where((lane == i) & top, jnp.sum(value), row)
        return row

    message[pl.ds(0, 8)] = packed(squares)
    message[pl.ds(8, 8)] = zero
    message[pl.ds(8, 3)] = small[pl.ds(0, 3)]
    side = 2 * WS - 1
    cell = lax.broadcasted_iota(jnp.int32, (128, 384), 0)
    spot = lax.broadcasted_iota(jnp.int32, (128, 384), 1)
    put = ((cell // WS) * side + lax.rem(cell, WS) == spot) & (cell < WS * WS)
    wide = jnp.dot(bias_sum[...], put.astype(F32), precision=HIGH, preferred_element_type=F32)
    middle = (WS - 1) * side + WS - 1
    column = jnp.zeros((1, 384), F32)
    for j in range(WS * WS):
        shift = middle - (j // WS) * side - j % WS
        column = column + pltpu.roll(wide[j : j + 1], shift, axis=1)
    for b in range(3):
        message[pl.ds(11 + b, 1)] = column[:, 128 * b : 128 * b + 128]
    for i in range(2):
        line = jnp.sum(leave_sums[i], axis=0, keepdims=True)
        for b in range(8):
            message[pl.ds(16 + 8 * i + b, 1)] = line[:, 128 * b : 128 * b + 128]

    events, end = gather_events(place, message, got)
    for event in sorted(events, key=lambda e: e[0]):
        event[1]()
    end[1]()

    place_of = lambda d: (d // 8, (d // 4) % 2, (d // 2) % 2, d % 2)
    found = functools.reduce(jnp.add, [got[place_of(d) + (pl.ds(0, 8),)] for d in range(devices)])
    late = functools.reduce(jnp.add, [got[place_of(d) + (pl.ds(16, 16),)] for d in range(devices)])
    for i in range(2):
        for b in range(8):
            vec_grad[pl.ds(i, 1), pl.ds(128 * b, 128)] = late[8 * i + b : 8 * i + b + 1] * scale
    for d in range(devices):
        block = got[place_of(d) + (pl.ds(8, 8),)] * scale
        q, b = d % 4, d // 4
        rows = block[:3] if q else block[2:3]
        vec_grad[pl.ds(3 * q if q else 2, rows.shape[0]), pl.ds(128 * b, 128)] = rows
        for j in range(3):
            heads_grad[pl.ds(d, 1), pl.ds(128 * j, 128)] = block[3 + j : 4 + j]
    entries = table.shape[0]
    small_grad = vec_grad[...]
    table_grad = heads_grad[...].T[:entries]

    total = lambda value: jnp.sum(value, keepdims=True)
    scalar = lambda k: total(jnp.where(top & (lane == k), found, 0.0))
    grad_square = scalar(0) + scalar(1) + scalar(2) + scalar(3)
    clip_norm = jnp.sqrt(
        grad_square + total(small_grad * small_grad) + total(table_grad * table_grad)
    )
    factor = jnp.minimum(1.0, CLIP_LIMIT / clip_norm)

    def moments(grad, first, second, weight):
        clipped = grad * factor
        first_new = MOMENT_ONE * first + (1.0 - MOMENT_ONE) * clipped
        second_new = MOMENT_TWO * second + (1.0 - MOMENT_TWO) * clipped * clipped
        update = (first_new * (1.0 / (1.0 - MOMENT_ONE**step_number))) / (
            jnp.sqrt(second_new * (1.0 / (1.0 - MOMENT_TWO**step_number))) + ADAM_EPS
        ) + DECAY * weight
        return first_new, second_new, update

    squares = [zero] * 4
    for piece in pieces:

        def body(k, at, source, carry):
            first, second, change = moments(
                grads_out[k][at], firsts[k][at], seconds[k][at], masters[k][at]
            )
            firsts_out[k][at] = first
            seconds_out[k][at] = second
            news_out[k][at] = change
            return carry + fold(change * change)

        squares[piece[0]] = over(piece, body, squares[piece[0]])
    message_two[pl.ds(0, 8)] = packed(squares)
    message_two[pl.ds(8, 8)] = zero

    events, end = gather_events(place, message_two, got_two)
    events = [event for _, event in sorted(events, key=lambda e: e[0])]
    events[0]()

    first, second, change = moments(small_grad, vec_first[...], vec_second[...], vec[...])
    rows = lambda value: jnp.sqrt(jnp.sum(value * value, axis=1, keepdims=True))
    vec_out[0][...] = small_grad
    vec_out[1][...] = first
    vec_out[2][...] = second
    vec_out[3][...] = vec[...] - LEARN_RATE * (rows(vec[...]) / rows(change)) * change
    first, second, change = moments(table_grad, table_first[...], table_second[...], table[...])
    table_out[0][...] = table_grad
    table_out[1][...] = first
    table_out[2][...] = second
    ratio = jnp.sqrt(total(table[...] * table[...])) / jnp.sqrt(total(change * change))
    table_out[3][...] = table[...] - LEARN_RATE * ratio * change

    for event in events[1:]:
        event()
    end[1]()
    second_found = functools.reduce(
        jnp.add, [got_two[place_of(d) + (pl.ds(0, 8),)] for d in range(devices)]
    )
    norms = jnp.where(top & (lane == 8), clip_norm, 0.0)
    for k in range(4):
        weight_norm = jnp.sqrt(scalar(4 + k))
        update_norm = jnp.sqrt(total(jnp.where(top & (lane == k), second_found, 0.0)))
        norms = jnp.where(top & (lane == k), weight_norm, norms)
        norms = jnp.where(top & (lane == 4 + k), update_norm, norms)
        ratio = LEARN_RATE * (weight_norm / update_norm)
        for piece in pieces:
            if piece[0] != k:
                continue

            def body(k, at, source, carry):
                fresh = masters[k][at] - ratio * news_out[k][at]
                news_out[k][at] = fresh
                copies_out[k][at] = fresh.astype(BF)
                return carry

            over(piece, body, 0)
    norms_out[...] = norms


def update(nz, collective, inverse, leave_sums, bias_sum, small, pieces, masters, firsts, seconds, vectors, tables):
    vmem = pl.BlockSpec(memory_space=pltpu.VMEM)
    ins = [inverse, leave_sums, bias_sum, small] + [p[3] for p in pieces]
    ins += list(masters) + list(firsts) + list(seconds) + list(vectors) + list(tables)
    like = lambda arrays, dtype=F32: [struct(a.shape, dtype) for a in arrays]
    outs = like(masters) * 4 + like(masters, BF)
    outs += [struct(vectors[0].shape, F32)] * 4 + [struct(tables[0].shape, F32)] * 4
    outs += [struct((8, 128), F32)]
    made = pl.pallas_call(
        functools.partial(update_kernel, nz, [p[:3] for p in pieces], STEP),
        name="update",
        out_shape=outs,
        in_specs=[pl.BlockSpec(memory_space=pltpu.SMEM)] + [vmem] * (len(ins) - 1),
        out_specs=[vmem] * len(outs),
        scratch_shapes=[
            pltpu.VMEM((32, 128), F32),
            pltpu.VMEM((nz, 2, 2, 2, 32, 128), F32),
            pltpu.VMEM((16, 128), F32),
            pltpu.VMEM((nz, 2, 2, 2, 16, 128), F32),
            pltpu.VMEM(vectors[0].shape, F32),
            pltpu.VMEM((nz * 8, 384), F32),
            pltpu.SemaphoreType.DMA((2 * gather_sems(nz),)),
        ],
        compiler_params=pltpu.CompilerParams(
            collective_id=collective, has_side_effects=True, vmem_limit_bytes=VMEM_LIMIT
        ),
    )(*ins)
    matrices = [[made[4 * j + k] for j in range(5)] for k in range(4)]
    norms = made[-1]
    return matrices, made[20:24], made[24:28], norms[0, 8], norms[0, :8].reshape(2, 4)


def local(
    ndp,
    nfs,
    patches,
    cotangent,
    pad_mask,
    attend_weight,
    attend_first,
    attend_second,
    output_weight,
    output_first,
    output_second,
    expand_weight,
    expand_first,
    expand_second,
    shrink_weight,
    shrink_first,
    shrink_second,
    vector_params,
    vector_first,
    vector_second,
    position_table,
    table_first,
    table_second,
):
    windows, cells, width = patches.shape
    keep = pad_mask.astype(jnp.float32)
    local_count = jnp.sum(keep)
    devices = ndp * nfs
    nz = ndp // 2
    shard_rows = min(attend_weight.shape[0], shrink_weight.shape[0])
    direct = nfs == 4 and devices == HEADS and shard_rows % 32 == 0
    masters = (attend_weight, output_weight, expand_weight, shrink_weight)
    part_rows = shrink_weight.shape[0] // 2

    def with_moves(collective, step_us, *moves):
        if not direct:
            return {}
        return dict(moves=moves, nz=nz, collective=collective, step_us=step_us)

    def gathered(k, made):
        if direct:
            return made.reshape(-1, made.shape[-1])
        return lax.all_gather(masters[k].astype(BF), AXES, axis=0, tiled=True)

    def parts(grad):
        return grad.reshape(nz, 2, 2, 2, -1, grad.shape[-1])

    def scattered(grad):
        return lax.psum_scatter(grad.astype(F32), AXES, scatter_dimension=0, tiled=True)

    high = -(-cells // 8) * 8
    keep_rows = jnp.pad(keep, ((0, 0), (0, high - cells)))[:, :, None]
    keep_rows = jnp.broadcast_to(keep_rows, (windows, high, 128))
    there = (jnp.arange(high) < cells)[None, :, None]
    mask = jnp.where(there, (keep_rows - 1.0) * MASK_FILL, -1e30)
    relative = position_table.shape[0]
    index = jnp.pad(position_index(WS).T, ((0, high - cells), (0, 128 - cells)), constant_values=-1)
    onehot = (
        index.reshape(-1)[None, :] == jnp.arange(relative, dtype=jnp.int32)[:, None]
    ).astype(BF)
    terms, rest = [], position_table.T
    for _ in range(3):
        term = lax.reduce_precision(rest, 8, 7)
        terms.append(term.astype(BF))
        rest = rest - term
    bias = times(jnp.concatenate(terms), onehot).reshape(3, -1, high, 128)
    bias = bias[0] + bias[1] + bias[2]
    expand_bias = vector_params[8:].reshape(1, -1)
    (hidden_one, source, upstream, shrink_sum), made = enter(
        patches,
        cotangent,
        keep_rows,
        vector_params,
        **with_moves(
            1,
            1.5,
            ("gather", 0.0, F32, jnp.full((16, 128), local_count, F32)),
            ("gather", 0.0, BF, attend_weight),
        ),
    )
    made = made or (None,) * 2
    if direct:
        total = jnp.sum(made[0][..., 0, 0])
    else:
        total = lax.psum(local_count, AXES)
    w_attend = gathered(0, made[1])
    (query, keys, values, probs, attended), made = attend(
        hidden_one,
        w_attend,
        vector_params,
        bias,
        mask,
        **with_moves(
            2, 3.2, ("gather", 0.0, BF, output_weight), ("gather", 8.0, BF, expand_weight)
        ),
    )
    made = made or (None,) * 2
    w_output, w_expand = gathered(1, made[0]), gathered(2, made[1])
    (middle, hidden_t, activated, slope, grad_shrink), made = expand(
        attended,
        source,
        upstream,
        w_output,
        w_expand,
        vector_params,
        expand_bias,
        **with_moves(3, 4.9, ("gather", 0.0, BF, shrink_weight)),
    )
    made = made or (None,)
    w_shrink = gathered(3, made[0])
    (block_out, grad_before, grad_expand_bias, grad_expand), made = shrink(
        activated,
        slope,
        w_shrink,
        upstream,
        hidden_t,
        middle,
        vector_params,
        windows,
        cells,
        **with_moves(4, 4.0, ("scatter", 0.0, (0, part_rows), parts(grad_shrink))),
    )
    made = made or (None,)
    shrink_low = made[0]
    (grad_middle, grad_output, dout, inner_sums), made = inner(
        grad_before,
        w_expand,
        middle,
        upstream,
        attended,
        w_output,
        vector_params,
        windows,
        **with_moves(5, 3.7, ("scatter", 0.0, (part_rows, part_rows), parts(grad_shrink))),
    )
    made = made or (None,)
    shrink_high = made[0]
    (joint, grad_attend, grad_bias, joint_sums), made = unattend(
        query,
        keys,
        values,
        dout,
        probs,
        hidden_one,
        **with_moves(
            6,
            3.2,
            ("scatter", 0.0, (0, expand_weight.shape[0]), parts(grad_expand)),
            ("scatter", 8.0, (0, output_weight.shape[0]), parts(grad_output)),
        ),
    )
    made = made or (None,) * 2
    expand_owned, output_owned = made
    inner_rows = jnp.sum(inner_sums, axis=1)
    vector_local = jnp.concatenate(
        [
            jnp.zeros((2, width), F32),
            joint_sums[:, :width],
            joint_sums[:, 2 * width :],
            inner_rows[2:3],
            inner_rows[:2],
            jnp.sum(shrink_sum, axis=0, keepdims=True),
            grad_expand_bias.reshape(-1, width),
        ],
        axis=0,
    )
    moves = ()
    if direct:
        small = vector_local.astype(BF).reshape(4, -1, 8, 128).transpose(2, 0, 1, 3)
        small = small.reshape(devices, -1, 128)
        small = jnp.pad(small, ((0, 0), (0, 32 - small.shape[1]), (0, 0)))
        moves = (
            ("scatter", 0.0, (0, attend_weight.shape[0]), parts(grad_attend)),
            ("scatter", 1.0, (0, 32), small.reshape(nz, 2, 2, 2, 32, 128)),
            ("scatter", 1.0, (0, 128), grad_bias.reshape(nz, 2, 2, 2, 128, 128)),
        )
    inverse = (1.0 / total).reshape(1, 1)
    (input_grad, leave_sums), made = leave(
        joint,
        w_attend,
        source,
        grad_middle,
        vector_params,
        inverse,
        windows,
        cells,
        **with_moves(7, 3.3, *moves),
    )
    firsts = (attend_first, output_first, expand_first, shrink_first)
    seconds = (attend_second, output_second, expand_second, shrink_second)
    if direct:
        attend_owned, small_owned, bias_owned = made
        pieces = [
            (0, 0, attend_weight.shape[0], attend_owned),
            (1, 0, output_weight.shape[0], output_owned),
            (2, 0, expand_weight.shape[0], expand_owned),
            (3, 0, part_rows, shrink_low),
            (3, part_rows, part_rows, shrink_high),
        ]
        matrices, vector_outs, table_outs, clip_norm, matrix_norms = update(
            nz,
            8,
            inverse,
            leave_sums,
            bias_owned,
            small_owned,
            pieces,
            masters,
            firsts,
            seconds,
            (vector_params, vector_first, vector_second),
            (position_table, table_first, table_second),
        )
        outs = [block_out, input_grad]
        for matrix in matrices:
            outs += matrix
        return (*outs, *vector_outs, *table_outs, clip_norm, matrix_norms)
    owned = [
        scattered(g) for g in (grad_attend, grad_output, grad_expand, grad_shrink)
    ]
    grad_table = lax.dot_general(
        onehot.astype(F32),
        grad_bias[:, :high].astype(F32).reshape(HEADS, -1),
        (((1,), (1,)), ((), ())),
        precision=HIGH,
    )
    vector_local = vector_local.at[:2].set(jnp.sum(leave_sums, axis=1))
    vector_sum, table_sum = lax.psum((vector_local, grad_table), AXES)
    vector_grad, table_grad = vector_sum / total, table_sum / total
    matrix_grads = tuple((g / total for g in owned))
    grad_squares = jnp.stack([jnp.sum(g * g) for g in matrix_grads])
    weight_squares = jnp.stack([jnp.sum(m * m) for m in masters])
    grad_total, weight_total = lax.psum((grad_squares, weight_squares), AXES)
    clip_norm = jnp.sqrt(
        jnp.sum(grad_total) + jnp.sum(vector_grad * vector_grad) + jnp.sum(table_grad * table_grad)
    )
    factor = jnp.minimum(1.0, CLIP_LIMIT / clip_norm)
    sectioned = [
        moments(matrix_grads[k], firsts[k], seconds[k], masters[k], factor) for k in range(4)
    ]
    update_squares = jnp.stack([jnp.sum(s[2] * s[2]) for s in sectioned])
    update_total = lax.psum(update_squares, AXES)
    weight_norms = jnp.sqrt(weight_total)
    update_norms = jnp.sqrt(update_total)
    matrix_outs = []
    for k in range(4):
        fresh = masters[k] - LEARN_RATE * (weight_norms[k] / update_norms[k]) * sectioned[k][2]
        matrix_outs.append(
            (matrix_grads[k], sectioned[k][0], sectioned[k][1], fresh, fresh.astype(jnp.bfloat16))
        )
    vec_first, vec_second, vec_update = moments(
        vector_grad, vector_first, vector_second, vector_params, factor
    )
    vec_ratio = jnp.sqrt(jnp.sum(vector_params * vector_params, axis=1, keepdims=True)) / jnp.sqrt(
        jnp.sum(vec_update * vec_update, axis=1, keepdims=True)
    )
    vec_fresh = vector_params - LEARN_RATE * vec_ratio * vec_update
    tab_first, tab_second, tab_update = moments(
        table_grad, table_first, table_second, position_table, factor
    )
    tab_ratio = jnp.sqrt(jnp.sum(position_table * position_table)) / jnp.sqrt(
        jnp.sum(tab_update * tab_update)
    )
    tab_fresh = position_table - LEARN_RATE * tab_ratio * tab_update
    matrix_norms = jnp.stack([weight_norms, update_norms])
    attend_o, output_o, expand_o, shrink_o = matrix_outs
    return (
        block_out,
        input_grad,
        attend_o[0],
        attend_o[1],
        attend_o[2],
        attend_o[3],
        attend_o[4],
        output_o[0],
        output_o[1],
        output_o[2],
        output_o[3],
        output_o[4],
        expand_o[0],
        expand_o[1],
        expand_o[2],
        expand_o[3],
        expand_o[4],
        shrink_o[0],
        shrink_o[1],
        shrink_o[2],
        shrink_o[3],
        shrink_o[4],
        vector_grad,
        vec_first,
        vec_second,
        vec_fresh,
        table_grad,
        tab_first,
        tab_second,
        tab_fresh,
        clip_norm,
        matrix_norms,
    )


def solution(mesh):
    in_specs = (
        P(("dp", "fsdp"), None, None),
        P(("dp", "fsdp"), None, None),
        P(("dp", "fsdp"), None),
        P(("dp", "fsdp"), None),
        P(("dp", "fsdp"), None),
        P(("dp", "fsdp"), None),
        P(("dp", "fsdp"), None),
        P(("dp", "fsdp"), None),
        P(("dp", "fsdp"), None),
        P(("dp", "fsdp"), None),
        P(("dp", "fsdp"), None),
        P(("dp", "fsdp"), None),
        P(("dp", "fsdp"), None),
        P(("dp", "fsdp"), None),
        P(("dp", "fsdp"), None),
        P(),
        P(),
        P(),
        P(),
        P(),
        P(),
    )
    out_specs = (
        P(("dp", "fsdp"), None, None),
        P(("dp", "fsdp"), None, None),
        P(("dp", "fsdp"), None),
        P(("dp", "fsdp"), None),
        P(("dp", "fsdp"), None),
        P(("dp", "fsdp"), None),
        P(("dp", "fsdp"), None),
        P(("dp", "fsdp"), None),
        P(("dp", "fsdp"), None),
        P(("dp", "fsdp"), None),
        P(("dp", "fsdp"), None),
        P(("dp", "fsdp"), None),
        P(("dp", "fsdp"), None),
        P(("dp", "fsdp"), None),
        P(("dp", "fsdp"), None),
        P(("dp", "fsdp"), None),
        P(("dp", "fsdp"), None),
        P(("dp", "fsdp"), None),
        P(("dp", "fsdp"), None),
        P(("dp", "fsdp"), None),
        P(("dp", "fsdp"), None),
        P(("dp", "fsdp"), None),
        P(),
        P(),
        P(),
        P(),
        P(),
        P(),
        P(),
        P(),
        P(),
        P(),
    )
    sizes = (mesh.shape["dp"], mesh.shape["fsdp"])
    return jax.shard_map(functools.partial(local, *sizes), mesh=mesh, in_specs=in_specs, out_specs=out_specs, check_vma=False)
```

```python
import functools

import jax
import jax.numpy as jnp
from jax import lax
from jax.experimental import pallas as pl
from jax.experimental.pallas import tpu as pltpu
from jax.sharding import PartitionSpec as P

MESH = pl.DeviceIdType.MESH
AXES = ("dp", "fsdp")
VMEM_LIMIT = 60 * 1024 * 1024

HEADS = 32
WS = 10
STEP = 10


EPSILON = 1e-05
MOMENT_ONE = 0.9
MOMENT_TWO = 0.999
LEARN_RATE = 0.3
DECAY = 0.01
ADAM_EPS = 1e-06
CLIP_LIMIT = 0.05
MASK_FILL = 10000.0
HIGH = lax.Precision.HIGHEST
BF, F32 = jnp.bfloat16, jnp.float32


def position_index(size):
    cells = jnp.arange(size * size, dtype=jnp.int32)
    rows = cells // size
    cols = cells % size
    drow = rows[:, None] - rows[None, :] + size - 1
    dcol = cols[:, None] - cols[None, :] + size - 1
    return drow * (2 * size - 1) + dcol


def moments(grad, first, second, weight, factor):
    clipped = grad * factor
    first_new = MOMENT_ONE * first + (1.0 - MOMENT_ONE) * clipped
    second_new = MOMENT_TWO * second + (1.0 - MOMENT_TWO) * clipped * clipped
    update = (
        first_new
        / (1.0 - MOMENT_ONE**STEP)
        / (jnp.sqrt(second_new / (1.0 - MOMENT_TWO**STEP)) + ADAM_EPS)
        + DECAY * weight
    )
    return (first_new, second_new, update)


def whole(shape):
    zeros = (0,) * len(shape)
    return pl.BlockSpec(shape, lambda *s: zeros, pipeline_mode=pl.Buffered(1))


def whole_out(shape):
    zeros = (0,) * len(shape)
    return pl.BlockSpec(shape, lambda *s: zeros, pipeline_mode=pl.Buffered(1))


def struct(shape, dtype):
    return jax.ShapeDtypeStruct(shape, dtype)


class Place:
    def __init__(self, sems):
        dp = lax.axis_index("dp")
        fsdp = lax.axis_index("fsdp")
        self.z, self.x = dp // 2, dp % 2
        self.y, self.c = fsdp // 2, fsdp % 2
        self.mate = self.z + 1 - 2 * lax.rem(self.z, 2)
        self.far = lax.rem(self.z + 2, 4)
        self.cross = 3 - self.z
        self.inner = (self.z == 1) | (self.z == 2)
        self.pair = 2 * (self.z // 2)
        self.sems = sems
        self.used = 0

    def sem(self):
        self.used += 1
        return self.sems.at[self.used - 1]

    def to(self, z=None, x=None, y=None, c=None):
        z = self.z if z is None else z
        x = self.x if x is None else x
        y = self.y if y is None else y
        c = self.c if c is None else c
        return (z * 2 + x, y * 2 + c)

    def peers(self):
        return [
            self.to(z=self.mate),
            self.to(z=self.far),
            self.to(z=self.cross),
            self.to(x=1 - self.x),
            self.to(y=1 - self.y),
            self.to(c=1 - self.c),
        ]

    def greet(self):
        barrier = pltpu.get_barrier_semaphore()
        peers = self.peers()
        for peer in peers:
            pl.semaphore_signal(barrier, inc=1, device_id=peer, device_id_type=MESH)
        pl.semaphore_wait(barrier, len(peers))

    def send(self, source, target, device, recv_sem=None):
        return pltpu.make_async_remote_copy(
            src_ref=source,
            dst_ref=target,
            send_sem=self.sem(),
            recv_sem=self.sem() if recv_sem is None else recv_sem,
            device_id=device,
            device_id_type=MESH,
        )

    def move(self, source, target):
        return pltpu.make_async_copy(source, target, self.sem())


def gather_sems(groups):
    return 1 + 2 * 5 + 2 * 5 * groups


def gather_events(place, own, out, groups, relay):
    z, x, y, c = place.z, place.x, place.y, place.c
    half = own.shape[0] // 2
    ox, oy, oc = 1 - x, 1 - y, 1 - c
    xp, yp, cp = place.to(x=ox), place.to(y=oy), place.to(c=oc)
    mate, cross = place.to(z=place.mate), place.to(z=place.cross)
    first = jnp.where(place.inner, place.cross, place.far)
    second = jnp.where(place.inner, place.far, place.cross)
    low, high = pl.ds(0, half), pl.ds(half, half)
    slot = lambda at: out.at[at, x, y, c]
    mine = place.move(own, slot(z))
    to_mate = place.send(own, slot(z), mate)
    if relay:
        came_one, came_two = place.sem(), place.sem()
        across_one = place.send(own, slot(z), cross, came_one)
        across_two = place.send(slot(place.mate), slot(place.mate), cross, came_two)
        on_one = place.send(slot(first), slot(first), mate, came_one)
        on_two = place.send(slot(second), slot(second), mate, came_two)
    else:
        to_far = place.send(own, slot(z), place.to(z=place.far))
        to_cross = place.send(own, slot(z), cross)
    if groups == 1:
        spans = [pl.ds(0, 4)]
    elif groups == 2:
        spans = [pl.ds(place.pair, 2), pl.ds(2 - place.pair, 2)]
    elif relay:
        spans = [pl.ds(at, 1) for at in (z, place.mate, first, second)]
    else:
        spans = [pl.ds(at, 1) for at in (z, place.mate, place.far, place.cross)]

    def forward(ref, device):
        return place.send(ref, ref, device)

    x_full = [forward(out.at[s, x, y, c], xp) for s in spans]
    y_full = [forward(out.at[s, x, y, c], yp) for s in spans]
    x_half = [forward(out.at[s, ox, y, c, low], yp) for s in spans]
    y_half = [forward(out.at[s, x, oy, c, high], xp) for s in spans]
    to_twin = [forward(out.at[s, :, :, c], cp) for s in spans]

    def begin():
        mine.start()
        to_mate.start()
        if relay:

            @pl.when(place.inner)
            def _():
                across_one.start()

        else:
            to_far.start()
            to_cross.start()
        mine.wait()
        if groups == 4:
            send_line(0)

    def send_line(g):
        x_full[g].start()
        y_full[g].start()

    def on_line():
        for copy in (to_mate, to_far, to_cross):
            copy.wait_recv()
        send_line(0)

    def on_place(g):
        (None, to_mate, to_far, to_cross)[g].wait_recv()
        send_line(g)

    def on_mate():
        to_mate.wait_recv()

        @pl.when(place.inner)
        def _():
            across_two.start()

        if groups == 2:
            send_line(0)
        if groups == 4:
            send_line(1)

    def relay_one():
        @pl.when(place.inner)
        def _():
            across_one.wait_recv()
            on_one.start()

    def on_first():
        @pl.when(jnp.logical_not(place.inner))
        def _():
            on_one.wait_recv()

        if groups == 4:
            send_line(2)

    def relay_two():
        @pl.when(place.inner)
        def _():
            across_two.wait_recv()
            on_two.start()

    def on_second():
        @pl.when(jnp.logical_not(place.inner))
        def _():
            on_two.wait_recv()

        send_line(groups - 1)

    def on_side(g):
        x_full[g].wait_recv()
        x_half[g].start()
        y_full[g].wait_recv()
        y_half[g].start()

    def on_corner(g):
        x_half[g].wait_recv()
        y_half[g].wait_recv()
        to_twin[g].start()

    def arrive():
        for copy in to_twin:
            copy.wait_recv()

    def finish():
        for copies in (to_twin, x_full, y_full, x_half, y_half, [to_mate]):
            for copy in copies:
                copy.wait_send()
        if relay:

            @pl.when(place.inner)
            def _():
                for copy in (across_one, across_two, on_one, on_two):
                    copy.wait_send()

        else:
            to_far.wait_send()
            to_cross.wait_send()

    size = 4 // groups
    lines = lambda g: [("x", size, ("xf", g)), ("y", size, ("yf", g))]
    if relay:
        one = {1: [], 2: [], 4: lines(0)}[groups]
        events = [
            (begin, [], [("z", 1, "mate"), ("w", 1, "a1")] + one),
            (on_mate, ["mate"], [("w", 1, "a2")] + {1: [], 2: lines(0), 4: lines(1 % groups)}[groups]),
            (relay_one, ["a1"], [("z", 1, "o1")]),
            (on_first, ["o1"], lines(2) if groups == 4 else []),
            (relay_two, ["a2"], [("z", 1, "o2")]),
            (on_second, ["o2"], lines(groups - 1)),
        ]
    elif groups == 4:
        events = [(begin, [], [("z", 1.33, ("z", g)) for g in (1, 2, 3)] + lines(0))]
        for g in (1, 2, 3):
            events.append((functools.partial(on_place, g), [("z", g)], lines(g)))
    else:
        events = [(begin, [], [("z", 4, "z")]), (on_line, ["z"], lines(0))]
    for g in range(groups):
        half_size = 0.5 * size
        halves = [("y", half_size, ("xh", g)), ("x", half_size, ("yh", g))]
        events.append((functools.partial(on_side, g), [("xf", g), ("yf", g)], halves))
    for g in range(groups):
        twins = [("c", size * 4, ("t", g))]
        events.append((functools.partial(on_corner, g), [("xh", g), ("yh", g)], twins))
    events.append((arrive, [("t", g) for g in range(groups)], []))
    return events, finish


def scatter_sems(groups):
    return groups * (1 + 2 * 5) + 2 * 3


def scatter_scratch(rows, columns):
    shape = lambda *lead: pltpu.VMEM(lead + (columns,), jnp.bfloat16)
    return [
        shape(4, 2, 2, rows),
        shape(4, 2, 2, rows),
        shape(4, rows // 2),
        shape(4, rows // 2),
        shape(4, rows),
        shape(4, rows),
        shape(3, rows),
    ]


def scatter_events(place, grads, part, total, scratch, groups):
    z, x, y, c = place.z, place.x, place.y, place.c
    held, twin, corner_low, corner_high, from_x, from_y, from_z = scratch
    rows, columns = total.shape
    half = rows // 2
    part = pl.ds(*part)
    ox, oy, oc = 1 - x, 1 - y, 1 - c
    xp, yp, cp = place.to(x=ox), place.to(y=oy), place.to(c=oc)
    if groups == 1:
        spans, lines = [(0, 4)], [[0, 1, 2, None]]
    elif groups == 2:
        spans = [(2 - place.pair, 2), (place.pair, 2)]
        lines = [[0, 1], [2, None]]
    else:
        spans = [(place.far, 1), (place.cross, 1), (place.mate, 1), (z, 1)]
        lines = [[0], [1], [2], [None]]
    ds = [pl.ds(*span) for span in spans]
    low, high = pl.ds(0, half), pl.ds(half, half)
    loads = [place.move(grads.at[d, :, :, c, part], held.at[d]) for d in ds]
    twins = [place.send(grads.at[d, :, :, oc, part], twin.at[d], cp) for d in ds]
    out_low = [place.send(held.at[d, ox, oy, low], corner_low.at[d], xp) for d in ds]
    out_high = [place.send(held.at[d, ox, oy, high], corner_high.at[d], yp) for d in ds]
    out_x = [place.send(held.at[d, ox, y], from_x.at[d], xp) for d in ds]
    out_y = [place.send(held.at[d, x, oy], from_y.at[d], yp) for d in ds]
    line = [place.far, place.cross, place.mate]
    out_z = [place.send(held.at[at, x, y], from_z.at[i], place.to(z=at)) for i, at in enumerate(line)]

    def summed(store, first, count, parts):
        def step(i, carry):
            at = pl.ds(pl.multiple_of(first + i * 16, 16), 16)
            store(at, functools.reduce(jnp.add, [part(at).astype(jnp.float32) for part in parts]))
            return carry

        lax.fori_loop(0, count // 16, step, 0)

    def read(ref, *index, lo=0):
        if lo:
            return lambda at: ref[index + (pl.ds(at.start - lo, 16),)]
        return lambda at: ref[index + (at,)]

    def write(ref, *index):
        def store(at, value):
            ref[index + (at,)] = value.astype(ref.dtype)

        return store

    def each(g, body):
        start, size = spans[g]

        def step(i, carry):
            body(start + i)
            return carry

        lax.fori_loop(0, size, step, 0)

    def begin():
        for g in range(len(spans)):
            twins[g].start()
            loads[g].start()

    def on_corner(g):
        loads[g].wait()
        twins[g].wait_recv()

        def body(at):
            here = (at, ox, oy)
            summed(write(held, *here), 0, rows, [read(held, *here), read(twin, *here)])

        each(g, body)
        out_low[g].start()
        out_high[g].start()

    def on_side(g):
        out_high[g].wait_recv()

        def body(at):
            here = (at, ox, y)
            own = [read(held, *here), read(twin, *here)]
            summed(write(held, *here), 0, half, own)
            summed(write(held, *here), half, half, own + [read(corner_high, at, lo=half)])

        each(g, body)
        out_x[g].start()
        out_low[g].wait_recv()

        def body(at):
            here = (at, x, oy)
            own = [read(held, *here), read(twin, *here)]
            summed(write(held, *here), half, half, own)
            summed(write(held, *here), 0, half, own + [read(corner_low, at)])

        each(g, body)
        out_y[g].start()

    def on_line(g):
        out_x[g].wait_recv()
        out_y[g].wait_recv()
        for i in lines[g]:
            at = z if i is None else line[i]
            here = (at, x, y)
            parts = [read(held, *here), read(twin, *here), read(from_x, at), read(from_y, at)]
            if i is None:
                for copy in out_z:
                    copy.wait_recv()
                parts += [read(from_z, j) for j in range(3)]
                summed(write(total), 0, rows, parts)
            else:
                summed(write(held, *here), 0, rows, parts)
                out_z[i].start()

    def finish():
        for copies in (twins, out_low, out_high, out_x, out_y, out_z):
            for copy in copies:
                copy.wait_send()

    size = 4 // groups
    events = [(begin, [], [("c", 4 * size, ("t", g)) for g in range(groups)])]
    for g in range(groups):
        halves = [("x", 0.5 * size, ("l", g)), ("y", 0.5 * size, ("h", g))]
        events.append((functools.partial(on_corner, g), [("t", g)], halves))
    for g in range(groups):
        fulls = [("x", size, ("x", g)), ("y", size, ("y", g))]
        events.append((functools.partial(on_side, g), [("l", g), ("h", g)], fulls))
    for g in range(groups):
        sent = [("z", 1.33, ("z", i)) for i in lines[g] if i is not None]
        waits = [("x", g), ("y", g)]
        if groups > 1 and g == groups - 1:
            waits += [("z", i) for i in range(2)]
        events.append((functools.partial(on_line, g), waits, sent))
    if groups == 4:
        events[-1][1].append(("z", 2))
    return events, finish


HOP = 2.5
LINK = 90e3
CORE = 500e3
BACKLOG = (0.5, 10.0)


def plan_of(lists, starts):
    free = {"x": 0.0, "y": 0.0, "z": 0.0, "w": 0.0, "c": 0.0}
    arrival, pending = {}, []
    for number, ((events, finish), move) in enumerate(lists):
        for order, (event, waits, sends) in enumerate(events):
            pending.append((number, order, event, [(number, w) for w in waits], sends, move))

    def ready(item):
        number, order, _, waits, _, move = item
        if any(w not in arrival for w in waits):
            return None
        if order:
            if any(p[0] == number and p[1] == 0 for p in pending):
                return None
        return max([arrival[w] for w in waits], default=0.0)

    def run(item, now):
        number, _, event, _, sends, move = item
        pending.remove(item)
        for link, units, name in sends:
            rate = CORE if link == "c" else LINK
            cores = 1 if link == "c" else 2
            took = units * cores * move["bytes"] / rate
            free[link] = max(free[link], now) + took
            arrival[number, name] = free[link] + HOP
        return event

    before, now = {}, 3.0
    for step in range(len(starts) + 1):
        last = step == len(starts)
        while True:
            found, forced_found = None, None
            top = min([p[0] for p in pending if p[5]["step"] <= step], default=0)
            pressed = any(p[5]["need"] is not None and p[5]["need"] <= step for p in pending)
            for item in pending:
                number, order, _, _, sends, move = item
                if move["step"] > step:
                    continue
                at = ready(item)
                if at is None:
                    continue
                if last or (move["need"] is not None and move["need"] <= step):
                    if forced_found is None or at < forced_found[0]:
                        forced_found = (at, item)
                elif number > top:
                    backlog = max((free[k] - now for k, _, _ in sends if k != "c"), default=0.0)
                    if backlog > BACKLOG[0 if pressed else 1]:
                        continue
                if at <= now and (found is None or number < found[1][0]):
                    found = (at, item)
            if found is None:
                found = forced_found
            if found is None:
                break
            now = max(now, found[0])
            before.setdefault(step, []).append(run(found[1], now))
        if not last:
            now += starts[step]
    after = before.pop(len(starts), [])
    assert not pending
    return before, after + [finish for (_, finish), _ in lists]


def gather(array, dtype, groups=4, relay=True, need=None, step=0, columns=None):
    columns = ((0, array.shape[1]),) if columns is None else columns
    shape = (array.shape[0], sum(n for _, n in columns))
    return dict(
        kind="gather",
        array=array,
        dtype=dtype,
        groups=groups,
        relay=relay,
        bytes=shape[0] * shape[1] * jnp.dtype(dtype).itemsize,
        need=need,
        step=step,
        columns=columns,
        shape=shape,
    )


def scatter(array, shape=None, groups=4, step=0):
    shape = array.shape[4:] if shape is None else shape
    size = 2 * shape[0] * shape[1]
    return dict(kind="scatter", array=array, shape=shape, groups=groups, bytes=size, need=None, step=step)


def fused_kernel(body, counts, moves, starts, *refs):
    n_in, n_out, n_scratch = counts
    numbers = []
    for move in moves:
        if isinstance(move["array"], int):
            numbers.append(None)
        else:
            same = [i for i, m in enumerate(moves) if m["array"] is move["array"]][0]
            known = numbers[same] if same < len(numbers) else None
            numbers.append(max([n for n in numbers if n is not None], default=-1) + 1 if known is None else known)
    n_given = max([n for n in numbers if n is not None], default=-1) + 1
    ins, given = refs[:n_in], list(refs[n_in : n_in + n_given])
    refs = refs[n_in + n_given :]
    outs, made = refs[:n_out], refs[n_out : n_out + len(moves)]
    refs = refs[n_out + len(moves) :]
    scratch, spare = refs[:n_scratch], list(refs[n_scratch:-1])
    step = pl.program_id(0)
    place = Place(refs[-1])
    lists, lows = [], []
    for move, target, number in zip(moves, made, numbers):
        source = scratch[move["array"]] if number is None else given[number]
        if move["kind"] == "gather":
            low = spare.pop(0)
            lows.append((source, low, move["columns"]))
            events = gather_events(place, low, target, move["groups"], move["relay"])
        else:
            buffers = [spare.pop(0) for _ in range(7)]
            rows = (0, move["shape"][0])
            events = scatter_events(place, source, rows, target, buffers, move["groups"])
        lists.append((events, move))
    before, after = plan_of(lists, starts)

    @pl.when(step == 0)
    def _():
        for source, low, columns in lows:
            put = 0
            for first, size in columns:
                low[:, put : put + size] = source[:, first : first + size].astype(low.dtype)
                put += size
        place.greet()

    for at in sorted(before):

        @pl.when(step == at)
        def _(events=before[at]):
            for event in events:
                event()

    body(made, *ins, *outs, *scratch)

    @pl.when(step == len(starts) - 1)
    def _():
        for event in after:
            event()


def call(body, name, steps, ins, in_specs, outs, out_specs, scratch=(), moves=(), collective=None, starts=()):
    scratch = list(scratch)
    params = dict(vmem_limit_bytes=VMEM_LIMIT)
    counts = (len(ins), len(outs), len(scratch))
    kernel = functools.partial(body, ())
    if moves:
        params.update(collective_id=collective, has_side_effects=True)
        kernel = functools.partial(fused_kernel, body, counts, moves, starts)
        assert len(starts) == steps
    ins, in_specs, outs, out_specs = list(ins), list(in_specs), list(outs), list(out_specs)
    sems = 0
    for move in moves:
        array = move["array"]
        if move["kind"] == "gather":
            if not any(array is other for other in ins[counts[0] :]):
                ins.append(array)
                in_specs.append(whole(array.shape))
            outs.append(struct((4, 2, 2, 2) + move["shape"], move["dtype"]))
            out_specs.append(pl.BlockSpec(memory_space=pl.ANY))
            scratch.append(pltpu.VMEM(move["shape"], move["dtype"]))
            sems += gather_sems(move["groups"])
        else:
            if not isinstance(array, int):
                ins.append(array)
                in_specs.append(pl.BlockSpec(memory_space=pl.ANY))
            outs.append(struct(move["shape"], F32))
            out_specs.append(whole_out(move["shape"]))
            scratch += scatter_scratch(*move["shape"])
            sems += scatter_sems(move["groups"])
    if moves:
        scratch.append(pltpu.SemaphoreType.DMA((sems,)))
    made = pl.pallas_call(
        kernel,
        name=name,
        grid=(steps,),
        out_shape=outs,
        in_specs=in_specs,
        out_specs=out_specs,
        scratch_shapes=scratch,
        compiler_params=pltpu.CompilerParams(**params),
    )(*ins)
    return made[: counts[1]], made[counts[1] :]


def times(left, right):
    return jnp.dot(left, right, preferred_element_type=jnp.float32)


def times_transpose(left, right):
    return lax.dot_general(
        left, right, (((1,), (1,)), ((), ())), preferred_element_type=jnp.float32
    )


def transpose_times(left, right):
    return lax.dot_general(
        left, right, (((0,), (0,)), ((), ())), preferred_element_type=jnp.float32
    )


def normalize(value):
    centre = value - jnp.mean(value, axis=-1, keepdims=True)
    rstd = lax.rsqrt(jnp.mean(centre * centre, axis=-1, keepdims=True) + EPSILON)
    return centre * rstd, rstd


def norm_back(grad_out, normed, rstd, gain):
    scaled = grad_out * gain
    mean_one = jnp.mean(scaled, axis=-1, keepdims=True)
    mean_two = jnp.mean(scaled * normed, axis=-1, keepdims=True)
    return rstd * (scaled - mean_one - normed * mean_two)


def eight(value):
    rows, columns = value.shape
    return jnp.sum(value.reshape(rows // 8, 8, columns), axis=0)


def gelu_parts(value):
    bell = jnp.exp(-0.5 * value * value)
    size = jnp.abs(value)
    t = 1.0 / (1.0 + 0.23164189 * size)
    tail = t * (
        0.127414796
        + t * (-0.142248368 + t * (0.7107068705 + t * (-0.7265760135 + t * 0.5307027145)))
    )
    tail = tail * bell
    phi_big = jnp.where(value >= 0.0, 1.0 - tail, tail)
    return phi_big, bell * 0.3989422804014327


STRIP = 32


def strips(rows, body, carry, unroll=2):
    def step(i, value):
        return body(pl.ds(pl.multiple_of(i * STRIP, STRIP), STRIP), value)

    return lax.fori_loop(0, rows // STRIP, step, carry, unroll=unroll)


def enter_step(pair, patches, cotangent, keep, vec, hidden, source, upstream, bias_sum, spare):
    cells, width = patches.shape[1:]
    high = spare.shape[0] // 2
    at = pl.ds(pl.multiple_of(pair * 2 * high, 16), 2 * high)
    gain, shift = vec[0:1], vec[1:2]
    spare[...] = jnp.zeros_like(spare)
    for w in range(2):
        spare[pl.ds(w * high, cells)] = patches[w].astype(F32)
    source[at] = spare[...].astype(BF)
    for w in range(2):
        normed, _ = normalize(spare[pl.ds(w * high, cells)])
        spare[pl.ds(w * high, cells)] = normed * gain + shift
    hidden[at] = spare[...].astype(BF)

    @pl.when(pair == 0)
    def _():
        bias_sum[...] = jnp.zeros_like(bias_sum)

    spare[...] = jnp.zeros_like(spare)
    for w in range(2):
        mask = jnp.concatenate([keep[w]] * (width // 128), axis=1)
        spare[pl.ds(w * high, cells)] = cotangent[w].astype(F32) * mask[:cells]
    bias_sum[...] += eight(spare[...])
    upstream[at] = spare[...].astype(BF)


def lanes_of(head):
    lane = lax.broadcasted_iota(jnp.int32, (1, 128), 1)
    return (lane // 32) == head


def pick(value, head):
    return jnp.where(lanes_of(head), value, jnp.zeros_like(value))


def attend_step(group, pair, hidden, weights, vec, bias, mask, query, keys, values, probs, out):
    windows, high, columns = query.shape

    @pl.when(pair == 0)
    def _():
        at = pl.ds(pl.multiple_of(group * columns, columns), columns)
        for j, (target, bias_row) in enumerate(((query, 2), (keys, None), (values, 3))):
            product = times(hidden[...], weights(j))
            if bias_row is not None:
                product = product + vec[bias_row : bias_row + 1, at]
            for w in range(windows):
                target[w] = product[w * high : (w + 1) * high].astype(BF)

    scale = 32 ** (-0.5)
    done = []
    for w in range(2):
        window = pair * 2 + w
        parts = []
        for g in range(columns // 128):
            at = pl.ds(g * 128, 128)
            q, k, v = query[window, :, at], keys[window, :, at], values[window, :, at]
            vt = v.T
            heads = []
            for h in range(4):
                score = times_transpose(pick(k, h), q) * scale
                score = score + bias[g * 4 + h, :, :high] + mask[window, :, :high]
                score = jnp.exp(score - jnp.max(score, axis=0, keepdims=True))
                prob = (score * (1.0 / jnp.sum(score, axis=0, keepdims=True))).astype(BF)
                probs[w, g * 4 + h, :, :high] = prob
                heads.append(times(vt[32 * h : 32 * h + 32], prob))
            parts.append(jnp.concatenate(heads, axis=0).T)
        done.append(jnp.concatenate(parts, axis=1))
    rows = pl.ds(pl.multiple_of(pair * 2 * high, 16), 2 * high)
    at = pl.ds(pl.multiple_of(group * columns, columns), columns)
    out[rows, at] = jnp.concatenate(done, axis=0).astype(BF)


def flat(value):
    return value.reshape(-1, value.shape[-1])


def forward_body(direct, made, *refs):
    refs = list(refs)
    take = lambda n: [refs.pop(0) for _ in range(n)]
    patches, cotangent, keep, vec, bias, mask, be = take(7)
    *w_attend, w_output, w_expand = made[:6] if direct else take(6)
    hidden_t, source, upstream, bias_sum, query, keys, values, probs = take(8)
    attended, middle, hidden_two_t, act, slope, grad = take(6)
    spare, hidden, wqkv, wo, we, hidden_two, before, sems = refs
    step = pl.program_id(0)
    rows, width = hidden.shape
    windows, high, columns = query.shape
    pairs, groups = windows // 2, width // columns
    enters, attends = pairs, pairs * groups
    chunk = act.shape[1]
    chunks = w_expand.shape[-1] // chunk

    @pl.when(step < enters)
    def _():
        enter_step(step, patches, cotangent, keep, vec, hidden, source, upstream, bias_sum, spare)

    inner_step = step - enters
    group, pair = inner_step // pairs, lax.rem(inner_step, pairs)

    def load_qkv(number):
        slot = number % 2
        return pltpu.make_async_copy(w_attend[number], wqkv.at[slot], sems.at[slot])

    load_wo = pltpu.make_async_copy(w_output, wo, sems.at[2])

    def load_we(index):
        slot = lax.rem(index, 2)
        at = pl.ds(pl.multiple_of(index * chunk, chunk), chunk)
        return pltpu.make_async_copy(w_expand.at[:, :, :, :, :, at], we.at[slot], sems.at[3 + slot])

    @pl.when((inner_step >= 0) & (inner_step < attends))
    def _():
        @pl.when(inner_step == 0)
        def _():
            hidden_t[...] = hidden[...].T

        for number in range(groups):

            @pl.when(inner_step == number * pairs)
            def _(number=number):
                copy = load_qkv(number)
                copy.start()
                copy.wait()

        slot = lax.rem(group, 2)
        weights = lambda j: flat(wqkv[slot, :, :, :, :, :, pl.ds(j * columns, columns)])
        attend_step(group, pair, hidden, weights, vec, bias, mask, query, keys, values, probs, attended)

    @pl.when(inner_step == attends)
    def _():
        load_wo.start()
        load_we(0).start()
        load_wo.wait()
        for j in range(2):
            at = pl.ds(j * (width // 2), width // 2)
            middle[:, at] = times(attended[...], flat(wo[:, :, :, :, :, at])) + vec[4:5, at]

        def strip(at, carry):
            value = middle[at] + source[at].astype(F32)
            middle[at] = value
            normed, _ = normalize(value)
            hidden_two[at] = (normed * vec[5:6] + vec[6:7]).astype(BF)
            return carry

        strips(rows, strip, 0)
        hidden_two_t[...] = hidden_two[...].T

    @pl.when(inner_step > attends)
    def _():
        index = inner_step - attends - 1
        load_we(index).wait()

        @pl.when(index + 1 < chunks)
        def _():
            load_we(index + 1).start()

        before[...] = times(hidden_two[...], flat(we[lax.rem(index, 2)]))

        def strip(at, carry):
            value = before[at] + be[...]
            big, small = gelu_parts(value)
            act[at] = (value * big).astype(BF)
            slope[at] = (big + value * small).astype(BF)
            return carry

        strips(rows, strip, 0)
        grad[...] = transpose_times(act[...], upstream[...]).astype(BF)


def forward(patches, cotangent, keep, vec, bias, mask, be, gathered, moves, collective):
    windows, cells, width = patches.shape
    high = mask.shape[1]
    rows = windows * high
    heads = bias.shape[0]
    ff = be.shape[1]
    columns, chunk = 256, 512
    groups, pairs = width // columns, windows // 2
    per = columns // 32
    direct = bool(moves)
    enters, attends = pairs, pairs * groups
    steps = enters + attends + 1 + ff // chunk
    group = lambda s: jnp.clip((s - enters) // pairs, 0, groups - 1)
    pair = lambda s: jnp.where(
        s < enters, 0, jnp.where(s < enters + attends, lax.rem(s - enters, pairs), pairs - 1)
    )
    later = lambda s: jnp.maximum(s - enters - attends - 1, 0)
    first = lambda s: (jnp.minimum(s, enters - 1), 0, 0)
    seen = pl.BlockSpec((windows, high, columns), lambda s: (0, 0, group(s)))
    wide = pl.BlockSpec((rows, chunk), lambda s: (0, later(s)))
    any_place = pl.BlockSpec(memory_space=pl.ANY)
    starts = [1.5] * enters + [4.4, 2.7, 2.7, 2.7] * groups + [5.0] + [4.9] * (ff // chunk)
    lead = (4, 2, 2, 2, width // 32)
    return call(
        functools.partial(forward_body, direct),
        "forward",
        steps=steps,
        ins=[patches, cotangent, keep, vec, bias, mask, be] + list(gathered),
        in_specs=[
            pl.BlockSpec((2, cells, width), first),
            pl.BlockSpec((2, cells, width), first),
            pl.BlockSpec((2, high, 128), first),
            whole(vec.shape),
            pl.BlockSpec((per, high, 128), lambda s: (group(s), 0, 0)),
            whole(mask.shape),
            pl.BlockSpec((1, chunk), lambda s: (0, later(s))),
        ]
        + [any_place] * len(gathered),
        outs=[
            struct((width, rows), BF),
            struct((rows, width), BF),
            struct((rows, width), BF),
            struct((8, width), F32),
            struct((windows, high, width), BF),
            struct((windows, high, width), BF),
            struct((windows, high, width), BF),
            struct((windows, heads, high, 128), BF),
            struct((rows, width), BF),
            struct((rows, width), F32),
            struct((width, rows), BF),
            struct((rows, ff), BF),
            struct((rows, ff), BF),
            struct((ff, width), BF),
        ],
        out_specs=[
            whole_out((width, rows)),
            whole_out((rows, width)),
            whole_out((rows, width)),
            whole_out((8, width)),
            seen,
            seen,
            seen,
            pl.BlockSpec((2, per, high, 128), lambda s: (pair(s), group(s), 0, 0)),
            whole_out((rows, width)),
            whole_out((rows, width)),
            whole_out((width, rows)),
            wide,
            wide,
            pl.BlockSpec((chunk, width), lambda s: (later(s), 0)),
        ],
        scratch=[
            pltpu.VMEM((2 * high, width), F32),
            pltpu.VMEM((rows, width), BF),
            pltpu.VMEM((2,) + lead + (3 * columns,), BF),
            pltpu.VMEM(lead + (width,), BF),
            pltpu.VMEM((2,) + lead + (chunk,), BF),
            pltpu.VMEM((rows, width), BF),
            pltpu.VMEM((rows, chunk), F32),
            pltpu.SemaphoreType.DMA((5,)),
        ],
        moves=moves,
        collective=collective,
        starts=starts,
    )


def middle_body(made, *refs):
    refs = list(refs)
    take = lambda n: [refs.pop(0) for _ in range(n)]
    act, slope, ws, we, wo, upstream, hidden_t, middle, attended, vec = take(10)
    result, back_sum, grad_e, mid, grad_o, dout, sums = take(7)
    total, back, branch = refs
    step = pl.program_id(0)
    chunks = back.shape[0]
    rows, width = total.shape
    windows, cells, _ = result.shape
    high = rows // windows

    @pl.when(step == 0)
    def _():
        total[...] = middle[...] + vec[7:8]

    @pl.when(step < chunks)
    def _():
        total[...] += times(act[...], ws[...])
        product = times_transpose(upstream[...], ws[...])
        here = (product * slope[...].astype(F32)).astype(BF)
        back[step] = here
        back_sum[...] = jnp.sum(here.astype(F32), axis=0, keepdims=True)
        grad_e[...] = times(hidden_t[...], here).astype(BF)

    @pl.when(step == chunks - 1)
    def _():
        for w in range(windows):
            result[w] = total[pl.ds(w * high, cells)].astype(BF)
        total[...] = jnp.zeros_like(total)

    @pl.when(step >= chunks)
    def _():
        total[...] += times_transpose(back[step - chunks], we[...])

    @pl.when(step == 2 * chunks - 1)
    def _():
        zero = jnp.zeros((8, width), F32)

        def strip(at, carry):
            gain_sum, shift_sum, out_sum = carry
            normed, rstd = normalize(middle[at])
            value = total[at]
            grad_mid = upstream[at].astype(F32) + norm_back(value, normed, rstd, vec[5:6])
            mid[at] = grad_mid
            low = grad_mid.astype(BF)
            branch[at] = low
            return (
                gain_sum + eight(value * normed),
                shift_sum + eight(value),
                out_sum + eight(low.astype(F32)),
            )

        found = strips(rows, strip, (zero, zero, zero), unroll=1)
        for i in range(3):
            sums[i] = found[i]
        for j in range(2):
            at = pl.ds(j * (width // 2), width // 2)
            grad_o[:, at] = transpose_times(attended[...], branch[:, at]).astype(BF)
            product = times_transpose(branch[...], wo[at])
            for w in range(windows):
                dout[w, :, at] = product[w * high : (w + 1) * high].astype(BF)


def middle_part(act, slope, w_shrink, w_expand, w_output, upstream, hidden_t, middle, attended, vec, windows, cells, moves, collective):
    rows, ff = act.shape
    width = middle.shape[1]
    high = rows // windows
    chunk = 512
    chunks = ff // chunk
    early = lambda s: jnp.minimum(s, chunks - 1)
    later = lambda s: jnp.maximum(s - chunks, 0)
    wide = pl.BlockSpec((rows, chunk), lambda s: (0, early(s)))
    starts = [4.0] * chunks + [1.6] * chunks
    return call(
        middle_body,
        "middle",
        steps=2 * chunks,
        ins=[act, slope, w_shrink, w_expand, w_output, upstream, hidden_t, middle, attended, vec],
        in_specs=[
            wide,
            wide,
            pl.BlockSpec((chunk, width), lambda s: (early(s), 0)),
            pl.BlockSpec((width, chunk), lambda s: (0, later(s))),
            whole((width, width)),
            whole((rows, width)),
            whole((width, rows)),
            whole((rows, width)),
            whole((rows, width)),
            whole(vec.shape),
        ],
        outs=[
            struct((windows, cells, width), BF),
            struct((1, ff), F32),
            struct((width, ff), BF),
            struct((rows, width), F32),
            struct((width, width), BF),
            struct((windows, high, width), BF),
            struct((3, 8, width), F32),
        ],
        out_specs=[
            whole_out((windows, cells, width)),
            pl.BlockSpec((1, chunk), lambda s: (0, early(s))),
            pl.BlockSpec((width, chunk), lambda s: (0, early(s))),
            whole_out((rows, width)),
            whole_out((width, width)),
            whole_out((windows, high, width)),
            whole_out((3, 8, width)),
        ],
        scratch=[
            pltpu.VMEM((rows, width), F32),
            pltpu.VMEM((chunks, rows, chunk), BF),
            pltpu.VMEM((rows, width), BF),
        ],
        moves=moves,
        collective=collective,
        starts=starts,
    )


def backward_body(groups, made, *refs):
    refs = list(refs)
    take = lambda n: [refs.pop(0) for _ in range(n)]
    query, keys, values, dout, probs, hidden_t, source, mid, vec, inverse = take(10)
    w_attend = take(groups)
    out, late = take(2)
    pieces = take(groups)
    bias_low, joint, bias, total, wa, sems = refs
    step = pl.program_id(0)
    windows, high, columns = query.shape
    width, rows = hidden_t.shape
    cells = out.shape[1]
    pairs = windows // 2
    pair = lax.rem(step, pairs)
    group = step // pairs
    scale = 32 ** (-0.5)

    @pl.when(step == 0)
    def _():
        bias_low[...] = jnp.zeros_like(bias_low)
        total[...] = jnp.zeros_like(total)

    @pl.when(step < pairs * groups)
    def _():
        @pl.when(pair == 0)
        def _():
            bias[...] = jnp.zeros_like(bias)

        done = []
        for w in range(2):
            window = pair * 2 + w
            parts = []
            for g in range(columns // 128):
                at = pl.ds(g * 128, 128)
                q, k, v = query[window, :, at], keys[window, :, at], values[window, :, at]
                d = dout[window, :, at]
                kt = k.T
                dq, dk, dv = [], None, None
                for h in range(4):
                    prob = probs[w, g * 4 + h, :, :high]
                    dp = times_transpose(pick(v, h), d)
                    soft = prob.astype(F32)
                    both = soft * dp
                    ds = (both - soft * jnp.sum(both, axis=0, keepdims=True)).astype(BF)
                    bias[g * 4 + h, :, :high] += ds.astype(F32)
                    dq.append(times(kt[32 * h : 32 * h + 32], ds))
                    one, two = pick(times(ds, q), h), pick(times(prob, d), h)
                    dk = one if dk is None else dk + one
                    dv = two if dv is None else dv + two
                parts.append((jnp.concatenate(dq, axis=0).T * scale, dk * scale, dv))
            done.append([jnp.concatenate([p[j] for p in parts], axis=1) for j in range(3)])
        at_rows = pl.ds(pl.multiple_of(pair * 2 * high, 16), 2 * high)
        for j in range(3):
            joint[group, at_rows, pl.ds(j * columns, columns)] = jnp.concatenate([done[0][j], done[1][j]], axis=0).astype(BF)

    for g in range(groups):

        @pl.when(step == pairs * (g + 1) - 1)
        def _(g=g):
            per = columns // 32
            for h in range(per):
                d = g * per + h
                bias_low[d // 8, (d // 4) % 2, (d // 2) % 2, d % 2, :high] = bias[h].astype(BF)
            for j in range(3):
                here = joint[g, :, j * columns : (j + 1) * columns]
                product = times(hidden_t[...], here).astype(BF)
                at = pl.ds(j * columns, columns)
                pieces[g][:, :, :, :, :, at] = product.reshape(pieces[g].shape[:5] + (columns,))
                if j != 1:
                    row = pl.ds(2 if j == 0 else 3, 1)
                    here = jnp.sum(here.astype(F32), axis=0, keepdims=True)
                    late[row, pl.ds(g * columns, columns)] = here

    load = lambda g: pltpu.make_async_copy(w_attend[g], wa.at[g % 2], sems.at[g % 2])

    @pl.when(step == pairs * groups - 1)
    def _():
        load(0).start()

    for g in range(groups):

        @pl.when(step == pairs * groups + g)
        def _(g=g):
            load(g).wait()
            if g + 1 < groups:
                load(g + 1).start()
            total[...] += times_transpose(joint[g], flat(wa[g % 2]))

    @pl.when(step == pl.num_programs(0) - 1)
    def _():
        zero = jnp.zeros((8, width), F32)

        def strip(at, carry):
            gain_sum, shift_sum = carry
            normed, rstd = normalize(source[at].astype(F32))
            value = total[at]
            full = mid[at] + norm_back(value, normed, rstd, vec[0:1])
            total[at] = full * inverse[0, 0]
            return gain_sum + eight(value * normed), shift_sum + eight(value)

        found = strips(rows, strip, (zero, zero), unroll=1)
        for i in range(2):
            late[pl.ds(i, 1)] = jnp.sum(found[i], axis=0, keepdims=True)
        for w in range(windows):
            out[w] = total[pl.ds(w * high, cells)]


def backward_part(query, keys, values, dout, probs, hidden_t, w_attend, source, mid, vec, inverse, cells, moves, collective):
    windows, high, width = query.shape
    rows = hidden_t.shape[1]
    columns = 256
    groups, pairs = width // columns, windows // 2
    per = columns // 32
    steps = groups * pairs
    group = lambda s: jnp.minimum(s // pairs, groups - 1)
    pair = lambda s: jnp.where(s < steps, lax.rem(s, pairs), pairs - 1)
    seen = pl.BlockSpec((windows, high, columns), lambda s: (0, 0, group(s)))
    lead = (4, 2, 2, 2)
    pieces = [(lead + (width // 32, 3 * columns), BF)] * groups + [(lead + (128, 128), BF)]
    outs = [struct((windows, cells, width), F32), struct((4, width), F32)]
    out_specs = [whole_out((windows, cells, width)), whole_out((4, width))]
    scratch = [
        pltpu.VMEM((groups, rows, 3 * columns), BF),
        pltpu.VMEM((per, high, 128), F32),
        pltpu.VMEM((rows, width), F32),
        pltpu.VMEM((2,) + lead + (width // 32, 3 * columns), BF),
        pltpu.SemaphoreType.DMA((2,)),
    ]
    if moves:
        scratch = [pltpu.VMEM(*p) for p in pieces] + scratch
    else:
        outs += [struct(*p) for p in pieces]
        out_specs += [whole_out(p[0]) for p in pieces]
    starts = [4.0, 4.0, 4.0, 6.0] * groups + [2.2] * (groups - 1) + [8.0]
    return call(
        functools.partial(backward_body, groups),
        "backward",
        steps=steps + groups,
        ins=[query, keys, values, dout, probs, hidden_t, source, mid, vec, inverse] + list(w_attend),
        in_specs=[seen] * 4
        + [
            pl.BlockSpec((2, per, high, 128), lambda s: (pair(s), group(s), 0, 0)),
            whole((width, rows)),
            whole((rows, width)),
            whole((rows, width)),
            whole(vec.shape),
            pl.BlockSpec(memory_space=pltpu.SMEM),
        ]
        + [pl.BlockSpec(memory_space=pl.ANY)] * groups,
        outs=outs,
        out_specs=out_specs,
        scratch=scratch,
        moves=moves,
        collective=collective,
        starts=starts,
    )


def update_kernel(pieces, step_number, *refs):
    refs = list(refs)
    take = lambda n: [refs.pop(0) for _ in range(n)]
    inverse, late_sums, bias_sum, small = take(4)
    sums = take(1 + max(p[4] for p in pieces))
    masters, firsts, seconds = take(4), take(4), take(4)
    vec, vec_first, vec_second, table, table_first, table_second = take(6)
    grads_out, firsts_out, seconds_out, news_out, copies_out = (take(4) for _ in range(5))
    vec_out, table_out = take(4), take(4)
    (norms_out,) = take(1)
    message, got, message_two, got_two, vec_grad, heads_grad, sems = refs
    place = Place(sems)
    place.greet()
    devices = got.shape[0] * 8
    scale = inverse[0, 0]
    lane = lax.broadcasted_iota(jnp.int32, (8, 128), 1)
    top = lax.broadcasted_iota(jnp.int32, (8, 128), 0) == 0

    def over(rows, body, carry):
        def step(i, value):
            return body(pl.multiple_of(i * 16, 16), value)

        return lax.fori_loop(0, rows // 16, step, carry)

    def fold(value):
        value = eight(value)
        return functools.reduce(
            jnp.add, [value[:, i : i + 128] for i in range(0, value.shape[1], 128)]
        )

    zero = jnp.zeros((8, 128), F32)
    squares = [zero] * 8
    for k, (row, rows), (column, columns), source_column, number in pieces:
        columns_at = pl.ds(column, columns)

        def body(at, carry):
            here = (pl.ds(row + at, 16), columns_at)
            grad = sums[number][pl.ds(at, 16), pl.ds(source_column, columns)] * scale
            grads_out[k][here] = grad
            weight = masters[k][here]
            return carry[0] + fold(grad * grad), carry[1] + fold(weight * weight)

        squares[k], squares[4 + k] = over(rows, body, (squares[k], squares[4 + k]))

    def packed(values):
        row = zero
        for i, value in enumerate(values):
            row = jnp.where((lane == i) & top, jnp.sum(value), row)
        return row

    message[pl.ds(0, 8)] = packed(squares)
    message[pl.ds(8, 8)] = zero
    message[pl.ds(8, 2)] = small[pl.ds(0, 2)]
    side = 2 * WS - 1
    cell = lax.broadcasted_iota(jnp.int32, (128, 384), 0)
    spot = lax.broadcasted_iota(jnp.int32, (128, 384), 1)
    put = ((cell // WS) * side + lax.rem(cell, WS) == spot) & (cell < WS * WS)
    wide = jnp.dot(bias_sum[...], put.astype(F32), precision=HIGH, preferred_element_type=F32)
    middle = (WS - 1) * side + WS - 1
    column = jnp.zeros((1, 384), F32)
    for j in range(WS * WS):
        shift = middle - (j // WS) * side - j % WS
        column = column + pltpu.roll(wide[j : j + 1], shift, axis=1)
    for b in range(3):
        message[pl.ds(11 + b, 1)] = column[:, 128 * b : 128 * b + 128]
    late_rows = late_sums.shape[0]
    for i in range(late_rows):
        for b in range(8):
            message[pl.ds(16 + 8 * i + b, 1)] = late_sums[i : i + 1, 128 * b : 128 * b + 128]

    events, end = gather_events(place, message, got, 1, False)
    for event, _, _ in events:
        event()
    end()

    place_of = lambda d: (d // 8, (d // 4) % 2, (d // 2) % 2, d % 2)
    found = functools.reduce(jnp.add, [got[place_of(d) + (pl.ds(0, 8),)] for d in range(devices)])
    late = functools.reduce(jnp.add, [got[place_of(d) + (pl.ds(16, 8 * late_rows),)] for d in range(devices)])
    for i in range(late_rows):
        for b in range(8):
            vec_grad[pl.ds(i, 1), pl.ds(128 * b, 128)] = late[8 * i + b : 8 * i + b + 1] * scale
    for d in range(devices):
        block = got[place_of(d) + (pl.ds(8, 8),)] * scale
        vec_grad[pl.ds(4 + 2 * (d % 4), 2), pl.ds(128 * (d // 4), 128)] = block[:2]
        for j in range(3):
            heads_grad[pl.ds(d, 1), pl.ds(128 * j, 128)] = block[3 + j : 4 + j]
    entries = table.shape[0]
    small_grad = vec_grad[...]
    table_grad = heads_grad[...].T[:entries]

    total = lambda value: jnp.sum(value, keepdims=True)
    scalar = lambda k: total(jnp.where(top & (lane == k), found, 0.0))
    grad_square = scalar(0) + scalar(1) + scalar(2) + scalar(3)
    clip_norm = jnp.sqrt(
        grad_square + total(small_grad * small_grad) + total(table_grad * table_grad)
    )
    factor = jnp.minimum(1.0, CLIP_LIMIT / clip_norm)

    def moments(grad, first, second, weight):
        clipped = grad * factor
        first_new = MOMENT_ONE * first + (1.0 - MOMENT_ONE) * clipped
        second_new = MOMENT_TWO * second + (1.0 - MOMENT_TWO) * clipped * clipped
        update = (first_new * (1.0 / (1.0 - MOMENT_ONE**step_number))) / (
            jnp.sqrt(second_new * (1.0 / (1.0 - MOMENT_TWO**step_number))) + ADAM_EPS
        ) + DECAY * weight
        return first_new, second_new, update

    squares = [zero] * 4
    for k in range(4):

        def body(at, carry):
            at = pl.ds(at, 16)
            first, second, change = moments(
                grads_out[k][at], firsts[k][at], seconds[k][at], masters[k][at]
            )
            firsts_out[k][at] = first
            seconds_out[k][at] = second
            news_out[k][at] = change
            return carry + fold(change * change)

        squares[k] = over(masters[k].shape[0], body, squares[k])
    message_two[pl.ds(0, 8)] = packed(squares)
    message_two[pl.ds(8, 8)] = zero

    events, end = gather_events(place, message_two, got_two, 1, False)
    events = [event for event, _, _ in events]
    events[0]()

    first, second, change = moments(small_grad, vec_first[...], vec_second[...], vec[...])
    rows = lambda value: jnp.sqrt(jnp.sum(value * value, axis=1, keepdims=True))
    vec_out[0][...] = small_grad
    vec_out[1][...] = first
    vec_out[2][...] = second
    vec_out[3][...] = vec[...] - LEARN_RATE * (rows(vec[...]) / rows(change)) * change
    first, second, change = moments(table_grad, table_first[...], table_second[...], table[...])
    table_out[0][...] = table_grad
    table_out[1][...] = first
    table_out[2][...] = second
    ratio = jnp.sqrt(total(table[...] * table[...])) / jnp.sqrt(total(change * change))
    table_out[3][...] = table[...] - LEARN_RATE * ratio * change

    for event in events[1:]:
        event()
    end()
    second_found = functools.reduce(
        jnp.add, [got_two[place_of(d) + (pl.ds(0, 8),)] for d in range(devices)]
    )
    norms = jnp.where(top & (lane == 8), clip_norm, 0.0)
    for k in range(4):
        weight_norm = jnp.sqrt(scalar(4 + k))
        update_norm = jnp.sqrt(total(jnp.where(top & (lane == k), second_found, 0.0)))
        norms = jnp.where(top & (lane == k), weight_norm, norms)
        norms = jnp.where(top & (lane == 4 + k), update_norm, norms)
        ratio = LEARN_RATE * (weight_norm / update_norm)

        def body(at, carry):
            at = pl.ds(at, 16)
            fresh = masters[k][at] - ratio * news_out[k][at]
            news_out[k][at] = fresh
            copies_out[k][at] = fresh.astype(BF)
            return carry

        over(masters[k].shape[0], body, 0)
    norms_out[...] = norms


def update(collective, inverse, late_sums, bias_sum, small, sums, pieces, masters, firsts, seconds, vectors, tables):
    vmem = pl.BlockSpec(memory_space=pltpu.VMEM)
    ins = [inverse, late_sums, bias_sum, small] + list(sums)
    ins += list(masters) + list(firsts) + list(seconds) + list(vectors) + list(tables)
    like = lambda arrays, dtype=F32: [struct(a.shape, dtype) for a in arrays]
    outs = like(masters) * 4 + like(masters, BF)
    outs += [struct(vectors[0].shape, F32)] * 4 + [struct(tables[0].shape, F32)] * 4
    outs += [struct((8, 128), F32)]
    made = pl.pallas_call(
        functools.partial(update_kernel, pieces, STEP),
        name="update",
        out_shape=outs,
        in_specs=[pl.BlockSpec(memory_space=pltpu.SMEM)] + [vmem] * (len(ins) - 1),
        out_specs=[vmem] * len(outs),
        scratch_shapes=[
            pltpu.VMEM((48, 128), F32),
            pltpu.VMEM((4, 2, 2, 2, 48, 128), F32),
            pltpu.VMEM((16, 128), F32),
            pltpu.VMEM((4, 2, 2, 2, 16, 128), F32),
            pltpu.VMEM(vectors[0].shape, F32),
            pltpu.VMEM((32, 384), F32),
            pltpu.SemaphoreType.DMA((2 * gather_sems(1),)),
        ],
        compiler_params=pltpu.CompilerParams(
            collective_id=collective, has_side_effects=True, vmem_limit_bytes=VMEM_LIMIT
        ),
    )(*ins)
    matrices = [[made[4 * j + k] for j in range(5)] for k in range(4)]
    norms = made[-1]
    return matrices, made[20:24], made[24:28], norms[0, 8], norms[0, :8].reshape(2, 4)


def local(
    ndp,
    nfs,
    patches,
    cotangent,
    pad_mask,
    attend_weight,
    attend_first,
    attend_second,
    output_weight,
    output_first,
    output_second,
    expand_weight,
    expand_first,
    expand_second,
    shrink_weight,
    shrink_first,
    shrink_second,
    vector_params,
    vector_first,
    vector_second,
    position_table,
    table_first,
    table_second,
):
    windows, cells, width = patches.shape
    keep = pad_mask.astype(jnp.float32)
    local_count = jnp.sum(keep)
    devices = ndp * nfs
    shard_rows = min(attend_weight.shape[0], shrink_weight.shape[0])
    direct = nfs == 4 and ndp == 8 and shard_rows % 32 == 0
    masters = (attend_weight, output_weight, expand_weight, shrink_weight)
    part_rows = shrink_weight.shape[0] // 2

    high = -(-cells // 8) * 8
    keep_rows = jnp.pad(keep, ((0, 0), (0, high - cells)))[:, :, None]
    keep_rows = jnp.broadcast_to(keep_rows, (windows, high, 128))
    there = (jnp.arange(high) < cells)[None, :, None]
    mask = jnp.where(there, (keep_rows - 1.0) * MASK_FILL, -1e30)
    relative = position_table.shape[0]
    index = jnp.pad(position_index(WS).T, ((0, high - cells), (0, 128 - cells)), constant_values=-1)
    onehot = (
        index.reshape(-1)[None, :] == jnp.arange(relative, dtype=jnp.int32)[:, None]
    ).astype(BF)
    terms, rest = [], position_table.T
    for _ in range(3):
        term = lax.reduce_precision(rest, 8, 7)
        terms.append(term.astype(BF))
        rest = rest - term
    bias = times(jnp.concatenate(terms), onehot).reshape(3, -1, high, 128)
    bias = bias[0] + bias[1] + bias[2]
    expand_bias = vector_params[8:].reshape(1, -1)
    lead = (4, 2, 2, 2, -1)
    group_columns = [[(j * width + g * 256, 256) for j in range(3)] for g in range(4)]
    gathered, moves = [], []
    if direct:
        moves = [
            *[
                gather(attend_weight, BF, relay=False, need=4 + 4 * g, columns=columns)
                for g, columns in enumerate(group_columns)
            ],
            gather(output_weight, BF, need=20),
            gather(expand_weight, BF, need=20),
            gather(shrink_weight, BF),
            gather(jnp.full((16, 128), local_count, F32), F32, 1, False),
        ]
    else:
        gathered = [
            lax.all_gather(m.astype(BF), AXES, axis=0, tiled=True).reshape(lead + m.shape[1:])
            for m in masters
        ]
        w_attend = [
            jnp.concatenate([gathered[0][..., a : a + n] for a, n in columns], axis=-1)
            for columns in group_columns
        ]
        gathered = w_attend + gathered[1:]
    forward_outs, made = forward(
        patches,
        cotangent,
        keep_rows,
        vector_params,
        bias,
        mask,
        expand_bias,
        () if direct else gathered[:6],
        moves,
        1,
    )
    hidden_t, source, upstream, shrink_sum, query, keys, values, probs = forward_outs[:8]
    attended, middle, hidden_two_t, activated, slope, grad_shrink = forward_outs[8:]
    if direct:
        total = jnp.sum(made[-1][..., 0, 0])
        gathered = made[:-1]
    else:
        total = lax.psum(local_count, AXES)
    w_attend = gathered[:4]
    w_output, w_expand, w_shrink = (w.reshape(-1, w.shape[-1]) for w in gathered[4:])
    inverse = (1.0 / total).reshape(1, 1)

    def parts(grad):
        return grad.reshape(lead + grad.shape[-1:])

    if direct:
        moves = [scatter(parts(grad_shrink))]
    middle_outs, owned_shrink = middle_part(
        activated,
        slope,
        w_shrink,
        w_expand,
        w_output,
        upstream,
        hidden_two_t,
        middle,
        attended,
        vector_params,
        windows,
        cells,
        moves,
        2,
    )
    block_out, grad_expand_bias, grad_expand, grad_middle, grad_output, dout, inner_sums = middle_outs
    inner_rows = jnp.sum(inner_sums, axis=1)
    early_sums = jnp.concatenate(
        [
            inner_rows[2:3],
            inner_rows[:2],
            jnp.sum(shrink_sum, axis=0, keepdims=True),
            grad_expand_bias.reshape(-1, width),
        ],
        axis=0,
    )
    if direct:
        small = early_sums.astype(BF).reshape(4, 2, 8, 128).transpose(2, 0, 1, 3)
        small = jnp.pad(small.reshape(devices, 2, 128), ((0, 0), (0, 30), (0, 0)))
        piece_shape = (width // 32, 3 * 256)
        moves = [
            scatter(parts(grad_expand)),
            scatter(parts(grad_output)),
            scatter(parts(small), groups=1),
        ]
        moves += [scatter(g, piece_shape, step=4 * (g + 1)) for g in range(4)]
        moves.append(scatter(4, (128, 128), groups=1, step=16))
    backward_outs, made = backward_part(
        query,
        keys,
        values,
        dout,
        probs,
        hidden_t,
        w_attend,
        source,
        grad_middle,
        vector_params,
        inverse,
        cells,
        moves,
        3,
    )
    input_grad, late_sums = backward_outs[:2]
    grad_pieces, grad_bias = backward_outs[2:-1], backward_outs[-1]

    def finish_direct(block_out, input_grad, late_sums, made, owned_shrink, firsts, seconds):
        expand_owned, output_owned, small_owned = made[:3]
        bias_owned = made[-1]
        sums = list(made[3:-1]) + [output_owned, expand_owned, owned_shrink[0]]
        pieces = [
            (0, (0, attend_weight.shape[0]), (j * width + g * 256, 256), j * 256, g)
            for g in range(4)
            for j in range(3)
        ]
        pieces += [
            (k, (0, masters[k].shape[0]), (0, masters[k].shape[1]), 0, 3 + k) for k in (1, 2, 3)
        ]
        matrices, vector_outs, table_outs, clip_norm, matrix_norms = update(
            4,
            inverse,
            late_sums,
            bias_owned,
            small_owned,
            sums,
            pieces,
            masters,
            firsts,
            seconds,
            (vector_params, vector_first, vector_second),
            (position_table, table_first, table_second),
        )
        outs = [block_out, input_grad]
        for matrix in matrices:
            outs += matrix
        return (*outs, *vector_outs, *table_outs, clip_norm, matrix_norms)

    firsts = (attend_first, output_first, expand_first, shrink_first)
    seconds = (attend_second, output_second, expand_second, shrink_second)
    if direct:
        return finish_direct(
            block_out, input_grad, late_sums, made, owned_shrink, firsts, seconds
        )
    grad_attend = jnp.stack([p.reshape(width, 3, -1) for p in grad_pieces], axis=2)
    grad_attend = grad_attend.reshape(width, -1)
    owned = [
        lax.psum_scatter(g.astype(F32), AXES, scatter_dimension=0, tiled=True)
        for g in (grad_attend, grad_output, grad_expand, grad_shrink)
    ]
    grad_table = lax.dot_general(
        onehot.astype(F32),
        grad_bias.reshape(HEADS, 128, 128)[:, :high].astype(F32).reshape(HEADS, -1),
        (((1,), (1,)), ((), ())),
        precision=HIGH,
    )
    vector_local = jnp.concatenate([late_sums, early_sums], axis=0)
    vector_sum, table_sum = lax.psum((vector_local, grad_table), AXES)
    vector_grad, table_grad = vector_sum / total, table_sum / total
    matrix_grads = tuple((g / total for g in owned))
    grad_squares = jnp.stack([jnp.sum(g * g) for g in matrix_grads])
    weight_squares = jnp.stack([jnp.sum(m * m) for m in masters])
    grad_total, weight_total = lax.psum((grad_squares, weight_squares), AXES)
    clip_norm = jnp.sqrt(
        jnp.sum(grad_total) + jnp.sum(vector_grad * vector_grad) + jnp.sum(table_grad * table_grad)
    )
    factor = jnp.minimum(1.0, CLIP_LIMIT / clip_norm)
    sectioned = [
        moments(matrix_grads[k], firsts[k], seconds[k], masters[k], factor) for k in range(4)
    ]
    update_squares = jnp.stack([jnp.sum(s[2] * s[2]) for s in sectioned])
    update_total = lax.psum(update_squares, AXES)
    weight_norms = jnp.sqrt(weight_total)
    update_norms = jnp.sqrt(update_total)
    matrix_outs = []
    for k in range(4):
        fresh = masters[k] - LEARN_RATE * (weight_norms[k] / update_norms[k]) * sectioned[k][2]
        matrix_outs.append(
            (matrix_grads[k], sectioned[k][0], sectioned[k][1], fresh, fresh.astype(jnp.bfloat16))
        )
    vec_first, vec_second, vec_update = moments(
        vector_grad, vector_first, vector_second, vector_params, factor
    )
    vec_ratio = jnp.sqrt(jnp.sum(vector_params * vector_params, axis=1, keepdims=True)) / jnp.sqrt(
        jnp.sum(vec_update * vec_update, axis=1, keepdims=True)
    )
    vec_fresh = vector_params - LEARN_RATE * vec_ratio * vec_update
    tab_first, tab_second, tab_update = moments(
        table_grad, table_first, table_second, position_table, factor
    )
    tab_ratio = jnp.sqrt(jnp.sum(position_table * position_table)) / jnp.sqrt(
        jnp.sum(tab_update * tab_update)
    )
    tab_fresh = position_table - LEARN_RATE * tab_ratio * tab_update
    matrix_norms = jnp.stack([weight_norms, update_norms])
    attend_o, output_o, expand_o, shrink_o = matrix_outs
    return (
        block_out,
        input_grad,
        attend_o[0],
        attend_o[1],
        attend_o[2],
        attend_o[3],
        attend_o[4],
        output_o[0],
        output_o[1],
        output_o[2],
        output_o[3],
        output_o[4],
        expand_o[0],
        expand_o[1],
        expand_o[2],
        expand_o[3],
        expand_o[4],
        shrink_o[0],
        shrink_o[1],
        shrink_o[2],
        shrink_o[3],
        shrink_o[4],
        vector_grad,
        vec_first,
        vec_second,
        vec_fresh,
        table_grad,
        tab_first,
        tab_second,
        tab_fresh,
        clip_norm,
        matrix_norms,
    )


def solution(mesh):
    in_specs = (
        P(("dp", "fsdp"), None, None),
        P(("dp", "fsdp"), None, None),
        P(("dp", "fsdp"), None),
        P(("dp", "fsdp"), None),
        P(("dp", "fsdp"), None),
        P(("dp", "fsdp"), None),
        P(("dp", "fsdp"), None),
        P(("dp", "fsdp"), None),
        P(("dp", "fsdp"), None),
        P(("dp", "fsdp"), None),
        P(("dp", "fsdp"), None),
        P(("dp", "fsdp"), None),
        P(("dp", "fsdp"), None),
        P(("dp", "fsdp"), None),
        P(("dp", "fsdp"), None),
        P(),
        P(),
        P(),
        P(),
        P(),
        P(),
    )
    out_specs = (
        P(("dp", "fsdp"), None, None),
        P(("dp", "fsdp"), None, None),
        P(("dp", "fsdp"), None),
        P(("dp", "fsdp"), None),
        P(("dp", "fsdp"), None),
        P(("dp", "fsdp"), None),
        P(("dp", "fsdp"), None),
        P(("dp", "fsdp"), None),
        P(("dp", "fsdp"), None),
        P(("dp", "fsdp"), None),
        P(("dp", "fsdp"), None),
        P(("dp", "fsdp"), None),
        P(("dp", "fsdp"), None),
        P(("dp", "fsdp"), None),
        P(("dp", "fsdp"), None),
        P(("dp", "fsdp"), None),
        P(("dp", "fsdp"), None),
        P(("dp", "fsdp"), None),
        P(("dp", "fsdp"), None),
        P(("dp", "fsdp"), None),
        P(("dp", "fsdp"), None),
        P(("dp", "fsdp"), None),
        P(),
        P(),
        P(),
        P(),
        P(),
        P(),
        P(),
        P(),
        P(),
        P(),
    )
    sizes = (mesh.shape["dp"], mesh.shape["fsdp"])
    return jax.shard_map(functools.partial(local, *sizes), mesh=mesh, in_specs=in_specs, out_specs=out_specs, check_vma=False)
```

```python
import functools

import jax
import jax.numpy as jnp
from jax import lax
from jax.experimental import pallas as pl
from jax.experimental.pallas import tpu as pltpu
from jax.sharding import PartitionSpec as P

MESH = pl.DeviceIdType.MESH
AXES = ("dp", "fsdp")
VMEM_LIMIT = 61 * 1024 * 1024

HEADS = 32
WS = 10
STEP = 10


EPSILON = 1e-05
MOMENT_ONE = 0.9
MOMENT_TWO = 0.999
LEARN_RATE = 0.3
DECAY = 0.01
ADAM_EPS = 1e-06
CLIP_LIMIT = 0.05
MASK_FILL = 10000.0
HIGH = lax.Precision.HIGHEST
BF, F32 = jnp.bfloat16, jnp.float32


def position_index(size):
    cells = jnp.arange(size * size, dtype=jnp.int32)
    rows = cells // size
    cols = cells % size
    drow = rows[:, None] - rows[None, :] + size - 1
    dcol = cols[:, None] - cols[None, :] + size - 1
    return drow * (2 * size - 1) + dcol


def moments(grad, first, second, weight, factor):
    clipped = grad * factor
    first_new = MOMENT_ONE * first + (1.0 - MOMENT_ONE) * clipped
    second_new = MOMENT_TWO * second + (1.0 - MOMENT_TWO) * clipped * clipped
    update = (
        first_new
        / (1.0 - MOMENT_ONE**STEP)
        / (jnp.sqrt(second_new / (1.0 - MOMENT_TWO**STEP)) + ADAM_EPS)
        + DECAY * weight
    )
    return (first_new, second_new, update)


def whole(shape):
    zeros = (0,) * len(shape)
    return pl.BlockSpec(shape, lambda *s: zeros, pipeline_mode=pl.Buffered(1))


def whole_out(shape):
    zeros = (0,) * len(shape)
    return pl.BlockSpec(shape, lambda *s: zeros, pipeline_mode=pl.Buffered(1))


def struct(shape, dtype):
    return jax.ShapeDtypeStruct(shape, dtype)


class Place:
    def __init__(self, sems):
        dp = lax.axis_index("dp")
        fsdp = lax.axis_index("fsdp")
        self.z, self.x = dp // 2, dp % 2
        self.y, self.c = fsdp // 2, fsdp % 2
        self.mate = self.z + 1 - 2 * lax.rem(self.z, 2)
        self.far = lax.rem(self.z + 2, 4)
        self.cross = 3 - self.z
        self.inner = (self.z == 1) | (self.z == 2)
        self.pair = 2 * (self.z // 2)
        self.sems = sems
        self.used = 0

    def sem(self):
        self.used += 1
        return self.sems.at[self.used - 1]

    def to(self, z=None, x=None, y=None, c=None):
        z = self.z if z is None else z
        x = self.x if x is None else x
        y = self.y if y is None else y
        c = self.c if c is None else c
        return (z * 2 + x, y * 2 + c)

    def peers(self):
        return [
            self.to(z=self.mate),
            self.to(z=self.far),
            self.to(z=self.cross),
            self.to(x=1 - self.x),
            self.to(y=1 - self.y),
            self.to(c=1 - self.c),
        ]

    def plane(self):
        found = []
        for i in range(1, 8):
            x = self.x + (i // 4) * (1 - 2 * self.x)
            y = self.y + (i // 2 % 2) * (1 - 2 * self.y)
            c = self.c + (i % 2) * (1 - 2 * self.c)
            found.append(self.to(x=x, y=y, c=c))
        return found

    def greet(self, plane=False):
        barrier = pltpu.get_barrier_semaphore()
        peers = self.peers()[:3] + self.plane() if plane else self.peers()
        for peer in peers:
            pl.semaphore_signal(barrier, inc=1, device_id=peer, device_id_type=MESH)
        pl.semaphore_wait(barrier, len(peers))

    def send(self, source, target, device, recv_sem=None):
        return pltpu.make_async_remote_copy(
            src_ref=source,
            dst_ref=target,
            send_sem=self.sem(),
            recv_sem=self.sem() if recv_sem is None else recv_sem,
            device_id=device,
            device_id_type=MESH,
        )

    def move(self, source, target):
        return pltpu.make_async_copy(source, target, self.sem())


def gather_sems(groups):
    return 1 + 2 * 5 + 2 * 5 * groups


def gather_events(place, own, out, groups, relay):
    z, x, y, c = place.z, place.x, place.y, place.c
    half = own.shape[0] // 2
    ox, oy, oc = 1 - x, 1 - y, 1 - c
    xp, yp, cp = place.to(x=ox), place.to(y=oy), place.to(c=oc)
    mate, cross = place.to(z=place.mate), place.to(z=place.cross)
    first = jnp.where(place.inner, place.cross, place.far)
    second = jnp.where(place.inner, place.far, place.cross)
    low, high = pl.ds(0, half), pl.ds(half, half)
    slot = lambda at: out.at[at, x, y, c]
    mine = place.move(own, slot(z))
    to_mate = place.send(own, slot(z), mate)
    if relay:
        came_one, came_two = place.sem(), place.sem()
        across_one = place.send(own, slot(z), cross, came_one)
        across_two = place.send(slot(place.mate), slot(place.mate), cross, came_two)
        on_one = place.send(slot(first), slot(first), mate, came_one)
        on_two = place.send(slot(second), slot(second), mate, came_two)
    else:
        to_far = place.send(own, slot(z), place.to(z=place.far))
        to_cross = place.send(own, slot(z), cross)
    if groups == 1:
        spans = [pl.ds(0, 4)]
    elif groups == 2:
        spans = [pl.ds(place.pair, 2), pl.ds(2 - place.pair, 2)]
    elif relay:
        spans = [pl.ds(at, 1) for at in (z, place.mate, first, second)]
    else:
        spans = [pl.ds(at, 1) for at in (z, place.mate, place.far, place.cross)]

    def forward(ref, device):
        return place.send(ref, ref, device)

    x_full = [forward(out.at[s, x, y, c], xp) for s in spans]
    y_full = [forward(out.at[s, x, y, c], yp) for s in spans]
    x_half = [forward(out.at[s, ox, y, c, low], yp) for s in spans]
    y_half = [forward(out.at[s, x, oy, c, high], xp) for s in spans]
    to_twin = [forward(out.at[s, :, :, c], cp) for s in spans]

    def begin():
        mine.start()
        to_mate.start()
        if relay:

            @pl.when(place.inner)
            def _():
                across_one.start()

        else:
            to_far.start()
            to_cross.start()
        mine.wait()
        if groups == 4:
            send_line(0)

    def send_line(g):
        x_full[g].start()
        y_full[g].start()

    def on_line():
        for copy in (to_mate, to_far, to_cross):
            copy.wait_recv()
        send_line(0)

    def on_place(g):
        (None, to_mate, to_far, to_cross)[g].wait_recv()
        send_line(g)

    def on_mate():
        to_mate.wait_recv()

        @pl.when(place.inner)
        def _():
            across_two.start()

        if groups == 2:
            send_line(0)
        if groups == 4:
            send_line(1)

    def relay_one():
        @pl.when(place.inner)
        def _():
            across_one.wait_recv()
            on_one.start()

    def on_first():
        @pl.when(jnp.logical_not(place.inner))
        def _():
            on_one.wait_recv()

        if groups == 4:
            send_line(2)

    def relay_two():
        @pl.when(place.inner)
        def _():
            across_two.wait_recv()
            on_two.start()

    def on_second():
        @pl.when(jnp.logical_not(place.inner))
        def _():
            on_two.wait_recv()

        send_line(groups - 1)

    def on_side(g):
        x_full[g].wait_recv()
        x_half[g].start()
        y_full[g].wait_recv()
        y_half[g].start()

    def on_corner(g):
        x_half[g].wait_recv()
        y_half[g].wait_recv()
        to_twin[g].start()

    def arrive():
        for copy in to_twin:
            copy.wait_recv()

    def finish():
        for copies in (to_twin, x_full, y_full, x_half, y_half, [to_mate]):
            for copy in copies:
                copy.wait_send()
        if relay:

            @pl.when(place.inner)
            def _():
                for copy in (across_one, across_two, on_one, on_two):
                    copy.wait_send()

        else:
            to_far.wait_send()
            to_cross.wait_send()

    size = 4 // groups
    lines = lambda g: [("x", size, ("xf", g)), ("y", size, ("yf", g))]
    if relay:
        one = {1: [], 2: [], 4: lines(0)}[groups]
        events = [
            (begin, [], [("z", 1, "mate"), ("w", 1, "a1")] + one),
            (on_mate, ["mate"], [("w", 1, "a2")] + {1: [], 2: lines(0), 4: lines(1 % groups)}[groups]),
            (relay_one, ["a1"], [("z", 1, "o1")]),
            (on_first, ["o1"], lines(2) if groups == 4 else []),
            (relay_two, ["a2"], [("z", 1, "o2")]),
            (on_second, ["o2"], lines(groups - 1)),
        ]
    elif groups == 4:
        events = [(begin, [], [("z", 1.33, ("z", g)) for g in (1, 2, 3)] + lines(0))]
        for g in (1, 2, 3):
            events.append((functools.partial(on_place, g), [("z", g)], lines(g)))
    else:
        events = [(begin, [], [("z", 4, "z")]), (on_line, ["z"], lines(0))]
    for g in range(groups):
        half_size = 0.5 * size
        halves = [("y", half_size, ("xh", g)), ("x", half_size, ("yh", g))]
        events.append((functools.partial(on_side, g), [("xf", g), ("yf", g)], halves))
    for g in range(groups):
        twins = [("c", size * 4, ("t", g))]
        events.append((functools.partial(on_corner, g), [("xh", g), ("yh", g)], twins))
    events.append((arrive, [("t", g) for g in range(groups)], []))
    return events, finish


def scatter_sems(groups):
    return groups * (1 + 2 * 5) + 2 * 3


def scatter_scratch(rows, columns):
    shape = lambda *lead: pltpu.VMEM(lead + (columns,), jnp.bfloat16)
    return [
        shape(4, 2, 2, rows),
        shape(4, 2, 2, rows),
        shape(4, rows // 2),
        shape(4, rows // 2),
        shape(4, rows),
        shape(4, rows),
        shape(3, rows),
    ]


def scatter_events(place, grads, part, total, scratch, groups):
    z, x, y, c = place.z, place.x, place.y, place.c
    held, twin, corner_low, corner_high, from_x, from_y, from_z = scratch
    rows, columns = total.shape
    half = rows // 2
    part = pl.ds(*part)
    ox, oy, oc = 1 - x, 1 - y, 1 - c
    xp, yp, cp = place.to(x=ox), place.to(y=oy), place.to(c=oc)
    if groups == 1:
        spans, lines = [(0, 4)], [[0, 1, 2, None]]
    elif groups == 2:
        spans = [(2 - place.pair, 2), (place.pair, 2)]
        lines = [[0, 1], [2, None]]
    else:
        spans = [(place.far, 1), (place.cross, 1), (place.mate, 1), (z, 1)]
        lines = [[0], [1], [2], [None]]
    ds = [pl.ds(*span) for span in spans]
    low, high = pl.ds(0, half), pl.ds(half, half)
    loads = [place.move(grads.at[d, :, :, c, part], held.at[d]) for d in ds]
    twins = [place.send(grads.at[d, :, :, oc, part], twin.at[d], cp) for d in ds]
    out_low = [place.send(held.at[d, ox, oy, low], corner_low.at[d], xp) for d in ds]
    out_high = [place.send(held.at[d, ox, oy, high], corner_high.at[d], yp) for d in ds]
    out_x = [place.send(held.at[d, ox, y], from_x.at[d], xp) for d in ds]
    out_y = [place.send(held.at[d, x, oy], from_y.at[d], yp) for d in ds]
    line = [place.far, place.cross, place.mate]
    out_z = [place.send(held.at[at, x, y], from_z.at[i], place.to(z=at)) for i, at in enumerate(line)]

    def summed(store, first, count, parts):
        def step(i, carry):
            at = pl.ds(pl.multiple_of(first + i * 16, 16), 16)
            store(at, functools.reduce(jnp.add, [part(at).astype(jnp.float32) for part in parts]))
            return carry

        lax.fori_loop(0, count // 16, step, 0)

    def read(ref, *index, lo=0):
        if lo:
            return lambda at: ref[index + (pl.ds(at.start - lo, 16),)]
        return lambda at: ref[index + (at,)]

    def write(ref, *index):
        def store(at, value):
            ref[index + (at,)] = value.astype(ref.dtype)

        return store

    def each(g, body):
        start, size = spans[g]

        def step(i, carry):
            body(start + i)
            return carry

        lax.fori_loop(0, size, step, 0)

    def begin():
        for g in range(len(spans)):
            twins[g].start()
            loads[g].start()

    def on_corner(g):
        loads[g].wait()
        twins[g].wait_recv()

        def body(at):
            here = (at, ox, oy)
            summed(write(held, *here), 0, rows, [read(held, *here), read(twin, *here)])

        each(g, body)
        out_low[g].start()
        out_high[g].start()

    def on_side(g):
        out_high[g].wait_recv()

        def body(at):
            here = (at, ox, y)
            own = [read(held, *here), read(twin, *here)]
            summed(write(held, *here), 0, half, own)
            summed(write(held, *here), half, half, own + [read(corner_high, at, lo=half)])

        each(g, body)
        out_x[g].start()
        out_low[g].wait_recv()

        def body(at):
            here = (at, x, oy)
            own = [read(held, *here), read(twin, *here)]
            summed(write(held, *here), half, half, own)
            summed(write(held, *here), 0, half, own + [read(corner_low, at)])

        each(g, body)
        out_y[g].start()

    def on_line(g):
        out_x[g].wait_recv()
        out_y[g].wait_recv()
        for i in lines[g]:
            at = z if i is None else line[i]
            here = (at, x, y)
            parts = [read(held, *here), read(twin, *here), read(from_x, at), read(from_y, at)]
            if i is None:
                for copy in out_z:
                    copy.wait_recv()
                parts += [read(from_z, j) for j in range(3)]
                summed(write(total), 0, rows, parts)
            else:
                summed(write(held, *here), 0, rows, parts)
                out_z[i].start()

    def finish():
        for copies in (twins, out_low, out_high, out_x, out_y, out_z):
            for copy in copies:
                copy.wait_send()

    size = 4 // groups
    events = [(begin, [], [("c", 4 * size, ("t", g)) for g in range(groups)])]
    for g in range(groups):
        halves = [("x", 0.5 * size, ("l", g)), ("y", 0.5 * size, ("h", g))]
        events.append((functools.partial(on_corner, g), [("t", g)], halves))
    for g in range(groups):
        fulls = [("x", size, ("x", g)), ("y", size, ("y", g))]
        events.append((functools.partial(on_side, g), [("l", g), ("h", g)], fulls))
    for g in range(groups):
        sent = [("z", 1.33, ("z", i)) for i in lines[g] if i is not None]
        waits = [("x", g), ("y", g)]
        if groups > 1 and g == groups - 1:
            waits += [("z", i) for i in range(2)]
        events.append((functools.partial(on_line, g), waits, sent))
    if groups == 4:
        events[-1][1].append(("z", 2))
    return events, finish


HOP = 2.5
LINK = 90e3
CORE = 500e3
SLACK = 1.2
BACKLOGS = [(a, b) for a in (0.0, 1.0, 2.0, 4.0) for b in (0.5, 2.0, 4.0, 8.0, 16.0)]


def plan_of(lists, starts):
    return min((simulate(lists, starts, limits) for limits in BACKLOGS), key=lambda plan: plan[0])[1:]


def simulate(lists, starts, limits):
    free = {"x": 0.0, "y": 0.0, "z": 0.0, "w": 0.0, "c": 0.0}
    arrival, pending = {}, []
    for number, ((events, finish), move) in enumerate(lists):
        for order, (event, waits, sends) in enumerate(events):
            pending.append((number, order, event, [(number, w) for w in waits], sends, move))

    def ready(item):
        number, order, _, waits, _, move = item
        if any(w not in arrival for w in waits):
            return None
        if order:
            if any(p[0] == number and p[1] == 0 for p in pending):
                return None
        return max([arrival[w] for w in waits], default=0.0)

    def run(item, now):
        number, _, event, _, sends, move = item
        pending.remove(item)
        for link, units, name in sends:
            rate = CORE if link == "c" else LINK
            cores = 1 if link == "c" else 2
            took = units * cores * move["bytes"] / rate
            free[link] = max(free[link], now) + took
            arrival[number, name] = free[link] + HOP
        return event

    before, now = {}, 3.0
    places = [(i, j, took) for i, parts in enumerate(starts) for j, took in enumerate(parts)]
    for step, part, took in places + [(len(starts), 0, 0.0)]:
        last = step == len(starts)
        while True:
            found, forced_found = None, None
            top = min([p[0] for p in pending if p[5]["step"] <= step], default=0)
            pressed = any(p[5]["need"] is not None and p[5]["need"] <= step for p in pending)
            for item in pending:
                number, order, _, _, sends, move = item
                if move["step"] > step:
                    continue
                at = ready(item)
                if at is None:
                    continue
                if last or (move["need"] is not None and move["need"] <= step):
                    if forced_found is None or at < forced_found[0]:
                        forced_found = (at, item)
                elif number > top:
                    backlog = max((free[k] - now for k, _, _ in sends if k != "c"), default=0.0)
                    if backlog > limits[0 if pressed else 1]:
                        continue
                if at <= now and (found is None or number < found[1][0]):
                    found = (at, item)
            if found is None:
                found = forced_found
            if found is None:
                break
            now = max(now, found[0])
            before.setdefault((step, part), []).append(run(found[1], now))
        now += SLACK * took
    after = before.pop((len(starts), 0), [])
    assert not pending
    return now, before, after + [finish for (_, finish), _ in lists]


def gather(array, dtype, groups=4, relay=True, need=None, step=0, columns=None):
    columns = ((0, array.shape[1]),) if columns is None else columns
    shape = (array.shape[0], sum(n for _, n in columns))
    return dict(
        kind="gather",
        array=array,
        dtype=dtype,
        groups=groups,
        relay=relay,
        bytes=shape[0] * shape[1] * jnp.dtype(dtype).itemsize,
        need=need,
        step=step,
        columns=columns,
        shape=shape,
    )


def scatter(array, shape=None, groups=4, step=0):
    shape = array.shape[4:] if shape is None else shape
    size = 2 * shape[0] * shape[1]
    return dict(kind="scatter", array=array, shape=shape, groups=groups, bytes=size, need=None, step=step)


def fused_kernel(body, counts, moves, starts, *refs):
    n_in, n_out, n_scratch = counts
    numbers = []
    for move in moves:
        if isinstance(move["array"], int):
            numbers.append(None)
        else:
            same = [i for i, m in enumerate(moves) if m["array"] is move["array"]][0]
            known = numbers[same] if same < len(numbers) else None
            numbers.append(max([n for n in numbers if n is not None], default=-1) + 1 if known is None else known)
    n_given = max([n for n in numbers if n is not None], default=-1) + 1
    ins, given = refs[:n_in], list(refs[n_in : n_in + n_given])
    refs = refs[n_in + n_given :]
    outs, made = refs[:n_out], refs[n_out : n_out + len(moves)]
    refs = refs[n_out + len(moves) :]
    scratch, spare = refs[:n_scratch], list(refs[n_scratch:-1])
    step = pl.program_id(0)
    place = Place(refs[-1])
    lists, lows = [], []
    for move, target, number in zip(moves, made, numbers):
        source = scratch[move["array"]] if number is None else given[number]
        if move["kind"] == "gather":
            low = spare.pop(0)
            lows.append((source, low, move["columns"]))
            events = gather_events(place, low, target, move["groups"], move["relay"])
        else:
            buffers = [spare.pop(0) for _ in range(7)]
            rows = (0, move["shape"][0])
            events = scatter_events(place, source, rows, target, buffers, move["groups"])
        lists.append((events, move))
    before, after = plan_of(lists, starts)

    @pl.when(step == 0)
    def _():
        for source, low, columns in lows:
            put = 0
            for first, size in columns:
                low[:, put : put + size] = source[:, first : first + size].astype(low.dtype)
                put += size
        place.greet()

    def hook(part):
        steps = sorted(at for at, number in before if number == part)

        def one(at):
            @pl.when(step == at)
            def _():
                for event in before[at, part]:
                    event()

        def among(steps):
            if len(steps) == 1:
                one(steps[0])
            elif steps:
                middle = len(steps) // 2
                lax.cond(
                    step < steps[middle],
                    lambda: among(steps[:middle]),
                    lambda: among(steps[middle:]),
                )

        among(steps)

    hook(0)
    body(made, hook, *ins, *outs, *scratch)

    @pl.when(step == len(starts) - 1)
    def _():
        for event in after:
            event()


def call(body, name, steps, ins, in_specs, outs, out_specs, scratch=(), moves=(), collective=None, starts=()):
    scratch = list(scratch)
    params = dict(vmem_limit_bytes=VMEM_LIMIT)
    counts = (len(ins), len(outs), len(scratch))
    kernel = functools.partial(body, (), lambda part: None)
    if moves:
        params.update(collective_id=collective, has_side_effects=True)
        kernel = functools.partial(fused_kernel, body, counts, moves, starts)
        assert len(starts) == steps
    ins, in_specs, outs, out_specs = list(ins), list(in_specs), list(outs), list(out_specs)
    sems = 0
    for move in moves:
        array = move["array"]
        if move["kind"] == "gather":
            if not any(array is other for other in ins[counts[0] :]):
                ins.append(array)
                in_specs.append(whole(array.shape))
            outs.append(struct((4, 2, 2, 2) + move["shape"], move["dtype"]))
            out_specs.append(pl.BlockSpec(memory_space=pl.ANY))
            scratch.append(pltpu.VMEM(move["shape"], move["dtype"]))
            sems += gather_sems(move["groups"])
        else:
            if not isinstance(array, int):
                ins.append(array)
                in_specs.append(pl.BlockSpec(memory_space=pl.ANY))
            outs.append(struct(move["shape"], F32))
            out_specs.append(whole_out(move["shape"]))
            scratch += scatter_scratch(*move["shape"])
            sems += scatter_sems(move["groups"])
    if moves:
        scratch.append(pltpu.SemaphoreType.DMA((sems,)))
    made = pl.pallas_call(
        kernel,
        name=name,
        grid=(steps,),
        out_shape=outs,
        in_specs=in_specs,
        out_specs=out_specs,
        scratch_shapes=scratch,
        compiler_params=pltpu.CompilerParams(**params),
    )(*ins)
    return made[: counts[1]], made[counts[1] :]


def times(left, right):
    return jnp.dot(left, right, preferred_element_type=jnp.float32)


def times_transpose(left, right):
    return lax.dot_general(
        left, right, (((1,), (1,)), ((), ())), preferred_element_type=jnp.float32
    )


def transpose_times(left, right):
    return lax.dot_general(
        left, right, (((0,), (0,)), ((), ())), preferred_element_type=jnp.float32
    )


def normalize(value):
    centre = value - jnp.mean(value, axis=-1, keepdims=True)
    rstd = lax.rsqrt(jnp.mean(centre * centre, axis=-1, keepdims=True) + EPSILON)
    return centre * rstd, rstd


def norm_back(grad_out, normed, rstd, gain):
    scaled = grad_out * gain
    mean_one = jnp.mean(scaled, axis=-1, keepdims=True)
    mean_two = jnp.mean(scaled * normed, axis=-1, keepdims=True)
    return rstd * (scaled - mean_one - normed * mean_two)


def eight(value):
    rows, columns = value.shape
    return jnp.sum(value.reshape(rows // 8, 8, columns), axis=0)


def gelu_parts(value):
    bell = jnp.exp(-0.5 * value * value)
    size = jnp.abs(value)
    t = 1.0 / (1.0 + 0.23164189 * size)
    tail = t * (
        0.127414796
        + t * (-0.142248368 + t * (0.7107068705 + t * (-0.7265760135 + t * 0.5307027145)))
    )
    tail = tail * bell
    phi_big = jnp.where(value >= 0.0, 1.0 - tail, tail)
    return phi_big, bell * 0.3989422804014327


STRIP = 32


def strips(rows, body, carry, unroll=2, hooks=()):
    def step(i, value):
        return body(pl.ds(pl.multiple_of(i * STRIP, STRIP), STRIP), value)

    count, parts = rows // STRIP, max(len(hooks), 1)
    for part in range(parts):
        if hooks:
            hooks[part]()
        first, last = part * count // parts, (part + 1) * count // parts
        carry = lax.fori_loop(first, last, step, carry, unroll=unroll)
    return carry


def enter_step(step, patches, cotangent, keep, vec, hidden, source, upstream, bias_sum, spare, wide):
    cells, windows, width = patches.shape
    high = spare.shape[0] // 2
    gain, shift = vec[0:1], vec[1:2]

    @pl.when(step == 0)
    def _():
        spare[...] = jnp.zeros_like(spare)
        wide[...] = patches[...].astype(F32)

    @pl.when(step == 2)
    def _():
        bias_sum[...] = jnp.zeros_like(bias_sum)
        wide[...] = cotangent[...].astype(F32)

    for pair in range(windows // 2):
        at = pl.ds(pair * 2 * high, 2 * high)
        half = windows // 4

        @pl.when(step == pair // half)
        def _(pair=pair, at=at):
            for w in range(2):
                spare[pl.ds(w * high, cells)] = wide[:, 2 * pair + w, :]
            source[at] = spare[...].astype(BF)
            for w in range(2):
                normed, _ = normalize(spare[pl.ds(w * high, cells)])
                spare[pl.ds(w * high, cells)] = normed * gain + shift
            hidden[at] = spare[...].astype(BF)

        @pl.when(step == 2 + pair // half)
        def _(pair=pair, at=at):
            for w in range(2):
                mask = jnp.concatenate([keep[2 * pair + w]] * (width // 128), axis=1)
                spare[pl.ds(w * high, cells)] = wide[:, 2 * pair + w, :] * mask[:cells]
            bias_sum[...] += eight(spare[...])
            upstream[at] = spare[...].astype(BF)


def bias_step(step, table, bias, padded, stack):
    heads, high, _ = bias.shape
    cells = WS * WS
    side = 2 * WS - 1
    middle = (WS - 1) * side + WS - 1
    spot = lax.broadcasted_iota(jnp.int32, (256, 128), 0)
    cell = lax.broadcasted_iota(jnp.int32, (256, 128), 1)
    put = ((cell // WS) * side + lax.rem(cell, WS) == spot) & (cell < cells)

    @pl.when(step == 0)
    def _():
        padded[...] = jnp.zeros_like(padded)
        padded[:, : table.shape[1]] = table[...]
        bias[:, pl.ds(cells, high - cells)] = jnp.zeros((heads, high - cells, 128), F32)

    count = cells // 4
    for part in range(4):

        @pl.when(step == part)
        def _(part=part):
            for n in range(count):
                j = part * count + n
                shift = middle - (j // WS) * side - j % WS
                rolled = pltpu.roll(padded[...], (384 - shift) % 384, axis=1)
                stack[pl.ds(heads * n, heads)] = rolled[:, :256]
            found = jnp.dot(stack[...], put.astype(F32), precision=HIGH, preferred_element_type=F32)
            for n in range(count):
                bias[:, part * count + n, :] = found[heads * n : heads * n + heads]


def lanes_of(head):
    lane = lax.broadcasted_iota(jnp.int32, (1, 128), 1)
    return (lane // 32) == head


def pick(value, head):
    return jnp.where(lanes_of(head), value, jnp.zeros_like(value))


def spread_heads(value):
    head = lax.broadcasted_iota(jnp.int32, value.shape, 0) // 32
    return jnp.concatenate([jnp.where(head == h, value, jnp.zeros_like(value)) for h in range(4)], axis=1)


def own_heads(value):
    return jnp.concatenate(
        [value[32 * h : 32 * h + 32, 128 * h : 128 * h + 128] for h in range(4)], axis=0
    )


def stack_heads(value):
    return jnp.concatenate([pick(value, h) for h in range(4)], axis=0)


def with_rows(value, rows):
    return jnp.concatenate([value, jnp.zeros((rows - value.shape[0], value.shape[1]), F32)], axis=0)


def attend_step(hook, group, pair, hidden, weights, vec, bias, mask, query, keys, values, probs, out):
    windows, _, columns = query.shape
    high = hidden.shape[0] // windows

    @pl.when(pair == 0)
    def _():
        at = pl.ds(pl.multiple_of(group * columns, columns), columns)
        for j, (target, bias_row) in enumerate(((query, 2), (keys, None), (values, 3))):
            product = times(hidden[...], weights(j))
            if bias_row is not None:
                product = product + vec[bias_row : bias_row + 1, at]
            for w in range(windows):
                here = with_rows(product[w * high : (w + 1) * high], target.shape[1])
                target[w] = here.astype(BF)

        hook(1)

    scale = 32 ** (-0.5)
    done = []
    for w in range(2):
        window = pair * 2 + w
        parts = []
        for g in range(columns // 128):
            at = pl.ds(g * 128, 128)
            q, k, v = query[window, :, at], keys[window, :, at], values[window, :, at]
            scores = times(k, spread_heads(q.T))
            found = []
            for h in range(4):
                head = group * (columns // 32) + g * 4 + h
                score = scores[:, 128 * h : 128 * h + 128] * scale + bias[head] + mask[window]
                score = jnp.exp(score - jnp.max(score, axis=0, keepdims=True))
                prob = (score * (1.0 / jnp.sum(score, axis=0, keepdims=True))).astype(BF)
                probs[w, g * 4 + h] = prob
                found.append(prob)
            mixed = times(v.T, jnp.concatenate(found, axis=1))
            parts.append(own_heads(mixed).T[:high])
        done.append(jnp.concatenate(parts, axis=1))
    rows = pl.ds(pl.multiple_of(pair * 2 * high, 16), 2 * high)
    at = pl.ds(pl.multiple_of(group * columns, columns), columns)
    out[rows, at] = jnp.concatenate(done, axis=0).astype(BF)


def flat(value):
    return value.reshape(-1, value.shape[-1])


def forward_body(direct, made, hook, *refs):
    refs = list(refs)
    take = lambda n: [refs.pop(0) for _ in range(n)]
    patches, cotangent, keep, vec, table = take(5)
    *w_attend, w_output, w_low, w_high = made[:7] if direct else take(7)
    hidden_t, source, upstream, bias_sum, query, keys, values, probs = take(8)
    attended, middle, hidden_two_t, act, slope, grad = take(6)
    spare, hidden, wqkv, wo, we, hidden_two, before, wide, bias, mask, padded, stack, sems = refs
    step = pl.program_id(0)
    rows, width = hidden.shape
    windows, _, columns = query.shape
    pairs, groups = windows // 2, width // columns
    enters, attends = pairs, pairs * groups
    chunk = act.shape[1]
    per_half = w_low.shape[-1] // chunk
    chunks = 2 * per_half

    @pl.when(step < enters)
    def _():
        enter_step(step, patches, cotangent, keep, vec, hidden, source, upstream, bias_sum, spare, wide)
        bias_step(step, table, bias, padded, stack)

    @pl.when(step == 0)
    def _():
        there = lax.broadcasted_iota(jnp.int32, mask.shape, 1) < patches.shape[0]
        mask[...] = jnp.where(there, (keep[...] - 1.0) * MASK_FILL, -1e30)

    inner_step = step - enters
    group, pair = inner_step // pairs, lax.rem(inner_step, pairs)

    def load_qkv(number):
        slot = number % 2
        return pltpu.make_async_copy(w_attend[number], wqkv.at[slot], sems.at[slot])

    load_wo = pltpu.make_async_copy(w_output, wo, sems.at[2])

    def load_we(half, index):
        slot = lax.rem(index, 2)
        at = pl.ds(pl.multiple_of(lax.rem(index, per_half) * chunk, chunk), chunk)
        source = (w_low, w_high)[half]
        return pltpu.make_async_copy(source.at[:, :, :, :, :, at], we.at[slot], sems.at[3 + slot])

    @pl.when((inner_step >= 0) & (inner_step < attends))
    def _():
        @pl.when(inner_step == 0)
        def _():
            hidden_t[...] = hidden[...].T

        for number in range(groups):

            @pl.when(inner_step == number * pairs)
            def _(number=number):
                copy = load_qkv(number)
                copy.start()
                copy.wait()

        slot = lax.rem(group, 2)
        weights = lambda j: flat(wqkv[slot, :, :, :, :, :, pl.ds(j * columns, columns)])
        attend_step(hook, group, pair, hidden, weights, vec, bias, mask, query, keys, values, probs, attended)

    @pl.when(inner_step == attends)
    def _():
        load_wo.start()
        load_wo.wait()
        for j in range(2):
            at = pl.ds(j * (width // 2), width // 2)
            middle[:, at] = times(attended[...], flat(wo[:, :, :, :, :, at])) + vec[4:5, at]

        hook(1)

        def strip(at, carry):
            value = middle[at] + source[at].astype(F32)
            middle[at] = value
            normed, _ = normalize(value)
            hidden_two[at] = (normed * vec[5:6] + vec[6:7]).astype(BF)
            return carry

        strips(rows, strip, 0)
        hidden_two_t[...] = hidden_two[...].T

    @pl.when(inner_step > attends)
    def _():
        index = inner_step - attends - 1
        for half in range(2):

            @pl.when(index == half * per_half)
            def _(half=half):
                load_we(half, index).start()

            @pl.when(index // per_half == half)
            def _(half=half):
                load_we(half, index).wait()

                @pl.when(lax.rem(index, per_half) < per_half - 1)
                def _():
                    load_we(half, index + 1).start()

        before[...] = times(hidden_two[...], flat(we[lax.rem(index, 2)]))
        per = width // chunk
        shift_at = pl.ds(pl.multiple_of(lax.rem(index, per) * chunk, chunk), chunk)
        shift = vec[pl.ds(8 + index // per, 1), shift_at]
        hook(1)

        def strip(at, carry):
            value = before[at] + shift
            big, small = gelu_parts(value)
            act[at] = (value * big).astype(BF)
            slope[at] = (big + value * small).astype(BF)
            return carry

        strips(rows, strip, 0)
        hook(2)
        grad[...] = transpose_times(act[...], upstream[...]).astype(BF)


def forward(patches, cotangent, keep, vec, table, ff, gathered, moves, collective):
    cells, windows, width = patches.shape
    high, tall, wide_rows = -(-cells // 8) * 8, keep.shape[1], -(-cells // 128) * 128
    rows = windows * high
    heads = table.shape[0]
    columns, chunk = 256, 512
    groups, pairs = width // columns, windows // 2
    per = columns // 32
    direct = bool(moves)
    enters, attends = pairs, pairs * groups
    steps = enters + attends + 1 + ff // chunk
    group = lambda s: jnp.clip((s - enters) // pairs, 0, groups - 1)
    pair = lambda s: jnp.where(
        s < enters, 0, jnp.where(s < enters + attends, lax.rem(s - enters, pairs), pairs - 1)
    )
    later = lambda s: jnp.maximum(s - enters - attends - 1, 0)
    seen = lambda n: pl.BlockSpec((windows, n, columns), lambda s: (0, 0, group(s)))
    wide = pl.BlockSpec((rows, chunk), lambda s: (0, later(s)))
    any_place = pl.BlockSpec(memory_space=pl.ANY)
    starts = [[3.0]] * enters + [[2.0, 1.3], [1.3], [1.3], [1.3]] * groups
    starts += [[2.0, 3.0]] + [[1.4, 2.0, 1.5]] * (ff // chunk)
    lead = (4, 2, 2, 2, width // 32)
    return call(
        functools.partial(forward_body, direct),
        "forward",
        steps=steps,
        ins=[patches, cotangent, keep, vec, table] + list(gathered),
        in_specs=[
            whole(patches.shape),
            whole(cotangent.shape),
            whole(keep.shape),
            whole(vec.shape),
            whole(table.shape),
        ]
        + [any_place] * len(gathered),
        outs=[
            struct((width, rows), BF),
            struct((rows, width), BF),
            struct((rows, width), BF),
            struct((8, width), F32),
            struct((windows, wide_rows, width), BF),
            struct((windows, tall, width), BF),
            struct((windows, tall, width), BF),
            struct((windows, heads, tall, 128), BF),
            struct((rows, width), BF),
            struct((rows, width), F32),
            struct((width, rows), BF),
            struct((rows, ff), BF),
            struct((rows, ff), BF),
            struct((ff, width), BF),
        ],
        out_specs=[
            whole_out((width, rows)),
            whole_out((rows, width)),
            whole_out((rows, width)),
            whole_out((8, width)),
            seen(wide_rows),
            seen(tall),
            seen(tall),
            pl.BlockSpec((2, per, tall, 128), lambda s: (pair(s), group(s), 0, 0)),
            whole_out((rows, width)),
            whole_out((rows, width)),
            whole_out((width, rows)),
            wide,
            wide,
            pl.BlockSpec((chunk, width), lambda s: (later(s), 0)),
        ],
        scratch=[
            pltpu.VMEM((2 * high, width), F32),
            pltpu.VMEM((rows, width), BF),
            pltpu.VMEM((2,) + lead + (3 * columns,), BF),
            pltpu.VMEM(lead + (width,), BF),
            pltpu.VMEM((2,) + lead + (chunk,), BF),
            pltpu.VMEM((rows, width), BF),
            pltpu.VMEM((rows, chunk), F32),
            pltpu.VMEM((cells, windows, width), F32),
            pltpu.VMEM((heads, tall, 128), F32),
            pltpu.VMEM((windows, tall, 128), F32),
            pltpu.VMEM((heads, 384), F32),
            pltpu.VMEM((heads * WS * WS // 4, 256), F32),
            pltpu.SemaphoreType.DMA((5,)),
        ],
        moves=moves,
        collective=collective,
        starts=starts,
    )


def middle_body(made, hook, *refs):
    refs = list(refs)
    take = lambda n: [refs.pop(0) for _ in range(n)]
    act, slope, ws, we_low, we_high, wo, upstream, hidden_t, middle, attended, vec, shrink_sum = take(12)
    result, grad_e, mid, grad_o, dout, small = take(6)
    grad_low, back, sums, rows_of, we, sems = refs
    total = mid
    step = pl.program_id(0)
    chunks = back.shape[0]
    rows, width = mid.shape
    windows, cells, _ = result.shape
    high = rows // windows
    chunk = back.shape[2]

    @pl.when(step == 0)
    def _():
        total[...] = middle[...] + vec[7:8]

    @pl.when(step < chunks)
    def _():
        total[...] += times(act[...], ws[...])
        hook(1)
        product = times_transpose(upstream[...], ws[...])
        here = (product * slope[...].astype(F32)).astype(BF)
        back[step] = here
        line = jnp.sum(here.astype(F32), axis=0, keepdims=True)
        per = width // chunk
        sums[pl.ds(4 + step // per, 1), pl.ds(pl.multiple_of(lax.rem(step, per) * chunk, chunk), chunk)] = line
        hook(2)
        product = times(hidden_t[...], here).astype(BF)

        @pl.when(step < chunks // 2)
        def _():
            at = pl.ds(pl.multiple_of(step * chunk, chunk), chunk)
            grad_low[:, :, :, :, :, at] = product.reshape(grad_low.shape[:5] + (chunk,))

        @pl.when(step >= chunks // 2)
        def _():
            grad_e[...] = product


    @pl.when(step == chunks - 1)
    def _():
        for w in range(windows):
            result[w] = total[pl.ds(w * high, cells)].astype(BF)
        total[...] = jnp.zeros_like(total)

    per_half = chunks // 2

    def load_we(half, index):
        slot = lax.rem(index, 2)
        at = pl.ds(pl.multiple_of((index - half * per_half) * chunk, chunk), chunk)
        return pltpu.make_async_copy((we_low, we_high)[half].at[:, at], we.at[slot], sems.at[slot])

    for half in range(2):

        @pl.when((step >= chunks + half * per_half - 1) & (step < chunks + (half + 1) * per_half - 1))
        def _(half=half):
            load_we(half, step - chunks + 1).start()

    @pl.when(step >= chunks)
    def _():
        index = step - chunks

        for half in range(2):

            @pl.when(index // per_half == half)
            def _(half=half):
                load_we(half, index).wait()

        total[...] += times_transpose(back[index], we[lax.rem(index, 2)])

    @pl.when(step == 2 * chunks - 1)
    def _():
        zero = jnp.zeros((8, width), F32)

        def strip(at, carry):
            gain_sum, shift_sum, out_sum = carry
            normed, rstd = normalize(middle[at])
            value = total[at]
            grad_mid = upstream[at].astype(F32) + norm_back(value, normed, rstd, vec[5:6])
            mid[at] = grad_mid
            low = grad_mid.astype(BF)
            for j in range(2):
                back[j, at] = low[:, j * chunk : j * chunk + chunk]
            return (
                gain_sum + eight(value * normed),
                shift_sum + eight(value),
                out_sum + eight(low.astype(F32)),
            )

        load_wo = [
            pltpu.make_async_copy(wo.at[:, pl.ds(j * chunk, chunk)], we.at[j], sems.at[j])
            for j in range(2)
        ]
        for copy in load_wo:
            copy.start()
        hooks = [functools.partial(hook, part) for part in (1, 2, 3, 4)]
        found = strips(rows, strip, (zero, zero, zero), unroll=1, hooks=hooks)
        gain_sum, shift_sum, out_sum = found
        for i, value in enumerate((out_sum, gain_sum, shift_sum, shrink_sum[...])):
            sums[i : i + 1] = jnp.sum(value, axis=0, keepdims=True)
        rows_of[...] = jnp.zeros_like(rows_of)
        for d in range(32):
            at = pl.ds(128 * (d // 4), 128)
            rows_of[pl.ds(32 * d, 2)] = sums[pl.ds(2 * (d % 4), 2), at]
        small[...] = rows_of[...].astype(BF).reshape(small.shape)
        for j in range(2):
            hook(5 + j)
            at = pl.ds(j * chunk, chunk)
            grad_o[:, at] = transpose_times(attended[...], back[j]).astype(BF)
            if j == 0:
                for copy in load_wo:
                    copy.wait()
            product = times_transpose(back[0], we[0, at])
            product = product + times_transpose(back[1], we[1, at])
            for w in range(windows):
                here = with_rows(product[w * high : (w + 1) * high], dout.shape[1])
                dout[w, :, at] = here.astype(BF)


def middle_part(act, slope, w_shrink, w_low, w_high, w_output, upstream, hidden_t, middle, attended, vec, shrink_sum, windows, cells, moves, collective):
    rows, ff = act.shape
    width = middle.shape[1]
    wide_rows = -(-cells // 128) * 128
    chunk = 512
    chunks = ff // chunk
    early = lambda s: jnp.minimum(s, chunks - 1)
    half = chunks // 2
    later = lambda first: lambda s: (0, jnp.clip(s - first, 0, half - 1))
    wide = pl.BlockSpec((rows, chunk), lambda s: (0, early(s)))
    starts = [[1.2, 1.3, 1.2]] * chunks + [[1.7]] * (chunks - 1) + [[1.7] + [1.5] * 4 + [2.5, 2.5]]
    low = ((4, 2, 2, 2, width // 32, ff // 2), BF)
    scratch = [pltpu.VMEM(*low)] if moves else []
    low_outs = [] if moves else [struct(*low)]
    return call(
        middle_body,
        "middle",
        steps=2 * chunks,
        ins=[act, slope, w_shrink, w_low, w_high, w_output, upstream, hidden_t, middle, attended, vec, shrink_sum],
        in_specs=[
            wide,
            wide,
            pl.BlockSpec((chunk, width), lambda s: (early(s), 0)),
            pl.BlockSpec(memory_space=pl.ANY),
            pl.BlockSpec(memory_space=pl.ANY),
            pl.BlockSpec(memory_space=pl.ANY),
            whole((rows, width)),
            whole((width, rows)),
            whole((rows, width)),
            whole((rows, width)),
            whole(vec.shape),
            whole(shrink_sum.shape),
        ],
        outs=[
            struct((windows, cells, width), BF),
            struct((width, ff // 2), BF),
            struct((rows, width), F32),
            struct((width, width), BF),
            struct((windows, wide_rows, width), BF),
            struct((4, 2, 2, 2, 32, 128), BF),
        ]
        + low_outs,
        out_specs=[
            whole_out((windows, cells, width)),
            pl.BlockSpec((width, chunk), later(half)),
            whole_out((rows, width)),
            whole_out((width, width)),
            whole_out((windows, wide_rows, width)),
            whole_out((4, 2, 2, 2, 32, 128)),
        ]
        + [whole_out(o.shape) for o in low_outs],
        scratch=scratch
        + [
            pltpu.VMEM((chunks, rows, chunk), BF),
            pltpu.VMEM((8, width), F32),
            pltpu.VMEM((32 * 32, 128), F32),
            pltpu.VMEM((2, width, chunk), BF),
            pltpu.SemaphoreType.DMA((2,)),
        ],
        moves=moves,
        collective=collective,
        starts=starts,
    )


def backward_body(groups, made, hook, *refs):
    refs = list(refs)
    take = lambda n: [refs.pop(0) for _ in range(n)]
    query, keys, values, dout, probs, hidden_t, source, mid, vec, counts = take(10)
    w_attend = take(groups)
    out, late = take(2)
    pieces = take(groups)
    bias_low, joint, bias, total, wa, sems = refs
    step = pl.program_id(0)
    windows, _, columns = query.shape
    width, rows = hidden_t.shape
    cells = out.shape[1]
    high = rows // windows
    pairs = windows // 2
    pair = lax.rem(step, pairs)
    group = step // pairs
    scale = 32 ** (-0.5)

    @pl.when(step == 0)
    def _():
        bias_low[...] = jnp.zeros_like(bias_low)
        total[...] = jnp.zeros_like(total)

    @pl.when(step < pairs * groups)
    def _():
        @pl.when(pair == 0)
        def _():
            bias[...] = jnp.zeros_like(bias)

        done = []
        for w in range(2):
            window = pair * 2 + w
            parts = []
            for g in range(columns // 128):
                at = pl.ds(g * 128, 128)
                q, k, v = query[window, :, at], keys[window, :, at], values[window, :, at]
                d = dout[window, :, at]
                slopes = times(v, spread_heads(d.T))
                found, low = [], []
                for h in range(4):
                    prob = probs[w, g * 4 + h]
                    soft = prob.astype(F32)
                    both = soft * slopes[:, 128 * h : 128 * h + 128]
                    ds = (both - soft * jnp.sum(both, axis=0, keepdims=True)).astype(BF)
                    bias[g * 4 + h] += ds.astype(F32)
                    found.append(ds)
                    low.append(prob)
                found = jnp.concatenate(found, axis=1)
                dq = own_heads(times(k.T, found)).T[:high] * scale
                dk = times(found, stack_heads(q))[:high] * scale
                dv = times(jnp.concatenate(low, axis=1), stack_heads(d))[:high]
                parts.append((dq, dk, dv))
            done.append([jnp.concatenate([p[j] for p in parts], axis=1) for j in range(3)])
        at_rows = pl.ds(pl.multiple_of(pair * 2 * high, 16), 2 * high)
        for j in range(3):
            joint[group, at_rows, pl.ds(j * columns, columns)] = jnp.concatenate([done[0][j], done[1][j]], axis=0).astype(BF)

    @pl.when((step < pairs * groups) & (pair == pairs - 1))
    def _():
        hook(1)

    for g in range(groups):

        @pl.when(step == pairs * (g + 1) - 1)
        def _(g=g):
            per = columns // 32
            for h in range(per):
                d = g * per + h
                bias_low[d // 8, (d // 4) % 2, (d // 2) % 2, d % 2, : bias.shape[1]] = bias[h].astype(BF)
            for j in range(3):
                here = joint[g, :, j * columns : (j + 1) * columns]
                product = times(hidden_t[...], here).astype(BF)
                at = pl.ds(j * columns, columns)
                pieces[g][:, :, :, :, :, at] = product.reshape(pieces[g].shape[:5] + (columns,))
                if j != 1:
                    row = pl.ds(2 if j == 0 else 3, 1)
                    here = jnp.sum(here.astype(F32), axis=0, keepdims=True)
                    late[row, pl.ds(g * columns, columns)] = here

    load = lambda g: pltpu.make_async_copy(w_attend[g], wa.at[g % 2], sems.at[g % 2])

    @pl.when(step == pairs * groups - 1)
    def _():
        load(0).start()

    for g in range(groups):

        @pl.when(step == pairs * groups + g)
        def _(g=g):
            load(g).wait()
            if g + 1 < groups:
                load(g + 1).start()
            total[...] += times_transpose(joint[g], flat(wa[g % 2]))

    @pl.when(step == pl.num_programs(0) - 1)
    def _():
        zero = jnp.zeros((8, width), F32)
        inverse = inverse_of(counts)

        def strip(at, carry):
            gain_sum, shift_sum = carry
            normed, rstd = normalize(source[at].astype(F32))
            value = total[at]
            full = mid[at] + norm_back(value, normed, rstd, vec[0:1])
            total[at] = full * inverse
            return gain_sum + eight(value * normed), shift_sum + eight(value)

        hooks = [functools.partial(hook, part) for part in (1, 2, 3, 4, 5, 6)]
        found = strips(rows, strip, (zero, zero), unroll=1, hooks=hooks)
        for i in range(2):
            late[pl.ds(i, 1)] = jnp.sum(found[i], axis=0, keepdims=True)
        for w in range(windows):
            out[w] = total[pl.ds(w * high, cells)]


def backward_part(query, keys, values, dout, probs, hidden_t, w_attend, source, mid, vec, counts, cells, moves, collective):
    windows, _, width = query.shape
    rows = hidden_t.shape[1]
    tall = keys.shape[1]
    columns = 256
    groups, pairs = width // columns, windows // 2
    per = columns // 32
    steps = groups * pairs
    group = lambda s: jnp.minimum(s // pairs, groups - 1)
    pair = lambda s: jnp.where(s < steps, lax.rem(s, pairs), pairs - 1)
    seen = lambda array: pl.BlockSpec((windows, array.shape[1], columns), lambda s: (0, 0, group(s)))
    lead = (4, 2, 2, 2)
    pieces = [(lead + (width // 32, 3 * columns), BF)] * groups + [(lead + (128, 128), BF)]
    outs = [struct((windows, cells, width), F32), struct((4, width), F32)]
    out_specs = [whole_out((windows, cells, width)), whole_out((4, width))]
    scratch = [
        pltpu.VMEM((groups, rows, 3 * columns), BF),
        pltpu.VMEM((per, tall, 128), F32),
        pltpu.VMEM((rows, width), F32),
        pltpu.VMEM((2,) + lead + (width // 32, 3 * columns), BF),
        pltpu.SemaphoreType.DMA((2,)),
    ]
    if moves:
        scratch = [pltpu.VMEM(*p) for p in pieces] + scratch
    else:
        outs += [struct(*p) for p in pieces]
        out_specs += [whole_out(p[0]) for p in pieces]
    starts = [[1.2], [1.2], [1.2], [1.2, 2.5]] * groups + [[2.2]] * (groups - 1) + [[2.2] + [1.2] * 6]
    return call(
        functools.partial(backward_body, groups),
        "backward",
        steps=steps + groups,
        ins=[query, keys, values, dout, probs, hidden_t, source, mid, vec, counts] + list(w_attend),
        in_specs=[seen(a) for a in (query, keys, values, dout)]
        + [
            pl.BlockSpec((2, per, tall, 128), lambda s: (pair(s), group(s), 0, 0)),
            whole((width, rows)),
            whole((rows, width)),
            whole((rows, width)),
            whole(vec.shape),
            whole(counts.shape),
        ]
        + [pl.BlockSpec(memory_space=pl.ANY)] * groups,
        outs=outs,
        out_specs=out_specs,
        scratch=scratch,
        moves=moves,
        collective=collective,
        starts=starts,
    )


def fresh_moments(grad, first, second, weight, factor):
    clipped = grad * factor
    first_new = MOMENT_ONE * first + (1.0 - MOMENT_ONE) * clipped
    second_new = MOMENT_TWO * second + (1.0 - MOMENT_TWO) * clipped * clipped
    change = (first_new * (1.0 / (1.0 - MOMENT_ONE**STEP))) / (
        jnp.sqrt(second_new * (1.0 / (1.0 - MOMENT_TWO**STEP))) + ADAM_EPS
    ) + DECAY * weight
    return first_new, second_new, change


def inverse_of(counts):
    places = [(d // 8, (d // 4) % 2, (d // 2) % 2, d % 2) for d in range(counts.shape[0] * 8)]
    found = functools.reduce(jnp.add, [counts[at + (pl.ds(0, 8),)] for at in places])
    return 1.0 / found[0:1, 0:1]


def norms_kernel(pieces, *refs):
    refs = list(refs)
    take = lambda n: [refs.pop(0) for _ in range(n)]
    counts, late_sums, bias_sum, small = take(4)
    sums = take(1 + max(p[4] for p in pieces))
    masters, firsts, seconds = take(4), take(4), take(4)
    vec_grad, heads_grad, norms_out = take(3)
    message, got, message_two, got_plane, got_line, sems = refs
    place = Place(sems)
    place.greet(True)
    devices = got.shape[0] * 8
    scale = inverse_of(counts)
    lane = lax.broadcasted_iota(jnp.int32, (8, 128), 1)
    top = lax.broadcasted_iota(jnp.int32, (8, 128), 0) == 0

    def over(rows, body, carry):
        def step(i, value):
            return body(pl.multiple_of(i * 16, 16), value)

        return lax.fori_loop(0, rows // 16, step, carry)

    def fold(value):
        value = eight(value)
        return functools.reduce(
            jnp.add, [value[:, i : i + 128] for i in range(0, value.shape[1], 128)]
        )

    zero = jnp.zeros((8, 128), F32)
    squares = [zero] * 8
    for k, (row, rows), (column, columns), source_column, number in pieces:
        columns_at = pl.ds(column, columns)

        def body(at, carry):
            here = (pl.ds(row + at, 16), columns_at)
            grad = sums[number][pl.ds(at, 16), pl.ds(source_column, columns)] * scale
            weight = masters[k][here]
            return carry[0] + fold(grad * grad), carry[1] + fold(weight * weight)

        squares[k], squares[4 + k] = over(rows, body, (squares[k], squares[4 + k]))

    def packed(values):
        row = zero
        for i, value in enumerate(values):
            row = jnp.where((lane == i) & top, jnp.sum(value), row)
        return row

    message[pl.ds(0, 8)] = packed(squares)
    message[pl.ds(8, 8)] = zero
    message[pl.ds(8, 2)] = small[pl.ds(0, 2)]
    side = 2 * WS - 1
    cell = lax.broadcasted_iota(jnp.int32, (128, 384), 0)
    spot = lax.broadcasted_iota(jnp.int32, (128, 384), 1)
    put = ((cell // WS) * side + lax.rem(cell, WS) == spot) & (cell < WS * WS)
    wide = jnp.dot(bias_sum[...], put.astype(F32), precision=HIGH, preferred_element_type=F32)
    middle = (WS - 1) * side + WS - 1
    column = jnp.zeros((1, 384), F32)
    for j in range(WS * WS):
        shift = middle - (j // WS) * side - j % WS
        column = column + pltpu.roll(wide[j : j + 1], shift, axis=1)
    for b in range(3):
        message[pl.ds(11 + b, 1)] = column[:, 128 * b : 128 * b + 128]
    late_rows = late_sums.shape[0]
    for i in range(late_rows):
        for b in range(8):
            message[pl.ds(16 + 8 * i + b, 1)] = late_sums[i : i + 1, 128 * b : 128 * b + 128]

    events, end = gather_events(place, message, got, 1, False)
    for event, _, _ in events:
        event()
    end()

    place_of = lambda d: (d // 8, (d // 4) % 2, (d // 2) % 2, d % 2)
    found = functools.reduce(jnp.add, [got[place_of(d) + (pl.ds(0, 8),)] for d in range(devices)])
    late = functools.reduce(
        jnp.add, [got[place_of(d) + (pl.ds(16, 8 * late_rows),)] for d in range(devices)]
    )
    for i in range(late_rows):
        for b in range(8):
            vec_grad[pl.ds(i, 1), pl.ds(128 * b, 128)] = late[8 * i + b : 8 * i + b + 1] * scale
    for d in range(devices):
        block = got[place_of(d) + (pl.ds(8, 8),)] * scale
        vec_grad[pl.ds(4 + 2 * (d % 4), 2), pl.ds(128 * (d // 4), 128)] = block[:2]
        for j in range(3):
            heads_grad[pl.ds(d, 1), pl.ds(128 * j, 128)] = block[3 + j : 4 + j]
    small_grad, table_grad = vec_grad[...], heads_grad[...]

    total = lambda value: jnp.sum(value, keepdims=True)
    scalar = lambda k: total(jnp.where(top & (lane == k), found, 0.0))
    grad_square = scalar(0) + scalar(1) + scalar(2) + scalar(3)
    clip_norm = jnp.sqrt(
        grad_square + total(small_grad * small_grad) + total(table_grad * table_grad)
    )
    factor = jnp.minimum(1.0, CLIP_LIMIT / clip_norm)
    squares = [zero] * 4
    for k, (row, rows), (column, columns), source_column, number in pieces:
        columns_at = pl.ds(column, columns)

        def body(at, carry):
            here = (pl.ds(row + at, 16), columns_at)
            grad = sums[number][pl.ds(at, 16), pl.ds(source_column, columns)] * scale
            _, _, change = fresh_moments(
                grad, firsts[k][here], seconds[k][here], masters[k][here], factor
            )
            return carry + fold(change * change)

        squares[k] = over(rows, body, squares[k])

    message_two[...] = packed(squares)
    spot = place.x * 4 + place.y * 2 + place.c
    got_plane[pl.ds(spot, 1)] = message_two[...][None]
    plane = [place.send(message_two, got_plane.at[spot], peer) for peer in place.plane()]
    for copy in plane:
        copy.start()
    for copy in plane:
        copy.wait_recv()
    plane_sum = functools.reduce(jnp.add, [got_plane[i] for i in range(8)])
    got_line[pl.ds(place.z, 1)] = plane_sum[None]
    line = [
        place.send(got_line.at[place.z], got_line.at[place.z], place.to(z=at))
        for at in (place.mate, place.far, place.cross)
    ]
    for copy in line:
        copy.start()
    for copy in line:
        copy.wait_recv()
    second_found = functools.reduce(jnp.add, [got_line[i] for i in range(4)])
    norms = jnp.where(top & (lane == 8), clip_norm, 0.0)
    norms = jnp.where(top & (lane == 9), factor, norms)
    for k in range(4):
        weight_norm = jnp.sqrt(scalar(4 + k))
        update_norm = jnp.sqrt(total(jnp.where(top & (lane == k), second_found, 0.0)))
        norms = jnp.where(top & (lane == k), weight_norm, norms)
        norms = jnp.where(top & (lane == 4 + k), update_norm, norms)
    norms_out[...] = norms
    for copy in plane + line:
        copy.wait_send()


def update_kernel(pieces, *refs):
    refs = list(refs)
    take = lambda n: [refs.pop(0) for _ in range(n)]
    counts, norms, vec_grad, heads_grad = take(4)
    sums = take(1 + max(p[4] for p in pieces))
    masters, firsts, seconds = take(4), take(4), take(4)
    vec, vec_first, vec_second, table, table_first, table_second = take(6)
    grads_out, firsts_out, seconds_out, news_out, copies_out = (take(4) for _ in range(5))
    vec_out, table_out = take(4), take(4)
    clip_out, norms_out = take(2)
    scale = inverse_of(counts)
    factor = norms[0:1, 9:10]
    for k, (row, rows), (column, columns), source_column, number in pieces:
        ratio = LEARN_RATE * (norms[0:1, k : k + 1] / norms[0:1, 4 + k : 5 + k])
        columns_at = pl.ds(column, columns)

        def body(i, carry):
            at = pl.multiple_of(i * 16, 16)
            here = (pl.ds(row + at, 16), columns_at)
            grad = sums[number][pl.ds(at, 16), pl.ds(source_column, columns)] * scale
            first, second, change = fresh_moments(
                grad, firsts[k][here], seconds[k][here], masters[k][here], factor
            )
            grads_out[k][here] = grad
            firsts_out[k][here] = first
            seconds_out[k][here] = second
            fresh = masters[k][here] - ratio * change
            news_out[k][here] = fresh
            copies_out[k][here] = fresh.astype(BF)
            return carry

        lax.fori_loop(0, rows // 16, body, 0)

    @pl.when(pl.program_id(0) == 0)
    def _():
        clip_out[...] = norms[0:1, 8:9]
        norms_out[0:1] = norms[0:1, 0:4]
        norms_out[1:2] = norms[0:1, 4:8]
        total = lambda value: jnp.sum(value, keepdims=True)
        grad = vec_grad[...]
        first, second, change = fresh_moments(
            grad, vec_first[...], vec_second[...], vec[...], factor
        )
        rows = lambda value: jnp.sqrt(jnp.sum(value * value, axis=1, keepdims=True))
        vec_out[0][...] = grad
        vec_out[1][...] = first
        vec_out[2][...] = second
        vec_out[3][...] = vec[...] - LEARN_RATE * (rows(vec[...]) / rows(change)) * change
        grad = heads_grad[:, : table.shape[1]]
        first, second, change = fresh_moments(
            grad, table_first[...], table_second[...], table[...], factor
        )
        table_out[0][...] = grad
        table_out[1][...] = first
        table_out[2][...] = second
        ratio = jnp.sqrt(total(table[...] * table[...])) / jnp.sqrt(total(change * change))
        table_out[3][...] = table[...] - LEARN_RATE * ratio * change


def update(collective, counts, late_sums, bias_sum, small, sums, pieces, masters, firsts, seconds, vectors, tables):
    vmem = pl.BlockSpec(memory_space=pltpu.VMEM)
    ins = [counts, late_sums, bias_sum, small] + list(sums)
    ins += list(masters) + list(firsts) + list(seconds)
    vec_grad, heads_grad, norms = pl.pallas_call(
        functools.partial(norms_kernel, pieces),
        name="norms",
        out_shape=[struct(vectors[0].shape, F32), struct((32, 384), F32), struct((8, 128), F32)],
        in_specs=[vmem] * len(ins),
        out_specs=[vmem] * 3,
        scratch_shapes=[
            pltpu.VMEM((48, 128), F32),
            pltpu.VMEM((4, 2, 2, 2, 48, 128), F32),
            pltpu.VMEM((8, 128), F32),
            pltpu.VMEM((8, 8, 128), F32),
            pltpu.VMEM((4, 8, 128), F32),
            pltpu.SemaphoreType.DMA((gather_sems(1) + 20,)),
        ],
        compiler_params=pltpu.CompilerParams(
            collective_id=collective, has_side_effects=True, vmem_limit_bytes=VMEM_LIMIT
        ),
    )(*ins)
    steps = 2
    rows = lambda array: pl.BlockSpec(
        (array.shape[0] // steps, array.shape[1]), lambda s: (s, 0)
    )
    halves = [(k, (row, n // steps), column, source, number) for k, (row, n), column, source, number in pieces]
    tables = [t.T for t in tables]
    ins = [counts, norms, vec_grad, heads_grad] + list(sums)
    ins += list(masters) + list(firsts) + list(seconds) + list(vectors) + list(tables)
    in_specs = [whole(a.shape) for a in (counts, norms, vec_grad, heads_grad)]
    in_specs += [rows(a) for a in list(sums) + list(masters) + list(firsts) + list(seconds)]
    in_specs += [whole(a.shape) for a in list(vectors) + list(tables)]
    like = lambda arrays, dtype=F32: [struct(a.shape, dtype) for a in arrays]
    outs = like(masters) * 4 + like(masters, BF)
    out_specs = [rows(a) for a in masters] * 5
    outs += like(vectors[:1]) * 4 + like(tables[:1]) * 4
    out_specs += [whole_out(vectors[0].shape)] * 4 + [whole_out(tables[0].shape)] * 4
    outs += [struct((1, 1), F32), struct((2, 4), F32)]
    out_specs += [whole_out((1, 1)), whole_out((2, 4))]
    made = pl.pallas_call(
        functools.partial(update_kernel, halves),
        name="update",
        grid=(steps,),
        out_shape=outs,
        in_specs=in_specs,
        out_specs=out_specs,
        compiler_params=pltpu.CompilerParams(vmem_limit_bytes=VMEM_LIMIT),
    )(*ins)
    matrices = [[made[4 * j + k] for j in range(5)] for k in range(4)]
    return matrices, made[20:24], [t.T for t in made[24:28]], made[28].reshape(()), made[29]


def local(
    ndp,
    nfs,
    patches,
    cotangent,
    pad_mask,
    attend_weight,
    attend_first,
    attend_second,
    output_weight,
    output_first,
    output_second,
    expand_weight,
    expand_first,
    expand_second,
    shrink_weight,
    shrink_first,
    shrink_second,
    vector_params,
    vector_first,
    vector_second,
    position_table,
    table_first,
    table_second,
):
    windows, cells, width = patches.shape
    keep = pad_mask.astype(jnp.float32)
    local_count = jnp.sum(keep)
    devices = ndp * nfs
    shard_rows = min(attend_weight.shape[0], shrink_weight.shape[0])
    direct = nfs == 4 and ndp == 8 and shard_rows % 32 == 0
    masters = (attend_weight, output_weight, expand_weight, shrink_weight)
    part_rows = shrink_weight.shape[0] // 2

    tall = -(-cells // 16) * 16
    keep_rows = jnp.pad(keep, ((0, 0), (0, tall - cells)))[:, :, None]
    keep_rows = jnp.broadcast_to(keep_rows, (windows, tall, 128))
    lead = (4, 2, 2, 2, -1)
    group_columns = [[(j * width + g * 256, 256) for j in range(3)] for g in range(4)]
    half_ff = expand_weight.shape[1] // 2
    gathered, moves = [], []
    if direct:
        moves = [
            *[
                gather(attend_weight, BF, relay=False, need=4 + 4 * g, columns=columns)
                for g, columns in enumerate(group_columns)
            ],
            gather(output_weight, BF, need=20),
            gather(expand_weight, BF, need=21, columns=[(0, half_ff)]),
            gather(expand_weight, BF, need=25, columns=[(half_ff, half_ff)]),
            gather(shrink_weight, BF),
            gather(jnp.full((16, 128), local_count, F32), F32, 1, False),
        ]
    else:
        gathered = [
            lax.all_gather(m.astype(BF), AXES, axis=0, tiled=True).reshape(lead + m.shape[1:])
            for m in masters
        ]
        w_attend = [
            jnp.concatenate([gathered[0][..., a : a + n] for a, n in columns], axis=-1)
            for columns in group_columns
        ]
        w_expand = [gathered[2][..., :half_ff], gathered[2][..., half_ff:]]
        gathered = w_attend + gathered[1:2] + w_expand + gathered[3:]
    forward_outs, made = forward(
        patches.transpose(1, 0, 2),
        cotangent.transpose(1, 0, 2),
        keep_rows,
        vector_params,
        position_table.T,
        expand_weight.shape[1],
        () if direct else gathered[:7],
        moves,
        1,
    )
    hidden_t, source, upstream, shrink_sum, query, keys, values, probs = forward_outs[:8]
    attended, middle, hidden_two_t, activated, slope, grad_shrink = forward_outs[8:]
    if direct:
        counts, gathered = made[-1], made[:-1]
    else:
        total = lax.psum(local_count, AXES)
        counts = jnp.full((4, 2, 2, 2, 16, 128), total / 32, F32)
    w_attend = gathered[:4]
    w_output, w_low, w_high, w_shrink = (w.reshape(-1, w.shape[-1]) for w in gathered[4:])

    def parts(grad):
        return grad.reshape(lead + grad.shape[-1:])

    if direct:
        moves = [scatter(parts(grad_shrink)), scatter(0, (width // 32, half_ff), step=4)]
    middle_outs, middle_made = middle_part(
        activated,
        slope,
        w_shrink,
        w_low,
        w_high,
        w_output,
        upstream,
        hidden_two_t,
        middle,
        attended,
        vector_params,
        shrink_sum,
        windows,
        cells,
        moves,
        2,
    )
    block_out, grad_expand, grad_middle, grad_output, dout, small = middle_outs[:6]
    if direct:
        piece_shape = (width // 32, 3 * 256)
        moves = [
            scatter(parts(grad_expand)),
            scatter(parts(grad_output)),
            scatter(small, groups=1),
        ]
        moves += [scatter(g, piece_shape, step=4 * (g + 1)) for g in range(4)]
        moves.append(scatter(4, (128, 128), groups=1, step=16))
    backward_outs, made = backward_part(
        query,
        keys,
        values,
        dout,
        probs,
        hidden_t,
        w_attend,
        source,
        grad_middle,
        vector_params,
        counts,
        cells,
        moves,
        3,
    )
    input_grad, late_sums = backward_outs[:2]
    grad_pieces, grad_bias = backward_outs[2:-1], backward_outs[-1]

    def finish_direct(block_out, input_grad, late_sums, made, middle_made, firsts, seconds):
        shrink_owned, low_owned = middle_made
        high_owned, output_owned, small_owned = made[:3]
        bias_owned = made[-1]
        sums = list(made[3:-1]) + [output_owned, low_owned, high_owned, shrink_owned]
        pieces = [
            (0, (0, attend_weight.shape[0]), (j * width + g * 256, 256), j * 256, g)
            for g in range(4)
            for j in range(3)
        ]
        rows = [(0, m.shape[0]) for m in masters]
        pieces += [
            (1, rows[1], (0, width), 0, 4),
            (2, rows[2], (0, half_ff), 0, 5),
            (2, rows[2], (half_ff, half_ff), 0, 6),
            (3, rows[3], (0, width), 0, 7),
        ]
        matrices, vector_outs, table_outs, clip_norm, matrix_norms = update(
            4,
            counts,
            late_sums,
            bias_owned,
            small_owned,
            sums,
            pieces,
            masters,
            firsts,
            seconds,
            (vector_params, vector_first, vector_second),
            (position_table, table_first, table_second),
        )
        outs = [block_out, input_grad]
        for matrix in matrices:
            outs += matrix
        return (*outs, *vector_outs, *table_outs, clip_norm, matrix_norms)

    firsts = (attend_first, output_first, expand_first, shrink_first)
    seconds = (attend_second, output_second, expand_second, shrink_second)
    if direct:
        return finish_direct(
            block_out, input_grad, late_sums, made, middle_made, firsts, seconds
        )
    grad_expand = jnp.concatenate([middle_outs[6].reshape(width, -1), grad_expand], axis=1)
    grad_attend = jnp.stack([p.reshape(width, 3, -1) for p in grad_pieces], axis=2)
    grad_attend = grad_attend.reshape(width, -1)
    owned = [
        lax.psum_scatter(g.astype(F32), AXES, scatter_dimension=0, tiled=True)
        for g in (grad_attend, grad_output, grad_expand, grad_shrink)
    ]
    index = jnp.pad(position_index(WS).T, ((0, tall - cells), (0, 128 - cells)), constant_values=-1)
    relative = jnp.arange(position_table.shape[0], dtype=jnp.int32)
    onehot = index.reshape(-1)[None, :] == relative[:, None]
    grad_table = lax.dot_general(
        onehot.astype(F32),
        grad_bias.reshape(HEADS, 128, 128)[:, :tall].astype(F32).reshape(HEADS, -1),
        (((1,), (1,)), ((), ())),
        precision=HIGH,
    )
    early_sums = small[..., :2, :].astype(F32).reshape(8, 4, 2, 128).transpose(1, 2, 0, 3).reshape(8, width)
    vector_local = jnp.concatenate([late_sums, early_sums], axis=0)
    vector_sum, table_sum = lax.psum((vector_local, grad_table), AXES)
    vector_grad, table_grad = vector_sum / total, table_sum / total
    matrix_grads = tuple((g / total for g in owned))
    grad_squares = jnp.stack([jnp.sum(g * g) for g in matrix_grads])
    weight_squares = jnp.stack([jnp.sum(m * m) for m in masters])
    grad_total, weight_total = lax.psum((grad_squares, weight_squares), AXES)
    clip_norm = jnp.sqrt(
        jnp.sum(grad_total) + jnp.sum(vector_grad * vector_grad) + jnp.sum(table_grad * table_grad)
    )
    factor = jnp.minimum(1.0, CLIP_LIMIT / clip_norm)
    sectioned = [
        moments(matrix_grads[k], firsts[k], seconds[k], masters[k], factor) for k in range(4)
    ]
    update_squares = jnp.stack([jnp.sum(s[2] * s[2]) for s in sectioned])
    update_total = lax.psum(update_squares, AXES)
    weight_norms = jnp.sqrt(weight_total)
    update_norms = jnp.sqrt(update_total)
    matrix_outs = []
    for k in range(4):
        fresh = masters[k] - LEARN_RATE * (weight_norms[k] / update_norms[k]) * sectioned[k][2]
        matrix_outs.append(
            (matrix_grads[k], sectioned[k][0], sectioned[k][1], fresh, fresh.astype(jnp.bfloat16))
        )
    vec_first, vec_second, vec_update = moments(
        vector_grad, vector_first, vector_second, vector_params, factor
    )
    vec_ratio = jnp.sqrt(jnp.sum(vector_params * vector_params, axis=1, keepdims=True)) / jnp.sqrt(
        jnp.sum(vec_update * vec_update, axis=1, keepdims=True)
    )
    vec_fresh = vector_params - LEARN_RATE * vec_ratio * vec_update
    tab_first, tab_second, tab_update = moments(
        table_grad, table_first, table_second, position_table, factor
    )
    tab_ratio = jnp.sqrt(jnp.sum(position_table * position_table)) / jnp.sqrt(
        jnp.sum(tab_update * tab_update)
    )
    tab_fresh = position_table - LEARN_RATE * tab_ratio * tab_update
    matrix_norms = jnp.stack([weight_norms, update_norms])
    attend_o, output_o, expand_o, shrink_o = matrix_outs
    return (
        block_out,
        input_grad,
        attend_o[0],
        attend_o[1],
        attend_o[2],
        attend_o[3],
        attend_o[4],
        output_o[0],
        output_o[1],
        output_o[2],
        output_o[3],
        output_o[4],
        expand_o[0],
        expand_o[1],
        expand_o[2],
        expand_o[3],
        expand_o[4],
        shrink_o[0],
        shrink_o[1],
        shrink_o[2],
        shrink_o[3],
        shrink_o[4],
        vector_grad,
        vec_first,
        vec_second,
        vec_fresh,
        table_grad,
        tab_first,
        tab_second,
        tab_fresh,
        clip_norm,
        matrix_norms,
    )


def solution(mesh):
    in_specs = (
        P(("dp", "fsdp"), None, None),
        P(("dp", "fsdp"), None, None),
        P(("dp", "fsdp"), None),
        P(("dp", "fsdp"), None),
        P(("dp", "fsdp"), None),
        P(("dp", "fsdp"), None),
        P(("dp", "fsdp"), None),
        P(("dp", "fsdp"), None),
        P(("dp", "fsdp"), None),
        P(("dp", "fsdp"), None),
        P(("dp", "fsdp"), None),
        P(("dp", "fsdp"), None),
        P(("dp", "fsdp"), None),
        P(("dp", "fsdp"), None),
        P(("dp", "fsdp"), None),
        P(),
        P(),
        P(),
        P(),
        P(),
        P(),
    )
    out_specs = (
        P(("dp", "fsdp"), None, None),
        P(("dp", "fsdp"), None, None),
        P(("dp", "fsdp"), None),
        P(("dp", "fsdp"), None),
        P(("dp", "fsdp"), None),
        P(("dp", "fsdp"), None),
        P(("dp", "fsdp"), None),
        P(("dp", "fsdp"), None),
        P(("dp", "fsdp"), None),
        P(("dp", "fsdp"), None),
        P(("dp", "fsdp"), None),
        P(("dp", "fsdp"), None),
        P(("dp", "fsdp"), None),
        P(("dp", "fsdp"), None),
        P(("dp", "fsdp"), None),
        P(("dp", "fsdp"), None),
        P(("dp", "fsdp"), None),
        P(("dp", "fsdp"), None),
        P(("dp", "fsdp"), None),
        P(("dp", "fsdp"), None),
        P(("dp", "fsdp"), None),
        P(("dp", "fsdp"), None),
        P(),
        P(),
        P(),
        P(),
        P(),
        P(),
        P(),
        P(),
        P(),
        P(),
    )
    sizes = (mesh.shape["dp"], mesh.shape["fsdp"])
    return jax.shard_map(functools.partial(local, *sizes), mesh=mesh, in_specs=in_specs, out_specs=out_specs, check_vma=False)
```

```python
import functools

import jax
import jax.numpy as jnp
from jax import lax
from jax.experimental import pallas as pl
from jax.experimental.pallas import tpu as pltpu
from jax.sharding import PartitionSpec as P

MESH = pl.DeviceIdType.MESH
AXES = ("dp", "fsdp")
VMEM_LIMIT = 61 * 1024 * 1024

HEADS = 32
WS = 10
STEP = 10


EPSILON = 1e-05
MOMENT_ONE = 0.9
MOMENT_TWO = 0.999
LEARN_RATE = 0.3
DECAY = 0.01
ADAM_EPS = 1e-06
CLIP_LIMIT = 0.05
MASK_FILL = 10000.0
HIGH = lax.Precision.HIGHEST
BF, F32 = jnp.bfloat16, jnp.float32


def position_index(size):
    cells = jnp.arange(size * size, dtype=jnp.int32)
    rows = cells // size
    cols = cells % size
    drow = rows[:, None] - rows[None, :] + size - 1
    dcol = cols[:, None] - cols[None, :] + size - 1
    return drow * (2 * size - 1) + dcol


def moments(grad, first, second, weight, factor):
    clipped = grad * factor
    first_new = MOMENT_ONE * first + (1.0 - MOMENT_ONE) * clipped
    second_new = MOMENT_TWO * second + (1.0 - MOMENT_TWO) * clipped * clipped
    update = (
        first_new
        / (1.0 - MOMENT_ONE**STEP)
        / (jnp.sqrt(second_new / (1.0 - MOMENT_TWO**STEP)) + ADAM_EPS)
        + DECAY * weight
    )
    return (first_new, second_new, update)


def whole(shape):
    zeros = (0,) * len(shape)
    return pl.BlockSpec(shape, lambda *s: zeros, pipeline_mode=pl.Buffered(1))


def whole_out(shape):
    zeros = (0,) * len(shape)
    return pl.BlockSpec(shape, lambda *s: zeros, pipeline_mode=pl.Buffered(1))


def struct(shape, dtype):
    return jax.ShapeDtypeStruct(shape, dtype)


class Place:
    def __init__(self, sems):
        dp = lax.axis_index("dp")
        fsdp = lax.axis_index("fsdp")
        self.z, self.x = dp // 2, dp % 2
        self.y, self.c = fsdp // 2, fsdp % 2
        self.mate = self.z + 1 - 2 * lax.rem(self.z, 2)
        self.far = lax.rem(self.z + 2, 4)
        self.cross = 3 - self.z
        self.inner = (self.z == 1) | (self.z == 2)
        self.pair = 2 * (self.z // 2)
        self.sems = sems
        self.used = 0

    def sem(self):
        self.used += 1
        return self.sems.at[self.used - 1]

    def to(self, z=None, x=None, y=None, c=None):
        z = self.z if z is None else z
        x = self.x if x is None else x
        y = self.y if y is None else y
        c = self.c if c is None else c
        return (z * 2 + x, y * 2 + c)

    def peers(self):
        return [
            self.to(z=self.mate),
            self.to(z=self.far),
            self.to(z=self.cross),
            self.to(x=1 - self.x),
            self.to(y=1 - self.y),
            self.to(c=1 - self.c),
        ]

    def plane(self):
        found = []
        for i in range(1, 8):
            x = self.x + (i // 4) * (1 - 2 * self.x)
            y = self.y + (i // 2 % 2) * (1 - 2 * self.y)
            c = self.c + (i % 2) * (1 - 2 * self.c)
            found.append(self.to(x=x, y=y, c=c))
        return found

    def greet(self, plane=False):
        barrier = pltpu.get_barrier_semaphore()
        peers = self.peers()[:3] + self.plane() if plane else self.peers()
        for peer in peers:
            pl.semaphore_signal(barrier, inc=1, device_id=peer, device_id_type=MESH)
        pl.semaphore_wait(barrier, len(peers))

    def send(self, source, target, device, recv_sem=None):
        return pltpu.make_async_remote_copy(
            src_ref=source,
            dst_ref=target,
            send_sem=self.sem(),
            recv_sem=self.sem() if recv_sem is None else recv_sem,
            device_id=device,
            device_id_type=MESH,
        )

    def move(self, source, target):
        return pltpu.make_async_copy(source, target, self.sem())


def gather_sems(groups):
    return 20 + 2 * 5 * groups


def gather_events(place, own, out, groups, relay):
    z, x, y, c = place.z, place.x, place.y, place.c
    half = own.shape[0] // 2
    ox, oy, oc = 1 - x, 1 - y, 1 - c
    xp, yp, cp = place.to(x=ox), place.to(y=oy), place.to(c=oc)
    mate, cross = place.to(z=place.mate), place.to(z=place.cross)
    first = jnp.where(place.inner, place.cross, place.far)
    second = jnp.where(place.inner, place.far, place.cross)
    low, high = pl.ds(0, half), pl.ds(half, half)
    slot = lambda at: out.at[at, x, y, c]
    mine = place.move(own, slot(z))
    to_mate = place.send(own, slot(z), mate)
    if relay:
        came_one, came_two = place.sem(), place.sem()
        across_one = place.send(own, slot(z), cross, came_one)
        across_two = place.send(slot(place.mate), slot(place.mate), cross, came_two)
        on_one = place.send(slot(first), slot(first), mate, came_one)
        on_two = place.send(slot(second), slot(second), mate, came_two)
    else:
        to_far = place.send(own, slot(z), place.to(z=place.far))
        to_cross = place.send(own, slot(z), cross)
    if groups == 1:
        spans = [pl.ds(0, 4)]
    elif groups == 2:
        spans = [pl.ds(place.pair, 2), pl.ds(2 - place.pair, 2)]
    elif relay:
        spans = [pl.ds(at, 1) for at in (z, place.mate, first, second)]
    else:
        spans = [pl.ds(at, 1) for at in (z, place.mate, place.far, place.cross)]

    def forward(ref, device):
        return place.send(ref, ref, device)

    x_full = [forward(out.at[s, x, y, c], xp) for s in spans]
    y_full = [forward(out.at[s, x, y, c], yp) for s in spans]
    x_half = [forward(out.at[s, ox, y, c, low], yp) for s in spans]
    y_half = [forward(out.at[s, x, oy, c, high], xp) for s in spans]
    to_twin = [forward(out.at[s, :, :, c], cp) for s in spans]

    def begin():
        mine.start()
        to_mate.start()
        if relay:

            @pl.when(place.inner)
            def _():
                across_one.start()

        else:
            to_far.start()
            to_cross.start()
        mine.wait()
        if groups == 4:
            send_line(0)

    def send_line(g):
        x_full[g].start()
        y_full[g].start()

    def on_line():
        for copy in (to_mate, to_far, to_cross):
            copy.wait_recv()
        send_line(0)

    def on_place(g):
        (None, to_mate, to_far, to_cross)[g].wait_recv()
        send_line(g)

    def on_mate():
        to_mate.wait_recv()

        @pl.when(place.inner)
        def _():
            across_two.start()

        if groups == 2:
            send_line(0)
        if groups == 4:
            send_line(1)

    def relay_one():
        @pl.when(place.inner)
        def _():
            across_one.wait_recv()
            on_one.start()

    def on_first():
        @pl.when(jnp.logical_not(place.inner))
        def _():
            on_one.wait_recv()

        if groups == 4:
            send_line(2)

    def relay_two():
        @pl.when(place.inner)
        def _():
            across_two.wait_recv()
            on_two.start()

    def on_second():
        @pl.when(jnp.logical_not(place.inner))
        def _():
            on_two.wait_recv()

        send_line(groups - 1)

    def on_side(g):
        x_full[g].wait_recv()
        x_half[g].start()
        y_full[g].wait_recv()
        y_half[g].start()

    def on_corner(g):
        x_half[g].wait_recv()
        y_half[g].wait_recv()
        to_twin[g].start()

    def arrive():
        for copy in to_twin:
            copy.wait_recv()

    def finish():
        for copies in (to_twin, x_full, y_full, x_half, y_half, [to_mate]):
            for copy in copies:
                copy.wait_send()
        if relay:

            @pl.when(place.inner)
            def _():
                for copy in (across_one, across_two, on_one, on_two):
                    copy.wait_send()

        else:
            to_far.wait_send()
            to_cross.wait_send()

    size = 4 // groups
    lines = lambda g: [("x", size, ("xf", g)), ("y", size, ("yf", g))]
    if relay:
        one = {1: [], 2: [], 4: lines(0)}[groups]
        events = [
            (begin, [], [("z", 1, "mate"), ("w", 1, "a1")] + one),
            (on_mate, ["mate"], [("w", 1, "a2")] + {1: [], 2: lines(0), 4: lines(1 % groups)}[groups]),
            (relay_one, ["a1"], [("z", 1, "o1")]),
            (on_first, ["o1"], lines(2) if groups == 4 else []),
            (relay_two, ["a2"], [("z", 1, "o2")]),
            (on_second, ["o2"], lines(groups - 1)),
        ]
    elif groups == 4:
        events = [(begin, [], [("z", 1.33, ("z", g)) for g in (1, 2, 3)] + lines(0))]
        for g in (1, 2, 3):
            events.append((functools.partial(on_place, g), [("z", g)], lines(g)))
    else:
        events = [(begin, [], [("z", 4, "z")]), (on_line, ["z"], lines(0))]
    for g in range(groups):
        half_size = 0.5 * size
        halves = [("y", half_size, ("xh", g)), ("x", half_size, ("yh", g))]
        events.append((functools.partial(on_side, g), [("xf", g), ("yf", g)], halves))
    for g in range(groups):
        twins = [("c", size * 4, ("t", g))]
        events.append((functools.partial(on_corner, g), [("xh", g), ("yh", g)], twins))
    events.append((arrive, [("t", g) for g in range(groups)], []))
    return events, finish


def gather_late_events(place, own, out):
    z, x, y, c = place.z, place.x, place.y, place.c
    half = own.shape[0] // 2
    ox, oy, oc = 1 - x, 1 - y, 1 - c
    xp, yp, cp = place.to(x=ox), place.to(y=oy), place.to(c=oc)
    mate, cross = place.to(z=place.mate), place.to(z=place.cross)
    first = jnp.where(place.inner, place.cross, place.far)
    second = jnp.where(place.inner, place.far, place.cross)
    low, high = pl.ds(0, half), pl.ds(half, half)
    quads = [(x, y), (ox, y), (x, oy), (ox, oy)]
    slot = lambda at, q: out.at[at, quads[q][0], quads[q][1], c]

    def forward(ref, device, recv_sem=None):
        return place.send(ref, ref, device, recv_sem)

    mine = place.move(own, slot(z, 0))
    x_full = place.send(own, slot(z, 0), xp)
    y_full = place.send(own, slot(z, 0), yp)
    x_half = forward(slot(z, 1).at[low], yp)
    y_half = forward(slot(z, 2).at[high], xp)
    to_mate = [forward(slot(z, q), mate) for q in range(4)]
    came_one = [place.sem() for _ in range(4)]
    came_two = [place.sem() for _ in range(4)]
    across_one = [forward(slot(z, q), cross, came_one[q]) for q in range(4)]
    across_two = [forward(slot(place.mate, q), cross, came_two[q]) for q in range(4)]
    on_one = [forward(slot(first, q), mate, came_one[q]) for q in range(4)]
    on_two = [forward(slot(second, q), mate, came_two[q]) for q in range(4)]
    to_twin = [
        forward(out.at[pl.ds(at, 1), :, :, c], cp) for at in (z, place.mate, first, second)
    ]

    def inside(body):
        pl.when(place.inner)(body)

    def outside(body):
        pl.when(jnp.logical_not(place.inner))(body)

    def line(q):
        to_mate[q].start()
        inside(across_one[q].start)

    def begin():
        mine.start()
        x_full.start()
        y_full.start()
        mine.wait()
        line(0)

    def on_x():
        x_full.wait_recv()
        x_half.start()
        line(1)

    def on_y():
        y_full.wait_recv()
        y_half.start()
        line(2)

    def on_corner():
        x_half.wait_recv()
        y_half.wait_recv()
        line(3)
        to_twin[0].start()

    def on_mate(q):
        to_mate[q].wait_recv()
        inside(across_two[q].start)

    def relay_one(q):
        def body():
            across_one[q].wait_recv()
            on_one[q].start()

        inside(body)

    def relay_two(q):
        def body():
            across_two[q].wait_recv()
            on_two[q].start()

        inside(body)

    def on_first(q):
        outside(on_one[q].wait_recv)

    def on_second(q):
        outside(on_two[q].wait_recv)

    def twin(i):
        to_twin[i].start()

    def arrive():
        for copy in to_twin:
            copy.wait_recv()

    def finish():
        for copy in [x_full, y_full, x_half, y_half] + to_mate + to_twin:
            copy.wait_send()

        def body():
            for copy in across_one + across_two + on_one + on_two:
                copy.wait_send()

        inside(body)

    part = functools.partial
    sent = lambda q: [("z", 1, ("mate", q)), ("w", 1, ("a1", q))]
    events = [
        (begin, [], [("x", 1, "xf"), ("y", 1, "yf")] + sent(0)),
        (on_x, ["xf"], [("y", 0.5, "xh")] + sent(1)),
        (on_y, ["yf"], [("x", 0.5, "yh")] + sent(2)),
        (on_corner, ["xh", "yh"], sent(3) + [("c", 4, ("t", 0))]),
    ]
    for q in range(4):
        events.append((part(on_mate, q), [("mate", q)], [("w", 1, ("a2", q)), ("n", 0, ("m", q))]))
        events.append((part(relay_one, q), [("a1", q)], [("z", 1, ("o1", q))]))
        events.append((part(on_first, q), [("o1", q)], [("n", 0, ("f", q))]))
        events.append((part(relay_two, q), [("a2", q)], [("z", 1, ("o2", q))]))
        events.append((part(on_second, q), [("o2", q)], [("n", 0, ("s", q))]))
    for i, name in ((1, "m"), (2, "f"), (3, "s")):
        events.append((part(twin, i), [(name, q) for q in range(4)], [("c", 4, ("t", i))]))
    events.append((arrive, [("t", i) for i in range(4)], []))
    return events, finish


def scatter_sems(groups):
    return groups * (1 + 2 * 5) + 2 * 3


def scatter_scratch(rows, columns):
    shape = lambda *lead: pltpu.VMEM(lead + (columns,), jnp.bfloat16)
    return [
        shape(4, 2, 2, rows),
        shape(4, 2, 2, rows),
        shape(4, rows // 2),
        shape(4, rows // 2),
        shape(4, rows),
        shape(4, rows),
        shape(3, rows),
    ]


def scatter_events(place, grads, part, total, scratch, groups):
    z, x, y, c = place.z, place.x, place.y, place.c
    held, twin, corner_low, corner_high, from_x, from_y, from_z = scratch
    rows, columns = total.shape
    half = rows // 2
    part = pl.ds(*part)
    ox, oy, oc = 1 - x, 1 - y, 1 - c
    xp, yp, cp = place.to(x=ox), place.to(y=oy), place.to(c=oc)
    if groups == 1:
        spans, lines = [(0, 4)], [[0, 1, 2, None]]
    elif groups == 2:
        spans = [(2 - place.pair, 2), (place.pair, 2)]
        lines = [[0, 1], [2, None]]
    else:
        spans = [(place.far, 1), (place.cross, 1), (place.mate, 1), (z, 1)]
        lines = [[0], [1], [2], [None]]
    ds = [pl.ds(*span) for span in spans]
    low, high = pl.ds(0, half), pl.ds(half, half)
    loads = [place.move(grads.at[d, :, :, c, part], held.at[d]) for d in ds]
    twins = [place.send(grads.at[d, :, :, oc, part], twin.at[d], cp) for d in ds]
    out_low = [place.send(held.at[d, ox, oy, low], corner_low.at[d], xp) for d in ds]
    out_high = [place.send(held.at[d, ox, oy, high], corner_high.at[d], yp) for d in ds]
    out_x = [place.send(held.at[d, ox, y], from_x.at[d], xp) for d in ds]
    out_y = [place.send(held.at[d, x, oy], from_y.at[d], yp) for d in ds]
    line = [place.far, place.cross, place.mate]
    out_z = [place.send(held.at[at, x, y], from_z.at[i], place.to(z=at)) for i, at in enumerate(line)]

    def summed(store, first, count, parts):
        def step(i, carry):
            at = pl.ds(pl.multiple_of(first + i * 16, 16), 16)
            store(at, functools.reduce(jnp.add, [part(at).astype(jnp.float32) for part in parts]))
            return carry

        lax.fori_loop(0, count // 16, step, 0)

    def read(ref, *index, lo=0):
        if lo:
            return lambda at: ref[index + (pl.ds(at.start - lo, 16),)]
        return lambda at: ref[index + (at,)]

    def write(ref, *index):
        def store(at, value):
            ref[index + (at,)] = value.astype(ref.dtype)

        return store

    def each(g, body):
        start, size = spans[g]

        def step(i, carry):
            body(start + i)
            return carry

        lax.fori_loop(0, size, step, 0)

    def begin():
        for g in range(len(spans)):
            twins[g].start()
            loads[g].start()

    def on_corner(g):
        loads[g].wait()
        twins[g].wait_recv()

        def body(at):
            here = (at, ox, oy)
            summed(write(held, *here), 0, rows, [read(held, *here), read(twin, *here)])

        each(g, body)
        out_low[g].start()
        out_high[g].start()

    def on_side(g):
        out_high[g].wait_recv()

        def body(at):
            here = (at, ox, y)
            own = [read(held, *here), read(twin, *here)]
            summed(write(held, *here), 0, half, own)
            summed(write(held, *here), half, half, own + [read(corner_high, at, lo=half)])

        each(g, body)
        out_x[g].start()
        out_low[g].wait_recv()

        def body(at):
            here = (at, x, oy)
            own = [read(held, *here), read(twin, *here)]
            summed(write(held, *here), half, half, own)
            summed(write(held, *here), 0, half, own + [read(corner_low, at)])

        each(g, body)
        out_y[g].start()

    def on_line(g):
        out_x[g].wait_recv()
        out_y[g].wait_recv()
        for i in lines[g]:
            at = z if i is None else line[i]
            here = (at, x, y)
            parts = [read(held, *here), read(twin, *here), read(from_x, at), read(from_y, at)]
            if i is None:
                for copy in out_z:
                    copy.wait_recv()
                parts += [read(from_z, j) for j in range(3)]
                summed(write(total), 0, rows, parts)
            else:
                summed(write(held, *here), 0, rows, parts)
                out_z[i].start()

    def finish():
        for copies in (twins, out_low, out_high, out_x, out_y, out_z):
            for copy in copies:
                copy.wait_send()

    size = 4 // groups
    events = [(begin, [], [("c", 4 * size, ("t", g)) for g in range(groups)])]
    for g in range(groups):
        halves = [("x", 0.5 * size, ("l", g)), ("y", 0.5 * size, ("h", g))]
        events.append((functools.partial(on_corner, g), [("t", g)], halves))
    for g in range(groups):
        fulls = [("x", size, ("x", g)), ("y", size, ("y", g))]
        events.append((functools.partial(on_side, g), [("l", g), ("h", g)], fulls))
    for g in range(groups):
        sent = [("z", 1.33, ("z", i)) for i in lines[g] if i is not None]
        waits = [("x", g), ("y", g)]
        if groups > 1 and g == groups - 1:
            waits += [("z", i) for i in range(2)]
        events.append((functools.partial(on_line, g), waits, sent))
    if groups == 4:
        events[-1][1].append(("z", 2))
    return events, finish


HOP = 2.5
LINK = 90e3
CORE = 500e3
SLACK = 1.2
BACKLOGS = [(a, b) for a in (0.0, 1.0, 2.0, 4.0) for b in (0.5, 2.0, 4.0, 8.0, 16.0)]


def plan_of(lists, starts):
    return min((simulate(lists, starts, limits) for limits in BACKLOGS), key=lambda plan: plan[0])[1:]


def simulate(lists, starts, limits):
    free = {"x": 0.0, "y": 0.0, "z": 0.0, "w": 0.0, "c": 0.0}
    arrival, pending = {}, []
    for number, ((events, finish), move) in enumerate(lists):
        for order, (event, waits, sends) in enumerate(events):
            pending.append((number, order, event, [(number, w) for w in waits], sends, move))

    def ready(item):
        number, order, _, waits, _, move = item
        if any(w not in arrival for w in waits):
            return None
        if order:
            if any(p[0] == number and p[1] == 0 for p in pending):
                return None
        return max([arrival[w] for w in waits], default=0.0)

    def run(item, now):
        number, _, event, _, sends, move = item
        pending.remove(item)
        for link, units, name in sends:
            if link == "n":
                arrival[number, name] = now
                continue
            rate = CORE if link == "c" else LINK
            cores = 1 if link == "c" else 2
            took = units * cores * move["bytes"] / rate
            free[link] = max(free[link], now) + took
            arrival[number, name] = free[link] + HOP
        return event

    before, now = {}, 3.0
    places = [(i, j, took) for i, parts in enumerate(starts) for j, took in enumerate(parts)]
    for step, part, took in places + [(len(starts), 0, 0.0)]:
        last = step == len(starts)
        while True:
            found, forced_found = None, None
            top = min([p[0] for p in pending if p[5]["step"] <= step], default=0)
            pressed = any(p[5]["need"] is not None and p[5]["need"] <= step for p in pending)
            for item in pending:
                number, order, _, _, sends, move = item
                if move["step"] > step:
                    continue
                at = ready(item)
                if at is None:
                    continue
                if last or (move["need"] is not None and move["need"] <= step):
                    if forced_found is None or at < forced_found[0]:
                        forced_found = (at, item)
                elif number > top:
                    backlog = max((free[k] - now for k, _, _ in sends if k in "xyzw"), default=0.0)
                    if backlog > limits[0 if pressed else 1]:
                        continue
                if at <= now and (found is None or number < found[1][0]):
                    found = (at, item)
            if found is None:
                found = forced_found
            if found is None:
                break
            now = max(now, found[0])
            before.setdefault((step, part), []).append(run(found[1], now))
        now += SLACK * took
    after = before.pop((len(starts), 0), [])
    assert not pending
    return now, before, after + [finish for (_, finish), _ in lists]


def gather(array, dtype, groups=4, relay=True, need=None, step=0, columns=None, late=False):
    columns = ((0, array.shape[1]),) if columns is None else columns
    shape = (array.shape[0], sum(n for _, n in columns))
    return dict(
        kind="gather",
        array=array,
        dtype=dtype,
        groups=groups,
        relay=relay,
        late=late,
        bytes=shape[0] * shape[1] * jnp.dtype(dtype).itemsize,
        need=need,
        step=step,
        columns=columns,
        shape=shape,
    )


def scatter(array, shape=None, groups=4, step=0):
    shape = array.shape[4:] if shape is None else shape
    size = 2 * shape[0] * shape[1]
    return dict(kind="scatter", array=array, shape=shape, groups=groups, bytes=size, need=None, step=step)


def fused_kernel(body, counts, moves, starts, *refs):
    n_in, n_out, n_scratch = counts
    numbers = []
    for move in moves:
        if isinstance(move["array"], int):
            numbers.append(None)
        else:
            same = [i for i, m in enumerate(moves) if m["array"] is move["array"]][0]
            known = numbers[same] if same < len(numbers) else None
            numbers.append(max([n for n in numbers if n is not None], default=-1) + 1 if known is None else known)
    n_given = max([n for n in numbers if n is not None], default=-1) + 1
    ins, given = refs[:n_in], list(refs[n_in : n_in + n_given])
    refs = refs[n_in + n_given :]
    outs, made = refs[:n_out], refs[n_out : n_out + len(moves)]
    refs = refs[n_out + len(moves) :]
    scratch, spare = refs[:n_scratch], list(refs[n_scratch:-1])
    step = pl.program_id(0)
    place = Place(refs[-1])
    lists, lows = [], []
    for move, target, number in zip(moves, made, numbers):
        source = scratch[move["array"]] if number is None else given[number]
        if move["kind"] == "gather":
            low = spare.pop(0)
            lows.append((source, low, move["columns"]))
            if move["late"]:
                events = gather_late_events(place, low, target)
            else:
                events = gather_events(place, low, target, move["groups"], move["relay"])
        else:
            buffers = [spare.pop(0) for _ in range(7)]
            rows = (0, move["shape"][0])
            events = scatter_events(place, source, rows, target, buffers, move["groups"])
        lists.append((events, move))
    before, after = plan_of(lists, starts)

    @pl.when(step == 0)
    def _():
        for source, low, columns in lows:
            put = 0
            for first, size in columns:
                low[:, put : put + size] = source[:, first : first + size].astype(low.dtype)
                put += size
        place.greet()

    def hook(part):
        steps = sorted(at for at, number in before if number == part)

        def one(at):
            @pl.when(step == at)
            def _():
                for event in before[at, part]:
                    event()

        def among(steps):
            if len(steps) == 1:
                one(steps[0])
            elif steps:
                middle = len(steps) // 2
                lax.cond(
                    step < steps[middle],
                    lambda: among(steps[:middle]),
                    lambda: among(steps[middle:]),
                )

        among(steps)

    hook(0)
    body(made, hook, *ins, *outs, *scratch)

    @pl.when(step == len(starts) - 1)
    def _():
        for event in after:
            event()


def call(body, name, steps, ins, in_specs, outs, out_specs, scratch=(), moves=(), collective=None, starts=()):
    scratch = list(scratch)
    params = dict(vmem_limit_bytes=VMEM_LIMIT)
    counts = (len(ins), len(outs), len(scratch))
    kernel = functools.partial(body, (), lambda part: None)
    if moves:
        params.update(collective_id=collective, has_side_effects=True)
        kernel = functools.partial(fused_kernel, body, counts, moves, starts)
        assert len(starts) == steps
    ins, in_specs, outs, out_specs = list(ins), list(in_specs), list(outs), list(out_specs)
    sems = 0
    for move in moves:
        array = move["array"]
        if move["kind"] == "gather":
            if not any(array is other for other in ins[counts[0] :]):
                ins.append(array)
                in_specs.append(whole(array.shape))
            outs.append(struct((4, 2, 2, 2) + move["shape"], move["dtype"]))
            out_specs.append(pl.BlockSpec(memory_space=pl.ANY))
            scratch.append(pltpu.VMEM(move["shape"], move["dtype"]))
            sems += gather_sems(move["groups"])
        else:
            if not isinstance(array, int):
                ins.append(array)
                in_specs.append(pl.BlockSpec(memory_space=pl.ANY))
            outs.append(struct(move["shape"], F32))
            out_specs.append(whole_out(move["shape"]))
            scratch += scatter_scratch(*move["shape"])
            sems += scatter_sems(move["groups"])
    if moves:
        scratch.append(pltpu.SemaphoreType.DMA((sems,)))
    made = pl.pallas_call(
        kernel,
        name=name,
        grid=(steps,),
        out_shape=outs,
        in_specs=in_specs,
        out_specs=out_specs,
        scratch_shapes=scratch,
        compiler_params=pltpu.CompilerParams(**params),
    )(*ins)
    return made[: counts[1]], made[counts[1] :]


def times(left, right):
    return jnp.dot(left, right, preferred_element_type=jnp.float32)


def times_transpose(left, right):
    return lax.dot_general(
        left, right, (((1,), (1,)), ((), ())), preferred_element_type=jnp.float32
    )


def transpose_times(left, right):
    return lax.dot_general(
        left, right, (((0,), (0,)), ((), ())), preferred_element_type=jnp.float32
    )


def normalize(value):
    centre = value - jnp.mean(value, axis=-1, keepdims=True)
    rstd = lax.rsqrt(jnp.mean(centre * centre, axis=-1, keepdims=True) + EPSILON)
    return centre * rstd, rstd


def norm_back(grad_out, normed, rstd, gain):
    scaled = grad_out * gain
    mean_one = jnp.mean(scaled, axis=-1, keepdims=True)
    mean_two = jnp.mean(scaled * normed, axis=-1, keepdims=True)
    return rstd * (scaled - mean_one - normed * mean_two)


def eight(value):
    rows, columns = value.shape
    return jnp.sum(value.reshape(rows // 8, 8, columns), axis=0)


def gelu_parts(value):
    bell = jnp.exp(-0.5 * value * value)
    size = jnp.abs(value)
    t = 1.0 / (1.0 + 0.23164189 * size)
    tail = t * (
        0.127414796
        + t * (-0.142248368 + t * (0.7107068705 + t * (-0.7265760135 + t * 0.5307027145)))
    )
    tail = tail * bell
    phi_big = jnp.where(value >= 0.0, 1.0 - tail, tail)
    return phi_big, bell * 0.3989422804014327


STRIP = 32


def strips(rows, body, carry, unroll=2, hooks=()):
    def step(i, value):
        return body(pl.ds(pl.multiple_of(i * STRIP, STRIP), STRIP), value)

    count, parts = rows // STRIP, max(len(hooks), 1)
    for part in range(parts):
        if hooks:
            hooks[part]()
        first, last = part * count // parts, (part + 1) * count // parts
        carry = lax.fori_loop(first, last, step, carry, unroll=unroll)
    return carry


def enter_step(step, patches, cotangent, keep, vec, hidden, source, upstream, bias_sum, spare, wide):
    cells, windows, width = patches.shape
    high = spare.shape[0] // 2
    gain, shift = vec[0:1], vec[1:2]

    @pl.when(step == 0)
    def _():
        spare[...] = jnp.zeros_like(spare)
        wide[...] = patches[...].astype(F32)

    @pl.when(step == 2)
    def _():
        bias_sum[...] = jnp.zeros_like(bias_sum)
        wide[...] = cotangent[...].astype(F32)

    for pair in range(windows // 2):
        at = pl.ds(pair * 2 * high, 2 * high)
        half = windows // 4

        @pl.when(step == pair // half)
        def _(pair=pair, at=at):
            for w in range(2):
                spare[pl.ds(w * high, cells)] = wide[:, 2 * pair + w, :]
            source[at] = spare[...].astype(BF)
            for w in range(2):
                normed, _ = normalize(spare[pl.ds(w * high, cells)])
                spare[pl.ds(w * high, cells)] = normed * gain + shift
            hidden[at] = spare[...].astype(BF)

        @pl.when(step == 2 + pair // half)
        def _(pair=pair, at=at):
            for w in range(2):
                mask = jnp.concatenate([keep[2 * pair + w]] * (width // 128), axis=1)
                spare[pl.ds(w * high, cells)] = wide[:, 2 * pair + w, :] * mask[:cells]
            bias_sum[...] += eight(spare[...])
            upstream[at] = spare[...].astype(BF)


def bias_step(step, table, bias, padded, stack):
    heads, high, _ = bias.shape
    cells = WS * WS
    side = 2 * WS - 1
    middle = (WS - 1) * side + WS - 1
    spot = lax.broadcasted_iota(jnp.int32, (256, 128), 0)
    cell = lax.broadcasted_iota(jnp.int32, (256, 128), 1)
    put = ((cell // WS) * side + lax.rem(cell, WS) == spot) & (cell < cells)

    @pl.when(step == 0)
    def _():
        padded[...] = jnp.zeros_like(padded)
        padded[:, : table.shape[1]] = table[...]
        bias[:, pl.ds(cells, high - cells)] = jnp.zeros((heads, high - cells, 128), F32)

    count = cells // 4
    for part in range(4):

        @pl.when(step == part)
        def _(part=part):
            for n in range(count):
                j = part * count + n
                shift = middle - (j // WS) * side - j % WS
                rolled = pltpu.roll(padded[...], (384 - shift) % 384, axis=1)
                stack[pl.ds(heads * n, heads)] = rolled[:, :256]
            found = jnp.dot(stack[...], put.astype(F32), precision=HIGH, preferred_element_type=F32)
            for n in range(count):
                bias[:, part * count + n, :] = found[heads * n : heads * n + heads]


def lanes_of(head):
    lane = lax.broadcasted_iota(jnp.int32, (1, 128), 1)
    return (lane // 32) == head


def pick(value, head):
    return jnp.where(lanes_of(head), value, jnp.zeros_like(value))


def spread_heads(value):
    head = lax.broadcasted_iota(jnp.int32, value.shape, 0) // 32
    return jnp.concatenate([jnp.where(head == h, value, jnp.zeros_like(value)) for h in range(4)], axis=1)


def own_heads(value):
    return jnp.concatenate(
        [value[32 * h : 32 * h + 32, 128 * h : 128 * h + 128] for h in range(4)], axis=0
    )


def stack_heads(value):
    return jnp.concatenate([pick(value, h) for h in range(4)], axis=0)


def with_rows(value, rows):
    return jnp.concatenate([value, jnp.zeros((rows - value.shape[0], value.shape[1]), F32)], axis=0)


def attend_step(hook, group, pair, hidden, weights, vec, bias, mask, query, keys, values, probs, out):
    windows, _, columns = query.shape
    high = hidden.shape[0] // windows

    @pl.when(pair == 0)
    def _():
        at = pl.ds(pl.multiple_of(group * columns, columns), columns)
        for j, (target, bias_row) in enumerate(((query, 2), (keys, None), (values, 3))):
            product = times(hidden[...], weights(j))
            if bias_row is not None:
                product = product + vec[bias_row : bias_row + 1, at]
            for w in range(windows):
                here = with_rows(product[w * high : (w + 1) * high], target.shape[1])
                target[w] = here.astype(BF)

        hook(1)

    scale = 32 ** (-0.5)
    done = []
    for w in range(2):
        window = pair * 2 + w
        parts = []
        for g in range(columns // 128):
            at = pl.ds(g * 128, 128)
            q, k, v = query[window, :, at], keys[window, :, at], values[window, :, at]
            scores = times(k, spread_heads(q.T))
            found = []
            for h in range(4):
                head = group * (columns // 32) + g * 4 + h
                score = scores[:, 128 * h : 128 * h + 128] * scale + bias[head] + mask[window]
                score = jnp.exp(score - jnp.max(score, axis=0, keepdims=True))
                prob = (score * (1.0 / jnp.sum(score, axis=0, keepdims=True))).astype(BF)
                probs[w, g * 4 + h] = prob
                found.append(prob)
            mixed = times(v.T, jnp.concatenate(found, axis=1))
            parts.append(own_heads(mixed).T[:high])
        done.append(jnp.concatenate(parts, axis=1))
    rows = pl.ds(pl.multiple_of(pair * 2 * high, 16), 2 * high)
    at = pl.ds(pl.multiple_of(group * columns, columns), columns)
    out[rows, at] = jnp.concatenate(done, axis=0).astype(BF)


def flat(value):
    return value.reshape(-1, value.shape[-1])


def forward_body(direct, made, hook, *refs):
    refs = list(refs)
    take = lambda n: [refs.pop(0) for _ in range(n)]
    patches, cotangent, keep, vec, table = take(5)
    *w_attend, w_output, w_low, w_high = made[:7] if direct else take(7)
    *kept, bias_sum, query, keys, values, probs = take(8)
    kept += take(3)
    act, slope, grad = take(3)
    held = take(6)
    hidden_t, source, upstream, attended, middle, hidden_two_t = held
    spare, hidden, wqkv, wo, we, hidden_two, before, wide, bias, mask, padded, stack, sems = refs
    step = pl.program_id(0)
    rows, width = hidden.shape
    windows, _, columns = query.shape
    pairs, groups = windows // 2, width // columns
    enters, attends = pairs, pairs * groups
    chunk = act.shape[1]
    per_half = w_low.shape[-1] // chunk
    chunks = 2 * per_half

    @pl.when(step < enters)
    def _():
        enter_step(step, patches, cotangent, keep, vec, hidden, source, upstream, bias_sum, spare, wide)
        bias_step(step, table, bias, padded, stack)

    @pl.when(step == 0)
    def _():
        there = lax.broadcasted_iota(jnp.int32, mask.shape, 1) < patches.shape[0]
        mask[...] = jnp.where(there, (keep[...] - 1.0) * MASK_FILL, -1e30)

    inner_step = step - enters
    group, pair = inner_step // pairs, lax.rem(inner_step, pairs)

    def load_qkv(number):
        slot = number % 2
        return pltpu.make_async_copy(w_attend[number], wqkv.at[slot], sems.at[slot])

    load_wo = pltpu.make_async_copy(w_output, wo, sems.at[2])

    def load_we(half, index):
        slot = lax.rem(index, 2)
        at = pl.ds(pl.multiple_of(lax.rem(index, per_half) * chunk, chunk), chunk)
        source = (w_low, w_high)[half]
        return pltpu.make_async_copy(source.at[:, :, :, :, :, at], we.at[slot], sems.at[3 + slot])

    @pl.when((inner_step >= 0) & (inner_step < attends))
    def _():
        @pl.when(inner_step == 0)
        def _():
            hidden_t[...] = hidden[...].T

        for number in range(groups):

            @pl.when(inner_step == number * pairs)
            def _(number=number):
                copy = load_qkv(number)
                copy.start()
                copy.wait()

        slot = lax.rem(group, 2)
        weights = lambda j: flat(wqkv[slot, :, :, :, :, :, pl.ds(j * columns, columns)])
        attend_step(hook, group, pair, hidden, weights, vec, bias, mask, query, keys, values, probs, attended)

    @pl.when(inner_step == attends)
    def _():
        load_wo.start()
        load_wo.wait()
        for j in range(2):
            at = pl.ds(j * (width // 2), width // 2)
            middle[:, at] = times(attended[...], flat(wo[:, :, :, :, :, at])) + vec[4:5, at]

        hook(1)

        def strip(at, carry):
            value = middle[at] + source[at].astype(F32)
            middle[at] = value
            normed, _ = normalize(value)
            hidden_two[at] = (normed * vec[5:6] + vec[6:7]).astype(BF)
            return carry

        strips(rows, strip, 0)
        hidden_two_t[...] = hidden_two[...].T

    write = [
        pltpu.make_async_copy(value, out, sems.at[5 + i])
        for i, (value, out) in enumerate(zip(held, kept))
    ]

    @pl.when(inner_step == attends + 1)
    def _():
        for copy in write:
            copy.start()

    @pl.when(inner_step == attends + chunks)
    def _():
        for copy in write:
            copy.wait()

    @pl.when(inner_step > attends)
    def _():
        index = inner_step - attends - 1
        for half in range(2):

            @pl.when(index == half * per_half)
            def _(half=half):
                load_we(half, index).start()

            @pl.when(index // per_half == half)
            def _(half=half):
                load_we(half, index).wait()

                @pl.when(lax.rem(index, per_half) < per_half - 1)
                def _():
                    load_we(half, index + 1).start()

        before[...] = times(hidden_two[...], flat(we[lax.rem(index, 2)]))
        per = width // chunk
        shift_at = pl.ds(pl.multiple_of(lax.rem(index, per) * chunk, chunk), chunk)
        shift = vec[pl.ds(8 + index // per, 1), shift_at]
        hook(1)

        def strip(at, carry):
            value = before[at] + shift
            big, small = gelu_parts(value)
            act[at] = (value * big).astype(BF)
            slope[at] = (big + value * small).astype(BF)
            return carry

        strips(rows, strip, 0)
        hook(2)
        grad[...] = transpose_times(act[...], upstream[...]).astype(BF)


def forward(patches, cotangent, keep, vec, table, ff, gathered, moves, collective):
    cells, windows, width = patches.shape
    high, tall, wide_rows = -(-cells // 8) * 8, keep.shape[1], -(-cells // 128) * 128
    rows = windows * high
    heads = table.shape[0]
    columns, chunk = 256, 512
    groups, pairs = width // columns, windows // 2
    per = columns // 32
    direct = bool(moves)
    enters, attends = pairs, pairs * groups
    steps = enters + attends + 1 + ff // chunk
    group = lambda s: jnp.clip((s - enters) // pairs, 0, groups - 1)
    pair = lambda s: jnp.where(
        s < enters, 0, jnp.where(s < enters + attends, lax.rem(s - enters, pairs), pairs - 1)
    )
    later = lambda s: jnp.maximum(s - enters - attends - 1, 0)
    seen = lambda n: pl.BlockSpec((windows, n, columns), lambda s: (0, 0, group(s)))
    wide = pl.BlockSpec((rows, chunk), lambda s: (0, later(s)))
    any_place = pl.BlockSpec(memory_space=pl.ANY)
    starts = [[2.5]] * enters + [[1.7, 1.1], [1.1], [1.1], [1.1]] * groups
    starts += [[1.7, 2.5]] + [[1.2, 1.7, 1.25]] * (ff // chunk)
    lead = (4, 2, 2, 2, width // 32)
    return call(
        functools.partial(forward_body, direct),
        "forward",
        steps=steps,
        ins=[patches, cotangent, keep, vec, table] + list(gathered),
        in_specs=[
            whole(patches.shape),
            whole(cotangent.shape),
            whole(keep.shape),
            whole(vec.shape),
            whole(table.shape),
        ]
        + [any_place] * len(gathered),
        outs=[
            struct((width, rows), BF),
            struct((rows, width), BF),
            struct((rows, width), BF),
            struct((8, width), F32),
            struct((windows, wide_rows, width), BF),
            struct((windows, tall, width), BF),
            struct((windows, tall, width), BF),
            struct((windows, heads, tall, 128), BF),
            struct((rows, width), BF),
            struct((rows, width), F32),
            struct((width, rows), BF),
            struct((rows, ff), BF),
            struct((rows, ff), BF),
            struct((ff, width), BF),
        ],
        out_specs=[
            any_place,
            any_place,
            any_place,
            whole_out((8, width)),
            seen(wide_rows),
            seen(tall),
            seen(tall),
            pl.BlockSpec((2, per, tall, 128), lambda s: (pair(s), group(s), 0, 0)),
            any_place,
            any_place,
            any_place,
            wide,
            wide,
            pl.BlockSpec((chunk, width), lambda s: (later(s), 0)),
        ],
        scratch=[
            pltpu.VMEM((width, rows), BF),
            pltpu.VMEM((rows, width), BF),
            pltpu.VMEM((rows, width), BF),
            pltpu.VMEM((rows, width), BF),
            pltpu.VMEM((rows, width), F32),
            pltpu.VMEM((width, rows), BF),
            pltpu.VMEM((2 * high, width), F32),
            pltpu.VMEM((rows, width), BF),
            pltpu.VMEM((2,) + lead + (3 * columns,), BF),
            pltpu.VMEM(lead + (width,), BF),
            pltpu.VMEM((2,) + lead + (chunk,), BF),
            pltpu.VMEM((rows, width), BF),
            pltpu.VMEM((rows, chunk), F32),
            pltpu.VMEM((cells, windows, width), F32),
            pltpu.VMEM((heads, tall, 128), F32),
            pltpu.VMEM((windows, tall, 128), F32),
            pltpu.VMEM((heads, 384), F32),
            pltpu.VMEM((heads * WS * WS // 4, 256), F32),
            pltpu.SemaphoreType.DMA((11,)),
        ],
        moves=moves,
        collective=collective,
        starts=starts,
    )


def middle_body(made, hook, *refs):
    refs = list(refs)
    take = lambda n: [refs.pop(0) for _ in range(n)]
    act, slope, ws, we_low, we_high, wo, upstream, hidden_t, middle, attended, vec, shrink_sum = take(12)
    result, grad_e, mid, grad_o, dout, small = take(6)
    grad_low, back, sums, rows_of, we, sems = refs
    total = mid
    step = pl.program_id(0)
    chunks = back.shape[0]
    rows, width = mid.shape
    windows, cells, _ = result.shape
    high = rows // windows
    chunk = back.shape[2]

    @pl.when(step == 0)
    def _():
        total[...] = middle[...] + vec[7:8]

    @pl.when(step < chunks)
    def _():
        total[...] += times(act[...], ws[...])
        hook(1)
        product = times_transpose(upstream[...], ws[...])
        here = (product * slope[...].astype(F32)).astype(BF)
        back[step] = here
        line = jnp.sum(here.astype(F32), axis=0, keepdims=True)
        per = width // chunk
        sums[pl.ds(4 + step // per, 1), pl.ds(pl.multiple_of(lax.rem(step, per) * chunk, chunk), chunk)] = line
        hook(2)
        product = times(hidden_t[...], here).astype(BF)

        @pl.when(step < chunks // 2)
        def _():
            at = pl.ds(pl.multiple_of(step * chunk, chunk), chunk)
            grad_low[:, :, :, :, :, at] = product.reshape(grad_low.shape[:5] + (chunk,))

        @pl.when(step >= chunks // 2)
        def _():
            grad_e[...] = product


    @pl.when(step == chunks - 1)
    def _():
        for w in range(windows):
            result[w] = total[pl.ds(w * high, cells)].astype(BF)
        total[...] = jnp.zeros_like(total)

    per_half = chunks // 2

    def load_we(half, index):
        slot = lax.rem(index, 2)
        at = pl.ds(pl.multiple_of((index - half * per_half) * chunk, chunk), chunk)
        return pltpu.make_async_copy((we_low, we_high)[half].at[:, at], we.at[slot], sems.at[slot])

    for half in range(2):

        @pl.when((step >= chunks + half * per_half - 1) & (step < chunks + (half + 1) * per_half - 1))
        def _(half=half):
            load_we(half, step - chunks + 1).start()

    @pl.when(step >= chunks)
    def _():
        index = step - chunks

        for half in range(2):

            @pl.when(index // per_half == half)
            def _(half=half):
                load_we(half, index).wait()

        total[...] += times_transpose(back[index], we[lax.rem(index, 2)])

    @pl.when(step == 2 * chunks - 1)
    def _():
        zero = jnp.zeros((8, width), F32)

        def strip(at, carry):
            gain_sum, shift_sum, out_sum = carry
            normed, rstd = normalize(middle[at])
            value = total[at]
            grad_mid = upstream[at].astype(F32) + norm_back(value, normed, rstd, vec[5:6])
            mid[at] = grad_mid
            low = grad_mid.astype(BF)
            for j in range(2):
                back[j, at] = low[:, j * chunk : j * chunk + chunk]
            return (
                gain_sum + eight(value * normed),
                shift_sum + eight(value),
                out_sum + eight(low.astype(F32)),
            )

        load_wo = [
            pltpu.make_async_copy(wo.at[:, pl.ds(j * chunk, chunk)], we.at[j], sems.at[j])
            for j in range(2)
        ]
        for copy in load_wo:
            copy.start()
        hooks = [functools.partial(hook, part) for part in (1, 2, 3, 4)]
        found = strips(rows, strip, (zero, zero, zero), unroll=1, hooks=hooks)
        gain_sum, shift_sum, out_sum = found
        for i, value in enumerate((out_sum, gain_sum, shift_sum, shrink_sum[...])):
            sums[i : i + 1] = jnp.sum(value, axis=0, keepdims=True)
        rows_of[...] = jnp.zeros_like(rows_of)
        for d in range(32):
            at = pl.ds(128 * (d // 4), 128)
            rows_of[pl.ds(32 * d, 2)] = sums[pl.ds(2 * (d % 4), 2), at]
        small[...] = rows_of[...].astype(BF).reshape(small.shape)
        for j in range(2):
            hook(5 + j)
            at = pl.ds(j * chunk, chunk)
            grad_o[:, at] = transpose_times(attended[...], back[j]).astype(BF)
            if j == 0:
                for copy in load_wo:
                    copy.wait()
            product = times_transpose(back[0], we[0, at])
            product = product + times_transpose(back[1], we[1, at])
            for w in range(windows):
                here = with_rows(product[w * high : (w + 1) * high], dout.shape[1])
                dout[w, :, at] = here.astype(BF)


def middle_part(act, slope, w_shrink, w_low, w_high, w_output, upstream, hidden_t, middle, attended, vec, shrink_sum, windows, cells, moves, collective):
    rows, ff = act.shape
    width = middle.shape[1]
    wide_rows = -(-cells // 128) * 128
    chunk = 512
    chunks = ff // chunk
    early = lambda s: jnp.minimum(s, chunks - 1)
    half = chunks // 2
    later = lambda first: lambda s: (0, jnp.clip(s - first, 0, half - 1))
    wide = pl.BlockSpec((rows, chunk), lambda s: (0, early(s)))
    starts = [[1.2, 1.3, 1.2]] * chunks + [[1.7]] * (chunks - 1) + [[1.7] + [1.5] * 4 + [2.5, 2.5]]
    low = ((4, 2, 2, 2, width // 32, ff // 2), BF)
    scratch = [pltpu.VMEM(*low)] if moves else []
    low_outs = [] if moves else [struct(*low)]
    return call(
        middle_body,
        "middle",
        steps=2 * chunks,
        ins=[act, slope, w_shrink, w_low, w_high, w_output, upstream, hidden_t, middle, attended, vec, shrink_sum],
        in_specs=[
            wide,
            wide,
            pl.BlockSpec((chunk, width), lambda s: (early(s), 0)),
            pl.BlockSpec(memory_space=pl.ANY),
            pl.BlockSpec(memory_space=pl.ANY),
            pl.BlockSpec(memory_space=pl.ANY),
            whole((rows, width)),
            whole((width, rows)),
            whole((rows, width)),
            whole((rows, width)),
            whole(vec.shape),
            whole(shrink_sum.shape),
        ],
        outs=[
            struct((windows, cells, width), BF),
            struct((width, ff // 2), BF),
            struct((rows, width), F32),
            struct((width, width), BF),
            struct((windows, wide_rows, width), BF),
            struct((4, 2, 2, 2, 32, 128), BF),
        ]
        + low_outs,
        out_specs=[
            whole_out((windows, cells, width)),
            pl.BlockSpec((width, chunk), later(half)),
            whole_out((rows, width)),
            whole_out((width, width)),
            whole_out((windows, wide_rows, width)),
            whole_out((4, 2, 2, 2, 32, 128)),
        ]
        + [whole_out(o.shape) for o in low_outs],
        scratch=scratch
        + [
            pltpu.VMEM((chunks, rows, chunk), BF),
            pltpu.VMEM((8, width), F32),
            pltpu.VMEM((32 * 32, 128), F32),
            pltpu.VMEM((2, width, chunk), BF),
            pltpu.SemaphoreType.DMA((2,)),
        ],
        moves=moves,
        collective=collective,
        starts=starts,
    )


def backward_body(groups, made, hook, *refs):
    refs = list(refs)
    take = lambda n: [refs.pop(0) for _ in range(n)]
    query, keys, values, dout, probs, hidden_t, source, mid, vec, counts = take(10)
    w_attend = take(groups)
    out, late = take(2)
    pieces = take(groups)
    bias_low, joint, bias, total, wa, sems = refs
    step = pl.program_id(0)
    windows, _, columns = query.shape
    width, rows = hidden_t.shape
    cells = out.shape[0]
    high = rows // windows
    pairs = windows // 2
    pair = lax.rem(step, pairs)
    group = step // pairs
    scale = 32 ** (-0.5)

    @pl.when(step == 0)
    def _():
        bias_low[...] = jnp.zeros_like(bias_low)
        total[...] = jnp.zeros_like(total)

    @pl.when(step < pairs * groups)
    def _():
        @pl.when(pair == 0)
        def _():
            bias[...] = jnp.zeros_like(bias)

        done = []
        for w in range(2):
            window = pair * 2 + w
            parts = []
            for g in range(columns // 128):
                at = pl.ds(g * 128, 128)
                q, k, v = query[window, :, at], keys[window, :, at], values[window, :, at]
                d = dout[window, :, at]
                slopes = times(v, spread_heads(d.T))
                found, low = [], []
                for h in range(4):
                    prob = probs[w, g * 4 + h]
                    soft = prob.astype(F32)
                    both = soft * slopes[:, 128 * h : 128 * h + 128]
                    ds = (both - soft * jnp.sum(both, axis=0, keepdims=True)).astype(BF)
                    bias[g * 4 + h] += ds.astype(F32)
                    found.append(ds)
                    low.append(prob)
                found = jnp.concatenate(found, axis=1)
                dq = own_heads(times(k.T, found)).T[:high] * scale
                dk = times(found, stack_heads(q))[:high] * scale
                dv = times(jnp.concatenate(low, axis=1), stack_heads(d))[:high]
                parts.append((dq, dk, dv))
            done.append([jnp.concatenate([p[j] for p in parts], axis=1) for j in range(3)])
        at_rows = pl.ds(pl.multiple_of(pair * 2 * high, 16), 2 * high)
        for j in range(3):
            joint[group, at_rows, pl.ds(j * columns, columns)] = jnp.concatenate([done[0][j], done[1][j]], axis=0).astype(BF)

    @pl.when((step < pairs * groups) & (pair == pairs - 1))
    def _():
        hook(1)

    for g in range(groups):

        @pl.when(step == pairs * (g + 1) - 1)
        def _(g=g):
            per = columns // 32
            for h in range(per):
                d = g * per + h
                bias_low[d // 8, (d // 4) % 2, (d // 2) % 2, d % 2, : bias.shape[1]] = bias[h].astype(BF)
            for j in range(3):
                here = joint[g, :, j * columns : (j + 1) * columns]
                product = times(hidden_t[...], here).astype(BF)
                at = pl.ds(j * columns, columns)
                pieces[g][:, :, :, :, :, at] = product.reshape(pieces[g].shape[:5] + (columns,))
                if j != 1:
                    row = pl.ds(2 if j == 0 else 3, 1)
                    here = jnp.sum(here.astype(F32), axis=0, keepdims=True)
                    late[row, pl.ds(g * columns, columns)] = here

    load = lambda g: pltpu.make_async_copy(w_attend[g], wa.at[g % 2], sems.at[g % 2])

    @pl.when(step == pairs * groups - 1)
    def _():
        load(0).start()

    for g in range(groups):

        @pl.when(step == pairs * groups + g)
        def _(g=g):
            load(g).wait()
            if g + 1 < groups:
                load(g + 1).start()
            total[...] += times_transpose(joint[g], flat(wa[g % 2]))

    @pl.when(step == pl.num_programs(0) - 1)
    def _():
        zero = jnp.zeros((8, width), F32)
        inverse = inverse_of(counts)

        def strip(at, carry):
            gain_sum, shift_sum = carry
            normed, rstd = normalize(source[at].astype(F32))
            value = total[at]
            full = mid[at] + norm_back(value, normed, rstd, vec[0:1])
            total[at] = full * inverse
            return gain_sum + eight(value * normed), shift_sum + eight(value)

        hooks = [functools.partial(hook, part) for part in (1, 2, 3, 4, 5, 6)]
        found = strips(rows, strip, (zero, zero), unroll=1, hooks=hooks)
        for i in range(2):
            late[pl.ds(i, 1)] = jnp.sum(found[i], axis=0, keepdims=True)
        for w in range(windows):
            out[:, w, :] = total[pl.ds(w * high, cells)]


def backward_part(query, keys, values, dout, probs, hidden_t, w_attend, source, mid, vec, counts, cells, moves, collective):
    windows, _, width = query.shape
    rows = hidden_t.shape[1]
    tall = keys.shape[1]
    columns = 256
    groups, pairs = width // columns, windows // 2
    per = columns // 32
    steps = groups * pairs
    group = lambda s: jnp.minimum(s // pairs, groups - 1)
    pair = lambda s: jnp.where(s < steps, lax.rem(s, pairs), pairs - 1)
    seen = lambda array: pl.BlockSpec((windows, array.shape[1], columns), lambda s: (0, 0, group(s)))
    lead = (4, 2, 2, 2)
    pieces = [(lead + (width // 32, 3 * columns), BF)] * groups + [(lead + (128, 128), BF)]
    outs = [struct((cells, windows, width), F32), struct((4, width), F32)]
    out_specs = [whole_out((cells, windows, width)), whole_out((4, width))]
    scratch = [
        pltpu.VMEM((groups, rows, 3 * columns), BF),
        pltpu.VMEM((per, tall, 128), F32),
        pltpu.VMEM((rows, width), F32),
        pltpu.VMEM((2,) + lead + (width // 32, 3 * columns), BF),
        pltpu.SemaphoreType.DMA((2,)),
    ]
    if moves:
        scratch = [pltpu.VMEM(*p) for p in pieces] + scratch
    else:
        outs += [struct(*p) for p in pieces]
        out_specs += [whole_out(p[0]) for p in pieces]
    starts = [[1.5], [1.5], [1.5], [1.5, 3.1]] * groups + [[2.7]] * (groups - 1) + [[2.7] + [1.5] * 6]
    return call(
        functools.partial(backward_body, groups),
        "backward",
        steps=steps + groups,
        ins=[query, keys, values, dout, probs, hidden_t, source, mid, vec, counts] + list(w_attend),
        in_specs=[seen(a) for a in (query, keys, values, dout)]
        + [
            pl.BlockSpec((2, per, tall, 128), lambda s: (pair(s), group(s), 0, 0)),
            whole((width, rows)),
            whole((rows, width)),
            whole((rows, width)),
            whole(vec.shape),
            whole(counts.shape),
        ]
        + [pl.BlockSpec(memory_space=pl.ANY)] * groups,
        outs=outs,
        out_specs=out_specs,
        scratch=scratch,
        moves=moves,
        collective=collective,
        starts=starts,
    )


def fresh_moments(grad, first, second, weight, factor):
    clipped = grad * factor
    first_new = MOMENT_ONE * first + (1.0 - MOMENT_ONE) * clipped
    second_new = MOMENT_TWO * second + (1.0 - MOMENT_TWO) * clipped * clipped
    change = (first_new * (1.0 / (1.0 - MOMENT_ONE**STEP))) / (
        jnp.sqrt(second_new * (1.0 / (1.0 - MOMENT_TWO**STEP))) + ADAM_EPS
    ) + DECAY * weight
    return first_new, second_new, change


def inverse_of(counts):
    places = [(d // 8, (d // 4) % 2, (d // 2) % 2, d % 2) for d in range(counts.shape[0] * 8)]
    found = functools.reduce(jnp.add, [counts[at] for at in places])
    return 1.0 / jnp.sum(found, keepdims=True)


def norms_kernel(pieces, *refs):
    refs = list(refs)
    take = lambda n: [refs.pop(0) for _ in range(n)]
    counts, late_sums, bias_sum, small = take(4)
    sums = take(1 + max(p[4] for p in pieces))
    masters, firsts, seconds = take(4), take(4), take(4)
    vec_grad, heads_grad, norms_out = take(3)
    message, got, message_two, got_plane, got_line, sems = refs
    place = Place(sems)
    place.greet(True)
    devices = got.shape[0] * 8
    scale = inverse_of(counts)
    lane = lax.broadcasted_iota(jnp.int32, (8, 128), 1)
    top = lax.broadcasted_iota(jnp.int32, (8, 128), 0) == 0

    def over(rows, body, carry):
        def step(i, value):
            return body(pl.multiple_of(i * 16, 16), value)

        return lax.fori_loop(0, rows // 16, step, carry)

    def fold(value):
        value = eight(value)
        return functools.reduce(
            jnp.add, [value[:, i : i + 128] for i in range(0, value.shape[1], 128)]
        )

    zero = jnp.zeros((8, 128), F32)
    squares = [zero] * 8
    for k, (row, rows), (column, columns), source_column, number in pieces:
        columns_at = pl.ds(column, columns)

        def body(at, carry):
            here = (pl.ds(row + at, 16), columns_at)
            grad = sums[number][pl.ds(at, 16), pl.ds(source_column, columns)] * scale
            weight = masters[k][here]
            return carry[0] + fold(grad * grad), carry[1] + fold(weight * weight)

        squares[k], squares[4 + k] = over(rows, body, (squares[k], squares[4 + k]))

    def packed(values):
        row = zero
        for i, value in enumerate(values):
            row = jnp.where((lane == i) & top, jnp.sum(value), row)
        return row

    message[pl.ds(0, 8)] = packed(squares)
    message[pl.ds(8, 8)] = zero
    message[pl.ds(8, 2)] = small[pl.ds(0, 2)]
    side = 2 * WS - 1
    cell = lax.broadcasted_iota(jnp.int32, (128, 384), 0)
    spot = lax.broadcasted_iota(jnp.int32, (128, 384), 1)
    put = ((cell // WS) * side + lax.rem(cell, WS) == spot) & (cell < WS * WS)
    wide = jnp.dot(bias_sum[...], put.astype(F32), precision=HIGH, preferred_element_type=F32)
    middle = (WS - 1) * side + WS - 1
    column = jnp.zeros((1, 384), F32)
    for j in range(WS * WS):
        shift = middle - (j // WS) * side - j % WS
        column = column + pltpu.roll(wide[j : j + 1], shift, axis=1)
    for b in range(3):
        message[pl.ds(11 + b, 1)] = column[:, 128 * b : 128 * b + 128]
    late_rows = late_sums.shape[0]
    for i in range(late_rows):
        for b in range(8):
            message[pl.ds(16 + 8 * i + b, 1)] = late_sums[i : i + 1, 128 * b : 128 * b + 128]

    events, end = gather_events(place, message, got, 1, False)
    for event, _, _ in events:
        event()
    end()

    place_of = lambda d: (d // 8, (d // 4) % 2, (d // 2) % 2, d % 2)
    found = functools.reduce(jnp.add, [got[place_of(d) + (pl.ds(0, 8),)] for d in range(devices)])
    late = functools.reduce(
        jnp.add, [got[place_of(d) + (pl.ds(16, 8 * late_rows),)] for d in range(devices)]
    )
    for i in range(late_rows):
        for b in range(8):
            vec_grad[pl.ds(i, 1), pl.ds(128 * b, 128)] = late[8 * i + b : 8 * i + b + 1] * scale
    for d in range(devices):
        block = got[place_of(d) + (pl.ds(8, 8),)] * scale
        vec_grad[pl.ds(4 + 2 * (d % 4), 2), pl.ds(128 * (d // 4), 128)] = block[:2]
        for j in range(3):
            heads_grad[pl.ds(d, 1), pl.ds(128 * j, 128)] = block[3 + j : 4 + j]
    small_grad, table_grad = vec_grad[...], heads_grad[...]

    total = lambda value: jnp.sum(value, keepdims=True)
    scalar = lambda k: total(jnp.where(top & (lane == k), found, 0.0))
    grad_square = scalar(0) + scalar(1) + scalar(2) + scalar(3)
    clip_norm = jnp.sqrt(
        grad_square + total(small_grad * small_grad) + total(table_grad * table_grad)
    )
    factor = jnp.minimum(1.0, CLIP_LIMIT / clip_norm)
    squares = [zero] * 4
    for k, (row, rows), (column, columns), source_column, number in pieces:
        columns_at = pl.ds(column, columns)

        def body(at, carry):
            here = (pl.ds(row + at, 16), columns_at)
            grad = sums[number][pl.ds(at, 16), pl.ds(source_column, columns)] * scale
            _, _, change = fresh_moments(
                grad, firsts[k][here], seconds[k][here], masters[k][here], factor
            )
            return carry + fold(change * change)

        squares[k] = over(rows, body, squares[k])

    message_two[...] = packed(squares)
    spot = place.x * 4 + place.y * 2 + place.c
    got_plane[pl.ds(spot, 1)] = message_two[...][None]
    plane = [place.send(message_two, got_plane.at[spot], peer) for peer in place.plane()]
    for copy in plane:
        copy.start()
    for copy in plane:
        copy.wait_recv()
    plane_sum = functools.reduce(jnp.add, [got_plane[i] for i in range(8)])
    got_line[pl.ds(place.z, 1)] = plane_sum[None]
    line = [
        place.send(got_line.at[place.z], got_line.at[place.z], place.to(z=at))
        for at in (place.mate, place.far, place.cross)
    ]
    for copy in line:
        copy.start()
    for copy in line:
        copy.wait_recv()
    second_found = functools.reduce(jnp.add, [got_line[i] for i in range(4)])
    norms = jnp.where(top & (lane == 8), clip_norm, 0.0)
    norms = jnp.where(top & (lane == 9), factor, norms)
    for k in range(4):
        weight_norm = jnp.sqrt(scalar(4 + k))
        update_norm = jnp.sqrt(total(jnp.where(top & (lane == k), second_found, 0.0)))
        norms = jnp.where(top & (lane == k), weight_norm, norms)
        norms = jnp.where(top & (lane == 4 + k), update_norm, norms)
    norms_out[...] = norms
    for copy in plane + line:
        copy.wait_send()


def update_kernel(pieces, *refs):
    refs = list(refs)
    take = lambda n: [refs.pop(0) for _ in range(n)]
    counts, norms, vec_grad, heads_grad = take(4)
    sums = take(1 + max(p[4] for p in pieces))
    masters, firsts, seconds = take(4), take(4), take(4)
    vec, vec_first, vec_second, table, table_first, table_second = take(6)
    grads_out, firsts_out, seconds_out, news_out, copies_out = (take(4) for _ in range(5))
    vec_out, table_out = take(4), take(4)
    clip_out, norms_out = take(2)
    scale = inverse_of(counts)
    factor = norms[0:1, 9:10]
    for k, (row, rows), (column, columns), source_column, number in pieces:
        ratio = LEARN_RATE * (norms[0:1, k : k + 1] / norms[0:1, 4 + k : 5 + k])
        columns_at = pl.ds(column, columns)

        def body(i, carry):
            at = pl.multiple_of(i * 16, 16)
            here = (pl.ds(row + at, 16), columns_at)
            grad = sums[number][pl.ds(at, 16), pl.ds(source_column, columns)] * scale
            first, second, change = fresh_moments(
                grad, firsts[k][here], seconds[k][here], masters[k][here], factor
            )
            grads_out[k][here] = grad
            firsts_out[k][here] = first
            seconds_out[k][here] = second
            fresh = masters[k][here] - ratio * change
            news_out[k][here] = fresh
            copies_out[k][here] = fresh.astype(BF)
            return carry

        lax.fori_loop(0, rows // 16, body, 0)

    @pl.when(pl.program_id(0) == 0)
    def _():
        clip_out[...] = norms[0:1, 8:9]
        norms_out[0:1] = norms[0:1, 0:4]
        norms_out[1:2] = norms[0:1, 4:8]
        total = lambda value: jnp.sum(value, keepdims=True)
        grad = vec_grad[...]
        first, second, change = fresh_moments(
            grad, vec_first[...], vec_second[...], vec[...], factor
        )
        rows = lambda value: jnp.sqrt(jnp.sum(value * value, axis=1, keepdims=True))
        vec_out[0][...] = grad
        vec_out[1][...] = first
        vec_out[2][...] = second
        vec_out[3][...] = vec[...] - LEARN_RATE * (rows(vec[...]) / rows(change)) * change
        grad = heads_grad[:, : table.shape[1]]
        first, second, change = fresh_moments(
            grad, table_first[...], table_second[...], table[...], factor
        )
        table_out[0][...] = grad
        table_out[1][...] = first
        table_out[2][...] = second
        ratio = jnp.sqrt(total(table[...] * table[...])) / jnp.sqrt(total(change * change))
        table_out[3][...] = table[...] - LEARN_RATE * ratio * change


def update(collective, counts, late_sums, bias_sum, small, sums, pieces, masters, firsts, seconds, vectors, tables):
    vmem = pl.BlockSpec(memory_space=pltpu.VMEM)
    ins = [counts, late_sums, bias_sum, small] + list(sums)
    ins += list(masters) + list(firsts) + list(seconds)
    vec_grad, heads_grad, norms = pl.pallas_call(
        functools.partial(norms_kernel, pieces),
        name="norms",
        out_shape=[struct(vectors[0].shape, F32), struct((32, 384), F32), struct((8, 128), F32)],
        in_specs=[vmem] * len(ins),
        out_specs=[vmem] * 3,
        scratch_shapes=[
            pltpu.VMEM((48, 128), F32),
            pltpu.VMEM((4, 2, 2, 2, 48, 128), F32),
            pltpu.VMEM((8, 128), F32),
            pltpu.VMEM((8, 8, 128), F32),
            pltpu.VMEM((4, 8, 128), F32),
            pltpu.SemaphoreType.DMA((gather_sems(1) + 20,)),
        ],
        compiler_params=pltpu.CompilerParams(
            collective_id=collective, has_side_effects=True, vmem_limit_bytes=VMEM_LIMIT
        ),
    )(*ins)
    steps = 2
    rows = lambda array: pl.BlockSpec(
        (array.shape[0] // steps, array.shape[1]), lambda s: (s, 0)
    )
    halves = [(k, (row, n // steps), column, source, number) for k, (row, n), column, source, number in pieces]
    tables = [t.T for t in tables]
    ins = [counts, norms, vec_grad, heads_grad] + list(sums)
    ins += list(masters) + list(firsts) + list(seconds) + list(vectors) + list(tables)
    in_specs = [whole(a.shape) for a in (counts, norms, vec_grad, heads_grad)]
    in_specs += [rows(a) for a in list(sums) + list(masters) + list(firsts) + list(seconds)]
    in_specs += [whole(a.shape) for a in list(vectors) + list(tables)]
    like = lambda arrays, dtype=F32: [struct(a.shape, dtype) for a in arrays]
    outs = like(masters) * 4 + like(masters, BF)
    out_specs = [rows(a) for a in masters] * 5
    outs += like(vectors[:1]) * 4 + like(tables[:1]) * 4
    out_specs += [whole_out(vectors[0].shape)] * 4 + [whole_out(tables[0].shape)] * 4
    outs += [struct((1, 1), F32), struct((2, 4), F32)]
    out_specs += [whole_out((1, 1)), whole_out((2, 4))]
    made = pl.pallas_call(
        functools.partial(update_kernel, halves),
        name="update",
        grid=(steps,),
        out_shape=outs,
        in_specs=in_specs,
        out_specs=out_specs,
        compiler_params=pltpu.CompilerParams(vmem_limit_bytes=VMEM_LIMIT),
    )(*ins)
    matrices = [[made[4 * j + k] for j in range(5)] for k in range(4)]
    return matrices, made[20:24], [t.T for t in made[24:28]], made[28].reshape(()), made[29]


def local(
    ndp,
    nfs,
    patches,
    cotangent,
    pad_mask,
    attend_weight,
    attend_first,
    attend_second,
    output_weight,
    output_first,
    output_second,
    expand_weight,
    expand_first,
    expand_second,
    shrink_weight,
    shrink_first,
    shrink_second,
    vector_params,
    vector_first,
    vector_second,
    position_table,
    table_first,
    table_second,
):
    windows, cells, width = patches.shape
    keep = pad_mask.astype(jnp.float32)
    keep_block = jnp.pad(keep, ((0, -windows % 16), (0, -cells % 128)))
    devices = ndp * nfs
    shard_rows = min(attend_weight.shape[0], shrink_weight.shape[0])
    direct = nfs == 4 and ndp == 8 and shard_rows % 32 == 0
    masters = (attend_weight, output_weight, expand_weight, shrink_weight)
    part_rows = shrink_weight.shape[0] // 2

    tall = -(-cells // 16) * 16
    keep_rows = jnp.pad(keep, ((0, 0), (0, tall - cells)))[:, :, None]
    keep_rows = jnp.broadcast_to(keep_rows, (windows, tall, 128))
    lead = (4, 2, 2, 2, -1)
    group_columns = [[(j * width + g * 256, 256) for j in range(3)] for g in range(4)]
    half_ff = expand_weight.shape[1] // 2
    gathered, moves = [], []
    if direct:
        moves = [
            *[
                gather(attend_weight, BF, relay=False, need=4 + 4 * g, columns=columns)
                for g, columns in enumerate(group_columns)
            ],
            gather(output_weight, BF, need=20),
            gather(expand_weight, BF, need=21, columns=[(0, half_ff)]),
            gather(expand_weight, BF, need=25, columns=[(half_ff, half_ff)], late=True),
            gather(shrink_weight, BF),
            gather(keep_block, F32, 1, False),
        ]
    else:
        gathered = [
            lax.all_gather(m.astype(BF), AXES, axis=0, tiled=True).reshape(lead + m.shape[1:])
            for m in masters
        ]
        w_attend = [
            jnp.concatenate([gathered[0][..., a : a + n] for a, n in columns], axis=-1)
            for columns in group_columns
        ]
        w_expand = [gathered[2][..., :half_ff], gathered[2][..., half_ff:]]
        gathered = w_attend + gathered[1:2] + w_expand + gathered[3:]
    forward_outs, made = forward(
        patches.transpose(1, 0, 2),
        cotangent.transpose(1, 0, 2),
        keep_rows,
        vector_params,
        position_table.T,
        expand_weight.shape[1],
        () if direct else gathered[:7],
        moves,
        1,
    )
    hidden_t, source, upstream, shrink_sum, query, keys, values, probs = forward_outs[:8]
    attended, middle, hidden_two_t, activated, slope, grad_shrink = forward_outs[8:]
    if direct:
        counts, gathered = made[-1], made[:-1]
    else:
        total = lax.psum(jnp.sum(keep), AXES)
        counts = jnp.zeros((4, 2, 2, 2, 16, 128), F32).at[0, 0, 0, 0, 0, 0].set(total)
    w_attend = gathered[:4]
    w_output, w_low, w_high, w_shrink = (w.reshape(-1, w.shape[-1]) for w in gathered[4:])

    def parts(grad):
        return grad.reshape(lead + grad.shape[-1:])

    if direct:
        moves = [scatter(parts(grad_shrink)), scatter(0, (width // 32, half_ff), step=4)]
    middle_outs, middle_made = middle_part(
        activated,
        slope,
        w_shrink,
        w_low,
        w_high,
        w_output,
        upstream,
        hidden_two_t,
        middle,
        attended,
        vector_params,
        shrink_sum,
        windows,
        cells,
        moves,
        2,
    )
    block_out, grad_expand, grad_middle, grad_output, dout, small = middle_outs[:6]
    if direct:
        piece_shape = (width // 32, 3 * 256)
        moves = [
            scatter(parts(grad_expand)),
            scatter(parts(grad_output)),
            scatter(small, groups=1),
        ]
        moves += [scatter(g, piece_shape, step=4 * (g + 1)) for g in range(4)]
        moves.append(scatter(4, (128, 128), groups=1, step=16))
    backward_outs, made = backward_part(
        query,
        keys,
        values,
        dout,
        probs,
        hidden_t,
        w_attend,
        source,
        grad_middle,
        vector_params,
        counts,
        cells,
        moves,
        3,
    )
    input_grad, late_sums = backward_outs[0].transpose(1, 0, 2), backward_outs[1]
    grad_pieces, grad_bias = backward_outs[2:-1], backward_outs[-1]

    def finish_direct(block_out, input_grad, late_sums, made, middle_made, firsts, seconds):
        shrink_owned, low_owned = middle_made
        high_owned, output_owned, small_owned = made[:3]
        bias_owned = made[-1]
        sums = list(made[3:-1]) + [output_owned, low_owned, high_owned, shrink_owned]
        pieces = [
            (0, (0, attend_weight.shape[0]), (j * width + g * 256, 256), j * 256, g)
            for g in range(4)
            for j in range(3)
        ]
        rows = [(0, m.shape[0]) for m in masters]
        pieces += [
            (1, rows[1], (0, width), 0, 4),
            (2, rows[2], (0, half_ff), 0, 5),
            (2, rows[2], (half_ff, half_ff), 0, 6),
            (3, rows[3], (0, width), 0, 7),
        ]
        matrices, vector_outs, table_outs, clip_norm, matrix_norms = update(
            4,
            counts,
            late_sums,
            bias_owned,
            small_owned,
            sums,
            pieces,
            masters,
            firsts,
            seconds,
            (vector_params, vector_first, vector_second),
            (position_table, table_first, table_second),
        )
        outs = [block_out, input_grad]
        for matrix in matrices:
            outs += matrix
        return (*outs, *vector_outs, *table_outs, clip_norm, matrix_norms)

    firsts = (attend_first, output_first, expand_first, shrink_first)
    seconds = (attend_second, output_second, expand_second, shrink_second)
    if direct:
        return finish_direct(
            block_out, input_grad, late_sums, made, middle_made, firsts, seconds
        )
    grad_expand = jnp.concatenate([middle_outs[6].reshape(width, -1), grad_expand], axis=1)
    grad_attend = jnp.stack([p.reshape(width, 3, -1) for p in grad_pieces], axis=2)
    grad_attend = grad_attend.reshape(width, -1)
    owned = [
        lax.psum_scatter(g.astype(F32), AXES, scatter_dimension=0, tiled=True)
        for g in (grad_attend, grad_output, grad_expand, grad_shrink)
    ]
    index = jnp.pad(position_index(WS).T, ((0, tall - cells), (0, 128 - cells)), constant_values=-1)
    relative = jnp.arange(position_table.shape[0], dtype=jnp.int32)
    onehot = index.reshape(-1)[None, :] == relative[:, None]
    grad_table = lax.dot_general(
        onehot.astype(F32),
        grad_bias.reshape(HEADS, 128, 128)[:, :tall].astype(F32).reshape(HEADS, -1),
        (((1,), (1,)), ((), ())),
        precision=HIGH,
    )
    early_sums = small[..., :2, :].astype(F32).reshape(8, 4, 2, 128).transpose(1, 2, 0, 3).reshape(8, width)
    vector_local = jnp.concatenate([late_sums, early_sums], axis=0)
    vector_sum, table_sum = lax.psum((vector_local, grad_table), AXES)
    vector_grad, table_grad = vector_sum / total, table_sum / total
    matrix_grads = tuple((g / total for g in owned))
    grad_squares = jnp.stack([jnp.sum(g * g) for g in matrix_grads])
    weight_squares = jnp.stack([jnp.sum(m * m) for m in masters])
    grad_total, weight_total = lax.psum((grad_squares, weight_squares), AXES)
    clip_norm = jnp.sqrt(
        jnp.sum(grad_total) + jnp.sum(vector_grad * vector_grad) + jnp.sum(table_grad * table_grad)
    )
    factor = jnp.minimum(1.0, CLIP_LIMIT / clip_norm)
    sectioned = [
        moments(matrix_grads[k], firsts[k], seconds[k], masters[k], factor) for k in range(4)
    ]
    update_squares = jnp.stack([jnp.sum(s[2] * s[2]) for s in sectioned])
    update_total = lax.psum(update_squares, AXES)
    weight_norms = jnp.sqrt(weight_total)
    update_norms = jnp.sqrt(update_total)
    matrix_outs = []
    for k in range(4):
        fresh = masters[k] - LEARN_RATE * (weight_norms[k] / update_norms[k]) * sectioned[k][2]
        matrix_outs.append(
            (matrix_grads[k], sectioned[k][0], sectioned[k][1], fresh, fresh.astype(jnp.bfloat16))
        )
    vec_first, vec_second, vec_update = moments(
        vector_grad, vector_first, vector_second, vector_params, factor
    )
    vec_ratio = jnp.sqrt(jnp.sum(vector_params * vector_params, axis=1, keepdims=True)) / jnp.sqrt(
        jnp.sum(vec_update * vec_update, axis=1, keepdims=True)
    )
    vec_fresh = vector_params - LEARN_RATE * vec_ratio * vec_update
    tab_first, tab_second, tab_update = moments(
        table_grad, table_first, table_second, position_table, factor
    )
    tab_ratio = jnp.sqrt(jnp.sum(position_table * position_table)) / jnp.sqrt(
        jnp.sum(tab_update * tab_update)
    )
    tab_fresh = position_table - LEARN_RATE * tab_ratio * tab_update
    matrix_norms = jnp.stack([weight_norms, update_norms])
    attend_o, output_o, expand_o, shrink_o = matrix_outs
    return (
        block_out,
        input_grad,
        attend_o[0],
        attend_o[1],
        attend_o[2],
        attend_o[3],
        attend_o[4],
        output_o[0],
        output_o[1],
        output_o[2],
        output_o[3],
        output_o[4],
        expand_o[0],
        expand_o[1],
        expand_o[2],
        expand_o[3],
        expand_o[4],
        shrink_o[0],
        shrink_o[1],
        shrink_o[2],
        shrink_o[3],
        shrink_o[4],
        vector_grad,
        vec_first,
        vec_second,
        vec_fresh,
        table_grad,
        tab_first,
        tab_second,
        tab_fresh,
        clip_norm,
        matrix_norms,
    )


def solution(mesh):
    in_specs = (
        P(("dp", "fsdp"), None, None),
        P(("dp", "fsdp"), None, None),
        P(("dp", "fsdp"), None),
        P(("dp", "fsdp"), None),
        P(("dp", "fsdp"), None),
        P(("dp", "fsdp"), None),
        P(("dp", "fsdp"), None),
        P(("dp", "fsdp"), None),
        P(("dp", "fsdp"), None),
        P(("dp", "fsdp"), None),
        P(("dp", "fsdp"), None),
        P(("dp", "fsdp"), None),
        P(("dp", "fsdp"), None),
        P(("dp", "fsdp"), None),
        P(("dp", "fsdp"), None),
        P(),
        P(),
        P(),
        P(),
        P(),
        P(),
    )
    out_specs = (
        P(("dp", "fsdp"), None, None),
        P(("dp", "fsdp"), None, None),
        P(("dp", "fsdp"), None),
        P(("dp", "fsdp"), None),
        P(("dp", "fsdp"), None),
        P(("dp", "fsdp"), None),
        P(("dp", "fsdp"), None),
        P(("dp", "fsdp"), None),
        P(("dp", "fsdp"), None),
        P(("dp", "fsdp"), None),
        P(("dp", "fsdp"), None),
        P(("dp", "fsdp"), None),
        P(("dp", "fsdp"), None),
        P(("dp", "fsdp"), None),
        P(("dp", "fsdp"), None),
        P(("dp", "fsdp"), None),
        P(("dp", "fsdp"), None),
        P(("dp", "fsdp"), None),
        P(("dp", "fsdp"), None),
        P(("dp", "fsdp"), None),
        P(("dp", "fsdp"), None),
        P(("dp", "fsdp"), None),
        P(),
        P(),
        P(),
        P(),
        P(),
        P(),
        P(),
        P(),
        P(),
        P(),
    )
    sizes = (mesh.shape["dp"], mesh.shape["fsdp"])
    return jax.shard_map(functools.partial(local, *sizes), mesh=mesh, in_specs=in_specs, out_specs=out_specs, check_vma=False)
```

```python
import functools

import jax
import jax.numpy as jnp
from jax import lax
from jax.experimental import pallas as pl
from jax.experimental.pallas import tpu as pltpu
from jax.sharding import PartitionSpec as P

MESH = pl.DeviceIdType.MESH
AXES = ("dp", "fsdp")
VMEM_LIMIT = 61 * 1024 * 1024

HEADS = 32
WS = 10
STEP = 10


EPSILON = 1e-05
MOMENT_ONE = 0.9
MOMENT_TWO = 0.999
LEARN_RATE = 0.3
DECAY = 0.01
ADAM_EPS = 1e-06
CLIP_LIMIT = 0.05
MASK_FILL = 10000.0
HIGH = lax.Precision.HIGHEST
BF, F32 = jnp.bfloat16, jnp.float32


def position_index(size):
    cells = jnp.arange(size * size, dtype=jnp.int32)
    rows = cells // size
    cols = cells % size
    drow = rows[:, None] - rows[None, :] + size - 1
    dcol = cols[:, None] - cols[None, :] + size - 1
    return drow * (2 * size - 1) + dcol


def moments(grad, first, second, weight, factor):
    clipped = grad * factor
    first_new = MOMENT_ONE * first + (1.0 - MOMENT_ONE) * clipped
    second_new = MOMENT_TWO * second + (1.0 - MOMENT_TWO) * clipped * clipped
    update = (
        first_new
        / (1.0 - MOMENT_ONE**STEP)
        / (jnp.sqrt(second_new / (1.0 - MOMENT_TWO**STEP)) + ADAM_EPS)
        + DECAY * weight
    )
    return (first_new, second_new, update)


def whole(shape):
    zeros = (0,) * len(shape)
    return pl.BlockSpec(shape, lambda *s: zeros, pipeline_mode=pl.Buffered(1))


def whole_out(shape):
    zeros = (0,) * len(shape)
    return pl.BlockSpec(shape, lambda *s: zeros, pipeline_mode=pl.Buffered(1))


def struct(shape, dtype):
    return jax.ShapeDtypeStruct(shape, dtype)


class Place:
    def __init__(self, sems):
        dp = lax.axis_index("dp")
        fsdp = lax.axis_index("fsdp")
        self.z, self.x = dp // 2, dp % 2
        self.y, self.c = fsdp // 2, fsdp % 2
        self.mate = self.z + 1 - 2 * lax.rem(self.z, 2)
        self.far = lax.rem(self.z + 2, 4)
        self.cross = 3 - self.z
        self.inner = (self.z == 1) | (self.z == 2)
        self.pair = 2 * (self.z // 2)
        self.sems = sems
        self.used = 0

    def sem(self):
        self.used += 1
        return self.sems.at[self.used - 1]

    def to(self, z=None, x=None, y=None, c=None):
        z = self.z if z is None else z
        x = self.x if x is None else x
        y = self.y if y is None else y
        c = self.c if c is None else c
        return (z * 2 + x, y * 2 + c)

    def peers(self):
        return [
            self.to(z=self.mate),
            self.to(z=self.far),
            self.to(z=self.cross),
            self.to(x=1 - self.x),
            self.to(y=1 - self.y),
            self.to(c=1 - self.c),
        ]

    def plane(self):
        found = []
        for i in range(1, 8):
            x = self.x + (i // 4) * (1 - 2 * self.x)
            y = self.y + (i // 2 % 2) * (1 - 2 * self.y)
            c = self.c + (i % 2) * (1 - 2 * self.c)
            found.append(self.to(x=x, y=y, c=c))
        return found

    def greet(self, plane=False):
        barrier = pltpu.get_barrier_semaphore()
        peers = self.peers()[:3] + self.plane() if plane else self.peers()
        for peer in peers:
            pl.semaphore_signal(barrier, inc=1, device_id=peer, device_id_type=MESH)
        pl.semaphore_wait(barrier, len(peers))

    def send(self, source, target, device, recv_sem=None):
        return pltpu.make_async_remote_copy(
            src_ref=source,
            dst_ref=target,
            send_sem=self.sem(),
            recv_sem=self.sem() if recv_sem is None else recv_sem,
            device_id=device,
            device_id_type=MESH,
        )

    def move(self, source, target):
        return pltpu.make_async_copy(source, target, self.sem())


def gather_sems(groups):
    return 20 + 2 * 5 * groups


def gather_events(place, own, out, groups, relay):
    z, x, y, c = place.z, place.x, place.y, place.c
    half = own.shape[0] // 2
    ox, oy, oc = 1 - x, 1 - y, 1 - c
    xp, yp, cp = place.to(x=ox), place.to(y=oy), place.to(c=oc)
    mate, cross = place.to(z=place.mate), place.to(z=place.cross)
    first = jnp.where(place.inner, place.cross, place.far)
    second = jnp.where(place.inner, place.far, place.cross)
    low, high = pl.ds(0, half), pl.ds(half, half)
    slot = lambda at: out.at[at, x, y, c]
    mine = place.move(own, slot(z))
    to_mate = place.send(own, slot(z), mate)
    if relay:
        came_one, came_two = place.sem(), place.sem()
        across_one = place.send(own, slot(z), cross, came_one)
        across_two = place.send(slot(place.mate), slot(place.mate), cross, came_two)
        on_one = place.send(slot(first), slot(first), mate, came_one)
        on_two = place.send(slot(second), slot(second), mate, came_two)
    else:
        to_far = place.send(own, slot(z), place.to(z=place.far))
        to_cross = place.send(own, slot(z), cross)
    if groups == 1:
        spans = [pl.ds(0, 4)]
    elif groups == 2:
        spans = [pl.ds(place.pair, 2), pl.ds(2 - place.pair, 2)]
    elif relay:
        spans = [pl.ds(at, 1) for at in (z, place.mate, first, second)]
    else:
        spans = [pl.ds(at, 1) for at in (z, place.mate, place.far, place.cross)]

    def forward(ref, device):
        return place.send(ref, ref, device)

    x_full = [forward(out.at[s, x, y, c], xp) for s in spans]
    y_full = [forward(out.at[s, x, y, c], yp) for s in spans]
    x_half = [forward(out.at[s, ox, y, c, low], yp) for s in spans]
    y_half = [forward(out.at[s, x, oy, c, high], xp) for s in spans]
    to_twin = [forward(out.at[s, :, :, c], cp) for s in spans]

    def begin():
        mine.start()
        to_mate.start()
        if relay:

            @pl.when(place.inner)
            def _():
                across_one.start()

        else:
            to_far.start()
            to_cross.start()
        mine.wait()
        if groups == 4:
            send_line(0)

    def send_line(g):
        x_full[g].start()
        y_full[g].start()

    def on_line():
        for copy in (to_mate, to_far, to_cross):
            copy.wait_recv()
        send_line(0)

    def on_place(g):
        (None, to_mate, to_far, to_cross)[g].wait_recv()
        send_line(g)

    def on_mate():
        to_mate.wait_recv()

        @pl.when(place.inner)
        def _():
            across_two.start()

        if groups == 2:
            send_line(0)
        if groups == 4:
            send_line(1)

    def relay_one():
        @pl.when(place.inner)
        def _():
            across_one.wait_recv()
            on_one.start()

    def on_first():
        @pl.when(jnp.logical_not(place.inner))
        def _():
            on_one.wait_recv()

        if groups == 4:
            send_line(2)

    def relay_two():
        @pl.when(place.inner)
        def _():
            across_two.wait_recv()
            on_two.start()

    def on_second():
        @pl.when(jnp.logical_not(place.inner))
        def _():
            on_two.wait_recv()

        send_line(groups - 1)

    def on_side(g):
        x_full[g].wait_recv()
        x_half[g].start()
        y_full[g].wait_recv()
        y_half[g].start()

    def on_corner(g):
        x_half[g].wait_recv()
        y_half[g].wait_recv()
        to_twin[g].start()

    def arrive():
        for copy in to_twin:
            copy.wait_recv()

    def finish():
        for copies in (to_twin, x_full, y_full, x_half, y_half, [to_mate]):
            for copy in copies:
                copy.wait_send()
        if relay:

            @pl.when(place.inner)
            def _():
                for copy in (across_one, across_two, on_one, on_two):
                    copy.wait_send()

        else:
            to_far.wait_send()
            to_cross.wait_send()

    size = 4 // groups
    lines = lambda g: [("x", size, ("xf", g)), ("y", size, ("yf", g))]
    if relay:
        one = {1: [], 2: [], 4: lines(0)}[groups]
        events = [
            (begin, [], [("z", 1, "mate"), ("w", 1, "a1")] + one),
            (on_mate, ["mate"], [("w", 1, "a2")] + {1: [], 2: lines(0), 4: lines(1 % groups)}[groups]),
            (relay_one, ["a1"], [("z", 1, "o1")]),
            (on_first, ["o1"], lines(2) if groups == 4 else []),
            (relay_two, ["a2"], [("z", 1, "o2")]),
            (on_second, ["o2"], lines(groups - 1)),
        ]
    elif groups == 4:
        events = [(begin, [], [("z", 1.33, ("z", g)) for g in (1, 2, 3)] + lines(0))]
        for g in (1, 2, 3):
            events.append((functools.partial(on_place, g), [("z", g)], lines(g)))
    else:
        events = [(begin, [], [("z", 4, "z")]), (on_line, ["z"], lines(0))]
    for g in range(groups):
        half_size = 0.5 * size
        halves = [("y", half_size, ("xh", g)), ("x", half_size, ("yh", g))]
        events.append((functools.partial(on_side, g), [("xf", g), ("yf", g)], halves))
    for g in range(groups):
        twins = [("c", size * 4, ("t", g))]
        events.append((functools.partial(on_corner, g), [("xh", g), ("yh", g)], twins))
    events.append((arrive, [("t", g) for g in range(groups)], []))
    return events, finish


def gather_late_events(place, own, out):
    z, x, y, c = place.z, place.x, place.y, place.c
    half = own.shape[0] // 2
    ox, oy, oc = 1 - x, 1 - y, 1 - c
    xp, yp, cp = place.to(x=ox), place.to(y=oy), place.to(c=oc)
    mate, cross = place.to(z=place.mate), place.to(z=place.cross)
    first = jnp.where(place.inner, place.cross, place.far)
    second = jnp.where(place.inner, place.far, place.cross)
    low, high = pl.ds(0, half), pl.ds(half, half)
    quads = [(x, y), (ox, y), (x, oy), (ox, oy)]
    slot = lambda at, q: out.at[at, quads[q][0], quads[q][1], c]

    def forward(ref, device, recv_sem=None):
        return place.send(ref, ref, device, recv_sem)

    mine = place.move(own, slot(z, 0))
    x_full = place.send(own, slot(z, 0), xp)
    y_full = place.send(own, slot(z, 0), yp)
    x_half = forward(slot(z, 1).at[low], yp)
    y_half = forward(slot(z, 2).at[high], xp)
    to_mate = [forward(slot(z, q), mate) for q in range(4)]
    came_one = [place.sem() for _ in range(4)]
    came_two = [place.sem() for _ in range(4)]
    across_one = [forward(slot(z, q), cross, came_one[q]) for q in range(4)]
    across_two = [forward(slot(place.mate, q), cross, came_two[q]) for q in range(4)]
    on_one = [forward(slot(first, q), mate, came_one[q]) for q in range(4)]
    on_two = [forward(slot(second, q), mate, came_two[q]) for q in range(4)]
    to_twin = [
        forward(out.at[pl.ds(at, 1), :, :, c], cp) for at in (z, place.mate, first, second)
    ]

    def inside(body):
        pl.when(place.inner)(body)

    def outside(body):
        pl.when(jnp.logical_not(place.inner))(body)

    def line(q):
        to_mate[q].start()
        inside(across_one[q].start)

    def begin():
        mine.start()
        x_full.start()
        y_full.start()
        mine.wait()
        line(0)

    def on_x():
        x_full.wait_recv()
        x_half.start()
        line(1)

    def on_y():
        y_full.wait_recv()
        y_half.start()
        line(2)

    def on_corner():
        x_half.wait_recv()
        y_half.wait_recv()
        line(3)
        to_twin[0].start()

    def on_mate(q):
        to_mate[q].wait_recv()
        inside(across_two[q].start)

    def relay_one(q):
        def body():
            across_one[q].wait_recv()
            on_one[q].start()

        inside(body)

    def relay_two(q):
        def body():
            across_two[q].wait_recv()
            on_two[q].start()

        inside(body)

    def on_first(q):
        outside(on_one[q].wait_recv)

    def on_second(q):
        outside(on_two[q].wait_recv)

    def twin(i):
        to_twin[i].start()

    def arrive():
        for copy in to_twin:
            copy.wait_recv()

    def finish():
        for copy in [x_full, y_full, x_half, y_half] + to_mate + to_twin:
            copy.wait_send()

        def body():
            for copy in across_one + across_two + on_one + on_two:
                copy.wait_send()

        inside(body)

    part = functools.partial
    sent = lambda q: [("z", 1, ("mate", q)), ("w", 1, ("a1", q))]
    events = [
        (begin, [], [("x", 1, "xf"), ("y", 1, "yf")] + sent(0)),
        (on_x, ["xf"], [("y", 0.5, "xh")] + sent(1)),
        (on_y, ["yf"], [("x", 0.5, "yh")] + sent(2)),
        (on_corner, ["xh", "yh"], sent(3) + [("c", 4, ("t", 0))]),
    ]
    for q in range(4):
        events.append((part(on_mate, q), [("mate", q)], [("w", 1, ("a2", q)), ("n", 0, ("m", q))]))
        events.append((part(relay_one, q), [("a1", q)], [("z", 1, ("o1", q))]))
        events.append((part(on_first, q), [("o1", q)], [("n", 0, ("f", q))]))
        events.append((part(relay_two, q), [("a2", q)], [("z", 1, ("o2", q))]))
        events.append((part(on_second, q), [("o2", q)], [("n", 0, ("s", q))]))
    for i, name in ((1, "m"), (2, "f"), (3, "s")):
        events.append((part(twin, i), [(name, q) for q in range(4)], [("c", 4, ("t", i))]))
    events.append((arrive, [("t", i) for i in range(4)], []))
    return events, finish


def scatter_sems(groups):
    return groups * (1 + 2 * 5) + 2 * 3


def scatter_scratch(rows, columns):
    shape = lambda *lead: pltpu.VMEM(lead + (columns,), jnp.bfloat16)
    return [
        shape(4, 2, 2, rows),
        shape(4, 2, 2, rows),
        shape(4, rows // 2),
        shape(4, rows // 2),
        shape(4, rows),
        shape(4, rows),
        shape(3, rows),
    ]


def scatter_events(place, grads, part, total, scratch, groups):
    z, x, y, c = place.z, place.x, place.y, place.c
    held, twin, corner_low, corner_high, from_x, from_y, from_z = scratch
    rows, columns = total.shape
    half = rows // 2
    part = pl.ds(*part)
    ox, oy, oc = 1 - x, 1 - y, 1 - c
    xp, yp, cp = place.to(x=ox), place.to(y=oy), place.to(c=oc)
    if groups == 1:
        spans, lines = [(0, 4)], [[0, 1, 2, None]]
    elif groups == 2:
        spans = [(2 - place.pair, 2), (place.pair, 2)]
        lines = [[0, 1], [2, None]]
    else:
        spans = [(place.far, 1), (place.cross, 1), (place.mate, 1), (z, 1)]
        lines = [[0], [1], [2], [None]]
    ds = [pl.ds(*span) for span in spans]
    low, high = pl.ds(0, half), pl.ds(half, half)
    loads = [place.move(grads.at[d, :, :, c, part], held.at[d]) for d in ds]
    twins = [place.send(grads.at[d, :, :, oc, part], twin.at[d], cp) for d in ds]
    out_low = [place.send(held.at[d, ox, oy, low], corner_low.at[d], xp) for d in ds]
    out_high = [place.send(held.at[d, ox, oy, high], corner_high.at[d], yp) for d in ds]
    out_x = [place.send(held.at[d, ox, y], from_x.at[d], xp) for d in ds]
    out_y = [place.send(held.at[d, x, oy], from_y.at[d], yp) for d in ds]
    line = [place.far, place.cross, place.mate]
    out_z = [place.send(held.at[at, x, y], from_z.at[i], place.to(z=at)) for i, at in enumerate(line)]

    def summed(store, first, count, parts):
        def step(i, carry):
            at = pl.ds(pl.multiple_of(first + i * 16, 16), 16)
            store(at, functools.reduce(jnp.add, [part(at).astype(jnp.float32) for part in parts]))
            return carry

        lax.fori_loop(0, count // 16, step, 0)

    def read(ref, *index, lo=0):
        if lo:
            return lambda at: ref[index + (pl.ds(at.start - lo, 16),)]
        return lambda at: ref[index + (at,)]

    def write(ref, *index):
        def store(at, value):
            ref[index + (at,)] = value.astype(ref.dtype)

        return store

    def each(g, body):
        start, size = spans[g]

        def step(i, carry):
            body(start + i)
            return carry

        lax.fori_loop(0, size, step, 0)

    def begin():
        for g in range(len(spans)):
            twins[g].start()
            loads[g].start()

    def on_corner(g):
        loads[g].wait()
        twins[g].wait_recv()

        def body(at):
            here = (at, ox, oy)
            summed(write(held, *here), 0, rows, [read(held, *here), read(twin, *here)])

        each(g, body)
        out_low[g].start()
        out_high[g].start()

    def on_side(g):
        out_high[g].wait_recv()

        def body(at):
            here = (at, ox, y)
            own = [read(held, *here), read(twin, *here)]
            summed(write(held, *here), 0, half, own)
            summed(write(held, *here), half, half, own + [read(corner_high, at, lo=half)])

        each(g, body)
        out_x[g].start()
        out_low[g].wait_recv()

        def body(at):
            here = (at, x, oy)
            own = [read(held, *here), read(twin, *here)]
            summed(write(held, *here), half, half, own)
            summed(write(held, *here), 0, half, own + [read(corner_low, at)])

        each(g, body)
        out_y[g].start()

    def on_line(g):
        out_x[g].wait_recv()
        out_y[g].wait_recv()
        for i in lines[g]:
            at = z if i is None else line[i]
            here = (at, x, y)
            parts = [read(held, *here), read(twin, *here), read(from_x, at), read(from_y, at)]
            if i is None:
                for copy in out_z:
                    copy.wait_recv()
                parts += [read(from_z, j) for j in range(3)]
                summed(write(total), 0, rows, parts)
            else:
                summed(write(held, *here), 0, rows, parts)
                out_z[i].start()

    def finish():
        for copies in (twins, out_low, out_high, out_x, out_y, out_z):
            for copy in copies:
                copy.wait_send()

    size = 4 // groups
    events = [(begin, [], [("c", 4 * size, ("t", g)) for g in range(groups)])]
    for g in range(groups):
        halves = [("x", 0.5 * size, ("l", g)), ("y", 0.5 * size, ("h", g))]
        events.append((functools.partial(on_corner, g), [("t", g)], halves))
    for g in range(groups):
        fulls = [("x", size, ("x", g)), ("y", size, ("y", g))]
        events.append((functools.partial(on_side, g), [("l", g), ("h", g)], fulls))
    for g in range(groups):
        sent = [("z", 1.33, ("z", i)) for i in lines[g] if i is not None]
        waits = [("x", g), ("y", g)]
        if groups > 1 and g == groups - 1:
            waits += [("z", i) for i in range(2)]
        events.append((functools.partial(on_line, g), waits, sent))
    if groups == 4:
        events[-1][1].append(("z", 2))
    return events, finish


HOP = 2.5
LINK = 90e3
CORE = 500e3
SLACK = 1.2
BACKLOGS = [(a, b) for a in (0.0, 1.0, 2.0, 4.0) for b in (0.5, 2.0, 4.0, 8.0, 16.0)]


def plan_of(lists, starts):
    return min((simulate(lists, starts, limits) for limits in BACKLOGS), key=lambda plan: plan[0])[1:]


def simulate(lists, starts, limits):
    free = {"x": 0.0, "y": 0.0, "z": 0.0, "w": 0.0, "c": 0.0}
    arrival, pending = {}, []
    for number, ((events, finish), move) in enumerate(lists):
        for order, (event, waits, sends) in enumerate(events):
            pending.append((number, order, event, [(number, w) for w in waits], sends, move))

    def ready(item):
        number, order, _, waits, _, move = item
        if any(w not in arrival for w in waits):
            return None
        if order:
            if any(p[0] == number and p[1] == 0 for p in pending):
                return None
        return max([arrival[w] for w in waits], default=0.0)

    def run(item, now):
        number, _, event, _, sends, move = item
        pending.remove(item)
        for link, units, name in sends:
            if link == "n":
                arrival[number, name] = now
                continue
            rate = CORE if link == "c" else LINK
            cores = 1 if link == "c" else 2
            took = units * cores * move["bytes"] / rate
            free[link] = max(free[link], now) + took
            arrival[number, name] = free[link] + HOP
        return event

    before, now = {}, 3.0
    places = [(i, j, took) for i, parts in enumerate(starts) for j, took in enumerate(parts)]
    for step, part, took in places + [(len(starts), 0, 0.0)]:
        last = step == len(starts)
        while True:
            found, forced_found = None, None
            top = min([p[0] for p in pending if p[5]["step"] <= step], default=0)
            pressed = any(p[5]["need"] is not None and p[5]["need"] <= step for p in pending)
            for item in pending:
                number, order, _, _, sends, move = item
                if move["step"] > step:
                    continue
                at = ready(item)
                if at is None:
                    continue
                if last or (move["need"] is not None and move["need"] <= step):
                    if forced_found is None or at < forced_found[0]:
                        forced_found = (at, item)
                elif number > top:
                    backlog = max((free[k] - now for k, _, _ in sends if k in "xyzw"), default=0.0)
                    if backlog > limits[0 if pressed else 1]:
                        continue
                if at <= now and (found is None or number < found[1][0]):
                    found = (at, item)
            if found is None:
                found = forced_found
            if found is None:
                break
            now = max(now, found[0])
            before.setdefault((step, part), []).append(run(found[1], now))
        now += SLACK * took
    after = before.pop((len(starts), 0), [])
    assert not pending
    return now, before, after + [finish for (_, finish), _ in lists]


def gather(array, dtype, groups=4, relay=True, need=None, step=0, columns=None, late=False):
    columns = ((0, array.shape[1]),) if columns is None else columns
    shape = (array.shape[0], sum(n for _, n in columns))
    return dict(
        kind="gather",
        array=array,
        dtype=dtype,
        groups=groups,
        relay=relay,
        late=late,
        bytes=shape[0] * shape[1] * jnp.dtype(dtype).itemsize,
        need=need,
        step=step,
        columns=columns,
        shape=shape,
    )


def scatter(array, shape=None, groups=4, step=0):
    shape = array.shape[4:] if shape is None else shape
    size = 2 * shape[0] * shape[1]
    return dict(kind="scatter", array=array, shape=shape, groups=groups, bytes=size, need=None, step=step)


def fused_kernel(body, counts, moves, starts, *refs):
    n_in, n_out, n_scratch = counts
    numbers = []
    for move in moves:
        if isinstance(move["array"], int):
            numbers.append(None)
        else:
            same = [i for i, m in enumerate(moves) if m["array"] is move["array"]][0]
            known = numbers[same] if same < len(numbers) else None
            numbers.append(max([n for n in numbers if n is not None], default=-1) + 1 if known is None else known)
    n_given = max([n for n in numbers if n is not None], default=-1) + 1
    ins, given = refs[:n_in], list(refs[n_in : n_in + n_given])
    refs = refs[n_in + n_given :]
    outs, made = refs[:n_out], refs[n_out : n_out + len(moves)]
    refs = refs[n_out + len(moves) :]
    scratch, spare = refs[:n_scratch], list(refs[n_scratch:-1])
    step = pl.program_id(0)
    place = Place(refs[-1])
    lists, lows = [], []
    for move, target, number in zip(moves, made, numbers):
        source = scratch[move["array"]] if number is None else given[number]
        if move["kind"] == "gather":
            low = spare.pop(0)
            lows.append((source, low, move["columns"]))
            if move["late"]:
                events = gather_late_events(place, low, target)
            else:
                events = gather_events(place, low, target, move["groups"], move["relay"])
        else:
            buffers = [spare.pop(0) for _ in range(7)]
            rows = (0, move["shape"][0])
            events = scatter_events(place, source, rows, target, buffers, move["groups"])
        lists.append((events, move))
    before, after = plan_of(lists, starts)

    @pl.when(step == 0)
    def _():
        for source, low, columns in lows:
            put = 0
            for first, size in columns:
                low[:, put : put + size] = source[:, first : first + size].astype(low.dtype)
                put += size
        place.greet()

    def hook(part):
        steps = sorted(at for at, number in before if number == part)

        def one(at):
            @pl.when(step == at)
            def _():
                for event in before[at, part]:
                    event()

        def among(steps):
            if len(steps) == 1:
                one(steps[0])
            elif steps:
                middle = len(steps) // 2
                lax.cond(
                    step < steps[middle],
                    lambda: among(steps[:middle]),
                    lambda: among(steps[middle:]),
                )

        among(steps)

    hook(0)
    body(made, hook, *ins, *outs, *scratch)

    @pl.when(step == len(starts) - 1)
    def _():
        for event in after:
            event()


def call(body, name, steps, ins, in_specs, outs, out_specs, scratch=(), moves=(), collective=None, starts=()):
    scratch = list(scratch)
    params = dict(vmem_limit_bytes=VMEM_LIMIT)
    counts = (len(ins), len(outs), len(scratch))
    kernel = functools.partial(body, (), lambda part: None)
    if moves:
        params.update(collective_id=collective, has_side_effects=True)
        kernel = functools.partial(fused_kernel, body, counts, moves, starts)
        assert len(starts) == steps
    ins, in_specs, outs, out_specs = list(ins), list(in_specs), list(outs), list(out_specs)
    sems = 0
    for move in moves:
        array = move["array"]
        if move["kind"] == "gather":
            if not any(array is other for other in ins[counts[0] :]):
                ins.append(array)
                in_specs.append(whole(array.shape))
            outs.append(struct((4, 2, 2, 2) + move["shape"], move["dtype"]))
            out_specs.append(pl.BlockSpec(memory_space=pl.ANY))
            scratch.append(pltpu.VMEM(move["shape"], move["dtype"]))
            sems += gather_sems(move["groups"])
        else:
            if not isinstance(array, int):
                ins.append(array)
                in_specs.append(pl.BlockSpec(memory_space=pl.ANY))
            outs.append(struct(move["shape"], F32))
            out_specs.append(whole_out(move["shape"]))
            scratch += scatter_scratch(*move["shape"])
            sems += scatter_sems(move["groups"])
    if moves:
        scratch.append(pltpu.SemaphoreType.DMA((sems,)))
    made = pl.pallas_call(
        kernel,
        name=name,
        grid=(steps,),
        out_shape=outs,
        in_specs=in_specs,
        out_specs=out_specs,
        scratch_shapes=scratch,
        compiler_params=pltpu.CompilerParams(**params),
    )(*ins)
    return made[: counts[1]], made[counts[1] :]


def times(left, right):
    return jnp.dot(left, right, preferred_element_type=jnp.float32)


def times_transpose(left, right):
    return lax.dot_general(
        left, right, (((1,), (1,)), ((), ())), preferred_element_type=jnp.float32
    )


def transpose_times(left, right):
    return lax.dot_general(
        left, right, (((0,), (0,)), ((), ())), preferred_element_type=jnp.float32
    )


def normalize(value):
    centre = value - jnp.mean(value, axis=-1, keepdims=True)
    rstd = lax.rsqrt(jnp.mean(centre * centre, axis=-1, keepdims=True) + EPSILON)
    return centre * rstd, rstd


def norm_back(grad_out, normed, rstd, gain):
    scaled = grad_out * gain
    mean_one = jnp.mean(scaled, axis=-1, keepdims=True)
    mean_two = jnp.mean(scaled * normed, axis=-1, keepdims=True)
    return rstd * (scaled - mean_one - normed * mean_two)


def eight(value):
    rows, columns = value.shape
    return jnp.sum(value.reshape(rows // 8, 8, columns), axis=0)


def gelu_parts(value):
    bell = jnp.exp(-0.5 * value * value)
    size = jnp.abs(value)
    t = 1.0 / (1.0 + 0.23164189 * size)
    tail = t * (
        0.127414796
        + t * (-0.142248368 + t * (0.7107068705 + t * (-0.7265760135 + t * 0.5307027145)))
    )
    tail = tail * bell
    phi_big = jnp.where(value >= 0.0, 1.0 - tail, tail)
    return phi_big, bell * 0.3989422804014327


STRIP = 32


def strips(rows, body, carry, unroll=2, hooks=()):
    def step(i, value):
        return body(pl.ds(pl.multiple_of(i * STRIP, STRIP), STRIP), value)

    count, parts = rows // STRIP, max(len(hooks), 1)
    for part in range(parts):
        if hooks:
            hooks[part]()
        first, last = part * count // parts, (part + 1) * count // parts
        carry = lax.fori_loop(first, last, step, carry, unroll=unroll)
    return carry


def enter_step(step, patches, cotangent, keep, vec, hidden, source, upstream, bias_sum, spare, wide):
    cells, windows, width = patches.shape
    high = spare.shape[0] // 2
    gain, shift = vec[0:1], vec[1:2]

    @pl.when(step == 0)
    def _():
        spare[...] = jnp.zeros_like(spare)
        wide[...] = patches[...].astype(F32)

    @pl.when(step == 2)
    def _():
        bias_sum[...] = jnp.zeros_like(bias_sum)
        wide[...] = cotangent[...].astype(F32)

    for pair in range(windows // 2):
        at = pl.ds(pair * 2 * high, 2 * high)
        half = windows // 4

        @pl.when(step == pair // half)
        def _(pair=pair, at=at):
            for w in range(2):
                spare[pl.ds(w * high, cells)] = wide[:, 2 * pair + w, :]
            source[at] = spare[...].astype(BF)
            for w in range(2):
                normed, _ = normalize(spare[pl.ds(w * high, cells)])
                spare[pl.ds(w * high, cells)] = normed * gain + shift
            hidden[at] = spare[...].astype(BF)

        @pl.when(step == 2 + pair // half)
        def _(pair=pair, at=at):
            for w in range(2):
                mask = jnp.concatenate([keep[2 * pair + w]] * (width // 128), axis=1)
                spare[pl.ds(w * high, cells)] = wide[:, 2 * pair + w, :] * mask[:cells]
            bias_sum[...] += eight(spare[...])
            upstream[at] = spare[...].astype(BF)


def bias_step(step, table, bias, padded, stack):
    heads, high, _ = bias.shape
    cells = WS * WS
    side = 2 * WS - 1
    middle = (WS - 1) * side + WS - 1
    spot = lax.broadcasted_iota(jnp.int32, (256, 128), 0)
    cell = lax.broadcasted_iota(jnp.int32, (256, 128), 1)
    put = ((cell // WS) * side + lax.rem(cell, WS) == spot) & (cell < cells)

    @pl.when(step == 0)
    def _():
        padded[...] = jnp.zeros_like(padded)
        padded[:, : table.shape[1]] = table[...]
        bias[:, pl.ds(cells, high - cells)] = jnp.zeros((heads, high - cells, 128), F32)

    count = cells // 4
    for part in range(4):

        @pl.when(step == part)
        def _(part=part):
            for n in range(count):
                j = part * count + n
                shift = middle - (j // WS) * side - j % WS
                rolled = pltpu.roll(padded[...], (384 - shift) % 384, axis=1)
                stack[pl.ds(heads * n, heads)] = rolled[:, :256]
            found = jnp.dot(stack[...], put.astype(F32), precision=HIGH, preferred_element_type=F32)
            for n in range(count):
                bias[:, part * count + n, :] = found[heads * n : heads * n + heads]


def lanes_of(head):
    lane = lax.broadcasted_iota(jnp.int32, (1, 128), 1)
    return (lane // 32) == head


def pick(value, head):
    return jnp.where(lanes_of(head), value, jnp.zeros_like(value))


def spread_heads(value):
    head = lax.broadcasted_iota(jnp.int32, value.shape, 0) // 32
    return jnp.concatenate([jnp.where(head == h, value, jnp.zeros_like(value)) for h in range(4)], axis=1)


def own_heads(value):
    return jnp.concatenate(
        [value[32 * h : 32 * h + 32, 128 * h : 128 * h + 128] for h in range(4)], axis=0
    )


def stack_heads(value):
    return jnp.concatenate([pick(value, h) for h in range(4)], axis=0)


def with_rows(value, rows):
    return jnp.concatenate([value, jnp.zeros((rows - value.shape[0], value.shape[1]), F32)], axis=0)


def attend_step(hook, group, pair, hidden, weights, vec, bias, mask, query, keys, values, probs, out):
    windows, _, columns = query.shape
    high = hidden.shape[0] // windows

    @pl.when(pair == 0)
    def _():
        at = pl.ds(pl.multiple_of(group * columns, columns), columns)
        for j, (target, bias_row) in enumerate(((query, 2), (keys, None), (values, 3))):
            product = times(hidden[...], weights(j))
            if bias_row is not None:
                product = product + vec[bias_row : bias_row + 1, at]
            for w in range(windows):
                here = with_rows(product[w * high : (w + 1) * high], target.shape[1])
                target[w] = here.astype(BF)

        hook(1)

    scale = 32 ** (-0.5)
    done = []
    for w in range(2):
        window = pair * 2 + w
        parts = []
        for g in range(columns // 128):
            at = pl.ds(g * 128, 128)
            q, k, v = query[window, :, at], keys[window, :, at], values[window, :, at]
            scores = times(k, spread_heads(q.T))
            found = []
            for h in range(4):
                head = group * (columns // 32) + g * 4 + h
                score = scores[:, 128 * h : 128 * h + 128] * scale + bias[head] + mask[window]
                score = jnp.exp(score - jnp.max(score, axis=0, keepdims=True))
                prob = (score * (1.0 / jnp.sum(score, axis=0, keepdims=True))).astype(BF)
                probs[w, g * 4 + h] = prob
                found.append(prob)
            mixed = times(v.T, jnp.concatenate(found, axis=1))
            parts.append(own_heads(mixed).T[:high])
        done.append(jnp.concatenate(parts, axis=1))
    rows = pl.ds(pl.multiple_of(pair * 2 * high, 16), 2 * high)
    at = pl.ds(pl.multiple_of(group * columns, columns), columns)
    out[rows, at] = jnp.concatenate(done, axis=0).astype(BF)


def flat(value):
    return value.reshape(-1, value.shape[-1])


def forward_body(direct, made, hook, *refs):
    refs = list(refs)
    take = lambda n: [refs.pop(0) for _ in range(n)]
    patches, cotangent, keep, vec, table = take(5)
    *w_attend, w_output, w_low, w_high = made[:7] if direct else take(7)
    *kept, bias_sum, query, keys, values, probs = take(8)
    kept += take(3)
    act, slope, grad = take(3)
    held = take(6)
    hidden_t, source, upstream, attended, middle, hidden_two_t = held
    spare, hidden, wqkv, wo, we, hidden_two, before, wide, bias, mask, padded, stack, sems = refs
    step = pl.program_id(0)
    rows, width = hidden.shape
    windows, _, columns = query.shape
    pairs, groups = windows // 2, width // columns
    enters, attends = pairs, pairs * groups
    chunk = act.shape[1]
    per_half = w_low.shape[-1] // chunk
    chunks = 2 * per_half

    @pl.when(step < enters)
    def _():
        enter_step(step, patches, cotangent, keep, vec, hidden, source, upstream, bias_sum, spare, wide)
        bias_step(step, table, bias, padded, stack)

    @pl.when(step == 0)
    def _():
        there = lax.broadcasted_iota(jnp.int32, mask.shape, 1) < patches.shape[0]
        mask[...] = jnp.where(there, (keep[...] - 1.0) * MASK_FILL, -1e30)

    inner_step = step - enters
    group, pair = inner_step // pairs, lax.rem(inner_step, pairs)

    def load_qkv(number):
        slot = number % 2
        return pltpu.make_async_copy(w_attend[number], wqkv.at[slot], sems.at[slot])

    load_wo = pltpu.make_async_copy(w_output, wo, sems.at[2])

    def load_we(half, index):
        slot = lax.rem(index, 2)
        at = pl.ds(pl.multiple_of(lax.rem(index, per_half) * chunk, chunk), chunk)
        source = (w_low, w_high)[half]
        return pltpu.make_async_copy(source.at[:, :, :, :, :, at], we.at[slot], sems.at[3 + slot])

    @pl.when((inner_step >= 0) & (inner_step < attends))
    def _():
        @pl.when(inner_step == 0)
        def _():
            hidden_t[...] = hidden[...].T

        for number in range(groups):

            @pl.when(inner_step == number * pairs)
            def _(number=number):
                copy = load_qkv(number)
                copy.start()
                copy.wait()

        slot = lax.rem(group, 2)
        weights = lambda j: flat(wqkv[slot, :, :, :, :, :, pl.ds(j * columns, columns)])
        attend_step(hook, group, pair, hidden, weights, vec, bias, mask, query, keys, values, probs, attended)

    @pl.when(inner_step == attends)
    def _():
        load_wo.start()
        load_wo.wait()
        for j in range(2):
            at = pl.ds(j * (width // 2), width // 2)
            middle[:, at] = times(attended[...], flat(wo[:, :, :, :, :, at])) + vec[4:5, at]

        hook(1)

        def strip(at, carry):
            value = middle[at] + source[at].astype(F32)
            middle[at] = value
            normed, _ = normalize(value)
            hidden_two[at] = (normed * vec[5:6] + vec[6:7]).astype(BF)
            return carry

        strips(rows, strip, 0)
        hidden_two_t[...] = hidden_two[...].T

    write = [
        pltpu.make_async_copy(value, out, sems.at[5 + i])
        for i, (value, out) in enumerate(zip(held, kept))
    ]

    @pl.when(inner_step == attends + 1)
    def _():
        for copy in write:
            copy.start()

    @pl.when(inner_step == attends + chunks)
    def _():
        for copy in write:
            copy.wait()

    @pl.when(inner_step > attends)
    def _():
        index = inner_step - attends - 1
        for half in range(2):

            @pl.when(index == half * per_half)
            def _(half=half):
                load_we(half, index).start()

            @pl.when(index // per_half == half)
            def _(half=half):
                load_we(half, index).wait()

                @pl.when(lax.rem(index, per_half) < per_half - 1)
                def _():
                    load_we(half, index + 1).start()

        before[...] = times(hidden_two[...], flat(we[lax.rem(index, 2)]))
        per = width // chunk
        shift_at = pl.ds(pl.multiple_of(lax.rem(index, per) * chunk, chunk), chunk)
        shift = vec[pl.ds(8 + index // per, 1), shift_at]
        hook(1)

        def strip(at, carry):
            value = before[at] + shift
            big, small = gelu_parts(value)
            act[at] = (value * big).astype(BF)
            slope[at] = (big + value * small).astype(BF)
            return carry

        strips(rows, strip, 0)
        hook(2)
        grad[...] = transpose_times(act[...], upstream[...]).astype(BF)


def forward(patches, cotangent, keep, vec, table, ff, gathered, moves, collective):
    cells, windows, width = patches.shape
    high, tall, wide_rows = -(-cells // 8) * 8, keep.shape[1], -(-cells // 128) * 128
    rows = windows * high
    heads = table.shape[0]
    columns, chunk = 256, 512
    groups, pairs = width // columns, windows // 2
    per = columns // 32
    direct = bool(moves)
    enters, attends = pairs, pairs * groups
    steps = enters + attends + 1 + ff // chunk
    group = lambda s: jnp.clip((s - enters) // pairs, 0, groups - 1)
    pair = lambda s: jnp.where(
        s < enters, 0, jnp.where(s < enters + attends, lax.rem(s - enters, pairs), pairs - 1)
    )
    later = lambda s: jnp.maximum(s - enters - attends - 1, 0)
    seen = lambda n: pl.BlockSpec((windows, n, columns), lambda s: (0, 0, group(s)))
    wide = pl.BlockSpec((rows, chunk), lambda s: (0, later(s)))
    any_place = pl.BlockSpec(memory_space=pl.ANY)
    starts = [[2.5]] * enters + [[1.7, 1.1], [1.1], [1.1], [1.1]] * groups
    starts += [[1.7, 2.5]] + [[1.2, 1.7, 1.25]] * (ff // chunk)
    lead = (4, 2, 2, 2, width // 32)
    return call(
        functools.partial(forward_body, direct),
        "forward",
        steps=steps,
        ins=[patches, cotangent, keep, vec, table] + list(gathered),
        in_specs=[
            whole(patches.shape),
            whole(cotangent.shape),
            whole(keep.shape),
            whole(vec.shape),
            whole(table.shape),
        ]
        + [any_place] * len(gathered),
        outs=[
            struct((width, rows), BF),
            struct((rows, width), BF),
            struct((rows, width), BF),
            struct((8, width), F32),
            struct((windows, wide_rows, width), BF),
            struct((windows, tall, width), BF),
            struct((windows, tall, width), BF),
            struct((windows, heads, tall, 128), BF),
            struct((rows, width), BF),
            struct((rows, width), F32),
            struct((width, rows), BF),
            struct((rows, ff), BF),
            struct((rows, ff), BF),
            struct((ff, width), BF),
        ],
        out_specs=[
            any_place,
            any_place,
            any_place,
            whole_out((8, width)),
            seen(wide_rows),
            seen(tall),
            seen(tall),
            pl.BlockSpec((2, per, tall, 128), lambda s: (pair(s), group(s), 0, 0)),
            any_place,
            any_place,
            any_place,
            wide,
            wide,
            pl.BlockSpec((chunk, width), lambda s: (later(s), 0)),
        ],
        scratch=[
            pltpu.VMEM((width, rows), BF),
            pltpu.VMEM((rows, width), BF),
            pltpu.VMEM((rows, width), BF),
            pltpu.VMEM((rows, width), BF),
            pltpu.VMEM((rows, width), F32),
            pltpu.VMEM((width, rows), BF),
            pltpu.VMEM((2 * high, width), F32),
            pltpu.VMEM((rows, width), BF),
            pltpu.VMEM((2,) + lead + (3 * columns,), BF),
            pltpu.VMEM(lead + (width,), BF),
            pltpu.VMEM((2,) + lead + (chunk,), BF),
            pltpu.VMEM((rows, width), BF),
            pltpu.VMEM((rows, chunk), F32),
            pltpu.VMEM((cells, windows, width), F32),
            pltpu.VMEM((heads, tall, 128), F32),
            pltpu.VMEM((windows, tall, 128), F32),
            pltpu.VMEM((heads, 384), F32),
            pltpu.VMEM((heads * WS * WS // 4, 256), F32),
            pltpu.SemaphoreType.DMA((11,)),
        ],
        moves=moves,
        collective=collective,
        starts=starts,
    )


def middle_body(made, hook, *refs):
    refs = list(refs)
    take = lambda n: [refs.pop(0) for _ in range(n)]
    act, slope, ws, we_low, we_high, wo, upstream, hidden_t, middle, attended, vec, shrink_sum = take(12)
    result, grad_e, mid, grad_o, dout, small = take(6)
    grad_low, back, sums, rows_of, we, sems = refs
    total = mid
    step = pl.program_id(0)
    chunks = back.shape[0]
    rows, width = mid.shape
    windows, cells, _ = result.shape
    high = rows // windows
    chunk = back.shape[2]

    @pl.when(step == 0)
    def _():
        total[...] = middle[...] + vec[7:8]

    @pl.when(step < chunks)
    def _():
        total[...] += times(act[...], ws[...])
        hook(1)
        product = times_transpose(upstream[...], ws[...])
        here = (product * slope[...].astype(F32)).astype(BF)
        back[step] = here
        line = jnp.sum(here.astype(F32), axis=0, keepdims=True)
        per = width // chunk
        sums[pl.ds(4 + step // per, 1), pl.ds(pl.multiple_of(lax.rem(step, per) * chunk, chunk), chunk)] = line
        hook(2)
        product = times(hidden_t[...], here).astype(BF)

        @pl.when(step < chunks // 2)
        def _():
            at = pl.ds(pl.multiple_of(step * chunk, chunk), chunk)
            grad_low[:, :, :, :, :, at] = product.reshape(grad_low.shape[:5] + (chunk,))

        @pl.when(step >= chunks // 2)
        def _():
            grad_e[...] = product


    @pl.when(step == chunks - 1)
    def _():
        for w in range(windows):
            result[w] = total[pl.ds(w * high, cells)].astype(BF)
        total[...] = jnp.zeros_like(total)

    per_half = chunks // 2

    def load_we(half, index):
        slot = lax.rem(index, 2)
        at = pl.ds(pl.multiple_of((index - half * per_half) * chunk, chunk), chunk)
        return pltpu.make_async_copy((we_low, we_high)[half].at[:, at], we.at[slot], sems.at[slot])

    for half in range(2):

        @pl.when((step >= chunks + half * per_half - 1) & (step < chunks + (half + 1) * per_half - 1))
        def _(half=half):
            load_we(half, step - chunks + 1).start()

    @pl.when(step >= chunks)
    def _():
        index = step - chunks

        for half in range(2):

            @pl.when(index // per_half == half)
            def _(half=half):
                load_we(half, index).wait()

        total[...] += times_transpose(back[index], we[lax.rem(index, 2)])

    @pl.when(step == 2 * chunks - 1)
    def _():
        zero = jnp.zeros((8, width), F32)

        def strip(at, carry):
            gain_sum, shift_sum, out_sum = carry
            normed, rstd = normalize(middle[at])
            value = total[at]
            grad_mid = upstream[at].astype(F32) + norm_back(value, normed, rstd, vec[5:6])
            mid[at] = grad_mid
            low = grad_mid.astype(BF)
            for j in range(2):
                back[j, at] = low[:, j * chunk : j * chunk + chunk]
            return (
                gain_sum + eight(value * normed),
                shift_sum + eight(value),
                out_sum + eight(low.astype(F32)),
            )

        load_wo = [
            pltpu.make_async_copy(wo.at[:, pl.ds(j * chunk, chunk)], we.at[j], sems.at[j])
            for j in range(2)
        ]
        for copy in load_wo:
            copy.start()
        hooks = [functools.partial(hook, part) for part in (1, 2, 3, 4)]
        found = strips(rows, strip, (zero, zero, zero), unroll=1, hooks=hooks)
        gain_sum, shift_sum, out_sum = found
        for i, value in enumerate((out_sum, gain_sum, shift_sum, shrink_sum[...])):
            sums[i : i + 1] = jnp.sum(value, axis=0, keepdims=True)
        rows_of[...] = jnp.zeros_like(rows_of)
        for d in range(32):
            at = pl.ds(128 * (d // 4), 128)
            rows_of[pl.ds(32 * d, 2)] = sums[pl.ds(2 * (d % 4), 2), at]
        small[...] = rows_of[...].astype(BF).reshape(small.shape)
        for j in range(2):
            hook(5 + j)
            at = pl.ds(j * chunk, chunk)
            grad_o[:, at] = transpose_times(attended[...], back[j]).astype(BF)
            if j == 0:
                for copy in load_wo:
                    copy.wait()
            product = times_transpose(back[0], we[0, at])
            product = product + times_transpose(back[1], we[1, at])
            for w in range(windows):
                here = with_rows(product[w * high : (w + 1) * high], dout.shape[1])
                dout[w, :, at] = here.astype(BF)


def middle_part(act, slope, w_shrink, w_low, w_high, w_output, upstream, hidden_t, middle, attended, vec, shrink_sum, windows, cells, moves, collective):
    rows, ff = act.shape
    width = middle.shape[1]
    wide_rows = -(-cells // 128) * 128
    chunk = 512
    chunks = ff // chunk
    early = lambda s: jnp.minimum(s, chunks - 1)
    half = chunks // 2
    later = lambda first: lambda s: (0, jnp.clip(s - first, 0, half - 1))
    wide = pl.BlockSpec((rows, chunk), lambda s: (0, early(s)))
    starts = [[1.2, 1.3, 1.2]] * chunks + [[1.7]] * (chunks - 1) + [[1.7] + [1.5] * 4 + [2.5, 2.5]]
    low = ((4, 2, 2, 2, width // 32, ff // 2), BF)
    scratch = [pltpu.VMEM(*low)] if moves else []
    low_outs = [] if moves else [struct(*low)]
    return call(
        middle_body,
        "middle",
        steps=2 * chunks,
        ins=[act, slope, w_shrink, w_low, w_high, w_output, upstream, hidden_t, middle, attended, vec, shrink_sum],
        in_specs=[
            wide,
            wide,
            pl.BlockSpec((chunk, width), lambda s: (early(s), 0)),
            pl.BlockSpec(memory_space=pl.ANY),
            pl.BlockSpec(memory_space=pl.ANY),
            pl.BlockSpec(memory_space=pl.ANY),
            whole((rows, width)),
            whole((width, rows)),
            whole((rows, width)),
            whole((rows, width)),
            whole(vec.shape),
            whole(shrink_sum.shape),
        ],
        outs=[
            struct((windows, cells, width), BF),
            struct((width, ff // 2), BF),
            struct((rows, width), F32),
            struct((width, width), BF),
            struct((windows, wide_rows, width), BF),
            struct((4, 2, 2, 2, 32, 128), BF),
        ]
        + low_outs,
        out_specs=[
            whole_out((windows, cells, width)),
            pl.BlockSpec((width, chunk), later(half)),
            whole_out((rows, width)),
            whole_out((width, width)),
            whole_out((windows, wide_rows, width)),
            whole_out((4, 2, 2, 2, 32, 128)),
        ]
        + [whole_out(o.shape) for o in low_outs],
        scratch=scratch
        + [
            pltpu.VMEM((chunks, rows, chunk), BF),
            pltpu.VMEM((8, width), F32),
            pltpu.VMEM((32 * 32, 128), F32),
            pltpu.VMEM((2, width, chunk), BF),
            pltpu.SemaphoreType.DMA((2,)),
        ],
        moves=moves,
        collective=collective,
        starts=starts,
    )


def backward_body(groups, made, hook, *refs):
    refs = list(refs)
    take = lambda n: [refs.pop(0) for _ in range(n)]
    query, keys, values, dout, probs, hidden_t, source, mid, vec, counts = take(10)
    w_attend = take(groups)
    out, late = take(2)
    pieces = take(groups)
    bias_low, joint, bias, total, wa, sems = refs
    step = pl.program_id(0)
    windows, _, columns = query.shape
    width, rows = hidden_t.shape
    cells = out.shape[0]
    high = rows // windows
    pairs = windows // 2
    pair = lax.rem(step, pairs)
    group = step // pairs
    scale = 32 ** (-0.5)

    @pl.when(step == 0)
    def _():
        bias_low[...] = jnp.zeros_like(bias_low)
        total[...] = jnp.zeros_like(total)

    @pl.when(step < pairs * groups)
    def _():
        @pl.when(pair == 0)
        def _():
            bias[...] = jnp.zeros_like(bias)

        done = []
        for w in range(2):
            window = pair * 2 + w
            parts = []
            for g in range(columns // 128):
                at = pl.ds(g * 128, 128)
                q, k, v = query[window, :, at], keys[window, :, at], values[window, :, at]
                d = dout[window, :, at]
                slopes = times(v, spread_heads(d.T))
                found, low = [], []
                for h in range(4):
                    prob = probs[w, g * 4 + h]
                    soft = prob.astype(F32)
                    both = soft * slopes[:, 128 * h : 128 * h + 128]
                    ds = (both - soft * jnp.sum(both, axis=0, keepdims=True)).astype(BF)
                    bias[g * 4 + h] += ds.astype(F32)
                    found.append(ds)
                    low.append(prob)
                found = jnp.concatenate(found, axis=1)
                dq = own_heads(times(k.T, found)).T[:high] * scale
                dk = times(found, stack_heads(q))[:high] * scale
                dv = times(jnp.concatenate(low, axis=1), stack_heads(d))[:high]
                parts.append((dq, dk, dv))
            done.append([jnp.concatenate([p[j] for p in parts], axis=1) for j in range(3)])
        at_rows = pl.ds(pl.multiple_of(pair * 2 * high, 16), 2 * high)
        for j in range(3):
            joint[group, at_rows, pl.ds(j * columns, columns)] = jnp.concatenate([done[0][j], done[1][j]], axis=0).astype(BF)

    @pl.when((step < pairs * groups) & (pair == pairs - 1))
    def _():
        hook(1)

    for g in range(groups):

        @pl.when(step == pairs * (g + 1) - 1)
        def _(g=g):
            per = columns // 32
            for h in range(per):
                d = g * per + h
                bias_low[d // 8, (d // 4) % 2, (d // 2) % 2, d % 2, : bias.shape[1]] = bias[h].astype(BF)
            for j in range(3):
                here = joint[g, :, j * columns : (j + 1) * columns]
                product = times(hidden_t[...], here).astype(BF)
                at = pl.ds(j * columns, columns)
                pieces[g][:, :, :, :, :, at] = product.reshape(pieces[g].shape[:5] + (columns,))
                if j != 1:
                    row = pl.ds(2 if j == 0 else 3, 1)
                    here = jnp.sum(here.astype(F32), axis=0, keepdims=True)
                    late[row, pl.ds(g * columns, columns)] = here

    load = lambda g: pltpu.make_async_copy(w_attend[g], wa.at[g % 2], sems.at[g % 2])

    @pl.when(step == pairs * groups - 1)
    def _():
        load(0).start()

    for g in range(groups):

        @pl.when(step == pairs * groups + g)
        def _(g=g):
            load(g).wait()
            if g + 1 < groups:
                load(g + 1).start()
            total[...] += times_transpose(joint[g], flat(wa[g % 2]))

    @pl.when(step == pl.num_programs(0) - 1)
    def _():
        zero = jnp.zeros((8, width), F32)
        inverse = inverse_of(counts)

        def strip(at, carry):
            gain_sum, shift_sum = carry
            normed, rstd = normalize(source[at].astype(F32))
            value = total[at]
            full = mid[at] + norm_back(value, normed, rstd, vec[0:1])
            total[at] = full * inverse
            return gain_sum + eight(value * normed), shift_sum + eight(value)

        hooks = [functools.partial(hook, part) for part in (1, 2, 3, 4, 5, 6)]
        found = strips(rows, strip, (zero, zero), unroll=1, hooks=hooks)
        for i in range(2):
            late[pl.ds(i, 1)] = jnp.sum(found[i], axis=0, keepdims=True)
        for w in range(windows):
            out[:, w, :] = total[pl.ds(w * high, cells)]


def backward_part(query, keys, values, dout, probs, hidden_t, w_attend, source, mid, vec, counts, cells, moves, collective):
    windows, _, width = query.shape
    rows = hidden_t.shape[1]
    tall = keys.shape[1]
    columns = 256
    groups, pairs = width // columns, windows // 2
    per = columns // 32
    steps = groups * pairs
    group = lambda s: jnp.minimum(s // pairs, groups - 1)
    pair = lambda s: jnp.where(s < steps, lax.rem(s, pairs), pairs - 1)
    seen = lambda array: pl.BlockSpec((windows, array.shape[1], columns), lambda s: (0, 0, group(s)))
    lead = (4, 2, 2, 2)
    pieces = [(lead + (width // 32, 3 * columns), BF)] * groups + [(lead + (128, 128), BF)]
    outs = [struct((cells, windows, width), F32), struct((4, width), F32)]
    out_specs = [whole_out((cells, windows, width)), whole_out((4, width))]
    scratch = [
        pltpu.VMEM((groups, rows, 3 * columns), BF),
        pltpu.VMEM((per, tall, 128), F32),
        pltpu.VMEM((rows, width), F32),
        pltpu.VMEM((2,) + lead + (width // 32, 3 * columns), BF),
        pltpu.SemaphoreType.DMA((2,)),
    ]
    if moves:
        scratch = [pltpu.VMEM(*p) for p in pieces] + scratch
    else:
        outs += [struct(*p) for p in pieces]
        out_specs += [whole_out(p[0]) for p in pieces]
    starts = [[1.5], [1.5], [1.5], [1.5, 3.1]] * groups + [[2.7]] * (groups - 1) + [[2.7] + [1.5] * 6]
    return call(
        functools.partial(backward_body, groups),
        "backward",
        steps=steps + groups,
        ins=[query, keys, values, dout, probs, hidden_t, source, mid, vec, counts] + list(w_attend),
        in_specs=[seen(a) for a in (query, keys, values, dout)]
        + [
            pl.BlockSpec((2, per, tall, 128), lambda s: (pair(s), group(s), 0, 0)),
            whole((width, rows)),
            whole((rows, width)),
            whole((rows, width)),
            whole(vec.shape),
            whole(counts.shape),
        ]
        + [pl.BlockSpec(memory_space=pl.ANY)] * groups,
        outs=outs,
        out_specs=out_specs,
        scratch=scratch,
        moves=moves,
        collective=collective,
        starts=starts,
    )


def fresh_moments(grad, first, second, weight, factor):
    clipped = grad * factor
    first_new = MOMENT_ONE * first + (1.0 - MOMENT_ONE) * clipped
    second_new = MOMENT_TWO * second + (1.0 - MOMENT_TWO) * clipped * clipped
    change = (first_new * (1.0 / (1.0 - MOMENT_ONE**STEP))) / (
        jnp.sqrt(second_new * (1.0 / (1.0 - MOMENT_TWO**STEP))) + ADAM_EPS
    ) + DECAY * weight
    return first_new, second_new, change


def inverse_of(counts):
    places = [(d // 8, (d // 4) % 2, (d // 2) % 2, d % 2) for d in range(counts.shape[0] * 8)]
    found = functools.reduce(jnp.add, [counts[at] for at in places])
    return 1.0 / jnp.sum(found, keepdims=True)


def norms_kernel(pieces, *refs):
    refs = list(refs)
    take = lambda n: [refs.pop(0) for _ in range(n)]
    counts, late_sums, bias_sum, small = take(4)
    sums = take(1 + max(p[4] for p in pieces))
    masters, firsts, seconds = take(4), take(4), take(4)
    vec_grad, heads_grad, norms_out = take(3)
    message, got, message_two, got_plane, got_line, sems = refs
    place = Place(sems)
    place.greet(True)
    devices = got.shape[0] * 8
    scale = inverse_of(counts)
    lane = lax.broadcasted_iota(jnp.int32, (8, 128), 1)
    top = lax.broadcasted_iota(jnp.int32, (8, 128), 0) == 0

    def over(rows, body, carry):
        def step(i, value):
            return body(pl.multiple_of(i * 16, 16), value)

        return lax.fori_loop(0, rows // 16, step, carry)

    def fold(value):
        value = eight(value)
        return functools.reduce(
            jnp.add, [value[:, i : i + 128] for i in range(0, value.shape[1], 128)]
        )

    zero = jnp.zeros((8, 128), F32)
    squares = [zero] * 8
    for k, (row, rows), (column, columns), source_column, number in pieces:
        columns_at = pl.ds(column, columns)

        def body(at, carry):
            here = (pl.ds(row + at, 16), columns_at)
            grad = sums[number][pl.ds(at, 16), pl.ds(source_column, columns)] * scale
            weight = masters[k][here]
            return carry[0] + fold(grad * grad), carry[1] + fold(weight * weight)

        squares[k], squares[4 + k] = over(rows, body, (squares[k], squares[4 + k]))

    def packed(values):
        row = zero
        for i, value in enumerate(values):
            row = jnp.where((lane == i) & top, jnp.sum(value), row)
        return row

    message[pl.ds(0, 8)] = packed(squares)
    message[pl.ds(8, 8)] = zero
    message[pl.ds(8, 2)] = small[pl.ds(0, 2)]
    side = 2 * WS - 1
    cell = lax.broadcasted_iota(jnp.int32, (128, 384), 0)
    spot = lax.broadcasted_iota(jnp.int32, (128, 384), 1)
    put = ((cell // WS) * side + lax.rem(cell, WS) == spot) & (cell < WS * WS)
    wide = jnp.dot(bias_sum[...], put.astype(F32), precision=HIGH, preferred_element_type=F32)
    middle = (WS - 1) * side + WS - 1
    column = jnp.zeros((1, 384), F32)
    for j in range(WS * WS):
        shift = middle - (j // WS) * side - j % WS
        column = column + pltpu.roll(wide[j : j + 1], shift, axis=1)
    for b in range(3):
        message[pl.ds(11 + b, 1)] = column[:, 128 * b : 128 * b + 128]
    late_rows = late_sums.shape[0]
    for i in range(late_rows):
        for b in range(8):
            message[pl.ds(16 + 8 * i + b, 1)] = late_sums[i : i + 1, 128 * b : 128 * b + 128]

    events, end = gather_events(place, message, got, 1, False)
    for event, _, _ in events:
        event()
    end()

    place_of = lambda d: (d // 8, (d // 4) % 2, (d // 2) % 2, d % 2)
    found = functools.reduce(jnp.add, [got[place_of(d) + (pl.ds(0, 8),)] for d in range(devices)])
    late = functools.reduce(
        jnp.add, [got[place_of(d) + (pl.ds(16, 8 * late_rows),)] for d in range(devices)]
    )
    for i in range(late_rows):
        for b in range(8):
            vec_grad[pl.ds(i, 1), pl.ds(128 * b, 128)] = late[8 * i + b : 8 * i + b + 1] * scale
    for d in range(devices):
        block = got[place_of(d) + (pl.ds(8, 8),)] * scale
        vec_grad[pl.ds(4 + 2 * (d % 4), 2), pl.ds(128 * (d // 4), 128)] = block[:2]
        for j in range(3):
            heads_grad[pl.ds(d, 1), pl.ds(128 * j, 128)] = block[3 + j : 4 + j]
    small_grad, table_grad = vec_grad[...], heads_grad[...]

    total = lambda value: jnp.sum(value, keepdims=True)
    scalar = lambda k: total(jnp.where(top & (lane == k), found, 0.0))
    grad_square = scalar(0) + scalar(1) + scalar(2) + scalar(3)
    clip_norm = jnp.sqrt(
        grad_square + total(small_grad * small_grad) + total(table_grad * table_grad)
    )
    factor = jnp.minimum(1.0, CLIP_LIMIT / clip_norm)
    squares = [zero] * 4
    for k, (row, rows), (column, columns), source_column, number in pieces:
        columns_at = pl.ds(column, columns)

        def body(at, carry):
            here = (pl.ds(row + at, 16), columns_at)
            grad = sums[number][pl.ds(at, 16), pl.ds(source_column, columns)] * scale
            _, _, change = fresh_moments(
                grad, firsts[k][here], seconds[k][here], masters[k][here], factor
            )
            return carry + fold(change * change)

        squares[k] = over(rows, body, squares[k])

    message_two[...] = packed(squares)
    spot = place.x * 4 + place.y * 2 + place.c
    got_plane[pl.ds(spot, 1)] = message_two[...][None]
    plane = [place.send(message_two, got_plane.at[spot], peer) for peer in place.plane()]
    for copy in plane:
        copy.start()
    for copy in plane:
        copy.wait_recv()
    plane_sum = functools.reduce(jnp.add, [got_plane[i] for i in range(8)])
    got_line[pl.ds(place.z, 1)] = plane_sum[None]
    line = [
        place.send(got_line.at[place.z], got_line.at[place.z], place.to(z=at))
        for at in (place.mate, place.far, place.cross)
    ]
    for copy in line:
        copy.start()
    for copy in line:
        copy.wait_recv()
    second_found = functools.reduce(jnp.add, [got_line[i] for i in range(4)])
    norms = jnp.where(top & (lane == 8), clip_norm, 0.0)
    norms = jnp.where(top & (lane == 9), factor, norms)
    for k in range(4):
        weight_norm = jnp.sqrt(scalar(4 + k))
        update_norm = jnp.sqrt(total(jnp.where(top & (lane == k), second_found, 0.0)))
        norms = jnp.where(top & (lane == k), weight_norm, norms)
        norms = jnp.where(top & (lane == 4 + k), update_norm, norms)
    norms_out[...] = norms
    for copy in plane + line:
        copy.wait_send()


def update_kernel(pieces, *refs):
    refs = list(refs)
    take = lambda n: [refs.pop(0) for _ in range(n)]
    counts, norms, vec_grad, heads_grad = take(4)
    sums = take(1 + max(p[4] for p in pieces))
    masters, firsts, seconds = take(4), take(4), take(4)
    vec, vec_first, vec_second, table, table_first, table_second, carried = take(7)
    grads_out, firsts_out, seconds_out, news_out, copies_out = (take(4) for _ in range(5))
    vec_out, table_out = take(4), take(4)
    clip_out, norms_out, carried_out = take(3)
    carried_out[...] = carried[...]
    scale = inverse_of(counts)
    factor = norms[0:1, 9:10]
    for k, (row, rows), (column, columns), source_column, number in pieces:
        ratio = LEARN_RATE * (norms[0:1, k : k + 1] / norms[0:1, 4 + k : 5 + k])
        columns_at = pl.ds(column, columns)

        def body(i, carry):
            at = pl.multiple_of(i * 16, 16)
            here = (pl.ds(row + at, 16), columns_at)
            grad = sums[number][pl.ds(at, 16), pl.ds(source_column, columns)] * scale
            first, second, change = fresh_moments(
                grad, firsts[k][here], seconds[k][here], masters[k][here], factor
            )
            grads_out[k][here] = grad
            firsts_out[k][here] = first
            seconds_out[k][here] = second
            fresh = masters[k][here] - ratio * change
            news_out[k][here] = fresh
            copies_out[k][here] = fresh.astype(BF)
            return carry

        lax.fori_loop(0, rows // 16, body, 0)

    @pl.when(pl.program_id(0) == 0)
    def _():
        clip_out[...] = norms[0:1, 8:9]
        norms_out[0:1] = norms[0:1, 0:4]
        norms_out[1:2] = norms[0:1, 4:8]
        total = lambda value: jnp.sum(value, keepdims=True)
        grad = vec_grad[...]
        first, second, change = fresh_moments(
            grad, vec_first[...], vec_second[...], vec[...], factor
        )
        rows = lambda value: jnp.sqrt(jnp.sum(value * value, axis=1, keepdims=True))
        vec_out[0][...] = grad
        vec_out[1][...] = first
        vec_out[2][...] = second
        vec_out[3][...] = vec[...] - LEARN_RATE * (rows(vec[...]) / rows(change)) * change
        grad = heads_grad[:, : table.shape[1]]
        first, second, change = fresh_moments(
            grad, table_first[...], table_second[...], table[...], factor
        )
        table_out[0][...] = grad
        table_out[1][...] = first
        table_out[2][...] = second
        ratio = jnp.sqrt(total(table[...] * table[...])) / jnp.sqrt(total(change * change))
        table_out[3][...] = table[...] - LEARN_RATE * ratio * change


def update(collective, counts, late_sums, bias_sum, small, sums, pieces, masters, firsts, seconds, vectors, tables, carried):
    vmem = pl.BlockSpec(memory_space=pltpu.VMEM)
    ins = [counts, late_sums, bias_sum, small] + list(sums)
    ins += list(masters) + list(firsts) + list(seconds)
    vec_grad, heads_grad, norms = pl.pallas_call(
        functools.partial(norms_kernel, pieces),
        name="norms",
        out_shape=[struct(vectors[0].shape, F32), struct((32, 384), F32), struct((8, 128), F32)],
        in_specs=[vmem] * len(ins),
        out_specs=[vmem] * 3,
        scratch_shapes=[
            pltpu.VMEM((48, 128), F32),
            pltpu.VMEM((4, 2, 2, 2, 48, 128), F32),
            pltpu.VMEM((8, 128), F32),
            pltpu.VMEM((8, 8, 128), F32),
            pltpu.VMEM((4, 8, 128), F32),
            pltpu.SemaphoreType.DMA((gather_sems(1) + 20,)),
        ],
        compiler_params=pltpu.CompilerParams(
            collective_id=collective, has_side_effects=True, vmem_limit_bytes=VMEM_LIMIT
        ),
    )(*ins)
    steps = 2
    rows = lambda array: pl.BlockSpec(
        (array.shape[0] // steps, array.shape[1]), lambda s: (s, 0)
    )
    halves = [(k, (row, n // steps), column, source, number) for k, (row, n), column, source, number in pieces]
    tables = [t.T for t in tables]
    ins = [counts, norms, vec_grad, heads_grad] + list(sums)
    ins += list(masters) + list(firsts) + list(seconds) + list(vectors) + list(tables) + [carried]
    in_specs = [whole(a.shape) for a in (counts, norms, vec_grad, heads_grad)]
    in_specs += [rows(a) for a in list(sums) + list(masters) + list(firsts) + list(seconds)]
    in_specs += [whole(a.shape) for a in list(vectors) + list(tables)]
    part = pl.BlockSpec((carried.shape[0] // steps,) + carried.shape[1:], lambda s: (s, 0, 0))
    in_specs.append(part)
    like = lambda arrays, dtype=F32: [struct(a.shape, dtype) for a in arrays]
    outs = like(masters) * 4 + like(masters, BF)
    out_specs = [rows(a) for a in masters] * 5
    outs += like(vectors[:1]) * 4 + like(tables[:1]) * 4
    out_specs += [whole_out(vectors[0].shape)] * 4 + [whole_out(tables[0].shape)] * 4
    outs += [struct((1, 1), F32), struct((2, 4), F32), struct(carried.shape, carried.dtype)]
    out_specs += [whole_out((1, 1)), whole_out((2, 4)), part]
    made = pl.pallas_call(
        functools.partial(update_kernel, halves),
        name="update",
        grid=(steps,),
        out_shape=outs,
        in_specs=in_specs,
        out_specs=out_specs,
        compiler_params=pltpu.CompilerParams(vmem_limit_bytes=VMEM_LIMIT),
    )(*ins)
    matrices = [[made[4 * j + k] for j in range(5)] for k in range(4)]
    return matrices, made[20:24], [t.T for t in made[24:28]], made[28].reshape(()), made[29], made[30]


def local(
    ndp,
    nfs,
    patches,
    cotangent,
    pad_mask,
    attend_weight,
    attend_first,
    attend_second,
    output_weight,
    output_first,
    output_second,
    expand_weight,
    expand_first,
    expand_second,
    shrink_weight,
    shrink_first,
    shrink_second,
    vector_params,
    vector_first,
    vector_second,
    position_table,
    table_first,
    table_second,
):
    windows, cells, width = patches.shape
    keep = pad_mask.astype(jnp.float32)
    keep_block = jnp.pad(keep, ((0, -windows % 16), (0, -cells % 128)))
    devices = ndp * nfs
    shard_rows = min(attend_weight.shape[0], shrink_weight.shape[0])
    direct = nfs == 4 and ndp == 8 and shard_rows % 32 == 0
    masters = (attend_weight, output_weight, expand_weight, shrink_weight)
    part_rows = shrink_weight.shape[0] // 2

    tall = -(-cells // 16) * 16
    keep_rows = jnp.pad(keep, ((0, 0), (0, tall - cells)))[:, :, None]
    keep_rows = jnp.broadcast_to(keep_rows, (windows, tall, 128))
    lead = (4, 2, 2, 2, -1)
    group_columns = [[(j * width + g * 256, 256) for j in range(3)] for g in range(4)]
    half_ff = expand_weight.shape[1] // 2
    gathered, moves = [], []
    if direct:
        moves = [
            *[
                gather(attend_weight, BF, relay=False, need=4 + 4 * g, columns=columns)
                for g, columns in enumerate(group_columns)
            ],
            gather(output_weight, BF, need=20),
            gather(expand_weight, BF, need=21, columns=[(0, half_ff)]),
            gather(expand_weight, BF, need=25, columns=[(half_ff, half_ff)], late=True),
            gather(shrink_weight, BF),
            gather(keep_block, F32, 1, False),
        ]
    else:
        gathered = [
            lax.all_gather(m.astype(BF), AXES, axis=0, tiled=True).reshape(lead + m.shape[1:])
            for m in masters
        ]
        w_attend = [
            jnp.concatenate([gathered[0][..., a : a + n] for a, n in columns], axis=-1)
            for columns in group_columns
        ]
        w_expand = [gathered[2][..., :half_ff], gathered[2][..., half_ff:]]
        gathered = w_attend + gathered[1:2] + w_expand + gathered[3:]
    forward_outs, made = forward(
        patches.transpose(1, 0, 2),
        cotangent.transpose(1, 0, 2),
        keep_rows,
        vector_params,
        position_table.T,
        expand_weight.shape[1],
        () if direct else gathered[:7],
        moves,
        1,
    )
    hidden_t, source, upstream, shrink_sum, query, keys, values, probs = forward_outs[:8]
    attended, middle, hidden_two_t, activated, slope, grad_shrink = forward_outs[8:]
    if direct:
        counts, gathered = made[-1], made[:-1]
    else:
        total = lax.psum(jnp.sum(keep), AXES)
        counts = jnp.zeros((4, 2, 2, 2, 16, 128), F32).at[0, 0, 0, 0, 0, 0].set(total)
    w_attend = gathered[:4]
    w_output, w_low, w_high, w_shrink = (w.reshape(-1, w.shape[-1]) for w in gathered[4:])

    def parts(grad):
        return grad.reshape(lead + grad.shape[-1:])

    if direct:
        moves = [scatter(parts(grad_shrink)), scatter(0, (width // 32, half_ff), step=4)]
    middle_outs, middle_made = middle_part(
        activated,
        slope,
        w_shrink,
        w_low,
        w_high,
        w_output,
        upstream,
        hidden_two_t,
        middle,
        attended,
        vector_params,
        shrink_sum,
        windows,
        cells,
        moves,
        2,
    )
    block_out, grad_expand, grad_middle, grad_output, dout, small = middle_outs[:6]
    if direct:
        piece_shape = (width // 32, 3 * 256)
        moves = [
            scatter(parts(grad_expand)),
            scatter(parts(grad_output)),
            scatter(small, groups=1),
        ]
        moves += [scatter(g, piece_shape, step=4 * (g + 1)) for g in range(4)]
        moves.append(scatter(4, (128, 128), groups=1, step=16))
    backward_outs, made = backward_part(
        query,
        keys,
        values,
        dout,
        probs,
        hidden_t,
        w_attend,
        source,
        grad_middle,
        vector_params,
        counts,
        cells,
        moves,
        3,
    )
    input_grad, late_sums = backward_outs[:2]
    grad_pieces, grad_bias = backward_outs[2:-1], backward_outs[-1]

    def finish_direct(block_out, input_grad, late_sums, made, middle_made, firsts, seconds):
        shrink_owned, low_owned = middle_made
        high_owned, output_owned, small_owned = made[:3]
        bias_owned = made[-1]
        sums = list(made[3:-1]) + [output_owned, low_owned, high_owned, shrink_owned]
        pieces = [
            (0, (0, attend_weight.shape[0]), (j * width + g * 256, 256), j * 256, g)
            for g in range(4)
            for j in range(3)
        ]
        rows = [(0, m.shape[0]) for m in masters]
        pieces += [
            (1, rows[1], (0, width), 0, 4),
            (2, rows[2], (0, half_ff), 0, 5),
            (2, rows[2], (half_ff, half_ff), 0, 6),
            (3, rows[3], (0, width), 0, 7),
        ]
        matrices, vector_outs, table_outs, clip_norm, matrix_norms, input_grad = update(
            4,
            counts,
            late_sums,
            bias_owned,
            small_owned,
            sums,
            pieces,
            masters,
            firsts,
            seconds,
            (vector_params, vector_first, vector_second),
            (position_table, table_first, table_second),
            input_grad,
        )
        outs = [block_out, input_grad.transpose(1, 0, 2)]
        for matrix in matrices:
            outs += matrix
        return (*outs, *vector_outs, *table_outs, clip_norm, matrix_norms)

    firsts = (attend_first, output_first, expand_first, shrink_first)
    seconds = (attend_second, output_second, expand_second, shrink_second)
    if direct:
        return finish_direct(
            block_out, input_grad, late_sums, made, middle_made, firsts, seconds
        )
    grad_expand = jnp.concatenate([middle_outs[6].reshape(width, -1), grad_expand], axis=1)
    grad_attend = jnp.stack([p.reshape(width, 3, -1) for p in grad_pieces], axis=2)
    grad_attend = grad_attend.reshape(width, -1)
    input_grad = input_grad.transpose(1, 0, 2)
    owned = [
        lax.psum_scatter(g.astype(F32), AXES, scatter_dimension=0, tiled=True)
        for g in (grad_attend, grad_output, grad_expand, grad_shrink)
    ]
    index = jnp.pad(position_index(WS).T, ((0, tall - cells), (0, 128 - cells)), constant_values=-1)
    relative = jnp.arange(position_table.shape[0], dtype=jnp.int32)
    onehot = index.reshape(-1)[None, :] == relative[:, None]
    grad_table = lax.dot_general(
        onehot.astype(F32),
        grad_bias.reshape(HEADS, 128, 128)[:, :tall].astype(F32).reshape(HEADS, -1),
        (((1,), (1,)), ((), ())),
        precision=HIGH,
    )
    early_sums = small[..., :2, :].astype(F32).reshape(8, 4, 2, 128).transpose(1, 2, 0, 3).reshape(8, width)
    vector_local = jnp.concatenate([late_sums, early_sums], axis=0)
    vector_sum, table_sum = lax.psum((vector_local, grad_table), AXES)
    vector_grad, table_grad = vector_sum / total, table_sum / total
    matrix_grads = tuple((g / total for g in owned))
    grad_squares = jnp.stack([jnp.sum(g * g) for g in matrix_grads])
    weight_squares = jnp.stack([jnp.sum(m * m) for m in masters])
    grad_total, weight_total = lax.psum((grad_squares, weight_squares), AXES)
    clip_norm = jnp.sqrt(
        jnp.sum(grad_total) + jnp.sum(vector_grad * vector_grad) + jnp.sum(table_grad * table_grad)
    )
    factor = jnp.minimum(1.0, CLIP_LIMIT / clip_norm)
    sectioned = [
        moments(matrix_grads[k], firsts[k], seconds[k], masters[k], factor) for k in range(4)
    ]
    update_squares = jnp.stack([jnp.sum(s[2] * s[2]) for s in sectioned])
    update_total = lax.psum(update_squares, AXES)
    weight_norms = jnp.sqrt(weight_total)
    update_norms = jnp.sqrt(update_total)
    matrix_outs = []
    for k in range(4):
        fresh = masters[k] - LEARN_RATE * (weight_norms[k] / update_norms[k]) * sectioned[k][2]
        matrix_outs.append(
            (matrix_grads[k], sectioned[k][0], sectioned[k][1], fresh, fresh.astype(jnp.bfloat16))
        )
    vec_first, vec_second, vec_update = moments(
        vector_grad, vector_first, vector_second, vector_params, factor
    )
    vec_ratio = jnp.sqrt(jnp.sum(vector_params * vector_params, axis=1, keepdims=True)) / jnp.sqrt(
        jnp.sum(vec_update * vec_update, axis=1, keepdims=True)
    )
    vec_fresh = vector_params - LEARN_RATE * vec_ratio * vec_update
    tab_first, tab_second, tab_update = moments(
        table_grad, table_first, table_second, position_table, factor
    )
    tab_ratio = jnp.sqrt(jnp.sum(position_table * position_table)) / jnp.sqrt(
        jnp.sum(tab_update * tab_update)
    )
    tab_fresh = position_table - LEARN_RATE * tab_ratio * tab_update
    matrix_norms = jnp.stack([weight_norms, update_norms])
    attend_o, output_o, expand_o, shrink_o = matrix_outs
    return (
        block_out,
        input_grad,
        attend_o[0],
        attend_o[1],
        attend_o[2],
        attend_o[3],
        attend_o[4],
        output_o[0],
        output_o[1],
        output_o[2],
        output_o[3],
        output_o[4],
        expand_o[0],
        expand_o[1],
        expand_o[2],
        expand_o[3],
        expand_o[4],
        shrink_o[0],
        shrink_o[1],
        shrink_o[2],
        shrink_o[3],
        shrink_o[4],
        vector_grad,
        vec_first,
        vec_second,
        vec_fresh,
        table_grad,
        tab_first,
        tab_second,
        tab_fresh,
        clip_norm,
        matrix_norms,
    )


def solution(mesh):
    in_specs = (
        P(("dp", "fsdp"), None, None),
        P(("dp", "fsdp"), None, None),
        P(("dp", "fsdp"), None),
        P(("dp", "fsdp"), None),
        P(("dp", "fsdp"), None),
        P(("dp", "fsdp"), None),
        P(("dp", "fsdp"), None),
        P(("dp", "fsdp"), None),
        P(("dp", "fsdp"), None),
        P(("dp", "fsdp"), None),
        P(("dp", "fsdp"), None),
        P(("dp", "fsdp"), None),
        P(("dp", "fsdp"), None),
        P(("dp", "fsdp"), None),
        P(("dp", "fsdp"), None),
        P(),
        P(),
        P(),
        P(),
        P(),
        P(),
    )
    out_specs = (
        P(("dp", "fsdp"), None, None),
        P(("dp", "fsdp"), None, None),
        P(("dp", "fsdp"), None),
        P(("dp", "fsdp"), None),
        P(("dp", "fsdp"), None),
        P(("dp", "fsdp"), None),
        P(("dp", "fsdp"), None),
        P(("dp", "fsdp"), None),
        P(("dp", "fsdp"), None),
        P(("dp", "fsdp"), None),
        P(("dp", "fsdp"), None),
        P(("dp", "fsdp"), None),
        P(("dp", "fsdp"), None),
        P(("dp", "fsdp"), None),
        P(("dp", "fsdp"), None),
        P(("dp", "fsdp"), None),
        P(("dp", "fsdp"), None),
        P(("dp", "fsdp"), None),
        P(("dp", "fsdp"), None),
        P(("dp", "fsdp"), None),
        P(("dp", "fsdp"), None),
        P(("dp", "fsdp"), None),
        P(),
        P(),
        P(),
        P(),
        P(),
        P(),
        P(),
        P(),
        P(),
        P(),
    )
    sizes = (mesh.shape["dp"], mesh.shape["fsdp"])
    return jax.shard_map(functools.partial(local, *sizes), mesh=mesh, in_specs=in_specs, out_specs=out_specs, check_vma=False)
```
